32 devices in a mesh: parts: 2 (over x), space: 8 (over z, y), dp: 2 (over core).
Axes of the slice: x: 2, y: 2, z: 4, core: 2. Of those that a mesh axis runs over, the one named last changes fastest.
Arguments:
- fields: bfloat16 [16, 16, 180, 768], P(('parts', 'dp'), 'space'), parts along dimension 0, may hold values from -6 to 6
- cotangent: bfloat16 [16, 16, 180, 768], P(('parts', 'dp'), 'space'), parts along dimension 0, may hold values from -6 to 6
- w_first: bfloat16 [2, 8, 96, 96], replicated, may hold values from -0.4375 to 0.4375
- b_first: float32 [2, 8, 96], replicated, may hold values from -4 to 4
- w_second: bfloat16 [2, 8, 96, 96], replicated, may hold values from -0.4375 to 0.4375
- b_second: float32 [2, 8, 96], replicated, may hold values from -3 to 3
Outputs:
- output: bfloat16 [16, 16, 180, 768], P(('parts', 'dp'), 'space'), parts along dimension 0
- grad_fields: bfloat16 [16, 16, 180, 768], P(('parts', 'dp'), 'space'), parts along dimension 0
- grad_w_first: float32 [4, 8, 96, 96], P('parts'), parts along dimension 0
- grad_b_first: float32 [4, 8, 96], P('parts'), parts along dimension 0
- grad_w_second: float32 [4, 8, 96, 96], P('parts'), parts along dimension 0
- grad_b_second: float32 [4, 8, 96], P('parts'), parts along dimension 0
The draws below stay inside these ranges and needn't reach their ends.
There are 2 independent parts, one for each index of `parts`. The reference program is written for one: setup_inputs(seed, part) draws one part's arguments, and reference() takes and returns one part's arrays. A program takes and returns all parts, laid end to end along the dimension named above; an argument that names none is the same for every part. Nothing has to cross between parts.
All inputs are finite; a program needn't handle non-finite values.
Results may differ from the reference program's by a relative error of at most 0.012.
The reference program's roundings to bfloat16 on the way count: a program that leaves them out, or rounds other values in their place, can miss the bound.
Values may be sent and summed in bfloat16 or wider, within the bound.
No kernel may reach another device: no remote copies, remote signals or barrier semaphores. Data moves between devices by JAX's collectives and lax.ppermute only.
A program may use at most 128 MiB of HBM per device.

```python
import math
import jax
import jax.numpy as jnp
from jax import lax

D = 768
NB = 8
W = 180
KW = 64
BS = 96
H = 16
B = 8


def block_scale(own_key, extent, pieces, low, largest):
    def one(dim, shards_of):
        heights = jax.random.uniform(jax.random.fold_in(jax.random.fold_in(own_key, 6), dim), (shards_of,), jnp.float32, low / len(pieces), largest / len(pieces))
        return jnp.repeat(jnp.exp(heights), extent[dim] // shards_of).reshape((-1,) + (1,) * (len(extent) - dim - 1))

    factor_of = one(*pieces[0])
    for cut in pieces[1:]:
        factor_of = factor_of * one(*cut)
    return factor_of


def scatter_about(stream_key, shape, spread, limit, pieces=(), kind=jnp.bfloat16):
    array = jax.random.normal(stream_key, shape, jnp.float32) * spread
    if len(pieces) > 0:
        array = block_scale(stream_key, shape, pieces, -0.22, 0.18) * array
    return jnp.clip(array, min=-limit, max=limit).astype(kind)


def setup_inputs(seed: int = 0, part: int = 0) -> dict:
    key_list = jax.random.split(jax.random.key(seed), 7)
    own_keys = jax.random.split(jax.random.fold_in(key_list[6], part), 7)
    return {
        "fields": scatter_about(own_keys[0], (B, H, W, D), 1.0, 6.0, ((0, 2), (1, 8))),
        "cotangent": scatter_about(own_keys[1], (B, H, W, D), 1.0, 6.0, ((0, 2), (1, 8))),
        "w_first": scatter_about(key_list[2], (2, NB, BS, BS), (2 * BS) ** -0.5, 0.4375),
        "b_first": scatter_about(key_list[3], (2, NB, BS), 1.0, 4.0, (), jnp.float32),
        "w_second": scatter_about(key_list[4], (2, NB, BS, BS), (2 * BS) ** -0.5, 0.4375),
        "b_second": scatter_about(key_list[5], (2, NB, BS), 0.5, 3.0, (), jnp.float32),
    }


shrink_level = 0.05

def product_of(pattern, former, latter):
    return jnp.einsum(pattern, former.astype(jnp.float32), latter.astype(jnp.float32), precision=lax.Precision.HIGHEST)

def lon_tables(mode_count, cell_count):
    wavenums = jnp.arange(mode_count, dtype=jnp.int32)
    columns = jnp.arange(cell_count, dtype=jnp.int32)
    phase_index = (wavenums[:, None] * columns[None, :] % cell_count).astype(jnp.float32)
    phases = phase_index * (2.0 * math.pi / cell_count)
    factor = 1.0 / math.sqrt(cell_count)
    forward = jnp.concatenate([jnp.cos(phases) * factor, -jnp.sin(phases) * factor], axis=0)
    doubling = jnp.where(wavenums == 0, 1.0, 2.0).astype(jnp.float32)
    doubling = jnp.concatenate([doubling, doubling])
    inverse = jnp.transpose(forward * doubling[:, None])
    return (forward.astype(jnp.bfloat16), inverse.astype(jnp.bfloat16))

def lat_table(row_count):
    indices = jnp.arange(row_count, dtype=jnp.int32)
    phase_index = (indices[:, None] * indices[None, :] % row_count).astype(jnp.float32)
    phases = phase_index * (2.0 * math.pi / row_count)
    factor = 1.0 / math.sqrt(row_count)
    cosine = jnp.cos(phases) * factor
    sine_part = jnp.sin(phases) * factor
    blocks = jnp.stack([jnp.stack([cosine, sine_part], axis=-1), jnp.stack([-sine_part, cosine], axis=-1)], axis=1)
    return blocks.reshape(2 * row_count, 2 * row_count).astype(jnp.bfloat16)

def to_modes(matrix, pattern, values):
    spectrum = product_of(pattern, matrix, values).astype(jnp.bfloat16)
    return spectrum.reshape(values.shape[0], values.shape[1], 2, -1, values.shape[3])

def to_cells(matrix, pattern, spectrum):
    flattened = spectrum.reshape(spectrum.shape[0], spectrum.shape[1], -1, spectrum.shape[4])
    return product_of(pattern, matrix, flattened)

def finish(base, matrix, pattern, spectrum):
    return (base.astype(jnp.float32) + to_cells(matrix, pattern, spectrum)).astype(jnp.bfloat16)

def lat_apply(matrix, spectrum):
    samples, lat_rows, parts_count, mode_count, channels = spectrum.shape
    flattened = spectrum.reshape(samples, lat_rows * parts_count, mode_count, channels)
    mixed = product_of('pq,bqkd->bpkd', matrix, flattened).astype(jnp.bfloat16)
    return mixed.reshape(samples, lat_rows, parts_count, mode_count, channels)

def split_parts(spectrum, block_count):
    samples, lat_rows, parts_count, mode_count, channels = spectrum.shape
    shape_out = (samples, lat_rows, mode_count, block_count, channels // block_count)
    return (spectrum[:, :, 0].reshape(shape_out), spectrum[:, :, 1].reshape(shape_out))

def join_parts(real_part, imag_part):
    samples, lat_rows, mode_count, block_count, block_size = real_part.shape
    merged = (samples, lat_rows, mode_count, block_count * block_size)
    return jnp.stack([real_part.reshape(merged), imag_part.reshape(merged)], axis=2)

def soft_shrink(values):
    return values - shrink_level * jnp.tanh(values / shrink_level)

def shrink_slope(values):
    bent = jnp.tanh(values / shrink_level)
    return bent * bent

def silu_slope(values):
    logistic = jax.nn.sigmoid(values)
    return logistic * (1.0 + values * (1.0 - logistic))

def complex_mix(real_part, imag_part, weight):
    pattern = 'bhknj,nji->bhkni'
    real_out = product_of(pattern, real_part, weight[0]) - product_of(pattern, imag_part, weight[1])
    imag_out = product_of(pattern, real_part, weight[1]) + product_of(pattern, imag_part, weight[0])
    return (real_out, imag_out)

def complex_back(real_part, imag_part, weight):
    pattern = 'bhkni,nji->bhknj'
    real_out = product_of(pattern, real_part, weight[0]) + product_of(pattern, imag_part, weight[1])
    imag_out = product_of(pattern, imag_part, weight[0]) - product_of(pattern, real_part, weight[1])
    return (real_out, imag_out)

def complex_grad(act_real, act_imag, grad_real, grad_imag):
    pattern = 'bhknj,bhkni->nji'
    real_out = product_of(pattern, act_real, grad_real) + product_of(pattern, act_imag, grad_imag)
    imag_out = product_of(pattern, act_real, grad_imag) - product_of(pattern, act_imag, grad_real)
    return jnp.stack([real_out, imag_out])

def summed_over(values):
    return lax.optimization_barrier(jnp.sum(values.astype(jnp.float32), axis=(0, 1, 2)))

def mlp_forward(mixed_in, w_first, b_first, w_second, b_second):
    real_in, imag_in = split_parts(mixed_in, w_first.shape[1])
    pre_real, pre_imag = complex_mix(real_in, imag_in, w_first)
    pre_real = pre_real + b_first[0]
    pre_imag = pre_imag + b_first[1]
    act_real = jax.nn.silu(pre_real).astype(jnp.bfloat16)
    act_imag = jax.nn.silu(pre_imag).astype(jnp.bfloat16)
    out_real, out_imag = complex_mix(act_real, act_imag, w_second)
    out_real = out_real + b_second[0]
    out_imag = out_imag + b_second[1]
    shrunk = join_parts(soft_shrink(out_real).astype(jnp.bfloat16), soft_shrink(out_imag).astype(jnp.bfloat16))
    return (shrunk, (real_in, imag_in, pre_real, pre_imag, act_real, act_imag, out_real, out_imag))

def shrink_back(cot_lat, forward_state, w_second):
    real_in, imag_in, pre_real, pre_imag, act_real, act_imag, out_real, out_imag = forward_state
    grad_real, grad_imag = split_parts(cot_lat, w_second.shape[1])
    kept_real = (grad_real.astype(jnp.float32) * shrink_slope(out_real)).astype(jnp.bfloat16)
    kept_imag = (grad_imag.astype(jnp.float32) * shrink_slope(out_imag)).astype(jnp.bfloat16)
    sum_w_second = complex_grad(act_real, act_imag, kept_real, kept_imag)
    sum_b_second = jnp.stack([summed_over(kept_real), summed_over(kept_imag)])
    return (kept_real, kept_imag, sum_w_second, sum_b_second)

def act_back(kept_real, kept_imag, forward_state, w_first, w_second):
    real_in, imag_in, pre_real, pre_imag, act_real, act_imag, out_real, out_imag = forward_state
    back_real, back_imag = complex_back(kept_real, kept_imag, w_second)
    gated_real = (back_real * silu_slope(pre_real)).astype(jnp.bfloat16)
    gated_imag = (back_imag * silu_slope(pre_imag)).astype(jnp.bfloat16)
    sum_w_first = complex_grad(real_in, imag_in, gated_real, gated_imag)
    sum_b_first = jnp.stack([summed_over(gated_real), summed_over(gated_imag)])
    into_real, into_imag = complex_back(gated_real, gated_imag, w_first)
    grad_mixed = join_parts(into_real.astype(jnp.bfloat16), into_imag.astype(jnp.bfloat16))
    return (grad_mixed, sum_w_first, sum_b_first)

def reference(fields, cotangent, w_first, b_first, w_second, b_second):
    forward_lon, inverse_lon = lon_tables(KW, W)
    lat_matrix = lat_table(H)
    lat_inverse = jnp.transpose(lat_matrix)
    spectrum = to_modes(forward_lon, 'kw,blwd->blkd', fields)
    mixed_in = lat_apply(lat_matrix, spectrum)
    shrunk, forward_state = mlp_forward(mixed_in, w_first, b_first, w_second, b_second)
    lat_image = lat_apply(lat_inverse, shrunk)
    output = finish(fields, inverse_lon, 'wk,blkd->blwd', lat_image)
    cot_spec = to_modes(inverse_lon, 'wk,blwd->blkd', cotangent)
    cot_lat = lat_apply(lat_matrix, cot_spec)
    kept_real, kept_imag, sum_w_second, sum_b_second = shrink_back(cot_lat, forward_state, w_second)
    grad_mixed, sum_w_first, sum_b_first = act_back(kept_real, kept_imag, forward_state, w_first, w_second)
    grad_spec = lat_apply(lat_inverse, grad_mixed)
    grad_fields = finish(cotangent, forward_lon, 'kw,blkd->blwd', grad_spec)
    factor = 1.0 / math.sqrt(B * H * KW)
    return (output, grad_fields, sum_w_first * factor, sum_b_first * factor, sum_w_second * factor, sum_b_second * factor)
```

```python
import functools
import math

import jax
import jax.numpy as jnp
from jax import lax
from jax.experimental import pallas as pl
from jax.experimental.pallas import tpu as pltpu
from jax.sharding import PartitionSpec as P

KW = 64
shrink_level = 0.05
VMEM_BYTES = 48 * 1024 * 1024


def product_of(former, latter):
    return jnp.dot(former, latter, preferred_element_type=jnp.float32)


def lon_tables(mode_count, cell_count):
    wavenums = jnp.arange(mode_count, dtype=jnp.int32)
    columns = jnp.arange(cell_count, dtype=jnp.int32)
    phase_index = (wavenums[:, None] * columns[None, :] % cell_count).astype(jnp.float32)
    phases = phase_index * (2.0 * math.pi / cell_count)
    factor = 1.0 / math.sqrt(cell_count)
    forward = jnp.concatenate([jnp.cos(phases) * factor, -jnp.sin(phases) * factor], axis=0)
    doubling = jnp.where(wavenums == 0, 1.0, 2.0).astype(jnp.float32)
    doubling = jnp.concatenate([doubling, doubling])
    scaled = forward * doubling[:, None]
    return (forward.astype(jnp.bfloat16), scaled.astype(jnp.bfloat16))


def by_owner(table, owners):
    cells = table.shape[1]
    split = table.reshape(2, owners, -1, cells)
    return jnp.transpose(split, (1, 0, 2, 3)).reshape(-1, cells)


def lat_table(row_count):
    indices = jnp.arange(row_count, dtype=jnp.int32)
    phase_index = (indices[:, None] * indices[None, :] % row_count).astype(jnp.float32)
    phases = phase_index * (2.0 * math.pi / row_count)
    factor = 1.0 / math.sqrt(row_count)
    cosine = jnp.cos(phases) * factor
    sine_part = jnp.sin(phases) * factor
    blocks = jnp.stack(
        [jnp.stack([cosine, sine_part], axis=-1), jnp.stack([-sine_part, cosine], axis=-1)], axis=0
    )
    return blocks.astype(jnp.bfloat16)


def lat_spread(row_count, modes):
    table = lat_table(row_count)
    same = jnp.eye(modes, dtype=jnp.bfloat16)
    spread = table[:, :, None, :, :, None] * same[None, None, :, None, None, :]
    size = 2 * row_count * modes
    return spread.reshape(size, size)


def block_weights(weight, groups):
    _, count, size, _ = weight.shape
    per = count // groups
    parts = weight.reshape(2, groups, per, size, size)
    same = jnp.eye(per, dtype=weight.dtype)
    spread = parts[:, :, :, :, None, :] * same[None, None, :, None, :, None]
    joined = spread.reshape(2, groups, per * size, per * size)
    real, imag = joined[0], joined[1]
    upper = jnp.concatenate([real, imag], axis=-1)
    lower = jnp.concatenate([-imag, real], axis=-1)
    return jnp.concatenate([upper, lower], axis=-2)


def block_bias(bias, groups):
    return jnp.transpose(bias.reshape(2, groups, 1, -1), (1, 2, 0, 3)).reshape(groups, 1, -1)


def params(*semantics):
    return pltpu.CompilerParams(vmem_limit_bytes=VMEM_BYTES, dimension_semantics=semantics)


def to_modes_kernel(table_ref, cells_ref, modes_ref):
    owners, _, rows, _, channels = modes_ref.shape
    for row in range(cells_ref.shape[1]):
        spectrum = product_of(table_ref[...], cells_ref[0, row]).astype(jnp.bfloat16)
        modes_ref[:, 0, row] = spectrum.reshape(owners, -1, channels)


def to_modes(table, cells, owners):
    samples, rows, width, channels = cells.shape
    size = table.shape[0]
    shape = (owners, samples, rows, size // owners, channels)
    return pl.pallas_call(
        to_modes_kernel,
        grid=(samples,),
        out_shape=jax.ShapeDtypeStruct(shape, jnp.bfloat16),
        in_specs=[
            pl.BlockSpec((size, width), lambda b: (0, 0)),
            pl.BlockSpec((1, rows, width, channels), lambda b: (b, 0, 0, 0)),
        ],
        out_specs=pl.BlockSpec((owners, 1) + shape[2:], lambda b: (0, b, 0, 0, 0)),
        compiler_params=params("arbitrary"),
        cost_estimate=pl.CostEstimate(
            flops=2 * samples * rows * size * width * channels,
            bytes_accessed=2 * samples * rows * channels * (width + size),
            transcendentals=0,
        ),
        name="to_modes",
    )(table, cells)


def to_cells_kernel(table_ref, modes_ref, base_ref, out_ref):
    channels = modes_ref.shape[-1]
    for row in range(base_ref.shape[1]):
        spectrum = modes_ref[:, 0, row].reshape(-1, channels)
        image = product_of(table_ref[...], spectrum)
        out_ref[0, row] = (base_ref[0, row].astype(jnp.float32) + image).astype(jnp.bfloat16)


def to_cells(table, modes, base):
    samples, rows, width, channels = base.shape
    size = table.shape[1]
    block = pl.BlockSpec((1, rows, width, channels), lambda b: (b, 0, 0, 0))
    return pl.pallas_call(
        to_cells_kernel,
        grid=(samples,),
        out_shape=jax.ShapeDtypeStruct(base.shape, jnp.bfloat16),
        in_specs=[
            pl.BlockSpec((width, size), lambda b: (0, 0)),
            pl.BlockSpec((modes.shape[0], 1) + modes.shape[2:], lambda b: (0, b, 0, 0, 0)),
            block,
        ],
        out_specs=block,
        compiler_params=params("arbitrary"),
        cost_estimate=pl.CostEstimate(
            flops=2 * samples * rows * size * width * channels,
            bytes_accessed=2 * samples * rows * channels * (2 * width + size),
            transcendentals=0,
        ),
        name="to_cells",
    )(table, modes, base)


def sigmoid_of(values):
    return 0.5 + 0.5 * jnp.tanh(0.5 * values)


def mix_lat(table_ref, bands_ref, mixed_ref):
    samples, width = bands_ref.shape[1], bands_ref.shape[-1]
    half = table_ref.shape[0] // 2
    for sample in range(samples):
        bands = bands_ref[:, sample].reshape(-1, width)
        mixed = product_of(table_ref[...], bands).astype(jnp.bfloat16)
        rows = pl.ds(sample * half, half)
        mixed_ref[rows, 0:width] = mixed[:half]
        mixed_ref[rows, width : 2 * width] = mixed[half:]


def unmix_lat(table_ref, mixed_ref, bands_ref):
    samples, width = bands_ref.shape[1], bands_ref.shape[-1]
    half = table_ref.shape[0] // 2
    for sample in range(samples):
        rows = pl.ds(sample * half, half)
        joined = jnp.concatenate(
            [mixed_ref[rows, 0:width], mixed_ref[rows, width : 2 * width]], axis=0
        )
        bands = product_of(table_ref[...], joined).astype(jnp.bfloat16)
        bands_ref[:, sample] = bands.reshape(
            bands_ref.shape[0], bands_ref.shape[2], bands_ref.shape[3], width
        )


def forward_kernel(
    lat_ref, unlat_ref, bands_ref, w1_ref, b1_ref, w2_ref, b2_ref,
    image_ref, mixed_ref, act_ref, gate_ref, bend_ref, shrunk_ref,
):
    mix_lat(lat_ref, bands_ref, mixed_ref.at[0])
    pre = product_of(mixed_ref[0], w1_ref[0]) + b1_ref[0]
    logistic = sigmoid_of(pre)
    act = pre * logistic
    act_ref[0] = act.astype(jnp.bfloat16)
    gate_ref[0] = logistic + act * (1.0 - logistic)
    out = product_of(act_ref[0], w2_ref[0]) + b2_ref[0]
    bent = jnp.tanh(out * (1.0 / shrink_level))
    bend_ref[0] = bent * bent
    shrunk_ref[...] = (out - shrink_level * bent).astype(jnp.bfloat16)
    unmix_lat(unlat_ref, shrunk_ref, image_ref)


def backward_kernel(
    lat_ref, unlat_ref, bands_ref, w1_ref, w2_ref, mixed_ref, act_ref, gate_ref, bend_ref,
    image_ref, g1_ref, g2_ref, gb1_ref, gb2_ref, cot_ref, kept_ref,
):
    transposed = (((1,), (1,)), ((), ()))
    summed = (((0,), (0,)), ((), ()))

    def times(former, latter, dims):
        return lax.dot_general(former, latter, dims, preferred_element_type=jnp.float32)

    def weight_sums(acts, grads, grad_ref):
        width = acts.shape[1] // 2
        size = grad_ref.shape[-1]
        full = times(acts, grads, summed)
        real = full[:width, :width] + full[width:, width:]
        imag = full[:width, width:] - full[width:, :width]
        for block in range(grad_ref.shape[2]):
            spot = slice(block * size, (block + 1) * size)
            grad_ref[0, 0, block] = real[spot, spot]
            grad_ref[1, 0, block] = imag[spot, spot]

    mix_lat(lat_ref, bands_ref, cot_ref)
    kept_ref[...] = (cot_ref[...].astype(jnp.float32) * bend_ref[0]).astype(jnp.bfloat16)
    gb2_ref[0] = jnp.sum(kept_ref[...].astype(jnp.float32), axis=0, keepdims=True)
    back = times(kept_ref[...], w2_ref[0], transposed)
    cot_ref[...] = (back * gate_ref[0]).astype(jnp.bfloat16)
    weight_sums(act_ref[0], kept_ref[...], g2_ref)
    gb1_ref[0] = jnp.sum(cot_ref[...].astype(jnp.float32), axis=0, keepdims=True)
    kept_ref[...] = times(cot_ref[...], w1_ref[0], transposed).astype(jnp.bfloat16)
    weight_sums(mixed_ref[0], cot_ref[...], g1_ref)
    unmix_lat(unlat_ref, kept_ref, image_ref)


def group_spec(*shape):
    return pl.BlockSpec((1,) + shape, lambda g: (g,) + (0,) * len(shape))


def bands_spec(bands, groups):
    return pl.BlockSpec(bands.shape[:-1] + (bands.shape[-1] // groups,), lambda g: (0, 0, 0, 0, g))


def forward_mid(lat, unlat, bands, w1, b1, w2, b2):
    groups, lanes, _ = w1.shape
    size = lat.shape[0]
    positions = bands.shape[1] * size // 2
    table = pl.BlockSpec((size, size), lambda g: (0, 0))
    state = (groups, positions, lanes)
    state_spec = group_spec(positions, lanes)
    return pl.pallas_call(
        forward_kernel,
        grid=(groups,),
        out_shape=(
            jax.ShapeDtypeStruct(bands.shape, jnp.bfloat16),
            jax.ShapeDtypeStruct(state, jnp.bfloat16),
            jax.ShapeDtypeStruct(state, jnp.bfloat16),
            jax.ShapeDtypeStruct(state, jnp.float32),
            jax.ShapeDtypeStruct(state, jnp.float32),
        ),
        in_specs=[
            table, table, bands_spec(bands, groups),
            group_spec(lanes, lanes), group_spec(1, lanes),
            group_spec(lanes, lanes), group_spec(1, lanes),
        ],
        out_specs=(bands_spec(bands, groups),) + (state_spec,) * 4,
        scratch_shapes=[pltpu.VMEM((positions, lanes), jnp.bfloat16)],
        compiler_params=params("arbitrary"),
        cost_estimate=pl.CostEstimate(
            flops=4 * groups * positions * lanes * lanes,
            bytes_accessed=16 * groups * positions * lanes + 4 * groups * lanes * lanes,
            transcendentals=2 * groups * positions * lanes,
        ),
        name="mix_forward",
    )(lat, unlat, bands, w1, b1, w2, b2)


def backward_mid(lat, unlat, bands, w1, w2, state, count):
    groups, lanes, _ = w1.shape
    size = lat.shape[0]
    positions = bands.shape[1] * size // 2
    table = pl.BlockSpec((size, size), lambda g: (0, 0))
    state_spec = group_spec(positions, lanes)
    per = count // groups
    edge = lanes // 2 // per
    grad = jax.ShapeDtypeStruct((2, groups, per, edge, edge), jnp.float32)
    grad_spec = pl.BlockSpec((2, 1, per, edge, edge), lambda g: (0, g, 0, 0, 0))
    bias = jax.ShapeDtypeStruct((groups, 1, lanes), jnp.float32)
    return pl.pallas_call(
        backward_kernel,
        grid=(groups,),
        out_shape=(
            jax.ShapeDtypeStruct(bands.shape, jnp.bfloat16), grad, grad, bias, bias,
        ),
        in_specs=[
            table, table, bands_spec(bands, groups),
            group_spec(lanes, lanes), group_spec(lanes, lanes),
        ] + [state_spec] * 4,
        out_specs=(
            bands_spec(bands, groups), grad_spec, grad_spec,
            group_spec(1, lanes), group_spec(1, lanes),
        ),
        scratch_shapes=[pltpu.VMEM((positions, lanes), jnp.bfloat16)] * 2,
        compiler_params=params("arbitrary"),
        cost_estimate=pl.CostEstimate(
            flops=8 * groups * positions * lanes * lanes,
            bytes_accessed=16 * groups * positions * lanes + 4 * groups * lanes * lanes,
            transcendentals=0,
        ),
        name="mix_backward",
    )(lat, unlat, bands, w1, w2, *state)


def body(fields, cotangent, w_first, b_first, w_second, b_second):
    samples, rows, width, channels = fields.shape
    owners = lax.axis_size("space")
    lat_total = rows * owners
    modes = KW // owners
    count = w_first.shape[1]
    groups = 2
    direct = 2 * modes % 16 == 0
    lead = owners if direct else 1
    share = (owners, samples, rows, 2 * modes, channels)

    def send_out(spectrum):
        if not direct:
            spectrum = spectrum.reshape(samples, rows, owners, 2 * modes, channels)
            spectrum = jnp.transpose(spectrum, (2, 0, 1, 3, 4))
        arrived = lax.all_to_all(spectrum, "space", split_axis=0, concat_axis=0, tiled=True)
        if not direct:
            arrived = jnp.transpose(arrived, (1, 0, 2, 3, 4)).reshape(1, samples, 1, -1, channels)
        return arrived

    def send_back(bands):
        if not direct:
            bands = bands.reshape(samples, owners, rows, 2 * modes, channels)
            bands = jnp.transpose(bands, (1, 0, 2, 3, 4))
        arrived = lax.all_to_all(bands, "space", split_axis=0, concat_axis=0, tiled=True)
        if not direct:
            arrived = jnp.transpose(arrived, (1, 2, 0, 3, 4)).reshape(1, samples, rows, -1, channels)
        return arrived

    plain, scaled = lon_tables(KW, width)
    plain, scaled = by_owner(plain, owners), by_owner(scaled, owners)
    spectrum = to_modes(plain, fields, lead)
    spectrum, cotangent, scaled, w_first, w_second = lax.optimization_barrier(
        (spectrum, cotangent, scaled, w_first, w_second)
    )
    gathered = send_out(spectrum)
    cot_spec = to_modes(scaled, cotangent, lead)
    cot_gathered = send_out(cot_spec)

    lat = lat_spread(lat_total, modes)
    unlat = jnp.transpose(lat)
    w1, w2 = block_weights(w_first, groups), block_weights(w_second, groups)
    b1, b2 = block_bias(b_first, groups), block_bias(b_second, groups)
    image, *state = forward_mid(lat, unlat, gathered, w1, b1, w2, b2)
    image_band = send_back(image)
    grad_image, sum_w_first, sum_w_second, sum_b_first, sum_b_second = backward_mid(
        lat, unlat, cot_gathered, w1, w2, state, count
    )
    grad_band = send_back(grad_image)
    output = to_cells(jnp.transpose(scaled), image_band, fields)
    grad_fields = to_cells(jnp.transpose(plain), grad_band, cotangent)

    def bias_of(sums):
        split = sums.reshape(groups, 2, count // groups, -1)
        return jnp.transpose(split, (1, 0, 2, 3)).reshape(b_first.shape)

    sums = lax.psum(
        (
            sum_w_first.reshape(w_first.shape), bias_of(sum_b_first),
            sum_w_second.reshape(w_first.shape), bias_of(sum_b_second),
        ),
        ("space", "dp"),
    )
    positions = samples * lax.axis_size("dp") * lat_total * KW
    factor = 1.0 / math.sqrt(positions)
    return (output, grad_fields) + tuple(value * factor for value in sums)


def solution(mesh):
    split = P(("parts", "dp"), "space", None, None)
    in_specs = (split, split, P(), P(), P(), P())
    out_specs = (
        split,
        split,
        P("parts", None, None, None),
        P("parts", None, None),
        P("parts", None, None, None),
        P("parts", None, None),
    )
    return jax.shard_map(body, mesh=mesh, in_specs=in_specs, out_specs=out_specs, check_vma=False)
```

```python
import functools
import math

import jax
import jax.numpy as jnp
from jax import lax
from jax.experimental import pallas as pl
from jax.experimental.pallas import tpu as pltpu
from jax.sharding import PartitionSpec as P
import ml_dtypes
import numpy as np

KW = 64
shrink_level = 0.05
VMEM_BYTES = 48 * 1024 * 1024


def product_of(former, latter):
    return jnp.dot(former, latter, preferred_element_type=jnp.float32)


def lon_tables(mode_count, cell_count, owners):
    wavenums = np.arange(mode_count, dtype=np.int32)
    columns = np.arange(cell_count, dtype=np.int32)
    phase_index = (wavenums[:, None] * columns[None, :] % cell_count).astype(np.float32)
    phases = phase_index * np.float32(2.0 * math.pi / cell_count)
    factor = np.float32(1.0 / math.sqrt(cell_count))
    forward = np.stack([np.cos(phases) * factor, -np.sin(phases) * factor])
    scaled = forward * np.where(wavenums == 0, 1.0, 2.0).astype(np.float32)[:, None]

    def ordered(table):
        split = table.reshape(2, owners, -1, cell_count).transpose(1, 0, 2, 3)
        return split.reshape(-1, cell_count).astype(ml_dtypes.bfloat16)

    return ordered(forward), ordered(scaled)


def lat_spread(row_count, modes):
    indices = np.arange(row_count, dtype=np.int32)
    phase_index = (indices[:, None] * indices[None, :] % row_count).astype(np.float32)
    phases = phase_index * np.float32(2.0 * math.pi / row_count)
    factor = np.float32(1.0 / math.sqrt(row_count))
    cosine = np.cos(phases) * factor
    sine_part = np.sin(phases) * factor
    table = np.stack([np.stack([cosine, sine_part], -1), np.stack([-sine_part, cosine], -1)])
    same = np.eye(modes, dtype=np.float32)
    spread = table[:, :, None, :, :, None] * same[None, None, :, None, None, :]
    size = 2 * row_count * modes
    return spread.reshape(size, size).astype(ml_dtypes.bfloat16)


def block_bias(bias, groups):
    return jnp.transpose(bias.reshape(2, groups, 1, -1), (1, 2, 0, 3)).reshape(groups, 1, -1)


def spread_kernel(*refs):
    half_way = len(refs) // 2
    for blocks_ref, joined_ref in zip(refs[:half_way], refs[half_way:]):
        _, per, size, _ = blocks_ref.shape
        width = per * size
        row = lax.broadcasted_iota(jnp.int32, (size, width), 0)
        lane = lax.broadcasted_iota(jnp.int32, (size, width), 1)
        for block in range(per):
            place = (row + block * size == lane).astype(jnp.bfloat16)
            real = product_of(blocks_ref[0, block], place).astype(jnp.bfloat16)
            imag = product_of(blocks_ref[1, block], place)
            upper = pl.ds(block * size, size)
            lower = pl.ds(width + block * size, size)
            joined_ref[0, upper, 0:width] = real
            joined_ref[0, upper, width : 2 * width] = imag.astype(jnp.bfloat16)
            joined_ref[0, lower, 0:width] = (-imag).astype(jnp.bfloat16)
            joined_ref[0, lower, width : 2 * width] = real


def spread_weights(groups, *weights):
    _, count, size, _ = weights[0].shape
    per = count // groups
    lanes = 2 * per * size
    shape = jax.ShapeDtypeStruct((groups, lanes, lanes), jnp.bfloat16)
    return pl.pallas_call(
        spread_kernel,
        grid=(groups,),
        out_shape=(shape,) * len(weights),
        in_specs=[pl.BlockSpec((2, per, size, size), lambda g: (0, g, 0, 0))] * len(weights),
        out_specs=(group_spec(lanes, lanes),) * len(weights),
        compiler_params=params("arbitrary"),
        cost_estimate=pl.CostEstimate(
            flops=len(weights) * 2 * count * size * size * lanes,
            bytes_accessed=len(weights) * 2 * groups * lanes * lanes,
            transcendentals=0,
        ),
        name="spread_weights",
    )(*weights)


def params(*semantics):
    return pltpu.CompilerParams(vmem_limit_bytes=VMEM_BYTES, dimension_semantics=semantics)


def to_modes_kernel(table_ref, cells_ref, modes_ref):
    owners, _, rows, _, channels = modes_ref.shape
    for row in range(cells_ref.shape[1]):
        spectrum = product_of(table_ref[...], cells_ref[0, row]).astype(jnp.bfloat16)
        modes_ref[:, 0, row] = spectrum.reshape(owners, -1, channels)


def to_modes(table, cells, owners):
    samples, rows, width, channels = cells.shape
    size = table.shape[0]
    shape = (owners, samples, rows, size // owners, channels)
    return pl.pallas_call(
        to_modes_kernel,
        grid=(samples,),
        out_shape=jax.ShapeDtypeStruct(shape, jnp.bfloat16),
        in_specs=[
            pl.BlockSpec((size, width), lambda b: (0, 0)),
            pl.BlockSpec((1, rows, width, channels), lambda b: (b, 0, 0, 0)),
        ],
        out_specs=pl.BlockSpec((owners, 1) + shape[2:], lambda b: (0, b, 0, 0, 0)),
        compiler_params=params("arbitrary"),
        cost_estimate=pl.CostEstimate(
            flops=2 * samples * rows * size * width * channels,
            bytes_accessed=2 * samples * rows * channels * (width + size),
            transcendentals=0,
        ),
        name="to_modes",
    )(table, cells)


def to_cells_kernel(table_ref, modes_ref, base_ref, out_ref):
    channels = modes_ref.shape[-1]
    for row in range(base_ref.shape[1]):
        spectrum = modes_ref[:, 0, row].reshape(-1, channels)
        image = product_of(table_ref[...], spectrum)
        out_ref[0, row] = (base_ref[0, row].astype(jnp.float32) + image).astype(jnp.bfloat16)


def to_cells(table, modes, base):
    samples, rows, width, channels = base.shape
    size = table.shape[1]
    block = pl.BlockSpec((1, rows, width, channels), lambda b: (b, 0, 0, 0))
    return pl.pallas_call(
        to_cells_kernel,
        grid=(samples,),
        out_shape=jax.ShapeDtypeStruct(base.shape, jnp.bfloat16),
        in_specs=[
            pl.BlockSpec((width, size), lambda b: (0, 0)),
            pl.BlockSpec((modes.shape[0], 1) + modes.shape[2:], lambda b: (0, b, 0, 0, 0)),
            block,
        ],
        out_specs=block,
        compiler_params=params("arbitrary"),
        cost_estimate=pl.CostEstimate(
            flops=2 * samples * rows * size * width * channels,
            bytes_accessed=2 * samples * rows * channels * (2 * width + size),
            transcendentals=0,
        ),
        name="to_cells",
    )(table, modes, base)


def sigmoid_of(values):
    return 0.5 + 0.5 * jnp.tanh(0.5 * values)


def mix_lat(table_ref, bands_ref, mixed_ref):
    samples, width = bands_ref.shape[1], bands_ref.shape[-1]
    half = table_ref.shape[0] // 2
    for sample in range(samples):
        bands = bands_ref[:, sample].reshape(-1, width)
        mixed = product_of(table_ref[...], bands).astype(jnp.bfloat16)
        rows = pl.ds(sample * half, half)
        mixed_ref[rows, 0:width] = mixed[:half]
        mixed_ref[rows, width : 2 * width] = mixed[half:]


def unmix_lat(table_ref, mixed_ref, bands_ref):
    samples, width = bands_ref.shape[1], bands_ref.shape[-1]
    half = table_ref.shape[0] // 2
    for sample in range(samples):
        rows = pl.ds(sample * half, half)
        joined = jnp.concatenate(
            [mixed_ref[rows, 0:width], mixed_ref[rows, width : 2 * width]], axis=0
        )
        bands = product_of(table_ref[...], joined).astype(jnp.bfloat16)
        bands_ref[:, sample] = bands.reshape(
            bands_ref.shape[0], bands_ref.shape[2], bands_ref.shape[3], width
        )


def forward_kernel(
    lat_ref, unlat_ref, bands_ref, w1_ref, b1_ref, w2_ref, b2_ref,
    image_ref, mixed_ref, act_ref, gate_ref, bend_ref, shrunk_ref,
):
    mix_lat(lat_ref, bands_ref, mixed_ref.at[0])
    pre = product_of(mixed_ref[0], w1_ref[0]) + b1_ref[0]
    logistic = sigmoid_of(pre)
    act = pre * logistic
    act_ref[0] = act.astype(jnp.bfloat16)
    gate_ref[0] = logistic + act * (1.0 - logistic)
    out = product_of(act_ref[0], w2_ref[0]) + b2_ref[0]
    bent = jnp.tanh(out * (1.0 / shrink_level))
    bend_ref[0] = bent * bent
    shrunk_ref[...] = (out - shrink_level * bent).astype(jnp.bfloat16)
    unmix_lat(unlat_ref, shrunk_ref, image_ref)


def backward_kernel(
    block_size, lat_ref, unlat_ref, bands_ref, w1_ref, w2_ref, mixed_ref, act_ref, gate_ref, bend_ref,
    image_ref, sums_ref, cot_ref, kept_ref,
):
    transposed = (((1,), (1,)), ((), ()))
    summed = (((0,), (0,)), ((), ()))

    def times(former, latter, dims):
        return lax.dot_general(former, latter, dims, preferred_element_type=jnp.float32)

    def weight_sums(acts, grads, slot):
        width = acts.shape[1] // 2
        full = times(acts, grads, summed)
        real = full[:width, :width] + full[width:, width:]
        imag = full[:width, width:] - full[width:, :width]
        bias = jnp.sum(grads.astype(jnp.float32), axis=0, keepdims=True)
        size = block_size
        owner = lax.broadcasted_iota(jnp.int32, (size, width), 1) // size
        extra = sums_ref.shape[3] - size
        first = lax.broadcasted_iota(jnp.int32, (extra, width), 0) == 0
        for part, values in enumerate((real, imag)):
            joined = values[:size]
            for block in range(1, width // size):
                joined = jnp.where(owner == block, values[block * size : (block + 1) * size], joined)
            sums_ref[slot, part, 0, 0:size] = joined
            row = bias[:, part * width : (part + 1) * width]
            sums_ref[slot, part, 0, size:] = jnp.where(first, row, 0.0)

    mix_lat(lat_ref, bands_ref, cot_ref)
    kept_ref[...] = (cot_ref[...].astype(jnp.float32) * bend_ref[0]).astype(jnp.bfloat16)
    back = times(kept_ref[...], w2_ref[0], transposed)
    cot_ref[...] = (back * gate_ref[0]).astype(jnp.bfloat16)
    weight_sums(act_ref[0], kept_ref[...], 1)
    kept_ref[...] = times(cot_ref[...], w1_ref[0], transposed).astype(jnp.bfloat16)
    weight_sums(mixed_ref[0], cot_ref[...], 0)
    unmix_lat(unlat_ref, kept_ref, image_ref)


def group_spec(*shape):
    return pl.BlockSpec((1,) + shape, lambda g: (g,) + (0,) * len(shape))


def bands_spec(bands, groups):
    return pl.BlockSpec(bands.shape[:-1] + (bands.shape[-1] // groups,), lambda g: (0, 0, 0, 0, g))


def forward_mid(lat, unlat, bands, w1, b1, w2, b2):
    groups, lanes, _ = w1.shape
    size = lat.shape[0]
    positions = bands.shape[1] * size // 2
    table = pl.BlockSpec((size, size), lambda g: (0, 0))
    state = (groups, positions, lanes)
    state_spec = group_spec(positions, lanes)
    return pl.pallas_call(
        forward_kernel,
        grid=(groups,),
        out_shape=(
            jax.ShapeDtypeStruct(bands.shape, jnp.bfloat16),
            jax.ShapeDtypeStruct(state, jnp.bfloat16),
            jax.ShapeDtypeStruct(state, jnp.bfloat16),
            jax.ShapeDtypeStruct(state, jnp.float32),
            jax.ShapeDtypeStruct(state, jnp.float32),
        ),
        in_specs=[
            table, table, bands_spec(bands, groups),
            group_spec(lanes, lanes), group_spec(1, lanes),
            group_spec(lanes, lanes), group_spec(1, lanes),
        ],
        out_specs=(bands_spec(bands, groups),) + (state_spec,) * 4,
        scratch_shapes=[pltpu.VMEM((positions, lanes), jnp.bfloat16)],
        compiler_params=params("arbitrary"),
        cost_estimate=pl.CostEstimate(
            flops=4 * groups * positions * lanes * lanes,
            bytes_accessed=16 * groups * positions * lanes + 4 * groups * lanes * lanes,
            transcendentals=2 * groups * positions * lanes,
        ),
        name="mix_forward",
    )(lat, unlat, bands, w1, b1, w2, b2)


def backward_mid(lat, unlat, bands, w1, w2, state, count):
    groups, lanes, _ = w1.shape
    size = lat.shape[0]
    positions = bands.shape[1] * size // 2
    table = pl.BlockSpec((size, size), lambda g: (0, 0))
    state_spec = group_spec(positions, lanes)
    size_of_block = lanes // 2 // (count // groups)
    rows = size_of_block + 16
    return pl.pallas_call(
        functools.partial(backward_kernel, size_of_block),
        grid=(groups,),
        out_shape=(
            jax.ShapeDtypeStruct(bands.shape, jnp.bfloat16),
            jax.ShapeDtypeStruct((2, 2, groups, rows, lanes // 2), jnp.float32),
        ),
        in_specs=[
            table, table, bands_spec(bands, groups),
            group_spec(lanes, lanes), group_spec(lanes, lanes),
        ] + [state_spec] * 4,
        out_specs=(
            bands_spec(bands, groups),
            pl.BlockSpec((2, 2, 1, rows, lanes // 2), lambda g: (0, 0, g, 0, 0)),
        ),
        scratch_shapes=[pltpu.VMEM((positions, lanes), jnp.bfloat16)] * 2,
        compiler_params=params("arbitrary"),
        cost_estimate=pl.CostEstimate(
            flops=8 * groups * positions * lanes * lanes,
            bytes_accessed=16 * groups * positions * lanes + 4 * groups * lanes * lanes,
            transcendentals=0,
        ),
        name="mix_backward",
    )(lat, unlat, bands, w1, w2, *state)


def swap_with(values, axis, distance):
    size = lax.axis_size(axis)
    return lax.ppermute(values, axis, [(i, i ^ distance) for i in range(size)])


def summed_over_group(sums):
    lanes = sums.shape[-1]
    held = sums.reshape(-1, lanes)
    steps = [("dp", 1, jnp.float32)]
    distance = 1
    while distance < lax.axis_size("space"):
        steps.append(("space", distance, jnp.float32 if distance == 1 else jnp.bfloat16))
        distance *= 2
    for axis, distance, kind in steps:
        side = lax.axis_index(axis) // distance % 2
        pair = held.reshape(2, -1, lanes)
        given = lax.dynamic_index_in_dim(pair, 1 - side, 0, keepdims=False).astype(kind)
        taken = swap_with(given, axis, distance)
        held = lax.dynamic_index_in_dim(pair, side, 0, keepdims=False) + taken.astype(jnp.float32)
    held = held.astype(jnp.bfloat16)
    for axis, distance, _ in reversed(steps):
        side = lax.axis_index(axis) // distance % 2
        taken = swap_with(held, axis, distance)
        held = jnp.where(
            side == 0, jnp.concatenate([held, taken]), jnp.concatenate([taken, held])
        )
    return held.reshape(sums.shape)


def body(fields, cotangent, w_first, b_first, w_second, b_second):
    samples, rows, width, channels = fields.shape
    owners = lax.axis_size("space")
    lat_total = rows * owners
    modes = KW // owners
    count, edge = w_first.shape[1:3]
    groups = 2
    direct = 2 * modes % 16 == 0
    lead = owners if direct else 1

    def send_out(spectrum):
        if not direct:
            spectrum = spectrum.reshape(samples, rows, owners, 2 * modes, channels)
            spectrum = jnp.transpose(spectrum, (2, 0, 1, 3, 4))
        arrived = lax.all_to_all(spectrum, "space", split_axis=0, concat_axis=0, tiled=True)
        if not direct:
            arrived = jnp.transpose(arrived, (1, 0, 2, 3, 4)).reshape(1, samples, 1, -1, channels)
        return arrived

    def send_back(bands):
        if not direct:
            bands = bands.reshape(samples, owners, rows, 2 * modes, channels)
            bands = jnp.transpose(bands, (1, 0, 2, 3, 4))
        arrived = lax.all_to_all(bands, "space", split_axis=0, concat_axis=0, tiled=True)
        if not direct:
            arrived = jnp.transpose(arrived, (1, 2, 0, 3, 4)).reshape(1, samples, rows, -1, channels)
        return arrived

    plain, scaled = lon_tables(KW, width, owners)
    lat = lat_spread(lat_total, modes)

    spectrum = to_modes(plain, fields, lead)
    spectrum, cotangent, w_first, w_second = lax.optimization_barrier(
        (spectrum, cotangent, w_first, w_second)
    )
    gathered = send_out(spectrum)
    cot_spec = to_modes(scaled, cotangent, lead)
    w1, w2 = spread_weights(groups, w_first, w_second)
    b1, b2 = block_bias(b_first, groups), block_bias(b_second, groups)
    cot_spec, w1, w2, b1, b2 = lax.optimization_barrier((cot_spec, w1, w2, b1, b2))
    cot_gathered = send_out(cot_spec)

    image, *state = forward_mid(lat, lat.T, gathered, w1, b1, w2, b2)
    image_band = send_back(image)
    grad_image, sums = backward_mid(lat, lat.T, cot_gathered, w1, w2, state, count)
    grad_band = send_back(grad_image)
    output = to_cells(scaled.T, image_band, fields)
    grad_fields = to_cells(plain.T, grad_band, cotangent)

    positions = samples * lax.axis_size("dp") * lat_total * KW
    factor = 1.0 / math.sqrt(positions)
    sums = summed_over_group(sums).astype(jnp.float32) * factor
    grads = []
    for which in range(2):
        blocks = sums[which, :, :, :edge].reshape(2, groups, edge, count // groups, edge)
        grads.append(jnp.transpose(blocks, (0, 1, 3, 2, 4)).reshape(w_first.shape))
        grads.append(sums[which, :, :, edge].reshape(b_first.shape))
    return (output, grad_fields) + tuple(grads)


def solution(mesh):
    split = P(("parts", "dp"), "space", None, None)
    in_specs = (split, split, P(), P(), P(), P())
    out_specs = (
        split,
        split,
        P("parts", None, None, None),
        P("parts", None, None),
        P("parts", None, None, None),
        P("parts", None, None),
    )
    return jax.shard_map(body, mesh=mesh, in_specs=in_specs, out_specs=out_specs, check_vma=False)
```

```python
import functools
import math

import jax
import jax.numpy as jnp
from jax import lax
from jax.experimental import pallas as pl
from jax.experimental.pallas import tpu as pltpu
from jax.sharding import PartitionSpec as P
import ml_dtypes
import numpy as np

KW = 64
shrink_level = 0.05
VMEM_BYTES = 48 * 1024 * 1024


def product_of(former, latter):
    return jnp.dot(former, latter, preferred_element_type=jnp.float32)


def lon_tables(mode_count, cell_count, owners):
    wavenums = np.arange(mode_count, dtype=np.int32)
    columns = np.arange(cell_count, dtype=np.int32)
    phase_index = (wavenums[:, None] * columns[None, :] % cell_count).astype(np.float32)
    phases = phase_index * np.float32(2.0 * math.pi / cell_count)
    factor = np.float32(1.0 / math.sqrt(cell_count))
    forward = np.stack([np.cos(phases) * factor, -np.sin(phases) * factor])
    scaled = forward * np.where(wavenums == 0, 1.0, 2.0).astype(np.float32)[:, None]

    def ordered(table):
        split = table.reshape(2, owners, -1, cell_count).transpose(1, 0, 2, 3)
        return split.reshape(-1, cell_count).astype(ml_dtypes.bfloat16)

    return ordered(forward), ordered(scaled)


def lat_spread(row_count, modes):
    indices = np.arange(row_count, dtype=np.int32)
    phase_index = (indices[:, None] * indices[None, :] % row_count).astype(np.float32)
    phases = phase_index * np.float32(2.0 * math.pi / row_count)
    factor = np.float32(1.0 / math.sqrt(row_count))
    cosine = np.cos(phases) * factor
    sine_part = np.sin(phases) * factor
    table = np.stack([np.stack([cosine, sine_part], -1), np.stack([-sine_part, cosine], -1)])
    same = np.eye(modes, dtype=np.float32)
    spread = table[:, :, None, :, :, None] * same[None, None, :, None, None, :]
    size = 2 * row_count * modes
    return spread.reshape(size, size).astype(ml_dtypes.bfloat16)


def block_bias(bias, groups):
    return jnp.transpose(bias.reshape(2, groups, 1, -1), (1, 2, 0, 3)).reshape(groups, 1, -1)


def spread_kernel(*refs):
    half_way = len(refs) // 2
    for blocks_ref, joined_ref in zip(refs[:half_way], refs[half_way:]):
        _, per, size, _ = blocks_ref.shape
        width = per * size
        row = lax.broadcasted_iota(jnp.int32, (size, width), 0)
        lane = lax.broadcasted_iota(jnp.int32, (size, width), 1)
        for block in range(per):
            place = (row + block * size == lane).astype(jnp.bfloat16)
            real = product_of(blocks_ref[0, block], place).astype(jnp.bfloat16)
            imag = product_of(blocks_ref[1, block], place)
            upper = pl.ds(block * size, size)
            lower = pl.ds(width + block * size, size)
            joined_ref[0, upper, 0:width] = real
            joined_ref[0, upper, width : 2 * width] = imag.astype(jnp.bfloat16)
            joined_ref[0, lower, 0:width] = (-imag).astype(jnp.bfloat16)
            joined_ref[0, lower, width : 2 * width] = real


def spread_weights(groups, *weights):
    _, count, size, _ = weights[0].shape
    per = count // groups
    lanes = 2 * per * size
    shape = jax.ShapeDtypeStruct((groups, lanes, lanes), jnp.bfloat16)
    return pl.pallas_call(
        spread_kernel,
        grid=(groups,),
        out_shape=(shape,) * len(weights),
        in_specs=[pl.BlockSpec((2, per, size, size), lambda g: (0, g, 0, 0))] * len(weights),
        out_specs=(group_spec(lanes, lanes),) * len(weights),
        compiler_params=params("arbitrary"),
        cost_estimate=pl.CostEstimate(
            flops=len(weights) * 2 * count * size * size * lanes,
            bytes_accessed=len(weights) * 2 * groups * lanes * lanes,
            transcendentals=0,
        ),
        name="spread_weights",
    )(*weights)


def params(*semantics):
    return pltpu.CompilerParams(vmem_limit_bytes=VMEM_BYTES, dimension_semantics=semantics)


def place_of(me_ref, offset, rows):
    return pl.ds(pl.multiple_of((me_ref[0] ^ offset) * rows, rows), rows)


def to_modes_kernel(me_ref, table_ref, cells_ref, *refs):
    modes_refs, held_ref = refs[:-1], refs[-1]
    share = modes_refs[0].shape[2]
    for row in range(cells_ref.shape[1]):
        spectrum = product_of(table_ref[...], cells_ref[0, row])
        held_ref[row] = spectrum.astype(jnp.bfloat16)
        for offset, modes_ref in enumerate(modes_refs):
            modes_ref[0, row] = held_ref[row, place_of(me_ref, offset, share)]


def to_modes(me, table, cells, owners):
    samples, rows, width, channels = cells.shape
    size = table.shape[0]
    share = (rows, size // owners, channels)
    return pl.pallas_call(
        to_modes_kernel,
        grid_spec=pltpu.PrefetchScalarGridSpec(
            num_scalar_prefetch=1,
            grid=(samples,),
            in_specs=[
                pl.BlockSpec((size, width), lambda b, _: (0, 0)),
                pl.BlockSpec((1, rows, width, channels), lambda b, _: (b, 0, 0, 0)),
            ],
            out_specs=(pl.BlockSpec((1,) + share, lambda b, _: (b, 0, 0, 0)),) * owners,
            scratch_shapes=[pltpu.VMEM((rows, size, channels), jnp.bfloat16)],
        ),
        out_shape=(jax.ShapeDtypeStruct((samples,) + share, jnp.bfloat16),) * owners,
        compiler_params=params("arbitrary"),
        cost_estimate=pl.CostEstimate(
            flops=2 * samples * rows * size * width * channels,
            bytes_accessed=2 * samples * rows * channels * (width + size),
            transcendentals=0,
        ),
        name="to_modes",
    )(me, table, cells)


def to_cells_kernel(me_ref, table_ref, base_ref, *refs):
    modes_refs, out_ref, held_ref = refs[:-2], refs[-2], refs[-1]
    share = modes_refs[0].shape[2]
    for row in range(base_ref.shape[1]):
        for offset, modes_ref in enumerate(modes_refs):
            held_ref[row, place_of(me_ref, offset, share)] = modes_ref[0, row]
        image = product_of(table_ref[...], held_ref[row])
        out_ref[0, row] = (base_ref[0, row].astype(jnp.float32) + image).astype(jnp.bfloat16)


def to_cells(me, table, modes, base):
    samples, rows, width, channels = base.shape
    size = table.shape[1]
    share = modes[0].shape[1:]
    block = pl.BlockSpec((1, rows, width, channels), lambda b, _: (b, 0, 0, 0))
    return pl.pallas_call(
        to_cells_kernel,
        grid_spec=pltpu.PrefetchScalarGridSpec(
            num_scalar_prefetch=1,
            grid=(samples,),
            in_specs=[pl.BlockSpec((width, size), lambda b, _: (0, 0)), block]
            + [pl.BlockSpec((1,) + share, lambda b, _: (b, 0, 0, 0))] * len(modes),
            out_specs=block,
            scratch_shapes=[pltpu.VMEM((rows, size, channels), jnp.bfloat16)],
        ),
        out_shape=jax.ShapeDtypeStruct(base.shape, jnp.bfloat16),
        compiler_params=params("arbitrary"),
        cost_estimate=pl.CostEstimate(
            flops=2 * samples * rows * size * width * channels,
            bytes_accessed=2 * samples * rows * channels * (2 * width + size),
            transcendentals=0,
        ),
        name="to_cells",
    )(me, table, base, *modes)


def sigmoid_of(values):
    return 0.5 + 0.5 * jnp.tanh(0.5 * values)


def mix_lat(me_ref, table_ref, bands_refs, band_ref, mixed_ref):
    samples, rows, share, width = bands_refs[0].shape
    half = table_ref.shape[0] // 2
    for sample in range(samples):
        for offset, bands_ref in enumerate(bands_refs):
            place = place_of(me_ref, offset, rows * share)
            band_ref[sample, place] = bands_ref[sample].reshape(rows * share, width)
        mixed = product_of(table_ref[...], band_ref[sample]).astype(jnp.bfloat16)
        spot = pl.ds(sample * half, half)
        mixed_ref[spot, 0:width] = mixed[:half]
        mixed_ref[spot, width : 2 * width] = mixed[half:]


def unmix_lat(me_ref, table_ref, mixed_ref, band_ref, bands_refs):
    samples, rows, share, width = bands_refs[0].shape
    half = table_ref.shape[0] // 2
    for sample in range(samples):
        spot = pl.ds(sample * half, half)
        joined = jnp.concatenate(
            [mixed_ref[spot, 0:width], mixed_ref[spot, width : 2 * width]], axis=0
        )
        band_ref[sample] = product_of(table_ref[...], joined).astype(jnp.bfloat16)
        for offset, bands_ref in enumerate(bands_refs):
            place = place_of(me_ref, offset, rows * share)
            bands_ref[sample] = band_ref[sample, place].reshape(rows, share, width)


def forward_kernel(owners, me_ref, lat_ref, unlat_ref, w1_ref, b1_ref, w2_ref, b2_ref, *refs):
    bands_refs, image_refs = refs[:owners], refs[owners : 2 * owners]
    mixed_ref, act_ref, gate_ref, bend_ref, shrunk_ref, band_ref = refs[2 * owners :]
    mix_lat(me_ref, lat_ref, bands_refs, band_ref, mixed_ref.at[0])
    pre = product_of(mixed_ref[0], w1_ref[0]) + b1_ref[0]
    logistic = sigmoid_of(pre)
    act = pre * logistic
    act_ref[0] = act.astype(jnp.bfloat16)
    gate_ref[0] = logistic + act * (1.0 - logistic)
    out = product_of(act_ref[0], w2_ref[0]) + b2_ref[0]
    bent = jnp.tanh(out * (1.0 / shrink_level))
    bend_ref[0] = bent * bent
    shrunk_ref[...] = (out - shrink_level * bent).astype(jnp.bfloat16)
    unmix_lat(me_ref, unlat_ref, shrunk_ref, band_ref, image_refs)


def backward_kernel(
    block_size, owners, me_ref, lat_ref, unlat_ref, w1_ref, w2_ref,
    mixed_ref, act_ref, gate_ref, bend_ref, *refs
):
    bands_refs, image_refs = refs[:owners], refs[owners : 2 * owners]
    sums_ref, cot_ref, kept_ref, band_ref = refs[2 * owners :]
    transposed = (((1,), (1,)), ((), ()))
    summed = (((0,), (0,)), ((), ()))

    def times(former, latter, dims):
        return lax.dot_general(former, latter, dims, preferred_element_type=jnp.float32)

    def weight_sums(acts, grads, slot):
        width = acts.shape[1] // 2
        full = times(acts, grads, summed)
        real = full[:width, :width] + full[width:, width:]
        imag = full[:width, width:] - full[width:, :width]
        bias = jnp.sum(grads.astype(jnp.float32), axis=0, keepdims=True)
        size = block_size
        owner = lax.broadcasted_iota(jnp.int32, (size, width), 1) // size
        extra = sums_ref.shape[3] - size
        first = lax.broadcasted_iota(jnp.int32, (extra, width), 0) == 0
        for part, values in enumerate((real, imag)):
            joined = values[:size]
            for block in range(1, width // size):
                joined = jnp.where(owner == block, values[block * size : (block + 1) * size], joined)
            sums_ref[slot, part, 0, 0:size] = joined
            row = bias[:, part * width : (part + 1) * width]
            sums_ref[slot, part, 0, size:] = jnp.where(first, row, 0.0)

    mix_lat(me_ref, lat_ref, bands_refs, band_ref, cot_ref)
    kept_ref[...] = (cot_ref[...].astype(jnp.float32) * bend_ref[0]).astype(jnp.bfloat16)
    back = times(kept_ref[...], w2_ref[0], transposed)
    cot_ref[...] = (back * gate_ref[0]).astype(jnp.bfloat16)
    weight_sums(act_ref[0], kept_ref[...], 1)
    kept_ref[...] = times(cot_ref[...], w1_ref[0], transposed).astype(jnp.bfloat16)
    weight_sums(mixed_ref[0], cot_ref[...], 0)
    unmix_lat(me_ref, unlat_ref, kept_ref, band_ref, image_refs)


def group_spec(*shape):
    return pl.BlockSpec((1,) + shape, lambda g, *_: (g,) + (0,) * len(shape))


def bands_specs(bands, groups):
    shape = bands[0].shape
    block = shape[:-1] + (shape[-1] // groups,)
    return (pl.BlockSpec(block, lambda g, *_: (0, 0, 0, g)),) * len(bands)


def shapes_of(bands):
    return tuple(jax.ShapeDtypeStruct(band.shape, band.dtype) for band in bands)


def forward_mid(me, lat, unlat, bands, w1, b1, w2, b2):
    groups, lanes, _ = w1.shape
    size = lat.shape[0]
    samples = bands[0].shape[0]
    positions = samples * size // 2
    table = pl.BlockSpec((size, size), lambda g, _: (0, 0))
    state = (groups, positions, lanes)
    state_spec = group_spec(positions, lanes)
    specs = bands_specs(bands, groups)
    results = pl.pallas_call(
        functools.partial(forward_kernel, len(bands)),
        grid_spec=pltpu.PrefetchScalarGridSpec(
            num_scalar_prefetch=1,
            grid=(groups,),
            in_specs=[
                table, table,
                group_spec(lanes, lanes), group_spec(1, lanes),
                group_spec(lanes, lanes), group_spec(1, lanes),
                *specs,
            ],
            out_specs=specs + (state_spec,) * 4,
            scratch_shapes=[
                pltpu.VMEM((positions, lanes), jnp.bfloat16),
                pltpu.VMEM((samples, size, lanes // 2), jnp.bfloat16),
            ],
        ),
        out_shape=shapes_of(bands) + (
            jax.ShapeDtypeStruct(state, jnp.bfloat16),
            jax.ShapeDtypeStruct(state, jnp.bfloat16),
            jax.ShapeDtypeStruct(state, jnp.float32),
            jax.ShapeDtypeStruct(state, jnp.float32),
        ),
        compiler_params=params("arbitrary"),
        cost_estimate=pl.CostEstimate(
            flops=4 * groups * positions * lanes * lanes,
            bytes_accessed=16 * groups * positions * lanes + 4 * groups * lanes * lanes,
            transcendentals=2 * groups * positions * lanes,
        ),
        name="mix_forward",
    )(me, lat, unlat, w1, b1, w2, b2, *bands)
    return results[: len(bands)], results[len(bands) :]


def backward_mid(me, lat, unlat, bands, w1, w2, state, count):
    groups, lanes, _ = w1.shape
    size = lat.shape[0]
    samples = bands[0].shape[0]
    positions = samples * size // 2
    table = pl.BlockSpec((size, size), lambda g, _: (0, 0))
    state_spec = group_spec(positions, lanes)
    specs = bands_specs(bands, groups)
    size_of_block = lanes // 2 // (count // groups)
    rows = size_of_block + 16
    results = pl.pallas_call(
        functools.partial(backward_kernel, size_of_block, len(bands)),
        grid_spec=pltpu.PrefetchScalarGridSpec(
            num_scalar_prefetch=1,
            grid=(groups,),
            in_specs=[
                table, table, group_spec(lanes, lanes), group_spec(lanes, lanes),
                *([state_spec] * 4), *specs,
            ],
            out_specs=specs + (
                pl.BlockSpec((2, 2, 1, rows, lanes // 2), lambda g, _: (0, 0, g, 0, 0)),
            ),
            scratch_shapes=[
                pltpu.VMEM((positions, lanes), jnp.bfloat16),
                pltpu.VMEM((positions, lanes), jnp.bfloat16),
                pltpu.VMEM((samples, size, lanes // 2), jnp.bfloat16),
            ],
        ),
        out_shape=shapes_of(bands)
        + (jax.ShapeDtypeStruct((2, 2, groups, rows, lanes // 2), jnp.float32),),
        compiler_params=params("arbitrary"),
        cost_estimate=pl.CostEstimate(
            flops=8 * groups * positions * lanes * lanes,
            bytes_accessed=16 * groups * positions * lanes + 4 * groups * lanes * lanes,
            transcendentals=0,
        ),
        name="mix_backward",
    )(me, lat, unlat, w1, w2, *state, *bands)
    return results[: len(bands)], results[len(bands)]


def swap_with(values, axis, distance):
    size = lax.axis_size(axis)
    return lax.ppermute(values, axis, [(i, i ^ distance) for i in range(size)])


def far_first(size):
    return sorted(range(1, size), key=lambda offset: (-(offset >> 2), offset))


def summed_over_group(sums):
    lanes = sums.shape[-1]
    size = lax.axis_size("space")
    me, side = lax.axis_index("space"), lax.axis_index("dp")
    halves = sums.reshape(2, -1, lanes)
    given = lax.dynamic_index_in_dim(halves, 1 - side, 0, keepdims=False)
    held = lax.dynamic_index_in_dim(halves, side, 0, keepdims=False) + swap_with(given, "dp", 1)
    shares = held.reshape(size, -1, lanes)
    total = lax.dynamic_index_in_dim(shares, me, 0, keepdims=False)
    for offset in far_first(size):
        given = lax.dynamic_index_in_dim(shares, me ^ offset, 0, keepdims=False)
        taken = swap_with(given.astype(jnp.bfloat16), "space", offset)
        total = total + taken.astype(jnp.float32)
    total = total.astype(jnp.bfloat16)
    parts = jnp.zeros((size,) + total.shape, total.dtype)
    parts = lax.dynamic_update_index_in_dim(parts, total, me, 0)
    for offset in far_first(size):
        taken = swap_with(total, "space", offset)
        parts = lax.dynamic_update_index_in_dim(parts, taken, me ^ offset, 0)
    other = swap_with(parts, "dp", 1)
    both = jnp.where(side == 0, jnp.stack([parts, other]), jnp.stack([other, parts]))
    return both.reshape(sums.shape)


def body(fields, cotangent, w_first, b_first, w_second, b_second):
    samples, rows, width, channels = fields.shape
    owners = lax.axis_size("space")
    lat_total = rows * owners
    modes = KW // owners
    count, edge = w_first.shape[1:3]
    groups = 2
    direct = 2 * modes % 16 == 0
    lead = owners if direct else 1

    def swapped(blocks):
        taken = {0: blocks[0]}
        for offset in far_first(owners):
            taken[offset] = swap_with(blocks[offset], "space", offset)
        return [taken[offset] for offset in range(owners)]

    def send_out(blocks):
        if direct:
            return swapped(blocks)
        spectrum = blocks[0].reshape(samples, rows, owners, 2 * modes, channels)
        spectrum = jnp.transpose(spectrum, (2, 0, 1, 3, 4))
        arrived = lax.all_to_all(spectrum, "space", split_axis=0, concat_axis=0, tiled=True)
        return [jnp.transpose(arrived, (1, 0, 2, 3, 4)).reshape(samples, 1, -1, channels)]

    def send_back(blocks):
        if direct:
            return swapped(blocks)
        bands = blocks[0].reshape(samples, owners, rows, 2 * modes, channels)
        bands = jnp.transpose(bands, (1, 0, 2, 3, 4))
        arrived = lax.all_to_all(bands, "space", split_axis=0, concat_axis=0, tiled=True)
        return [jnp.transpose(arrived, (1, 2, 0, 3, 4)).reshape(samples, rows, -1, channels)]

    me = lax.axis_index("space") if direct else 0
    me = jnp.full((1,), me, jnp.int32)
    plain, scaled = lon_tables(KW, width, owners)
    lat = lat_spread(lat_total, modes)

    spectrum = to_modes(me, plain, fields, lead)
    spectrum, cotangent, w_first, w_second = lax.optimization_barrier(
        (spectrum, cotangent, w_first, w_second)
    )
    gathered = send_out(spectrum)
    cot_gathered = send_out(to_modes(me, scaled, cotangent, lead))
    w1, w2 = spread_weights(groups, w_first, w_second)
    b1, b2 = block_bias(b_first, groups), block_bias(b_second, groups)

    image, state = forward_mid(me, lat, lat.T, gathered, w1, b1, w2, b2)
    image_band = send_back(image)
    grad_image, sums = backward_mid(me, lat, lat.T, cot_gathered, w1, w2, state, count)
    grad_band = send_back(grad_image)
    output = to_cells(me, scaled.T, image_band, fields)
    grad_fields = to_cells(me, plain.T, grad_band, cotangent)

    positions = samples * lax.axis_size("dp") * lat_total * KW
    factor = 1.0 / math.sqrt(positions)
    sums = summed_over_group(sums).astype(jnp.float32) * factor
    grads = []
    for which in range(2):
        blocks = sums[which, :, :, :edge].reshape(2, groups, edge, count // groups, edge)
        grads.append(jnp.transpose(blocks, (0, 1, 3, 2, 4)).reshape(w_first.shape))
        grads.append(sums[which, :, :, edge].reshape(b_first.shape))
    return (output, grad_fields) + tuple(grads)


def solution(mesh):
    split = P(("parts", "dp"), "space", None, None)
    in_specs = (split, split, P(), P(), P(), P())
    out_specs = (
        split,
        split,
        P("parts", None, None, None),
        P("parts", None, None),
        P("parts", None, None, None),
        P("parts", None, None),
    )
    return jax.shard_map(body, mesh=mesh, in_specs=in_specs, out_specs=out_specs, check_vma=False)
```

```python
import functools
import math

import jax
import jax.numpy as jnp
from jax import lax
from jax.experimental import pallas as pl
from jax.experimental.pallas import tpu as pltpu
from jax.sharding import PartitionSpec as P
import ml_dtypes
import numpy as np

KW = 64
shrink_level = 0.05
HELD = 5
MIB = 1024 * 1024


def product_of(former, latter):
    return jnp.dot(former, latter, preferred_element_type=jnp.float32)


def lon_tables(mode_count, cell_count, owners):
    wavenums = np.arange(mode_count, dtype=np.int32)
    columns = np.arange(cell_count, dtype=np.int32)
    phase_index = (wavenums[:, None] * columns[None, :] % cell_count).astype(np.float32)
    phases = phase_index * np.float32(2.0 * math.pi / cell_count)
    factor = np.float32(1.0 / math.sqrt(cell_count))
    forward = np.stack([np.cos(phases) * factor, -np.sin(phases) * factor])
    scaled = forward * np.where(wavenums == 0, 1.0, 2.0).astype(np.float32)[:, None]

    def ordered(table):
        split = table.reshape(2, owners, -1, cell_count).transpose(1, 0, 2, 3)
        return split.reshape(-1, cell_count).astype(ml_dtypes.bfloat16)

    return ordered(forward), ordered(scaled)


def lat_spread(row_count, modes):
    indices = np.arange(row_count, dtype=np.int32)
    phase_index = (indices[:, None] * indices[None, :] % row_count).astype(np.float32)
    phases = phase_index * np.float32(2.0 * math.pi / row_count)
    factor = np.float32(1.0 / math.sqrt(row_count))
    cosine = np.cos(phases) * factor
    sine_part = np.sin(phases) * factor
    table = np.stack([np.stack([cosine, sine_part], -1), np.stack([-sine_part, cosine], -1)])
    same = np.eye(modes, dtype=np.float32)
    spread = table[:, :, None, :, :, None] * same[None, None, :, None, None, :]
    size = 2 * row_count * modes
    return spread.reshape(size, size).astype(ml_dtypes.bfloat16)


def block_bias(bias, groups):
    return jnp.transpose(bias.reshape(2, groups, 1, -1), (1, 2, 0, 3)).reshape(groups, 1, -1)


def spread_kernel(*refs):
    half_way = len(refs) // 2
    for blocks_ref, joined_ref in zip(refs[:half_way], refs[half_way:]):
        _, per, size, _ = blocks_ref.shape
        width = per * size
        row = lax.broadcasted_iota(jnp.int32, (size, width), 0)
        lane = lax.broadcasted_iota(jnp.int32, (size, width), 1)
        for block in range(per):
            place = (row + block * size == lane).astype(jnp.bfloat16)
            real = product_of(blocks_ref[0, block], place).astype(jnp.bfloat16)
            imag = product_of(blocks_ref[1, block], place)
            upper = pl.ds(block * size, size)
            lower = pl.ds(width + block * size, size)
            joined_ref[0, upper, 0:width] = real
            joined_ref[0, upper, width : 2 * width] = imag.astype(jnp.bfloat16)
            joined_ref[0, lower, 0:width] = (-imag).astype(jnp.bfloat16)
            joined_ref[0, lower, width : 2 * width] = real


def spread_weights(groups, *weights):
    _, count, size, _ = weights[0].shape
    per = count // groups
    lanes = 2 * per * size
    shape = jax.ShapeDtypeStruct((groups, lanes, lanes), jnp.bfloat16)
    return pl.pallas_call(
        spread_kernel,
        grid=(groups,),
        out_shape=(shape,) * len(weights),
        in_specs=[pl.BlockSpec((2, per, size, size), lambda g: (0, g, 0, 0))] * len(weights),
        out_specs=(group_spec(lanes, lanes),) * len(weights),
        compiler_params=params(12),
        cost_estimate=pl.CostEstimate(
            flops=len(weights) * 2 * count * size * size * lanes,
            bytes_accessed=len(weights) * 2 * groups * lanes * lanes,
            transcendentals=0,
        ),
        name="spread_weights",
    )(*weights)


def params(mebibytes):
    return pltpu.CompilerParams(
        vmem_limit_bytes=mebibytes * MIB, dimension_semantics=("arbitrary",)
    )


def place_of(me_ref, offset, rows):
    return pl.ds(pl.multiple_of((me_ref[0] ^ offset) * rows, rows), rows)


def to_modes_kernel(me_ref, table_ref, cells_ref, *refs):
    modes_refs, held_ref = refs[:-1], refs[-1]
    share = modes_refs[0].shape[2]
    for row in range(cells_ref.shape[1]):
        spectrum = product_of(table_ref[...], cells_ref[0, row])
        held_ref[row] = spectrum.astype(jnp.bfloat16)
        for offset, modes_ref in enumerate(modes_refs):
            modes_ref[0, row] = held_ref[row, place_of(me_ref, offset, share)]


def to_modes(me, table, cells, owners):
    samples, rows, width, channels = cells.shape
    size = table.shape[0]
    share = (rows, size // owners, channels)
    return pl.pallas_call(
        to_modes_kernel,
        grid_spec=pltpu.PrefetchScalarGridSpec(
            num_scalar_prefetch=1,
            grid=(samples,),
            in_specs=[
                pl.BlockSpec((size, width), lambda b, _: (0, 0)),
                pl.BlockSpec((1, rows, width, channels), lambda b, _: (b, 0, 0, 0)),
            ],
            out_specs=(pl.BlockSpec((1,) + share, lambda b, _: (b, 0, 0, 0)),) * owners,
            scratch_shapes=[pltpu.VMEM((rows, size, channels), jnp.bfloat16)],
        ),
        out_shape=(jax.ShapeDtypeStruct((samples,) + share, jnp.bfloat16),) * owners,
        compiler_params=params(12),
        cost_estimate=pl.CostEstimate(
            flops=2 * samples * rows * size * width * channels,
            bytes_accessed=2 * samples * rows * channels * (width + size),
            transcendentals=0,
        ),
        name="to_modes",
    )(me, table, cells)


def to_cells_kernel(me_ref, table_ref, base_ref, *refs):
    modes_refs, out_ref, held_ref = refs[:-2], refs[-2], refs[-1]
    share = modes_refs[0].shape[2]
    for row in range(base_ref.shape[1]):
        for offset, modes_ref in enumerate(modes_refs):
            held_ref[row, place_of(me_ref, offset, share)] = modes_ref[0, row]
        image = product_of(table_ref[...], held_ref[row])
        out_ref[0, row] = (base_ref[0, row].astype(jnp.float32) + image).astype(jnp.bfloat16)


def to_cells(me, table, modes, base):
    samples, rows, width, channels = base.shape
    size = table.shape[1]
    share = modes[0].shape[1:]
    block = pl.BlockSpec((1, rows, width, channels), lambda b, _: (b, 0, 0, 0))
    return pl.pallas_call(
        to_cells_kernel,
        grid_spec=pltpu.PrefetchScalarGridSpec(
            num_scalar_prefetch=1,
            grid=(samples,),
            in_specs=[pl.BlockSpec((width, size), lambda b, _: (0, 0)), block]
            + [pl.BlockSpec((1,) + share, lambda b, _: (b, 0, 0, 0))] * len(modes),
            out_specs=block,
            scratch_shapes=[pltpu.VMEM((rows, size, channels), jnp.bfloat16)],
        ),
        out_shape=jax.ShapeDtypeStruct(base.shape, jnp.bfloat16),
        compiler_params=params(12),
        cost_estimate=pl.CostEstimate(
            flops=2 * samples * rows * size * width * channels,
            bytes_accessed=2 * samples * rows * channels * (2 * width + size),
            transcendentals=0,
        ),
        name="to_cells",
    )(me, table, base, *modes)


def sigmoid_of(values):
    return 0.5 + 0.5 * jnp.tanh(0.5 * values)


def mix_lat(me_ref, table_ref, bands_refs, band_ref, mixed_ref):
    samples, rows, share, width = bands_refs[0].shape
    half = table_ref.shape[0] // 2
    for sample in range(samples):
        for offset, bands_ref in enumerate(bands_refs):
            place = place_of(me_ref, offset, rows * share)
            band_ref[sample, place] = bands_ref[sample].reshape(rows * share, width)
        mixed = product_of(table_ref[...], band_ref[sample]).astype(jnp.bfloat16)
        spot = pl.ds(sample * half, half)
        mixed_ref[spot, 0:width] = mixed[:half]
        mixed_ref[spot, width : 2 * width] = mixed[half:]


def unmix_lat(me_ref, table_ref, mixed_ref, band_ref, bands_refs):
    samples, rows, share, width = bands_refs[0].shape
    half = table_ref.shape[0] // 2
    for sample in range(samples):
        spot = pl.ds(sample * half, half)
        joined = jnp.concatenate(
            [mixed_ref[spot, 0:width], mixed_ref[spot, width : 2 * width]], axis=0
        )
        band_ref[sample] = product_of(table_ref[...], joined).astype(jnp.bfloat16)
        for offset, bands_ref in enumerate(bands_refs):
            place = place_of(me_ref, offset, rows * share)
            bands_ref[sample] = band_ref[sample, place].reshape(rows, share, width)


def activate(mixed_ref, w1_ref, b1_ref):
    pre = product_of(mixed_ref[0], w1_ref[0]) + b1_ref[0]
    logistic = sigmoid_of(pre)
    return logistic, pre * logistic


def bend(act_ref, w2_ref, b2_ref):
    out = product_of(act_ref[...], w2_ref[0]) + b2_ref[0]
    return out, jnp.tanh(out * (1.0 / shrink_level))


def forward_kernel(owners, me_ref, lat_ref, unlat_ref, w1_ref, b1_ref, w2_ref, b2_ref, *refs):
    bands_refs, image_refs = refs[:owners], refs[owners : 2 * owners]
    mixed_ref, act_ref, band_ref = refs[2 * owners :]
    mix_lat(me_ref, lat_ref, bands_refs, band_ref, mixed_ref.at[0])
    act_ref[...] = activate(mixed_ref, w1_ref, b1_ref)[1].astype(jnp.bfloat16)
    out, bent = bend(act_ref, w2_ref, b2_ref)
    act_ref[...] = (out - shrink_level * bent).astype(jnp.bfloat16)
    unmix_lat(me_ref, unlat_ref, act_ref, band_ref, image_refs)


def backward_kernel(
    block_size, owners, me_ref, lat_ref, unlat_ref, w1_ref, b1_ref, w2_ref, b2_ref, mixed_ref, *refs
):
    bands_refs, image_refs = refs[:owners], refs[owners : 2 * owners]
    sums_ref, act_ref, gate_ref, cot_ref, kept_ref, band_ref = refs[2 * owners :]
    transposed = (((1,), (1,)), ((), ()))
    summed = (((0,), (0,)), ((), ()))

    def times(former, latter, dims):
        return lax.dot_general(former, latter, dims, preferred_element_type=jnp.float32)

    def weight_sums(acts, grads, slot):
        width = acts.shape[1] // 2
        full = times(acts, grads, summed)
        real = full[:width, :width] + full[width:, width:]
        imag = full[:width, width:] - full[width:, :width]
        bias = jnp.sum(grads.astype(jnp.float32), axis=0, keepdims=True)
        size = block_size
        owner = lax.broadcasted_iota(jnp.int32, (size, width), 1) // size
        extra = sums_ref.shape[3] - size
        first = lax.broadcasted_iota(jnp.int32, (extra, width), 0) == 0
        for part, values in enumerate((real, imag)):
            joined = values[:size]
            for block in range(1, width // size):
                joined = jnp.where(owner == block, values[block * size : (block + 1) * size], joined)
            sums_ref[slot, part, 0, 0:size] = joined
            row = bias[:, part * width : (part + 1) * width]
            sums_ref[slot, part, 0, size:] = jnp.where(first, row, 0.0)

    logistic, act = activate(mixed_ref, w1_ref, b1_ref)
    act_ref[...] = act.astype(jnp.bfloat16)
    gate_ref[...] = logistic + act * (1.0 - logistic)
    mix_lat(me_ref, lat_ref, bands_refs, band_ref, cot_ref)
    _, bent = bend(act_ref, w2_ref, b2_ref)
    kept_ref[...] = (cot_ref[...].astype(jnp.float32) * (bent * bent)).astype(jnp.bfloat16)
    back = times(kept_ref[...], w2_ref[0], transposed)
    cot_ref[...] = (back * gate_ref[...]).astype(jnp.bfloat16)
    weight_sums(act_ref[...], kept_ref[...], 1)
    kept_ref[...] = times(cot_ref[...], w1_ref[0], transposed).astype(jnp.bfloat16)
    weight_sums(mixed_ref[0], cot_ref[...], 0)
    unmix_lat(me_ref, unlat_ref, kept_ref, band_ref, image_refs)


def group_spec(*shape):
    return pl.BlockSpec((1,) + shape, lambda g, *_: (g,) + (0,) * len(shape))


def bands_specs(bands, groups):
    shape = bands[0].shape
    block = shape[:-1] + (shape[-1] // groups,)
    return (pl.BlockSpec(block, lambda g, *_: (0, 0, 0, g)),) * len(bands)


def shapes_of(bands):
    return tuple(jax.ShapeDtypeStruct(band.shape, band.dtype) for band in bands)


def forward_mid(me, lat, unlat, bands, w1, b1, w2, b2):
    groups, lanes, _ = w1.shape
    size = lat.shape[0]
    samples = bands[0].shape[0]
    positions = samples * size // 2
    table = pl.BlockSpec((size, size), lambda g, _: (0, 0))
    state = (groups, positions, lanes)
    state_spec = group_spec(positions, lanes)
    specs = bands_specs(bands, groups)
    results = pl.pallas_call(
        functools.partial(forward_kernel, len(bands)),
        grid_spec=pltpu.PrefetchScalarGridSpec(
            num_scalar_prefetch=1,
            grid=(groups,),
            in_specs=[
                table, table,
                group_spec(lanes, lanes), group_spec(1, lanes),
                group_spec(lanes, lanes), group_spec(1, lanes),
                *specs,
            ],
            out_specs=specs + (state_spec,),
            scratch_shapes=[
                pltpu.VMEM((positions, lanes), jnp.bfloat16),
                pltpu.VMEM((samples, size, lanes // 2), jnp.bfloat16),
            ],
        ),
        out_shape=shapes_of(bands) + (jax.ShapeDtypeStruct(state, jnp.bfloat16),),
        compiler_params=params(28),
        cost_estimate=pl.CostEstimate(
            flops=4 * groups * positions * lanes * lanes,
            bytes_accessed=16 * groups * positions * lanes + 4 * groups * lanes * lanes,
            transcendentals=2 * groups * positions * lanes,
        ),
        name="mix_forward",
    )(me, lat, unlat, w1, b1, w2, b2, *bands)
    return results[: len(bands)], results[len(bands)]


def backward_mid(me, lat, unlat, bands, w1, b1, w2, b2, state, count):
    groups, lanes, _ = w1.shape
    size = lat.shape[0]
    samples = bands[0].shape[0]
    positions = samples * size // 2
    table = pl.BlockSpec((size, size), lambda g, _: (0, 0))
    specs = bands_specs(bands, groups)
    size_of_block = lanes // 2 // (count // groups)
    rows = size_of_block + 16
    results = pl.pallas_call(
        functools.partial(backward_kernel, size_of_block, len(bands)),
        grid_spec=pltpu.PrefetchScalarGridSpec(
            num_scalar_prefetch=1,
            grid=(groups,),
            in_specs=[
                table, table,
                group_spec(lanes, lanes), group_spec(1, lanes),
                group_spec(lanes, lanes), group_spec(1, lanes),
                group_spec(positions, lanes), *specs,
            ],
            out_specs=specs + (
                pl.BlockSpec((2, 2, 1, rows, lanes // 2), lambda g, _: (0, 0, g, 0, 0)),
            ),
            scratch_shapes=[
                pltpu.VMEM((positions, lanes), jnp.bfloat16),
                pltpu.VMEM((positions, lanes), jnp.float32),
                pltpu.VMEM((positions, lanes), jnp.bfloat16),
                pltpu.VMEM((positions, lanes), jnp.bfloat16),
                pltpu.VMEM((samples, size, lanes // 2), jnp.bfloat16),
            ],
        ),
        out_shape=shapes_of(bands)
        + (jax.ShapeDtypeStruct((2, 2, groups, rows, lanes // 2), jnp.float32),),
        compiler_params=params(32),
        cost_estimate=pl.CostEstimate(
            flops=8 * groups * positions * lanes * lanes,
            bytes_accessed=16 * groups * positions * lanes + 4 * groups * lanes * lanes,
            transcendentals=0,
        ),
        name="mix_backward",
    )(me, lat, unlat, w1, b1, w2, b2, state, *bands)
    return results[: len(bands)], results[len(bands)]


def swap_with(values, axis, distance, after=()):
    if len(after) > 0:
        values, _ = lax.optimization_barrier((values, tuple(after)))
    pairs = [(i, i ^ distance) for i in range(lax.axis_size(axis))]
    return lax.ppermute(values, axis, pairs)


def mixed_order(size):
    far = list(range(size // 2, size))
    near = [offset for offset in (2, 3, 1) if offset < size // 2]
    near += list(range(4, size // 2))
    order = []
    while far or near:
        order += far[:1] + near[:1]
        far, near = far[1:], near[1:]
    return order


def pick(pair, side):
    return lax.dynamic_index_in_dim(pair, side, 0, keepdims=False)


def by_place(blocks, bits):
    shape = blocks.shape
    for level, bit in enumerate(bits):
        split = blocks.reshape((2**level, 2, -1) + shape[-2:])
        blocks = jnp.where(bit == 0, split, jnp.concatenate([split[:, 1:], split[:, :1]], axis=1))
    return blocks


class GroupSum:
    def __init__(self, sums):
        self.lanes = sums.shape[-1]
        self.shape = sums.shape
        self.side = lax.axis_index("dp")
        self.me = lax.axis_index("space")
        self.count = lax.axis_size("space") // 2
        self.held = sums.reshape(-1, self.lanes)

    def halve(self, axis, distance, bit, after):
        pair = self.held.reshape(2, -1, self.lanes)
        taken = swap_with(pick(pair, 1 - bit), axis, distance, after)
        self.held = pick(pair, bit) + taken

    def over_dp(self, after):
        self.halve("dp", 1, self.side, after)

    def over_next(self, after):
        self.halve("space", 1, self.me % 2, after)

    def scatter(self, after):
        shares = self.held.reshape(self.count, -1, self.lanes)
        place = self.me // 2
        total = pick(shares, place)
        for offset in range(1, self.count):
            given = pick(shares, place ^ offset).astype(jnp.bfloat16)
            total += swap_with(given, "space", 2 * offset, after).astype(jnp.float32)
        self.total = total.astype(jnp.bfloat16)

    def gather(self, after):
        taken = [self.total]
        for offset in range(1, self.count):
            taken.append(swap_with(self.total, "space", 2 * offset, after))
        self.quarter = jnp.stack(taken)

    def gather_next(self, after):
        self.half = jnp.stack([self.quarter, swap_with(self.quarter, "space", 1, after)])

    def join(self, after):
        both = jnp.stack([self.half, swap_with(self.half, "dp", 1, after)])
        bits = [self.side, self.me % 2]
        level = self.count
        while level > 1:
            bits.append(self.me // level % 2)
            level //= 2
        return by_place(both, bits).reshape(self.shape)


def body(fields, cotangent, w_first, b_first, w_second, b_second):
    samples, rows, width, channels = fields.shape
    owners = lax.axis_size("space")
    lat_total = rows * owners
    modes = KW // owners
    count, edge = w_first.shape[1:3]
    groups = 2
    direct = 2 * modes % 16 == 0
    lead = owners if direct else 1

    order = mixed_order(owners)

    def send_out(blocks):
        if direct:
            taken = {0: blocks[0]}
            for offset in order:
                taken[offset] = swap_with(blocks[offset], "space", offset)
            return [taken[offset] for offset in range(owners)]
        spectrum = blocks[0].reshape(samples, rows, owners, 2 * modes, channels)
        spectrum = jnp.transpose(spectrum, (2, 0, 1, 3, 4))
        arrived = lax.all_to_all(spectrum, "space", split_axis=0, concat_axis=0, tiled=True)
        return [jnp.transpose(arrived, (1, 0, 2, 3, 4)).reshape(samples, 1, -1, channels)]

    def send_back(blocks):
        bands = blocks[0].reshape(samples, owners, rows, 2 * modes, channels)
        bands = jnp.transpose(bands, (1, 0, 2, 3, 4))
        arrived = lax.all_to_all(bands, "space", split_axis=0, concat_axis=0, tiled=True)
        return [jnp.transpose(arrived, (1, 2, 0, 3, 4)).reshape(samples, rows, -1, channels)]

    me = lax.axis_index("space") if direct else 0
    me = jnp.full((1,), me, jnp.int32)
    plain, scaled = lon_tables(KW, width, owners)
    lat = lat_spread(lat_total, modes)

    spectrum = to_modes(me, plain, fields, lead)
    spectrum, cotangent, w_first, w_second = lax.optimization_barrier(
        (spectrum, cotangent, w_first, w_second)
    )
    gathered = send_out(spectrum)
    cot_gathered = send_out(to_modes(me, scaled, cotangent, lead))
    w1, w2 = spread_weights(groups, w_first, w_second)
    b1, b2 = block_bias(b_first, groups), block_bias(b_second, groups)

    image, state = forward_mid(me, lat, lat.T, gathered, w1, b1, w2, b2)
    image_band = send_out(image) if direct else send_back(image)
    grad_image, sums = backward_mid(
        me, lat, lat.T, cot_gathered, w1, b1, w2, b2, state, count
    )
    if direct:
        early = tuple(image_band[offset] for offset in order[:HELD])
        grad_image, sums, _ = lax.optimization_barrier((grad_image, sums, early))
        late = [image_band[offset] for offset in order[HELD:]]
        grad_band = send_out(grad_image)
        sent = [grad_band[offset] for offset in order]
    else:
        grad_band = send_back(grad_image)
        late, sent = [], []
    group_sum = GroupSum(sums)
    group_sum.over_dp([])
    group_sum.over_next(late)
    group_sum.scatter(sent[:2])
    group_sum.gather(sent[2:4])
    group_sum.gather_next(sent[4:6])
    output = to_cells(me, scaled.T, image_band, fields)
    grad_fields = to_cells(me, plain.T, grad_band, cotangent)

    positions = samples * lax.axis_size("dp") * lat_total * KW
    factor = 1.0 / math.sqrt(positions)
    sums = group_sum.join([]).astype(jnp.float32) * factor
    grads = []
    for which in range(2):
        blocks = sums[which, :, :, :edge].reshape(2, groups, edge, count // groups, edge)
        grads.append(jnp.transpose(blocks, (0, 1, 3, 2, 4)).reshape(w_first.shape))
        grads.append(sums[which, :, :, edge].reshape(b_first.shape))
    return (output, grad_fields) + tuple(grads)


def solution(mesh):
    split = P(("parts", "dp"), "space", None, None)
    in_specs = (split, split, P(), P(), P(), P())
    out_specs = (
        split,
        split,
        P("parts", None, None, None),
        P("parts", None, None),
        P("parts", None, None, None),
        P("parts", None, None),
    )
    return jax.shard_map(body, mesh=mesh, in_specs=in_specs, out_specs=out_specs, check_vma=False)
```

```python
import functools
import math

import jax
import jax.numpy as jnp
from jax import lax
from jax.experimental import pallas as pl
from jax.experimental.pallas import tpu as pltpu
from jax.sharding import PartitionSpec as P
import ml_dtypes
import numpy as np

KW = 64
shrink_level = 0.05
HELD = 5
FIRST = 4
STEPS_BEFORE = (0, 2, 3, 5, 6)
DEPTH = 5
MIB = 1024 * 1024


def product_of(former, latter):
    return jnp.dot(former, latter, preferred_element_type=jnp.float32)


def lon_tables(mode_count, cell_count, owners):
    wavenums = np.arange(mode_count, dtype=np.int32)
    columns = np.arange(cell_count, dtype=np.int32)
    phase_index = (wavenums[:, None] * columns[None, :] % cell_count).astype(np.float32)
    phases = phase_index * np.float32(2.0 * math.pi / cell_count)
    factor = np.float32(1.0 / math.sqrt(cell_count))
    forward = np.stack([np.cos(phases) * factor, -np.sin(phases) * factor])
    scaled = forward * np.where(wavenums == 0, 1.0, 2.0).astype(np.float32)[:, None]

    def ordered(table):
        split = table.reshape(2, owners, -1, cell_count).transpose(1, 0, 2, 3)
        return split.reshape(-1, cell_count).astype(ml_dtypes.bfloat16)

    return ordered(forward), ordered(scaled)


def lat_spread(row_count, modes):
    indices = np.arange(row_count, dtype=np.int32)
    phase_index = (indices[:, None] * indices[None, :] % row_count).astype(np.float32)
    phases = phase_index * np.float32(2.0 * math.pi / row_count)
    factor = np.float32(1.0 / math.sqrt(row_count))
    cosine = np.cos(phases) * factor
    sine_part = np.sin(phases) * factor
    table = np.stack([np.stack([cosine, sine_part], -1), np.stack([-sine_part, cosine], -1)])
    same = np.eye(modes, dtype=np.float32)
    spread = table[:, :, None, :, :, None] * same[None, None, :, None, None, :]
    size = 2 * row_count * modes
    return spread.reshape(size, size).astype(ml_dtypes.bfloat16)


def block_bias(bias, groups):
    return jnp.transpose(bias.reshape(2, groups, 1, -1), (1, 2, 0, 3)).reshape(groups, 1, -1)


def spread_kernel(*refs):
    half_way = len(refs) // 2
    for blocks_ref, joined_ref in zip(refs[:half_way], refs[half_way:]):
        _, per, size, _ = blocks_ref.shape
        width = per * size
        row = lax.broadcasted_iota(jnp.int32, (size, width), 0)
        lane = lax.broadcasted_iota(jnp.int32, (size, width), 1)
        for block in range(per):
            place = (row + block * size == lane).astype(jnp.bfloat16)
            real = product_of(blocks_ref[0, block], place).astype(jnp.bfloat16)
            imag = product_of(blocks_ref[1, block], place)
            upper = pl.ds(block * size, size)
            lower = pl.ds(width + block * size, size)
            joined_ref[0, upper, 0:width] = real
            joined_ref[0, upper, width : 2 * width] = imag.astype(jnp.bfloat16)
            joined_ref[0, lower, 0:width] = (-imag).astype(jnp.bfloat16)
            joined_ref[0, lower, width : 2 * width] = real


def spread_weights(groups, *weights):
    _, count, size, _ = weights[0].shape
    per = count // groups
    lanes = 2 * per * size
    shape = jax.ShapeDtypeStruct((groups, lanes, lanes), jnp.bfloat16)
    return pl.pallas_call(
        spread_kernel,
        grid=(groups,),
        out_shape=(shape,) * len(weights),
        in_specs=[pl.BlockSpec((2, per, size, size), lambda g: (0, g, 0, 0))] * len(weights),
        out_specs=(group_spec(lanes, lanes),) * len(weights),
        compiler_params=params(12),
        cost_estimate=pl.CostEstimate(
            flops=len(weights) * 2 * count * size * size * lanes,
            bytes_accessed=len(weights) * 2 * groups * lanes * lanes,
            transcendentals=0,
        ),
        name="spread_weights",
    )(*weights)


def params(mebibytes):
    return pltpu.CompilerParams(
        vmem_limit_bytes=mebibytes * MIB, dimension_semantics=("arbitrary",)
    )


def place_of(me_ref, offset, rows):
    return pl.ds(pl.multiple_of((me_ref[0] ^ offset) * rows, rows), rows)


def to_modes_kernel(me_ref, table_ref, cells_ref, *refs):
    modes_refs, held_ref = refs[:-1], refs[-1]
    share = modes_refs[0].shape[2]
    for row in range(cells_ref.shape[1]):
        spectrum = product_of(table_ref[...], cells_ref[0, row])
        held_ref[row] = spectrum.astype(jnp.bfloat16)
        for offset, modes_ref in enumerate(modes_refs):
            modes_ref[0, row] = held_ref[row, place_of(me_ref, offset, share)]


def to_modes(me, table, cells, owners):
    samples, rows, width, channels = cells.shape
    size = table.shape[0]
    share = (rows, size // owners, channels)
    return pl.pallas_call(
        to_modes_kernel,
        grid_spec=pltpu.PrefetchScalarGridSpec(
            num_scalar_prefetch=1,
            grid=(samples,),
            in_specs=[
                pl.BlockSpec((size, width), lambda b, _: (0, 0)),
                pl.BlockSpec((1, rows, width, channels), lambda b, _: (b, 0, 0, 0)),
            ],
            out_specs=(pl.BlockSpec((1,) + share, lambda b, _: (b, 0, 0, 0)),) * owners,
            scratch_shapes=[pltpu.VMEM((rows, size, channels), jnp.bfloat16)],
        ),
        out_shape=(in_hbm((samples,) + share, jnp.bfloat16),) * owners,
        compiler_params=params(12),
        cost_estimate=pl.CostEstimate(
            flops=2 * samples * rows * size * width * channels,
            bytes_accessed=2 * samples * rows * channels * (width + size),
            transcendentals=0,
        ),
        name="to_modes",
    )(me, table, cells)


def to_cells_kernel(me_ref, table_ref, base_ref, *refs):
    modes_refs, out_ref, held_ref = refs[:-2], refs[-2], refs[-1]
    share = modes_refs[0].shape[2]
    for row in range(base_ref.shape[1]):
        for offset, modes_ref in enumerate(modes_refs):
            held_ref[row, place_of(me_ref, offset, share)] = modes_ref[0, row]
        image = product_of(table_ref[...], held_ref[row])
        out_ref[0, row] = (base_ref[0, row].astype(jnp.float32) + image).astype(jnp.bfloat16)


def to_cells(me, table, modes, base):
    samples, rows, width, channels = base.shape
    size = table.shape[1]
    share = modes[0].shape[1:]
    block = pl.BlockSpec((1, rows, width, channels), lambda b, _: (b, 0, 0, 0))
    return pl.pallas_call(
        to_cells_kernel,
        grid_spec=pltpu.PrefetchScalarGridSpec(
            num_scalar_prefetch=1,
            grid=(samples,),
            in_specs=[pl.BlockSpec((width, size), lambda b, _: (0, 0)), block]
            + [pl.BlockSpec((1,) + share, lambda b, _: (b, 0, 0, 0))] * len(modes),
            out_specs=block,
            scratch_shapes=[pltpu.VMEM((rows, size, channels), jnp.bfloat16)],
        ),
        out_shape=jax.ShapeDtypeStruct(base.shape, jnp.bfloat16),
        compiler_params=params(12),
        cost_estimate=pl.CostEstimate(
            flops=2 * samples * rows * size * width * channels,
            bytes_accessed=2 * samples * rows * channels * (2 * width + size),
            transcendentals=0,
        ),
        name="to_cells",
    )(me, table, base, *held_in_hbm(modes))


def sigmoid_of(values):
    return 0.5 + 0.5 * jnp.tanh(0.5 * values)


def mix_lat(me_ref, table_ref, bands_refs, band_ref, mixed_ref):
    samples, rows, share, width = bands_refs[0].shape
    half = table_ref.shape[0] // 2
    for sample in range(samples):
        for offset, bands_ref in enumerate(bands_refs):
            place = place_of(me_ref, offset, rows * share)
            band_ref[sample, place] = bands_ref[sample].reshape(rows * share, width)
        mixed = product_of(table_ref[...], band_ref[sample]).astype(jnp.bfloat16)
        spot = pl.ds(sample * half, half)
        mixed_ref[spot, 0:width] = mixed[:half]
        mixed_ref[spot, width : 2 * width] = mixed[half:]


def unmix_lat(me_ref, table_ref, mixed_ref, band_ref, bands_refs):
    samples, rows, share, width = bands_refs[0].shape
    half = table_ref.shape[0] // 2
    for sample in range(samples):
        spot = pl.ds(sample * half, half)
        joined = jnp.concatenate(
            [mixed_ref[spot, 0:width], mixed_ref[spot, width : 2 * width]], axis=0
        )
        band_ref[sample] = product_of(table_ref[...], joined).astype(jnp.bfloat16)
        for offset, bands_ref in enumerate(bands_refs):
            place = place_of(me_ref, offset, rows * share)
            bands_ref[sample] = band_ref[sample, place].reshape(rows, share, width)


def activate(mixed_ref, w1_ref, b1_ref):
    pre = product_of(mixed_ref[0], w1_ref[0]) + b1_ref[0]
    logistic = sigmoid_of(pre)
    return logistic, pre * logistic


def bend(act_ref, w2_ref, b2_ref):
    out = product_of(act_ref[...], w2_ref[0]) + b2_ref[0]
    return out, jnp.tanh(out * (1.0 / shrink_level))


def forward_kernel(owners, me_ref, lat_ref, unlat_ref, w1_ref, b1_ref, w2_ref, b2_ref, *refs):
    bands_refs, image_refs = refs[:owners], refs[owners : 2 * owners]
    mixed_ref, act_ref, band_ref = refs[2 * owners :]
    mix_lat(me_ref, lat_ref, bands_refs, band_ref, mixed_ref.at[0])
    act_ref[...] = activate(mixed_ref, w1_ref, b1_ref)[1].astype(jnp.bfloat16)
    out, bent = bend(act_ref, w2_ref, b2_ref)
    act_ref[...] = (out - shrink_level * bent).astype(jnp.bfloat16)
    unmix_lat(me_ref, unlat_ref, act_ref, band_ref, image_refs)


def backward_kernel(
    block_size, owners, me_ref, lat_ref, unlat_ref, w1_ref, b1_ref, w2_ref, b2_ref, mixed_ref, *refs
):
    bands_refs, image_refs = refs[:owners], refs[owners : 2 * owners]
    sums_ref, act_ref, gate_ref, cot_ref, kept_ref, band_ref = refs[2 * owners :]
    transposed = (((1,), (1,)), ((), ()))
    summed = (((0,), (0,)), ((), ()))

    def times(former, latter, dims):
        return lax.dot_general(former, latter, dims, preferred_element_type=jnp.float32)

    def weight_sums(acts, grads, slot):
        width = acts.shape[1] // 2
        full = times(acts, grads, summed)
        real = full[:width, :width] + full[width:, width:]
        imag = full[:width, width:] - full[width:, :width]
        bias = jnp.sum(grads.astype(jnp.float32), axis=0, keepdims=True)
        size = block_size
        owner = lax.broadcasted_iota(jnp.int32, (size, width), 1) // size
        extra = sums_ref.shape[3] - size
        first = lax.broadcasted_iota(jnp.int32, (extra, width), 0) == 0
        for part, values in enumerate((real, imag)):
            joined = values[:size]
            for block in range(1, width // size):
                joined = jnp.where(owner == block, values[block * size : (block + 1) * size], joined)
            sums_ref[slot, part, 0, 0:size] = joined
            row = bias[:, part * width : (part + 1) * width]
            sums_ref[slot, part, 0, size:] = jnp.where(first, row, 0.0)

    logistic, act = activate(mixed_ref, w1_ref, b1_ref)
    act_ref[...] = act.astype(jnp.bfloat16)
    gate_ref[...] = logistic + act * (1.0 - logistic)
    mix_lat(me_ref, lat_ref, bands_refs, band_ref, cot_ref)
    _, bent = bend(act_ref, w2_ref, b2_ref)
    kept_ref[...] = (cot_ref[...].astype(jnp.float32) * (bent * bent)).astype(jnp.bfloat16)
    back = times(kept_ref[...], w2_ref[0], transposed)
    cot_ref[...] = (back * gate_ref[...]).astype(jnp.bfloat16)
    weight_sums(act_ref[...], kept_ref[...], 1)
    kept_ref[...] = times(cot_ref[...], w1_ref[0], transposed).astype(jnp.bfloat16)
    weight_sums(mixed_ref[0], cot_ref[...], 0)
    unmix_lat(me_ref, unlat_ref, kept_ref, band_ref, image_refs)


def group_spec(*shape):
    return pl.BlockSpec((1,) + shape, lambda g, *_: (g,) + (0,) * len(shape))


def bands_specs(bands, groups):
    shape = bands[0].shape
    block = shape[:-1] + (shape[-1] // groups,)
    return (pl.BlockSpec(block, lambda g, *_: (0, 0, 0, g)),) * len(bands)


def in_hbm(shape, dtype):
    return pltpu.HBM(shape, dtype)


def shapes_of(bands):
    return tuple(in_hbm(band.shape, band.dtype) for band in bands)


def held_in_hbm(bands):
    return [pltpu.with_memory_space_constraint(band, pltpu.HBM) for band in bands]


def forward_mid(me, lat, unlat, bands, w1, b1, w2, b2):
    groups, lanes, _ = w1.shape
    size = lat.shape[0]
    samples = bands[0].shape[0]
    positions = samples * size // 2
    table = pl.BlockSpec((size, size), lambda g, _: (0, 0))
    state = (groups, positions, lanes)
    state_spec = group_spec(positions, lanes)
    specs = bands_specs(bands, groups)
    results = pl.pallas_call(
        functools.partial(forward_kernel, len(bands)),
        grid_spec=pltpu.PrefetchScalarGridSpec(
            num_scalar_prefetch=1,
            grid=(groups,),
            in_specs=[
                table, table,
                group_spec(lanes, lanes), group_spec(1, lanes),
                group_spec(lanes, lanes), group_spec(1, lanes),
                *specs,
            ],
            out_specs=specs + (state_spec,),
            scratch_shapes=[
                pltpu.VMEM((positions, lanes), jnp.bfloat16),
                pltpu.VMEM((samples, size, lanes // 2), jnp.bfloat16),
            ],
        ),
        out_shape=shapes_of(bands) + (jax.ShapeDtypeStruct(state, jnp.bfloat16),),
        compiler_params=params(28),
        cost_estimate=pl.CostEstimate(
            flops=4 * groups * positions * lanes * lanes,
            bytes_accessed=16 * groups * positions * lanes + 4 * groups * lanes * lanes,
            transcendentals=2 * groups * positions * lanes,
        ),
        name="mix_forward",
    )(me, lat, unlat, w1, b1, w2, b2, *held_in_hbm(bands))
    return results[: len(bands)], results[len(bands)]


def backward_mid(me, lat, unlat, bands, w1, b1, w2, b2, state, count):
    groups, lanes, _ = w1.shape
    size = lat.shape[0]
    samples = bands[0].shape[0]
    positions = samples * size // 2
    table = pl.BlockSpec((size, size), lambda g, _: (0, 0))
    specs = bands_specs(bands, groups)
    size_of_block = lanes // 2 // (count // groups)
    rows = size_of_block + 16
    results = pl.pallas_call(
        functools.partial(backward_kernel, size_of_block, len(bands)),
        grid_spec=pltpu.PrefetchScalarGridSpec(
            num_scalar_prefetch=1,
            grid=(groups,),
            in_specs=[
                table, table,
                group_spec(lanes, lanes), group_spec(1, lanes),
                group_spec(lanes, lanes), group_spec(1, lanes),
                group_spec(positions, lanes), *specs,
            ],
            out_specs=specs + (
                pl.BlockSpec((2, 2, 1, rows, lanes // 2), lambda g, _: (0, 0, g, 0, 0)),
            ),
            scratch_shapes=[
                pltpu.VMEM((positions, lanes), jnp.bfloat16),
                pltpu.VMEM((positions, lanes), jnp.float32),
                pltpu.VMEM((positions, lanes), jnp.bfloat16),
                pltpu.VMEM((positions, lanes), jnp.bfloat16),
                pltpu.VMEM((samples, size, lanes // 2), jnp.bfloat16),
            ],
        ),
        out_shape=shapes_of(bands)
        + (jax.ShapeDtypeStruct((2, 2, groups, rows, lanes // 2), jnp.float32),),
        compiler_params=params(32),
        cost_estimate=pl.CostEstimate(
            flops=8 * groups * positions * lanes * lanes,
            bytes_accessed=16 * groups * positions * lanes + 4 * groups * lanes * lanes,
            transcendentals=0,
        ),
        name="mix_backward",
    )(me, lat, unlat, w1, b1, w2, b2, state, *held_in_hbm(bands))
    return results[: len(bands)], results[len(bands)]


def swap_with(values, axis, distance):
    pairs = [(i, i ^ distance) for i in range(lax.axis_size(axis))]
    return lax.ppermute(values, axis, pairs)


class Chain:
    def __init__(self, depth, arrived):
        self.depth = depth
        self.arrived = list(arrived)

    def swap(self, values, axis, distance):
        if len(self.arrived) >= self.depth:
            values, _ = lax.optimization_barrier((values, self.arrived[-self.depth]))
        self.arrived.append(swap_with(values, axis, distance))
        return self.arrived[-1]


def mixed_order(size):
    far = list(range(size // 2, size))
    near = [offset for offset in (2, 3, 1) if offset < size // 2]
    near += list(range(4, size // 2))
    order = []
    while far or near:
        order += far[:1] + near[:1]
        far, near = far[1:], near[1:]
    return order


def pick(pair, side):
    return lax.dynamic_index_in_dim(pair, side, 0, keepdims=False)


def by_place(blocks, bits):
    shape = blocks.shape
    for level, bit in enumerate(bits):
        split = blocks.reshape((2**level, 2, -1) + shape[-2:])
        blocks = jnp.where(bit == 0, split, jnp.concatenate([split[:, 1:], split[:, :1]], axis=1))
    return blocks


class GroupSum:
    def __init__(self, chain, sums):
        self.chain = chain
        self.lanes = sums.shape[-1]
        self.shape = sums.shape
        self.side = lax.axis_index("dp")
        self.me = lax.axis_index("space")
        self.count = lax.axis_size("space") // 2
        self.held = sums.reshape(-1, self.lanes)

    def halve(self, axis, distance, bit):
        pair = self.held.reshape(2, -1, self.lanes)
        taken = self.chain.swap(pick(pair, 1 - bit), axis, distance)
        self.held = pick(pair, bit) + taken

    def over_dp(self):
        self.halve("dp", 1, self.side)

    def over_next(self):
        self.halve("space", 1, self.me % 2)

    def scatter(self):
        shares = self.held.reshape(self.count, -1, self.lanes)
        place = self.me // 2
        total = pick(shares, place)
        for offset in range(1, self.count):
            given = pick(shares, place ^ offset).astype(jnp.bfloat16)
            total += self.chain.swap(given, "space", 2 * offset).astype(jnp.float32)
        self.total = total.astype(jnp.bfloat16)

    def gather(self):
        taken = [self.total]
        for offset in range(1, self.count):
            taken.append(self.chain.swap(self.total, "space", 2 * offset))
        self.quarter = jnp.stack(taken)

    def gather_next(self):
        self.half = jnp.stack([self.quarter, self.chain.swap(self.quarter, "space", 1)])

    def gather_dp(self):
        self.other = self.chain.swap(self.half, "dp", 1)

    def joined(self):
        bits = [self.side, self.me % 2]
        level = self.count
        while level > 1:
            bits.append(self.me // level % 2)
            level //= 2
        return by_place(jnp.stack([self.half, self.other]), bits).reshape(self.shape)


def finish_kernel(factor, me_ref, half_ref, other_ref, *out_refs):
    side, near, place = me_ref[0], me_ref[1], me_ref[2]
    for which in range(2):
        blocks_ref, bias_ref = out_refs[2 * which : 2 * which + 2]
        edge = blocks_ref.shape[-1]
        per_group = half_ref.shape[3] // edge
        groups = blocks_ref.shape[1] // per_group
        pieces = half_ref.shape[1] // groups
        height = half_ref.shape[2]
        for part in range(2):
            for piece in range(groups * pieces):
                spot = (part ^ near, piece ^ place)
                own = half_ref[spot].astype(jnp.float32)
                value = jnp.where(side == which, own, other_ref[spot].astype(jnp.float32)) * factor
                group, first = piece // pieces, piece % pieces * height
                count = max(0, min(edge - first, height))
                for block in range(per_group):
                    lanes = slice(block * edge, (block + 1) * edge)
                    index = group * per_group + block
                    if count > 0:
                        rows = pl.ds(first, count)
                        blocks_ref[part, index, rows] = value[:count, lanes]
                    if first <= edge < first + height:
                        row = edge - first
                        bias_ref[part, pl.ds(index, 1)] = value[row : row + 1, lanes]


def finish_sums(me, half, other, factor, weight_shape, bias_shape):
    outs = [weight_shape, bias_shape] * 2
    return pl.pallas_call(
        functools.partial(finish_kernel, factor),
        out_shape=[jax.ShapeDtypeStruct(shape, jnp.float32) for shape in outs],
        in_specs=[pl.BlockSpec(memory_space=pltpu.SMEM)]
        + [pl.BlockSpec(memory_space=pltpu.VMEM)] * 2,
        out_specs=[pl.BlockSpec(memory_space=pltpu.VMEM)] * 4,
        compiler_params=pltpu.CompilerParams(vmem_limit_bytes=12 * MIB),
        cost_estimate=pl.CostEstimate(flops=0, bytes_accessed=4 * MIB, transcendentals=0),
        name="finish_sums",
    )(me, half, other)


def body(fields, cotangent, w_first, b_first, w_second, b_second):
    samples, rows, width, channels = fields.shape
    owners = lax.axis_size("space")
    lat_total = rows * owners
    modes = KW // owners
    count, edge = w_first.shape[1:3]
    groups = 2
    direct = 2 * modes % 16 == 0
    lead = owners if direct else 1

    order = mixed_order(owners)

    def send_out(blocks):
        if direct:
            taken = {0: blocks[0]}
            for offset in order:
                taken[offset] = swap_with(blocks[offset], "space", offset)
            return [taken[offset] for offset in range(owners)]
        spectrum = blocks[0].reshape(samples, rows, owners, 2 * modes, channels)
        spectrum = jnp.transpose(spectrum, (2, 0, 1, 3, 4))
        arrived = lax.all_to_all(spectrum, "space", split_axis=0, concat_axis=0, tiled=True)
        return [jnp.transpose(arrived, (1, 0, 2, 3, 4)).reshape(samples, 1, -1, channels)]

    def send_back(blocks):
        bands = blocks[0].reshape(samples, owners, rows, 2 * modes, channels)
        bands = jnp.transpose(bands, (1, 0, 2, 3, 4))
        arrived = lax.all_to_all(bands, "space", split_axis=0, concat_axis=0, tiled=True)
        return [jnp.transpose(arrived, (1, 2, 0, 3, 4)).reshape(samples, rows, -1, channels)]

    me = lax.axis_index("space") if direct else 0
    me = jnp.full((1,), me, jnp.int32)
    plain, scaled = lon_tables(KW, width, owners)
    lat = lat_spread(lat_total, modes)

    spectrum = to_modes(me, plain, fields, lead)
    spectrum, cotangent, w_first, w_second = lax.optimization_barrier(
        (spectrum, cotangent, w_first, w_second)
    )
    gathered = send_out(spectrum)
    cot_spec = to_modes(me, scaled, cotangent, lead)
    w1, w2 = spread_weights(groups, w_first, w_second)
    b1, b2 = block_bias(b_first, groups), block_bias(b_second, groups)

    image, state = forward_mid(me, lat, lat.T, gathered, w1, b1, w2, b2)
    if direct:
        late = tuple(cot_spec[offset] for offset in order[FIRST:])
        late, image = lax.optimization_barrier((late, image))
        cot_spec = list(cot_spec)
        for offset, block in zip(order[FIRST:], late):
            cot_spec[offset] = block
    cot_gathered = send_out(cot_spec)
    image_band = send_out(image) if direct else send_back(image)
    grad_image, sums = backward_mid(
        me, lat, lat.T, cot_gathered, w1, b1, w2, b2, state, count
    )
    positions = samples * lax.axis_size("dp") * lat_total * KW
    factor = 1.0 / math.sqrt(positions)
    if direct:
        early = tuple(image_band[offset] for offset in order[:HELD])
        grad_image, sums, _ = lax.optimization_barrier((grad_image, sums, early))
        chain = Chain(DEPTH, [image_band[offset] for offset in order])
    else:
        chain = Chain(DEPTH, [])
    group_sum = GroupSum(chain, sums)
    steps = [
        group_sum.over_dp, group_sum.over_next, group_sum.scatter,
        group_sum.gather, group_sum.gather_next, group_sum.gather_dp,
    ]
    if direct:
        grad_band = [grad_image[0]] + [None] * (owners - 1)
        for place, offset in enumerate(order):
            for _ in range(STEPS_BEFORE.count(place)):
                steps.pop(0)()
            grad_band[offset] = chain.swap(grad_image[offset], "space", offset)
    else:
        grad_band = send_back(grad_image)
    for step in steps:
        step()
    output = to_cells(me, scaled.T, image_band, fields)
    grad_fields = to_cells(me, plain.T, grad_band, cotangent)

    if direct and owners // 2 % groups == 0:
        place = lax.axis_index("space")
        here = jnp.stack([lax.axis_index("dp"), place % 2, place // 2]).astype(jnp.int32)
        grads = finish_sums(
            here, group_sum.half, group_sum.other, factor, w_first.shape, b_first.shape
        )
        return (output, grad_fields) + tuple(grads)
    sums = group_sum.joined().astype(jnp.float32) * factor
    grads = []
    for which in range(2):
        blocks = sums[which, :, :, :edge].reshape(2, groups, edge, count // groups, edge)
        grads.append(jnp.transpose(blocks, (0, 1, 3, 2, 4)).reshape(w_first.shape))
        grads.append(sums[which, :, :, edge].reshape(b_first.shape))
    return (output, grad_fields) + tuple(grads)


def solution(mesh):
    split = P(("parts", "dp"), "space", None, None)
    in_specs = (split, split, P(), P(), P(), P())
    out_specs = (
        split,
        split,
        P("parts", None, None, None),
        P("parts", None, None),
        P("parts", None, None, None),
        P("parts", None, None),
    )
    return jax.shard_map(body, mesh=mesh, in_specs=in_specs, out_specs=out_specs, check_vma=False)
```

```python
import functools
import math

import jax
import jax.numpy as jnp
from jax import lax
from jax.experimental import pallas as pl
from jax.experimental.pallas import tpu as pltpu
from jax.sharding import PartitionSpec as P
import ml_dtypes
import numpy as np

KW = 64
shrink_level = 0.05
HELD = 5
FIRST = 4
MIB = 1024 * 1024


def product_of(former, latter):
    return jnp.dot(former, latter, preferred_element_type=jnp.float32)


def lon_tables(mode_count, cell_count, owners):
    wavenums = np.arange(mode_count, dtype=np.int32)
    columns = np.arange(cell_count, dtype=np.int32)
    phase_index = (wavenums[:, None] * columns[None, :] % cell_count).astype(np.float32)
    phases = phase_index * np.float32(2.0 * math.pi / cell_count)
    factor = np.float32(1.0 / math.sqrt(cell_count))
    forward = np.stack([np.cos(phases) * factor, -np.sin(phases) * factor])
    scaled = forward * np.where(wavenums == 0, 1.0, 2.0).astype(np.float32)[:, None]

    def ordered(table):
        split = table.reshape(2, owners, -1, cell_count).transpose(1, 0, 2, 3)
        return split.reshape(-1, cell_count).astype(ml_dtypes.bfloat16)

    return ordered(forward), ordered(scaled)


def lat_spread(row_count, modes):
    indices = np.arange(row_count, dtype=np.int32)
    phase_index = (indices[:, None] * indices[None, :] % row_count).astype(np.float32)
    phases = phase_index * np.float32(2.0 * math.pi / row_count)
    factor = np.float32(1.0 / math.sqrt(row_count))
    cosine = np.cos(phases) * factor
    sine_part = np.sin(phases) * factor
    table = np.stack([np.stack([cosine, sine_part], -1), np.stack([-sine_part, cosine], -1)])
    same = np.eye(modes, dtype=np.float32)
    spread = table[:, :, None, :, :, None] * same[None, None, :, None, None, :]
    size = 2 * row_count * modes
    return spread.reshape(size, size).astype(ml_dtypes.bfloat16)


def block_bias(bias, groups):
    return jnp.transpose(bias.reshape(2, groups, 1, -1), (1, 2, 0, 3)).reshape(groups, 1, -1)


def spread_kernel(*refs):
    half_way = len(refs) // 2
    for blocks_ref, joined_ref in zip(refs[:half_way], refs[half_way:]):
        _, per, size, _ = blocks_ref.shape
        width = per * size
        row = lax.broadcasted_iota(jnp.int32, (size, width), 0)
        lane = lax.broadcasted_iota(jnp.int32, (size, width), 1)
        for block in range(per):
            place = (row + block * size == lane).astype(jnp.bfloat16)
            real = product_of(blocks_ref[0, block], place).astype(jnp.bfloat16)
            imag = product_of(blocks_ref[1, block], place)
            upper = pl.ds(block * size, size)
            lower = pl.ds(width + block * size, size)
            joined_ref[0, upper, 0:width] = real
            joined_ref[0, upper, width : 2 * width] = imag.astype(jnp.bfloat16)
            joined_ref[0, lower, 0:width] = (-imag).astype(jnp.bfloat16)
            joined_ref[0, lower, width : 2 * width] = real


def spread_weights(groups, *weights):
    _, count, size, _ = weights[0].shape
    per = count // groups
    lanes = 2 * per * size
    shape = in_hbm((groups, lanes, lanes), jnp.bfloat16)
    return pl.pallas_call(
        spread_kernel,
        grid=(groups,),
        out_shape=(shape,) * len(weights),
        in_specs=[pl.BlockSpec((2, per, size, size), lambda g: (0, g, 0, 0))] * len(weights),
        out_specs=(group_spec(lanes, lanes),) * len(weights),
        compiler_params=params(12),
        cost_estimate=pl.CostEstimate(
            flops=len(weights) * 2 * count * size * size * lanes,
            bytes_accessed=len(weights) * 2 * groups * lanes * lanes,
            transcendentals=0,
        ),
        name="spread_weights",
    )(*weights)


def params(mebibytes):
    return pltpu.CompilerParams(
        vmem_limit_bytes=mebibytes * MIB, dimension_semantics=("arbitrary",)
    )


def place_of(me_ref, offset, rows):
    return pl.ds(pl.multiple_of((me_ref[0] ^ offset) * rows, rows), rows)


def in_hbm(shape, dtype):
    return pltpu.HBM(shape, dtype)


def hbm(*arrays):
    return [pltpu.with_memory_space_constraint(array, pltpu.HBM) for array in arrays]


def to_modes_kernel(me_ref, table_ref, cells_ref, *refs):
    modes_refs, held_ref = refs[:-1], refs[-1]
    rows = cells_ref.shape[1]
    share = modes_refs[0].shape[0] // rows
    for row in range(rows):
        spectrum = product_of(table_ref[...], cells_ref[0, row])
        held_ref[row] = spectrum.astype(jnp.bfloat16)
        for offset, modes_ref in enumerate(modes_refs):
            modes_ref[pl.ds(row * share, share)] = held_ref[row, place_of(me_ref, offset, share)]


def to_modes(me, table, cells, owners):
    samples, rows, width, channels = cells.shape
    size = table.shape[0]
    part = rows * size // owners
    return pl.pallas_call(
        to_modes_kernel,
        grid_spec=pltpu.PrefetchScalarGridSpec(
            num_scalar_prefetch=1,
            grid=(samples,),
            in_specs=[
                pl.BlockSpec((size, width), lambda b, _: (0, 0)),
                pl.BlockSpec((1, rows, width, channels), lambda b, _: (b, 0, 0, 0)),
            ],
            out_specs=(pl.BlockSpec((part, channels), lambda b, _: (b, 0)),) * owners,
            scratch_shapes=[pltpu.VMEM((rows, size, channels), jnp.bfloat16)],
        ),
        out_shape=(in_hbm((samples * part, channels), jnp.bfloat16),) * owners,
        compiler_params=params(12),
        cost_estimate=pl.CostEstimate(
            flops=2 * samples * rows * size * width * channels,
            bytes_accessed=2 * samples * rows * channels * (width + size),
            transcendentals=0,
        ),
        name="to_modes",
    )(me, table, *hbm(cells))


def to_cells_kernel(me_ref, table_ref, base_ref, *refs):
    modes_refs, out_ref, held_ref = refs[:-2], refs[-2], refs[-1]
    rows = base_ref.shape[1]
    share = modes_refs[0].shape[0] // rows
    for row in range(rows):
        for offset, modes_ref in enumerate(modes_refs):
            spot = place_of(me_ref, offset, share)
            held_ref[row, spot] = modes_ref[pl.ds(row * share, share)]
        image = product_of(table_ref[...], held_ref[row])
        out_ref[0, row] = (base_ref[0, row].astype(jnp.float32) + image).astype(jnp.bfloat16)


def to_cells(me, table, modes, base):
    samples, rows, width, channels = base.shape
    size = table.shape[1]
    part = rows * size // len(modes)
    block = pl.BlockSpec((1, rows, width, channels), lambda b, _: (b, 0, 0, 0))
    return pl.pallas_call(
        to_cells_kernel,
        grid_spec=pltpu.PrefetchScalarGridSpec(
            num_scalar_prefetch=1,
            grid=(samples,),
            in_specs=[pl.BlockSpec((width, size), lambda b, _: (0, 0)), block]
            + [pl.BlockSpec((part, channels), lambda b, _: (b, 0))] * len(modes),
            out_specs=block,
            scratch_shapes=[pltpu.VMEM((rows, size, channels), jnp.bfloat16)],
        ),
        out_shape=jax.ShapeDtypeStruct(base.shape, jnp.bfloat16),
        compiler_params=params(12),
        cost_estimate=pl.CostEstimate(
            flops=2 * samples * rows * size * width * channels,
            bytes_accessed=2 * samples * rows * channels * (2 * width + size),
            transcendentals=0,
        ),
        name="to_cells",
    )(me, table, *hbm(base, *modes))


def sigmoid_of(values):
    return 0.5 + 0.5 * jnp.tanh(0.5 * values)


def mix_lat(me_ref, table_ref, bands_refs, band_ref, mixed_ref):
    samples, size, width = band_ref.shape
    part, half = size // len(bands_refs), size // 2
    for sample in range(samples):
        for offset, bands_ref in enumerate(bands_refs):
            place = place_of(me_ref, offset, part)
            band_ref[sample, place] = bands_ref[pl.ds(sample * part, part)]
        mixed = product_of(table_ref[...], band_ref[sample]).astype(jnp.bfloat16)
        spot = pl.ds(sample * half, half)
        mixed_ref[spot, 0:width] = mixed[:half]
        mixed_ref[spot, width : 2 * width] = mixed[half:]


def unmix_lat(me_ref, table_ref, mixed_ref, band_ref, bands_refs):
    samples, size, width = band_ref.shape
    part, half = size // len(bands_refs), size // 2
    for sample in range(samples):
        spot = pl.ds(sample * half, half)
        joined = jnp.concatenate(
            [mixed_ref[spot, 0:width], mixed_ref[spot, width : 2 * width]], axis=0
        )
        band_ref[sample] = product_of(table_ref[...], joined).astype(jnp.bfloat16)
        for offset, bands_ref in enumerate(bands_refs):
            place = place_of(me_ref, offset, part)
            bands_ref[pl.ds(sample * part, part)] = band_ref[sample, place]


def activate(mixed_ref, w1_ref, b1_ref):
    pre = product_of(mixed_ref[0], w1_ref[0]) + b1_ref[0]
    logistic = sigmoid_of(pre)
    return logistic, pre * logistic


def bend(act_ref, w2_ref, b2_ref):
    out = product_of(act_ref[...], w2_ref[0]) + b2_ref[0]
    return out, jnp.tanh(out * (1.0 / shrink_level))


def forward_kernel(owners, me_ref, lat_ref, unlat_ref, w1_ref, b1_ref, w2_ref, b2_ref, *refs):
    bands_refs, image_refs = refs[:owners], refs[owners : 2 * owners]
    mixed_ref, act_ref, band_ref = refs[2 * owners :]
    mix_lat(me_ref, lat_ref, bands_refs, band_ref, mixed_ref.at[0])
    act_ref[...] = activate(mixed_ref, w1_ref, b1_ref)[1].astype(jnp.bfloat16)
    out, bent = bend(act_ref, w2_ref, b2_ref)
    act_ref[...] = (out - shrink_level * bent).astype(jnp.bfloat16)
    unmix_lat(me_ref, unlat_ref, act_ref, band_ref, image_refs)


def backward_kernel(
    block_size, owners, me_ref, lat_ref, unlat_ref, w1_ref, b1_ref, w2_ref, b2_ref, mixed_ref, *refs
):
    bands_refs, image_refs = refs[:owners], refs[owners : 2 * owners]
    sums_ref, act_ref, gate_ref, cot_ref, kept_ref, band_ref = refs[2 * owners :]
    size_of_image = band_ref.shape[0] * band_ref.shape[1] // owners
    transposed = (((1,), (1,)), ((), ()))
    summed = (((0,), (0,)), ((), ()))

    def times(former, latter, dims):
        return lax.dot_general(former, latter, dims, preferred_element_type=jnp.float32)

    def weight_sums(acts, grads, slot):
        width = acts.shape[1] // 2
        full = times(acts, grads, summed)
        real = full[:width, :width] + full[width:, width:]
        imag = full[:width, width:] - full[width:, :width]
        bias = jnp.sum(grads.astype(jnp.float32), axis=0, keepdims=True)
        size = block_size
        owner = lax.broadcasted_iota(jnp.int32, (size, width), 1) // size
        extra = sums_ref.shape[2] - size
        first = lax.broadcasted_iota(jnp.int32, (extra, width), 0) == 0
        for part, values in enumerate((real, imag)):
            joined = values[:size]
            for block in range(1, width // size):
                joined = jnp.where(owner == block, values[block * size : (block + 1) * size], joined)
            sums_ref[slot, part, 0:size] = joined.astype(sums_ref.dtype)
            row = bias[:, part * width : (part + 1) * width]
            sums_ref[slot, part, size:] = jnp.where(first, row, 0.0).astype(sums_ref.dtype)

    logistic, act = activate(mixed_ref, w1_ref, b1_ref)
    act_ref[...] = act.astype(jnp.bfloat16)
    gate_ref[...] = logistic + act * (1.0 - logistic)
    mix_lat(me_ref, lat_ref, bands_refs, band_ref, cot_ref)
    _, bent = bend(act_ref, w2_ref, b2_ref)
    kept_ref[...] = (cot_ref[...].astype(jnp.float32) * (bent * bent)).astype(jnp.bfloat16)
    back = times(kept_ref[...], w2_ref[0], transposed)
    cot_ref[...] = (back * gate_ref[...]).astype(jnp.bfloat16)
    weight_sums(act_ref[...], kept_ref[...], 1)
    kept_ref[...] = times(cot_ref[...], w1_ref[0], transposed).astype(jnp.bfloat16)
    weight_sums(mixed_ref[0], cot_ref[...], 0)
    unmix_lat(me_ref, unlat_ref, kept_ref, band_ref, image_refs)
    share = image_refs[0].shape[0] - size_of_image
    if share > 0:
        runs = sums_ref.shape[2] // share
        for offset, image_ref in enumerate(image_refs):
            owner = me_ref[0] ^ offset
            pair, run = owner // runs, owner % runs
            rows = pl.ds(pl.multiple_of(run * share, share), share)
            image_ref[pl.ds(size_of_image, share)] = sums_ref[pair // 2, pair % 2, rows].astype(
                jnp.bfloat16
            )


def group_spec(*shape):
    return pl.BlockSpec((1,) + shape, lambda g, *_: (g,) + (0,) * len(shape))


def bands_specs(rows, bands, groups):
    block = (rows, bands[0].shape[1] // groups)
    return (pl.BlockSpec(block, lambda g, *_: (0, g)),) * len(bands)


def forward_mid(me, lat, unlat, bands, w1, b1, w2, b2):
    groups, lanes, _ = w1.shape
    size = lat.shape[0]
    samples = bands[0].shape[0] * len(bands) // size
    positions = samples * size // 2
    table = pl.BlockSpec((size, size), lambda g, _: (0, 0))
    state = (groups, positions, lanes)
    specs = bands_specs(bands[0].shape[0], bands, groups)
    results = pl.pallas_call(
        functools.partial(forward_kernel, len(bands)),
        grid_spec=pltpu.PrefetchScalarGridSpec(
            num_scalar_prefetch=1,
            grid=(groups,),
            in_specs=[
                table, table,
                group_spec(lanes, lanes), group_spec(1, lanes),
                group_spec(lanes, lanes), group_spec(1, lanes),
                *specs,
            ],
            out_specs=specs + (group_spec(positions, lanes),),
            scratch_shapes=[
                pltpu.VMEM((positions, lanes), jnp.bfloat16),
                pltpu.VMEM((samples, size, lanes // 2), jnp.bfloat16),
            ],
        ),
        out_shape=tuple(in_hbm(band.shape, band.dtype) for band in bands)
        + (in_hbm(state, jnp.bfloat16),),
        compiler_params=params(28),
        cost_estimate=pl.CostEstimate(
            flops=4 * groups * positions * lanes * lanes,
            bytes_accessed=16 * groups * positions * lanes + 4 * groups * lanes * lanes,
            transcendentals=2 * groups * positions * lanes,
        ),
        name="mix_forward",
    )(me, lat, unlat, *hbm(w1), b1, *hbm(w2), b2, *hbm(*bands))
    return results[: len(bands)], results[len(bands)]


def backward_mid(me, lat, unlat, bands, w1, b1, w2, b2, state, count, share):
    groups, lanes, _ = w1.shape
    size = lat.shape[0]
    image_rows = bands[0].shape[0]
    samples = image_rows * len(bands) // size
    positions = samples * size // 2
    table = pl.BlockSpec((size, size), lambda g, _: (0, 0))
    size_of_block = lanes // 2 // (count // groups)
    rows = size_of_block + 16
    sums = (2, 2, rows, lanes // 2)
    out_shape = (in_hbm((image_rows + share, bands[0].shape[1]), jnp.bfloat16),) * len(bands)
    out_specs = bands_specs(image_rows + share, bands, groups)
    scratch_shapes = [
        pltpu.VMEM((positions, lanes), jnp.bfloat16),
        pltpu.VMEM((positions, lanes), jnp.float32),
        pltpu.VMEM((positions, lanes), jnp.bfloat16),
        pltpu.VMEM((positions, lanes), jnp.bfloat16),
        pltpu.VMEM((samples, size, lanes // 2), jnp.bfloat16),
    ]
    if share > 0:
        scratch_shapes = [pltpu.VMEM(sums, jnp.float32)] + scratch_shapes
    else:
        out_shape += (jax.ShapeDtypeStruct(sums[:3] + (groups * sums[3],), jnp.float32),)
        out_specs += (pl.BlockSpec(sums, lambda g, _: (0, 0, 0, g)),)
    results = pl.pallas_call(
        functools.partial(backward_kernel, size_of_block, len(bands)),
        grid_spec=pltpu.PrefetchScalarGridSpec(
            num_scalar_prefetch=1,
            grid=(groups,),
            in_specs=[
                table, table,
                group_spec(lanes, lanes), group_spec(1, lanes),
                group_spec(lanes, lanes), group_spec(1, lanes),
                group_spec(positions, lanes), *bands_specs(image_rows, bands, groups),
            ],
            out_specs=out_specs,
            scratch_shapes=scratch_shapes,
        ),
        out_shape=out_shape,
        compiler_params=params(32),
        cost_estimate=pl.CostEstimate(
            flops=8 * groups * positions * lanes * lanes,
            bytes_accessed=16 * groups * positions * lanes + 4 * groups * lanes * lanes,
            transcendentals=0,
        ),
        name="mix_backward",
    )(me, lat, unlat, *hbm(w1), b1, *hbm(w2), b2, *hbm(state, *bands))
    return results[: len(bands)], results[len(bands) :]


def swap_with(values, axis, distance):
    pairs = [(i, i ^ distance) for i in range(lax.axis_size(axis))]
    return lax.ppermute(values, axis, pairs)


def mixed_order(size):
    far = list(range(size // 2, size))
    near = [offset for offset in (2, 3, 1) if offset < size // 2]
    near += list(range(4, size // 2))
    order = []
    while far or near:
        order += far[:1] + near[:1]
        far, near = far[1:], near[1:]
    return order


def finish_kernel(factor, me_ref, *refs):
    shares_refs, out_refs = refs[:-5], refs[-5:-1]
    held_ref = refs[-1]
    run = shares_refs[0].shape[0]
    for offset, shares_ref in enumerate(shares_refs):
        held_ref[me_ref[0] ^ offset] = shares_ref[...].astype(jnp.float32) * factor
    runs = len(shares_refs) // 4
    for which in range(2):
        blocks_ref, bias_ref = out_refs[2 * which : 2 * which + 2]
        edge = blocks_ref.shape[-1]
        for part in range(2):
            for piece in range(runs):
                value = held_ref[(2 * which + part) * runs + piece]
                first = piece * run
                count = max(0, min(edge - first, run))
                for block in range(blocks_ref.shape[1]):
                    lanes = slice(block * edge, (block + 1) * edge)
                    if count > 0:
                        blocks_ref[part, block, pl.ds(first, count)] = value[:count, lanes]
                    if first <= edge < first + run:
                        row = edge - first
                        bias_ref[part, pl.ds(block, 1)] = value[row : row + 1, lanes]


def finish_sums(me, shares, factor, weight_shape, bias_shape):
    outs = [weight_shape, bias_shape] * 2
    return pl.pallas_call(
        functools.partial(finish_kernel, factor),
        out_shape=[jax.ShapeDtypeStruct(shape, jnp.float32) for shape in outs],
        in_specs=[pl.BlockSpec(memory_space=pltpu.SMEM)]
        + [pl.BlockSpec(memory_space=pltpu.VMEM)] * len(shares),
        out_specs=[pl.BlockSpec(memory_space=pltpu.VMEM)] * 4,
        scratch_shapes=[pltpu.VMEM((len(shares),) + shares[0].shape, jnp.float32)],
        compiler_params=pltpu.CompilerParams(vmem_limit_bytes=16 * MIB),
        cost_estimate=pl.CostEstimate(flops=0, bytes_accessed=4 * MIB, transcendentals=0),
        name="finish_sums",
    )(me, *shares)


def body(fields, cotangent, w_first, b_first, w_second, b_second):
    samples, rows, width, channels = fields.shape
    owners = lax.axis_size("space")
    lat_total = rows * owners
    modes = KW // owners
    count, edge = w_first.shape[1:3]
    groups = 2
    direct = 2 * modes % 16 == 0
    lead = owners if direct else 1

    order = mixed_order(owners)

    def send_out(blocks):
        if direct:
            taken = {0: blocks[0]}
            for offset in order:
                taken[offset] = swap_with(blocks[offset], "space", offset)
            return [taken[offset] for offset in range(owners)]
        spectrum = blocks[0].reshape(samples, rows, owners, 2 * modes, channels)
        spectrum = jnp.transpose(spectrum, (2, 0, 1, 3, 4))
        arrived = lax.all_to_all(spectrum, "space", split_axis=0, concat_axis=0, tiled=True)
        return [jnp.transpose(arrived, (1, 0, 2, 3, 4)).reshape(-1, channels)]

    def send_back(blocks):
        bands = blocks[0].reshape(samples, owners, rows, 2 * modes, channels)
        bands = jnp.transpose(bands, (1, 0, 2, 3, 4))
        arrived = lax.all_to_all(bands, "space", split_axis=0, concat_axis=0, tiled=True)
        return [jnp.transpose(arrived, (1, 2, 0, 3, 4)).reshape(-1, channels)]

    me = lax.axis_index("space") if direct else 0
    me = jnp.full((1,), me, jnp.int32)
    plain, scaled = lon_tables(KW, width, owners)
    lat = lat_spread(lat_total, modes)

    spectrum = to_modes(me, plain, fields, lead)
    spectrum, cotangent, w_first, w_second = lax.optimization_barrier(
        (spectrum, cotangent, w_first, w_second)
    )
    gathered = send_out(spectrum)
    cot_spec = to_modes(me, scaled, cotangent, lead)
    w1, w2 = spread_weights(groups, w_first, w_second)
    b1, b2 = block_bias(b_first, groups), block_bias(b_second, groups)

    image, state = forward_mid(me, lat, lat.T, gathered, w1, b1, w2, b2)
    if direct:
        late = tuple(cot_spec[offset] for offset in order[FIRST:])
        late, image = lax.optimization_barrier((late, image))
        cot_spec = list(cot_spec)
        for offset, block in zip(order[FIRST:], late):
            cot_spec[offset] = block
    cot_gathered = send_out(cot_spec)
    image_band = send_out(image) if direct else send_back(image)
    share = 4 * (edge + 16) // owners if direct else 0
    grad_image, rest = backward_mid(
        me, lat, lat.T, cot_gathered, w1, b1, w2, b2, state, count, share
    )
    positions = samples * lax.axis_size("dp") * lat_total * KW
    factor = 1.0 / math.sqrt(positions)
    if direct:
        early = tuple(image_band[offset] for offset in order[:HELD])
        grad_image, _ = lax.optimization_barrier((grad_image, early))
        grad_band = send_out(grad_image)
    else:
        grad_band = send_back(grad_image)
    output = to_cells(me, scaled.T, image_band, fields)
    grad_fields = to_cells(me, plain.T, grad_band, cotangent)

    if direct:
        total = sum(band[-share:].astype(jnp.float32) for band in grad_band)
        total = (total + swap_with(total, "dp", 1)).astype(jnp.bfloat16)
        grads = finish_sums(me, send_out([total] * owners), factor, w_first.shape, b_first.shape)
        return (output, grad_fields) + tuple(grads)
    sums = lax.psum(rest[0], ("space", "dp")) * factor
    grads = []
    for which in range(2):
        blocks = sums[which, :, :edge].reshape(2, edge, count, edge)
        grads.append(jnp.transpose(blocks, (0, 2, 1, 3)))
        grads.append(sums[which, :, edge].reshape(b_first.shape))
    return (output, grad_fields) + tuple(grads)


def solution(mesh):
    split = P(("parts", "dp"), "space", None, None)
    in_specs = (split, split, P(), P(), P(), P())
    out_specs = (
        split,
        split,
        P("parts", None, None, None),
        P("parts", None, None),
        P("parts", None, None, None),
        P("parts", None, None),
    )
    return jax.shard_map(body, mesh=mesh, in_specs=in_specs, out_specs=out_specs, check_vma=False)
```

```python
import functools
import math

import jax
import jax.numpy as jnp
from jax import lax
from jax.experimental import pallas as pl
from jax.experimental.pallas import tpu as pltpu
from jax.sharding import PartitionSpec as P
import ml_dtypes
import numpy as np

KW = 64
shrink_level = 0.05
HELD = 5
FIRST = 4
MIB = 1024 * 1024


def product_of(former, latter):
    return jnp.dot(former, latter, preferred_element_type=jnp.float32)


def lon_tables(mode_count, cell_count, owners):
    wavenums = np.arange(mode_count, dtype=np.int32)
    columns = np.arange(cell_count, dtype=np.int32)
    phase_index = (wavenums[:, None] * columns[None, :] % cell_count).astype(np.float32)
    phases = phase_index * np.float32(2.0 * math.pi / cell_count)
    factor = np.float32(1.0 / math.sqrt(cell_count))
    forward = np.stack([np.cos(phases) * factor, -np.sin(phases) * factor])
    scaled = forward * np.where(wavenums == 0, 1.0, 2.0).astype(np.float32)[:, None]

    def ordered(table):
        split = table.reshape(2, owners, -1, cell_count).transpose(1, 0, 2, 3)
        return split.reshape(-1, cell_count).astype(ml_dtypes.bfloat16)

    return ordered(forward), ordered(scaled)


def lat_spread(row_count, modes):
    indices = np.arange(row_count, dtype=np.int32)
    phase_index = (indices[:, None] * indices[None, :] % row_count).astype(np.float32)
    phases = phase_index * np.float32(2.0 * math.pi / row_count)
    factor = np.float32(1.0 / math.sqrt(row_count))
    cosine = np.cos(phases) * factor
    sine_part = np.sin(phases) * factor
    table = np.stack([np.stack([cosine, sine_part], -1), np.stack([-sine_part, cosine], -1)])
    same = np.eye(modes, dtype=np.float32)
    spread = table[:, :, None, :, :, None] * same[None, None, :, None, None, :]
    size = 2 * row_count * modes
    return spread.reshape(size, size).astype(ml_dtypes.bfloat16)


def block_bias(bias, groups):
    return jnp.transpose(bias.reshape(2, groups, 1, -1), (1, 2, 0, 3)).reshape(groups, 1, -1)


def spread_kernel(*refs):
    half_way = len(refs) // 2
    for blocks_ref, joined_ref in zip(refs[:half_way], refs[half_way:]):
        _, per, size, _ = blocks_ref.shape
        width = per * size
        row = lax.broadcasted_iota(jnp.int32, (size, width), 0)
        lane = lax.broadcasted_iota(jnp.int32, (size, width), 1)
        for block in range(per):
            place = (row + block * size == lane).astype(jnp.bfloat16)
            real = product_of(blocks_ref[0, block], place).astype(jnp.bfloat16)
            imag = product_of(blocks_ref[1, block], place)
            upper = pl.ds(block * size, size)
            lower = pl.ds(width + block * size, size)
            joined_ref[0, upper, 0:width] = real
            joined_ref[0, upper, width : 2 * width] = imag.astype(jnp.bfloat16)
            joined_ref[0, lower, 0:width] = (-imag).astype(jnp.bfloat16)
            joined_ref[0, lower, width : 2 * width] = real


def spread_weights(groups, *weights):
    _, count, size, _ = weights[0].shape
    per = count // groups
    lanes = 2 * per * size
    shape = in_hbm((groups, lanes, lanes), jnp.bfloat16)
    return pl.pallas_call(
        spread_kernel,
        grid=(groups,),
        out_shape=(shape,) * len(weights),
        in_specs=[pl.BlockSpec((2, per, size, size), lambda g: (0, g, 0, 0))] * len(weights),
        out_specs=(group_spec(lanes, lanes),) * len(weights),
        compiler_params=params(12),
        cost_estimate=pl.CostEstimate(
            flops=len(weights) * 2 * count * size * size * lanes,
            bytes_accessed=len(weights) * 2 * groups * lanes * lanes,
            transcendentals=0,
        ),
        name="spread_weights",
    )(*weights)


def params(mebibytes):
    return pltpu.CompilerParams(
        vmem_limit_bytes=mebibytes * MIB, dimension_semantics=("arbitrary",)
    )


def place_of(me_ref, offset, rows):
    return pl.ds(pl.multiple_of((me_ref[0] ^ offset) * rows, rows), rows)


def in_hbm(shape, dtype):
    return pltpu.HBM(shape, dtype)


def hbm(*arrays):
    return [pltpu.with_memory_space_constraint(array, pltpu.HBM) for array in arrays]


def to_modes_kernel(me_ref, table_ref, cells_ref, *refs):
    modes_refs, held_ref = refs[:-1], refs[-1]
    rows = cells_ref.shape[1]
    share = modes_refs[0].shape[0] // rows
    for row in range(rows):
        spectrum = product_of(table_ref[...], cells_ref[0, row])
        held_ref[row] = spectrum.astype(jnp.bfloat16)
        for offset, modes_ref in enumerate(modes_refs):
            modes_ref[pl.ds(row * share, share)] = held_ref[row, place_of(me_ref, offset, share)]


def to_modes(me, table, cells, owners):
    samples, rows, width, channels = cells.shape
    size = table.shape[0]
    part = rows * size // owners
    return pl.pallas_call(
        to_modes_kernel,
        grid_spec=pltpu.PrefetchScalarGridSpec(
            num_scalar_prefetch=1,
            grid=(samples,),
            in_specs=[
                pl.BlockSpec((size, width), lambda b, _: (0, 0)),
                pl.BlockSpec((1, rows, width, channels), lambda b, _: (b, 0, 0, 0)),
            ],
            out_specs=(pl.BlockSpec((part, channels), lambda b, _: (b, 0)),) * owners,
            scratch_shapes=[pltpu.VMEM((rows, size, channels), jnp.bfloat16)],
        ),
        out_shape=(in_hbm((samples * part, channels), jnp.bfloat16),) * owners,
        compiler_params=params(12),
        cost_estimate=pl.CostEstimate(
            flops=2 * samples * rows * size * width * channels,
            bytes_accessed=2 * samples * rows * channels * (width + size),
            transcendentals=0,
        ),
        name="to_modes",
    )(me, table, cells)


def to_cells_kernel(me_ref, table_ref, base_ref, *refs):
    modes_refs, out_ref, held_ref = refs[:-2], refs[-2], refs[-1]
    rows = base_ref.shape[1]
    share = modes_refs[0].shape[-2] // rows
    for row in range(rows):
        run = pl.ds(row * share, share)
        if len(modes_refs) == 1:
            spectrum = modes_refs[0][:, run].reshape(held_ref.shape[1:])
        else:
            for offset, modes_ref in enumerate(modes_refs):
                held_ref[row, place_of(me_ref, offset, share)] = modes_ref[run]
            spectrum = held_ref[row]
        image = product_of(table_ref[...], spectrum)
        out_ref[0, row] = (base_ref[0, row].astype(jnp.float32) + image).astype(jnp.bfloat16)


def to_cells(me, table, modes, base):
    samples, rows, width, channels = base.shape
    size = table.shape[1]
    block = pl.BlockSpec((1, rows, width, channels), lambda b, _: (b, 0, 0, 0))
    if len(modes) == 1:
        lead = modes[0].shape[0]
        part = rows * size // lead
        specs = [pl.BlockSpec((lead, part, channels), lambda b, _: (0, b, 0))]
    else:
        part = rows * size // len(modes)
        specs = [pl.BlockSpec((part, channels), lambda b, _: (b, 0))] * len(modes)
    return pl.pallas_call(
        to_cells_kernel,
        grid_spec=pltpu.PrefetchScalarGridSpec(
            num_scalar_prefetch=1,
            grid=(samples,),
            in_specs=[pl.BlockSpec((width, size), lambda b, _: (0, 0)), block] + specs,
            out_specs=block,
            scratch_shapes=[pltpu.VMEM((rows, size, channels), jnp.bfloat16)],
        ),
        out_shape=jax.ShapeDtypeStruct(base.shape, jnp.bfloat16),
        compiler_params=params(12),
        cost_estimate=pl.CostEstimate(
            flops=2 * samples * rows * size * width * channels,
            bytes_accessed=2 * samples * rows * channels * (2 * width + size),
            transcendentals=0,
        ),
        name="to_cells",
    )(me, table, base, *hbm(*modes))


def sigmoid_of(values):
    return 0.5 + 0.5 * jnp.tanh(0.5 * values)


def mix_lat(me_ref, table_ref, bands_refs, band_ref, mixed_ref):
    samples, size, width = band_ref.shape
    part, half = size // len(bands_refs), size // 2
    for sample in range(samples):
        for offset, bands_ref in enumerate(bands_refs):
            place = place_of(me_ref, offset, part)
            band_ref[sample, place] = bands_ref[pl.ds(sample * part, part)]
        mixed = product_of(table_ref[...], band_ref[sample]).astype(jnp.bfloat16)
        spot = pl.ds(sample * half, half)
        mixed_ref[spot, 0:width] = mixed[:half]
        mixed_ref[spot, width : 2 * width] = mixed[half:]


def unmix_lat(me_ref, table_ref, mixed_ref, band_ref, bands_refs):
    samples, size, width = band_ref.shape
    part, half = size // len(bands_refs), size // 2
    for sample in range(samples):
        spot = pl.ds(sample * half, half)
        joined = jnp.concatenate(
            [mixed_ref[spot, 0:width], mixed_ref[spot, width : 2 * width]], axis=0
        )
        bands = product_of(table_ref[...], joined).astype(jnp.bfloat16)
        if len(bands_refs) == 1:
            lead = bands_refs[0].shape[0]
            run = pl.ds(sample * size // lead, size // lead)
            bands_refs[0][:, run] = bands.reshape(lead, size // lead, width)
        else:
            band_ref[sample] = bands
            for offset, bands_ref in enumerate(bands_refs):
                place = place_of(me_ref, offset, part)
                bands_ref[pl.ds(sample * part, part)] = band_ref[sample, place]


def activate(mixed_ref, w1_ref, b1_ref):
    pre = product_of(mixed_ref[0], w1_ref[0]) + b1_ref[0]
    logistic = sigmoid_of(pre)
    return logistic, pre * logistic


def bend(act_ref, w2_ref, b2_ref):
    out = product_of(act_ref[...], w2_ref[0]) + b2_ref[0]
    return out, jnp.tanh(out * (1.0 / shrink_level))


def forward_kernel(blocks, me_ref, lat_ref, unlat_ref, w1_ref, b1_ref, w2_ref, b2_ref, *refs):
    bands_refs, image_refs = refs[:blocks], refs[blocks : 2 * blocks]
    mixed_ref, act_ref, band_ref = refs[2 * blocks :]
    mix_lat(me_ref, lat_ref, bands_refs, band_ref, mixed_ref.at[0])
    act_ref[...] = activate(mixed_ref, w1_ref, b1_ref)[1].astype(jnp.bfloat16)
    out, bent = bend(act_ref, w2_ref, b2_ref)
    act_ref[...] = (out - shrink_level * bent).astype(jnp.bfloat16)
    unmix_lat(me_ref, unlat_ref, act_ref, band_ref, image_refs)


def backward_kernel(
    block_size, blocks, me_ref, lat_ref, unlat_ref, w1_ref, b1_ref, w2_ref, b2_ref, mixed_ref, *refs
):
    bands_refs, image_ref = refs[:blocks], refs[blocks]
    sums_ref, act_ref, gate_ref, cot_ref, kept_ref, band_ref = refs[blocks + 1 :]
    transposed = (((1,), (1,)), ((), ()))
    summed = (((0,), (0,)), ((), ()))

    def times(former, latter, dims):
        return lax.dot_general(former, latter, dims, preferred_element_type=jnp.float32)

    def weight_sums(acts, grads, slot):
        width = acts.shape[1] // 2
        full = times(acts, grads, summed)
        real = full[:width, :width] + full[width:, width:]
        imag = full[:width, width:] - full[width:, :width]
        bias = jnp.sum(grads.astype(jnp.float32), axis=0, keepdims=True)
        size = block_size
        owner = lax.broadcasted_iota(jnp.int32, (size, width), 1) // size
        extra = sums_ref.shape[2] - size
        first = lax.broadcasted_iota(jnp.int32, (extra, width), 0) == 0
        for part, values in enumerate((real, imag)):
            joined = values[:size]
            for block in range(1, width // size):
                joined = jnp.where(owner == block, values[block * size : (block + 1) * size], joined)
            sums_ref[slot, part, 0:size] = joined.astype(sums_ref.dtype)
            row = bias[:, part * width : (part + 1) * width]
            sums_ref[slot, part, size:] = jnp.where(first, row, 0.0).astype(sums_ref.dtype)

    logistic, act = activate(mixed_ref, w1_ref, b1_ref)
    act_ref[...] = act.astype(jnp.bfloat16)
    gate_ref[...] = logistic + act * (1.0 - logistic)
    mix_lat(me_ref, lat_ref, bands_refs, band_ref, cot_ref)
    _, bent = bend(act_ref, w2_ref, b2_ref)
    kept_ref[...] = (cot_ref[...].astype(jnp.float32) * (bent * bent)).astype(jnp.bfloat16)
    back = times(kept_ref[...], w2_ref[0], transposed)
    cot_ref[...] = (back * gate_ref[...]).astype(jnp.bfloat16)
    weight_sums(act_ref[...], kept_ref[...], 1)
    kept_ref[...] = times(cot_ref[...], w1_ref[0], transposed).astype(jnp.bfloat16)
    weight_sums(mixed_ref[0], cot_ref[...], 0)
    unmix_lat(me_ref, unlat_ref, kept_ref, band_ref, [image_ref])


def group_spec(*shape):
    return pl.BlockSpec((1,) + shape, lambda g, *_: (g,) + (0,) * len(shape))


def bands_specs(rows, bands, groups):
    block = (rows, bands[0].shape[1] // groups)
    return (pl.BlockSpec(block, lambda g, *_: (0, g)),) * len(bands)


def stacked(lead, rows, groups, width):
    shape = in_hbm((lead, rows // lead, groups * width), jnp.bfloat16)
    return (shape,), (pl.BlockSpec((lead, rows // lead, width), lambda g, *_: (0, 0, g)),)


def forward_mid(me, lat, unlat, bands, w1, b1, w2, b2):
    groups, lanes, _ = w1.shape
    size = lat.shape[0]
    samples = bands[0].shape[0] * len(bands) // size
    positions = samples * size // 2
    table = pl.BlockSpec((size, size), lambda g, _: (0, 0))
    state = (groups, positions, lanes)
    specs = bands_specs(bands[0].shape[0], bands, groups)
    if len(bands) == 1:
        images, image_specs = stacked(1, samples * size, groups, lanes // 2)
    else:
        images = tuple(in_hbm(band.shape, band.dtype) for band in bands)
        image_specs = specs
    results = pl.pallas_call(
        functools.partial(forward_kernel, len(bands)),
        grid_spec=pltpu.PrefetchScalarGridSpec(
            num_scalar_prefetch=1,
            grid=(groups,),
            in_specs=[
                table, table,
                group_spec(lanes, lanes), group_spec(1, lanes),
                group_spec(lanes, lanes), group_spec(1, lanes),
                *specs,
            ],
            out_specs=image_specs + (group_spec(positions, lanes),),
            scratch_shapes=[
                pltpu.VMEM((positions, lanes), jnp.bfloat16),
                pltpu.VMEM((samples, size, lanes // 2), jnp.bfloat16),
            ],
        ),
        out_shape=images + (in_hbm(state, jnp.bfloat16),),
        compiler_params=params(28),
        cost_estimate=pl.CostEstimate(
            flops=4 * groups * positions * lanes * lanes,
            bytes_accessed=16 * groups * positions * lanes + 4 * groups * lanes * lanes,
            transcendentals=2 * groups * positions * lanes,
        ),
        name="mix_forward",
    )(me, lat, unlat, *hbm(w1), b1, *hbm(w2), b2, *hbm(*bands))
    return results[: len(bands)], results[len(bands)]


def backward_mid(me, lat, unlat, bands, w1, b1, w2, b2, state, count):
    groups, lanes, _ = w1.shape
    size = lat.shape[0]
    samples = bands[0].shape[0] * len(bands) // size
    positions = samples * size // 2
    table = pl.BlockSpec((size, size), lambda g, _: (0, 0))
    size_of_block = lanes // 2 // (count // groups)
    sums = (2, 2, size_of_block + 32, lanes // 2)
    image, image_specs = stacked(len(bands), samples * size, groups, lanes // 2)
    return pl.pallas_call(
        functools.partial(backward_kernel, size_of_block, len(bands)),
        grid_spec=pltpu.PrefetchScalarGridSpec(
            num_scalar_prefetch=1,
            grid=(groups,),
            in_specs=[
                table, table,
                group_spec(lanes, lanes), group_spec(1, lanes),
                group_spec(lanes, lanes), group_spec(1, lanes),
                group_spec(positions, lanes),
                *bands_specs(bands[0].shape[0], bands, groups),
            ],
            out_specs=image_specs + (pl.BlockSpec(sums, lambda g, _: (0, 0, 0, g)),),
            scratch_shapes=[
                pltpu.VMEM((positions, lanes), jnp.bfloat16),
                pltpu.VMEM((positions, lanes), jnp.float32),
                pltpu.VMEM((positions, lanes), jnp.bfloat16),
                pltpu.VMEM((positions, lanes), jnp.bfloat16),
                pltpu.VMEM((samples, size, lanes // 2), jnp.bfloat16),
            ],
        ),
        out_shape=image + (in_hbm(sums[:3] + (groups * sums[3],), jnp.float32),),
        compiler_params=params(32),
        cost_estimate=pl.CostEstimate(
            flops=8 * groups * positions * lanes * lanes,
            bytes_accessed=16 * groups * positions * lanes + 4 * groups * lanes * lanes,
            transcendentals=0,
        ),
        name="mix_backward",
    )(me, lat, unlat, *hbm(w1), b1, *hbm(w2), b2, *hbm(state, *bands))


def swap_with(values, axis, distance):
    pairs = [(i, i ^ distance) for i in range(lax.axis_size(axis))]
    return lax.ppermute(values, axis, pairs)


def mixed_order(size):
    far = list(range(size // 2, size))
    near = [offset for offset in (2, 3, 1) if offset < size // 2]
    near += list(range(4, size // 2))
    order = []
    while far or near:
        order += far[:1] + near[:1]
        far, near = far[1:], near[1:]
    return order


def pick(pair, side):
    return lax.dynamic_index_in_dim(pair, side, 0, keepdims=False)


class GroupSum:
    def __init__(self, sums):
        self.lanes = sums.shape[-1]
        self.side = lax.axis_index("dp")
        self.me = lax.axis_index("space")
        self.count = lax.axis_size("space") // 2
        self.held = sums.reshape(-1, self.lanes)

    def halve(self, axis, distance, bit):
        pair = self.held.reshape(2, -1, self.lanes)
        given = pick(pair, 1 - bit)
        self.held = pick(pair, bit) + swap_with(given, axis, distance)

    def scatter(self, arrived):
        self.halve("dp", 1, self.side)
        if len(arrived) > 0:
            self.held, _ = lax.optimization_barrier((self.held, tuple(arrived)))
        self.halve("space", 1, self.me % 2)
        shares = self.held.reshape(self.count, -1, self.lanes)
        place = self.me // 2
        total = pick(shares, place)
        for offset in range(1, self.count):
            given = pick(shares, place ^ offset).astype(jnp.bfloat16)
            total += swap_with(given, "space", 2 * offset).astype(jnp.float32)
        self.total = total.astype(jnp.bfloat16)

    def gather(self):
        taken = [self.total]
        for offset in range(1, self.count):
            taken.append(swap_with(self.total, "space", 2 * offset))
        quarter = jnp.stack(taken)
        half = jnp.stack([quarter, swap_with(quarter, "space", 1)])
        return half, swap_with(half, "dp", 1)


def finish_kernel(factor, me_ref, half_ref, other_ref, *out_refs):
    side, near, place = me_ref[0], me_ref[1], me_ref[2]
    run = half_ref.shape[2]
    for which in range(2):
        blocks_ref, bias_ref = out_refs[2 * which : 2 * which + 2]
        edge = blocks_ref.shape[-1]
        for part in range(2):
            for piece in range(half_ref.shape[1]):
                spot = (part ^ near, piece ^ place)
                own = half_ref[spot].astype(jnp.float32)
                value = jnp.where(side == which, own, other_ref[spot].astype(jnp.float32)) * factor
                first = piece * run
                count = max(0, min(edge - first, run))
                for block in range(blocks_ref.shape[1]):
                    lanes = slice(block * edge, (block + 1) * edge)
                    if count > 0:
                        blocks_ref[part, block, pl.ds(first, count)] = value[:count, lanes]
                    if first <= edge < first + run:
                        row = edge - first
                        bias_ref[part, pl.ds(block, 1)] = value[row : row + 1, lanes]


def finish_sums(here, half, other, factor, weight_shape, bias_shape):
    outs = [weight_shape, bias_shape] * 2
    return pl.pallas_call(
        functools.partial(finish_kernel, factor),
        out_shape=[jax.ShapeDtypeStruct(shape, jnp.float32) for shape in outs],
        in_specs=[pl.BlockSpec(memory_space=pltpu.SMEM)]
        + [pl.BlockSpec(memory_space=pltpu.VMEM)] * 2,
        out_specs=[pl.BlockSpec(memory_space=pltpu.VMEM)] * 4,
        compiler_params=pltpu.CompilerParams(vmem_limit_bytes=16 * MIB),
        cost_estimate=pl.CostEstimate(flops=0, bytes_accessed=4 * MIB, transcendentals=0),
        name="finish_sums",
    )(here, half, other)


def body(fields, cotangent, w_first, b_first, w_second, b_second):
    samples, rows, width, channels = fields.shape
    owners = lax.axis_size("space")
    lat_total = rows * owners
    modes = KW // owners
    count, edge = w_first.shape[1:3]
    groups = 2
    direct = 2 * modes % 16 == 0
    lead = owners if direct else 1

    order = mixed_order(owners)

    def send_out(blocks):
        if direct:
            taken = {0: blocks[0]}
            for offset in order:
                taken[offset] = swap_with(blocks[offset], "space", offset)
            return [taken[offset] for offset in range(owners)]
        spectrum = blocks[0].reshape(samples, rows, owners, 2 * modes, channels)
        spectrum = jnp.transpose(spectrum, (2, 0, 1, 3, 4))
        arrived = lax.all_to_all(spectrum, "space", split_axis=0, concat_axis=0, tiled=True)
        return [jnp.transpose(arrived, (1, 0, 2, 3, 4)).reshape(-1, channels)]

    def send_back(bands):
        if direct:
            return [lax.all_to_all(bands, "space", split_axis=0, concat_axis=0, tiled=True)]
        bands = bands.reshape(samples, owners, rows, 2 * modes, channels)
        bands = jnp.transpose(bands, (1, 0, 2, 3, 4))
        arrived = lax.all_to_all(bands, "space", split_axis=0, concat_axis=0, tiled=True)
        return [jnp.transpose(arrived, (1, 2, 0, 3, 4)).reshape(1, -1, channels)]

    me = lax.axis_index("space") if direct else 0
    me = jnp.full((1,), me, jnp.int32)
    plain, scaled = lon_tables(KW, width, owners)
    lat = lat_spread(lat_total, modes)

    spectrum = to_modes(me, plain, fields, lead)
    spectrum, cotangent, w_first, w_second = lax.optimization_barrier(
        (spectrum, cotangent, w_first, w_second)
    )
    gathered = send_out(spectrum)
    cot_spec = to_modes(me, scaled, cotangent, lead)
    w1, w2 = spread_weights(groups, w_first, w_second)
    b1, b2 = block_bias(b_first, groups), block_bias(b_second, groups)

    image, state = forward_mid(me, lat, lat.T, gathered, w1, b1, w2, b2)
    if direct:
        late = tuple(cot_spec[offset] for offset in order[FIRST:])
        late, image = lax.optimization_barrier((late, image))
        cot_spec = list(cot_spec)
        for offset, block in zip(order[FIRST:], late):
            cot_spec[offset] = block
    cot_gathered = send_out(cot_spec)
    image_band = send_out(image) if direct else send_back(image[0])
    grad_image, sums = backward_mid(
        me, lat, lat.T, cot_gathered, w1, b1, w2, b2, state, count
    )
    late = []
    if direct:
        early = tuple(image_band[offset] for offset in order[:HELD])
        late = [image_band[offset] for offset in order[HELD:]]
        grad_image, sums, _ = lax.optimization_barrier((grad_image, sums, early))
    grad_band = send_back(grad_image)
    output = to_cells(me, scaled.T, image_band, fields)
    grad_fields = to_cells(me, plain.T, grad_band, cotangent)

    positions = samples * lax.axis_size("dp") * lat_total * KW
    factor = 1.0 / math.sqrt(positions)
    if direct:
        group_sum = GroupSum(sums)
        group_sum.scatter(late)
        half, other = group_sum.gather()
        place = lax.axis_index("space")
        here = jnp.stack([lax.axis_index("dp"), place % 2, place // 2]).astype(jnp.int32)
        grads = finish_sums(here, half, other, factor, w_first.shape, b_first.shape)
        return (output, grad_fields) + tuple(grads)
    sums = lax.psum(sums, ("space", "dp")) * factor
    grads = []
    for which in range(2):
        blocks = sums[which, :, :edge].reshape(2, edge, count, edge)
        grads.append(jnp.transpose(blocks, (0, 2, 1, 3)))
        grads.append(sums[which, :, edge].reshape(b_first.shape))
    return (output, grad_fields) + tuple(grads)


def solution(mesh):
    split = P(("parts", "dp"), "space", None, None)
    in_specs = (split, split, P(), P(), P(), P())
    out_specs = (
        split,
        split,
        P("parts", None, None, None),
        P("parts", None, None),
        P("parts", None, None, None),
        P("parts", None, None),
    )
    return jax.shard_map(body, mesh=mesh, in_specs=in_specs, out_specs=out_specs, check_vma=False)
```

```python
import functools
import math

import jax
import jax.numpy as jnp
from jax import lax
from jax.experimental import pallas as pl
from jax.experimental.pallas import tpu as pltpu
from jax.sharding import PartitionSpec as P
import ml_dtypes
import numpy as np

KW = 64
shrink_level = 0.05
DEPTH = 3
DEPTH_LATE = 4
BESIDE = (3, 3)
STEPS_AHEAD = (0, 0, 1, 3, 5, 6)
MIB = 1024 * 1024


def product_of(former, latter):
    return jnp.dot(former, latter, preferred_element_type=jnp.float32)


def lon_tables(mode_count, cell_count, owners):
    wavenums = np.arange(mode_count, dtype=np.int32)
    columns = np.arange(cell_count, dtype=np.int32)
    phase_index = (wavenums[:, None] * columns[None, :] % cell_count).astype(np.float32)
    phases = phase_index * np.float32(2.0 * math.pi / cell_count)
    factor = np.float32(1.0 / math.sqrt(cell_count))
    forward = np.stack([np.cos(phases) * factor, -np.sin(phases) * factor])
    scaled = forward * np.where(wavenums == 0, 1.0, 2.0).astype(np.float32)[:, None]

    def ordered(table):
        split = table.reshape(2, owners, -1, cell_count).transpose(1, 0, 2, 3)
        return split.reshape(-1, cell_count).astype(ml_dtypes.bfloat16)

    return ordered(forward), ordered(scaled)


def lat_spread(row_count, modes):
    indices = np.arange(row_count, dtype=np.int32)
    phase_index = (indices[:, None] * indices[None, :] % row_count).astype(np.float32)
    phases = phase_index * np.float32(2.0 * math.pi / row_count)
    factor = np.float32(1.0 / math.sqrt(row_count))
    cosine = np.cos(phases) * factor
    sine_part = np.sin(phases) * factor
    table = np.stack([np.stack([cosine, sine_part], -1), np.stack([-sine_part, cosine], -1)])
    same = np.eye(modes, dtype=np.float32)
    spread = table[:, :, None, :, :, None] * same[None, None, :, None, None, :]
    size = 2 * row_count * modes
    return spread.reshape(size, size).astype(ml_dtypes.bfloat16)


def block_bias(bias, groups):
    return jnp.transpose(bias.reshape(2, groups, 1, -1), (1, 2, 0, 3)).reshape(groups, 1, -1)


def spread_kernel(*refs):
    half_way = len(refs) // 2
    for blocks_ref, joined_ref in zip(refs[:half_way], refs[half_way:]):
        _, per, size, _ = blocks_ref.shape
        width = per * size
        row = lax.broadcasted_iota(jnp.int32, (size, width), 0)
        lane = lax.broadcasted_iota(jnp.int32, (size, width), 1)
        for block in range(per):
            place = (row + block * size == lane).astype(jnp.bfloat16)
            real = product_of(blocks_ref[0, block], place).astype(jnp.bfloat16)
            imag = product_of(blocks_ref[1, block], place)
            upper = pl.ds(block * size, size)
            lower = pl.ds(width + block * size, size)
            joined_ref[0, upper, 0:width] = real
            joined_ref[0, upper, width : 2 * width] = imag.astype(jnp.bfloat16)
            joined_ref[0, lower, 0:width] = (-imag).astype(jnp.bfloat16)
            joined_ref[0, lower, width : 2 * width] = real


def spread_weights(groups, *weights):
    _, count, size, _ = weights[0].shape
    per = count // groups
    lanes = 2 * per * size
    shape = in_hbm((groups, lanes, lanes), jnp.bfloat16)
    return pl.pallas_call(
        spread_kernel,
        grid=(groups,),
        out_shape=(shape,) * len(weights),
        in_specs=[pl.BlockSpec((2, per, size, size), lambda g: (0, g, 0, 0))] * len(weights),
        out_specs=(group_spec(lanes, lanes),) * len(weights),
        compiler_params=params(12),
        cost_estimate=pl.CostEstimate(
            flops=len(weights) * 2 * count * size * size * lanes,
            bytes_accessed=len(weights) * 2 * groups * lanes * lanes,
            transcendentals=0,
        ),
        name="spread_weights",
    )(*weights)


def params(mebibytes):
    return pltpu.CompilerParams(
        vmem_limit_bytes=mebibytes * MIB, dimension_semantics=("arbitrary",)
    )


def place_of(me_ref, offset, rows):
    return pl.ds(pl.multiple_of((me_ref[0] ^ offset) * rows, rows), rows)


def in_hbm(shape, dtype):
    return pltpu.HBM(shape, dtype)


def hbm(*arrays):
    return [pltpu.with_memory_space_constraint(array, pltpu.HBM) for array in arrays]


def to_modes_kernel(me_ref, table_ref, cells_ref, *refs):
    modes_refs, held_ref = refs[:-1], refs[-1]
    rows = cells_ref.shape[1]
    share = modes_refs[0].shape[0] // rows
    for row in range(rows):
        spectrum = product_of(table_ref[...], cells_ref[0, row])
        held_ref[row] = spectrum.astype(jnp.bfloat16)
        for offset, modes_ref in enumerate(modes_refs):
            modes_ref[pl.ds(row * share, share)] = held_ref[row, place_of(me_ref, offset, share)]


def to_modes(me, table, cells, owners):
    samples, rows, width, channels = cells.shape
    size = table.shape[0]
    part = rows * size // owners
    return pl.pallas_call(
        to_modes_kernel,
        grid_spec=pltpu.PrefetchScalarGridSpec(
            num_scalar_prefetch=1,
            grid=(samples,),
            in_specs=[
                pl.BlockSpec((size, width), lambda b, _: (0, 0)),
                pl.BlockSpec((1, rows, width, channels), lambda b, _: (b, 0, 0, 0)),
            ],
            out_specs=(pl.BlockSpec((part, channels), lambda b, _: (b, 0)),) * owners,
            scratch_shapes=[pltpu.VMEM((rows, size, channels), jnp.bfloat16)],
        ),
        out_shape=(in_hbm((samples * part, channels), jnp.bfloat16),) * owners,
        compiler_params=params(12),
        cost_estimate=pl.CostEstimate(
            flops=2 * samples * rows * size * width * channels,
            bytes_accessed=2 * samples * rows * channels * (width + size),
            transcendentals=0,
        ),
        name="to_modes",
    )(me, table, cells)


def to_cells_kernel(me_ref, table_ref, base_ref, *refs):
    modes_refs, out_ref, held_ref = refs[:-2], refs[-2], refs[-1]
    rows = base_ref.shape[1]
    share = modes_refs[0].shape[-2] // rows
    for row in range(rows):
        run = pl.ds(row * share, share)
        if len(modes_refs) == 1:
            spectrum = modes_refs[0][:, run].reshape(held_ref.shape[1:])
        else:
            for offset, modes_ref in enumerate(modes_refs):
                held_ref[row, place_of(me_ref, offset, share)] = modes_ref[run]
            spectrum = held_ref[row]
        image = product_of(table_ref[...], spectrum)
        out_ref[0, row] = (base_ref[0, row].astype(jnp.float32) + image).astype(jnp.bfloat16)


def to_cells(me, table, modes, base):
    samples, rows, width, channels = base.shape
    size = table.shape[1]
    block = pl.BlockSpec((1, rows, width, channels), lambda b, _: (b, 0, 0, 0))
    if len(modes) == 1:
        lead = modes[0].shape[0]
        part = rows * size // lead
        specs = [pl.BlockSpec((lead, part, channels), lambda b, _: (0, b, 0))]
    else:
        part = rows * size // len(modes)
        specs = [pl.BlockSpec((part, channels), lambda b, _: (b, 0))] * len(modes)
    return pl.pallas_call(
        to_cells_kernel,
        grid_spec=pltpu.PrefetchScalarGridSpec(
            num_scalar_prefetch=1,
            grid=(samples,),
            in_specs=[pl.BlockSpec((width, size), lambda b, _: (0, 0)), block] + specs,
            out_specs=block,
            scratch_shapes=[pltpu.VMEM((rows, size, channels), jnp.bfloat16)],
        ),
        out_shape=jax.ShapeDtypeStruct(base.shape, jnp.bfloat16),
        compiler_params=params(12),
        cost_estimate=pl.CostEstimate(
            flops=2 * samples * rows * size * width * channels,
            bytes_accessed=2 * samples * rows * channels * (2 * width + size),
            transcendentals=0,
        ),
        name="to_cells",
    )(me, table, base, *hbm(*modes))


def sigmoid_of(values):
    return 0.5 + 0.5 * jnp.tanh(0.5 * values)


def mix_lat(me_ref, table_ref, bands_refs, band_ref, mixed_ref):
    samples, size, width = band_ref.shape
    part, half = size // len(bands_refs), size // 2
    for sample in range(samples):
        for offset, bands_ref in enumerate(bands_refs):
            place = place_of(me_ref, offset, part)
            band_ref[sample, place] = bands_ref[pl.ds(sample * part, part)]
        mixed = product_of(table_ref[...], band_ref[sample]).astype(jnp.bfloat16)
        spot = pl.ds(sample * half, half)
        mixed_ref[spot, 0:width] = mixed[:half]
        mixed_ref[spot, width : 2 * width] = mixed[half:]


def unmix_lat(me_ref, table_ref, mixed_ref, band_ref, bands_refs):
    samples, size, width = band_ref.shape
    part, half = size // len(bands_refs), size // 2
    for sample in range(samples):
        spot = pl.ds(sample * half, half)
        joined = jnp.concatenate(
            [mixed_ref[spot, 0:width], mixed_ref[spot, width : 2 * width]], axis=0
        )
        bands = product_of(table_ref[...], joined).astype(jnp.bfloat16)
        if len(bands_refs) == 1:
            lead = bands_refs[0].shape[0]
            run = pl.ds(sample * size // lead, size // lead)
            bands_refs[0][:, run] = bands.reshape(lead, size // lead, width)
        else:
            band_ref[sample] = bands
            for offset, bands_ref in enumerate(bands_refs):
                place = place_of(me_ref, offset, part)
                bands_ref[pl.ds(sample * part, part)] = band_ref[sample, place]


def activate(mixed_ref, w1_ref, b1_ref):
    pre = product_of(mixed_ref[0], w1_ref[0]) + b1_ref[0]
    logistic = sigmoid_of(pre)
    return logistic, pre * logistic


def bend(act_ref, w2_ref, b2_ref):
    out = product_of(act_ref[...], w2_ref[0]) + b2_ref[0]
    return out, jnp.tanh(out * (1.0 / shrink_level))


def forward_kernel(blocks, me_ref, lat_ref, unlat_ref, w1_ref, b1_ref, w2_ref, b2_ref, *refs):
    bands_refs, image_refs = refs[:blocks], refs[blocks : 2 * blocks]
    mixed_ref, act_ref, band_ref = refs[2 * blocks :]
    mix_lat(me_ref, lat_ref, bands_refs, band_ref, mixed_ref.at[0])
    act_ref[...] = activate(mixed_ref, w1_ref, b1_ref)[1].astype(jnp.bfloat16)
    out, bent = bend(act_ref, w2_ref, b2_ref)
    act_ref[...] = (out - shrink_level * bent).astype(jnp.bfloat16)
    unmix_lat(me_ref, unlat_ref, act_ref, band_ref, image_refs)


def backward_kernel(
    block_size, blocks, me_ref, lat_ref, unlat_ref, w1_ref, b1_ref, w2_ref, b2_ref, mixed_ref, *refs
):
    bands_refs, image_refs = refs[:blocks], refs[blocks : 2 * blocks]
    sums_ref, act_ref, gate_ref, cot_ref, kept_ref, band_ref = refs[2 * blocks :]
    transposed = (((1,), (1,)), ((), ()))
    summed = (((0,), (0,)), ((), ()))

    def times(former, latter, dims):
        return lax.dot_general(former, latter, dims, preferred_element_type=jnp.float32)

    def weight_sums(acts, grads, slot):
        width = acts.shape[1] // 2
        full = times(acts, grads, summed)
        real = full[:width, :width] + full[width:, width:]
        imag = full[:width, width:] - full[width:, :width]
        bias = jnp.sum(grads.astype(jnp.float32), axis=0, keepdims=True)
        size = block_size
        owner = lax.broadcasted_iota(jnp.int32, (size, width), 1) // size
        extra = sums_ref.shape[2] - size
        first = lax.broadcasted_iota(jnp.int32, (extra, width), 0) == 0
        for part, values in enumerate((real, imag)):
            joined = values[:size]
            for block in range(1, width // size):
                joined = jnp.where(owner == block, values[block * size : (block + 1) * size], joined)
            sums_ref[slot, part, 0:size] = joined.astype(sums_ref.dtype)
            row = bias[:, part * width : (part + 1) * width]
            sums_ref[slot, part, size:] = jnp.where(first, row, 0.0).astype(sums_ref.dtype)

    logistic, act = activate(mixed_ref, w1_ref, b1_ref)
    act_ref[...] = act.astype(jnp.bfloat16)
    gate_ref[...] = logistic + act * (1.0 - logistic)
    mix_lat(me_ref, lat_ref, bands_refs, band_ref, cot_ref)
    _, bent = bend(act_ref, w2_ref, b2_ref)
    kept_ref[...] = (cot_ref[...].astype(jnp.float32) * (bent * bent)).astype(jnp.bfloat16)
    back = times(kept_ref[...], w2_ref[0], transposed)
    cot_ref[...] = (back * gate_ref[...]).astype(jnp.bfloat16)
    weight_sums(act_ref[...], kept_ref[...], 1)
    kept_ref[...] = times(cot_ref[...], w1_ref[0], transposed).astype(jnp.bfloat16)
    weight_sums(mixed_ref[0], cot_ref[...], 0)
    unmix_lat(me_ref, unlat_ref, kept_ref, band_ref, image_refs)


def group_spec(*shape):
    return pl.BlockSpec((1,) + shape, lambda g, *_: (g,) + (0,) * len(shape))


def bands_specs(rows, bands, groups):
    block = (rows, bands[0].shape[1] // groups)
    return (pl.BlockSpec(block, lambda g, *_: (0, g)),) * len(bands)


def images_like(bands, samples, size, groups):
    if len(bands) > 1:
        shapes = tuple(in_hbm(band.shape, band.dtype) for band in bands)
        return shapes, bands_specs(bands[0].shape[0], bands, groups)
    channels = bands[0].shape[1]
    shape = (1, samples * size, channels)
    spec = pl.BlockSpec(shape[:2] + (channels // groups,), lambda g, *_: (0, 0, g))
    return (in_hbm(shape, jnp.bfloat16),), (spec,)


def forward_mid(me, lat, unlat, bands, w1, b1, w2, b2):
    groups, lanes, _ = w1.shape
    size = lat.shape[0]
    samples = bands[0].shape[0] * len(bands) // size
    positions = samples * size // 2
    table = pl.BlockSpec((size, size), lambda g, _: (0, 0))
    state = (groups, positions, lanes)
    specs = bands_specs(bands[0].shape[0], bands, groups)
    images, image_specs = images_like(bands, samples, size, groups)
    results = pl.pallas_call(
        functools.partial(forward_kernel, len(bands)),
        grid_spec=pltpu.PrefetchScalarGridSpec(
            num_scalar_prefetch=1,
            grid=(groups,),
            in_specs=[
                table, table,
                group_spec(lanes, lanes), group_spec(1, lanes),
                group_spec(lanes, lanes), group_spec(1, lanes),
                *specs,
            ],
            out_specs=image_specs + (group_spec(positions, lanes),),
            scratch_shapes=[
                pltpu.VMEM((positions, lanes), jnp.bfloat16),
                pltpu.VMEM((samples, size, lanes // 2), jnp.bfloat16),
            ],
        ),
        out_shape=images + (in_hbm(state, jnp.bfloat16),),
        compiler_params=params(28),
        cost_estimate=pl.CostEstimate(
            flops=4 * groups * positions * lanes * lanes,
            bytes_accessed=16 * groups * positions * lanes + 4 * groups * lanes * lanes,
            transcendentals=2 * groups * positions * lanes,
        ),
        name="mix_forward",
    )(me, lat, unlat, *hbm(w1), b1, *hbm(w2), b2, *hbm(*bands))
    return results[: len(bands)], results[len(bands)]


def backward_mid(me, lat, unlat, bands, w1, b1, w2, b2, state, count):
    groups, lanes, _ = w1.shape
    size = lat.shape[0]
    samples = bands[0].shape[0] * len(bands) // size
    positions = samples * size // 2
    table = pl.BlockSpec((size, size), lambda g, _: (0, 0))
    size_of_block = lanes // 2 // (count // groups)
    sums = (2, 2, size_of_block + 32, lanes // 2)
    images, image_specs = images_like(bands, samples, size, groups)
    results = pl.pallas_call(
        functools.partial(backward_kernel, size_of_block, len(bands)),
        grid_spec=pltpu.PrefetchScalarGridSpec(
            num_scalar_prefetch=1,
            grid=(groups,),
            in_specs=[
                table, table,
                group_spec(lanes, lanes), group_spec(1, lanes),
                group_spec(lanes, lanes), group_spec(1, lanes),
                group_spec(positions, lanes),
                *bands_specs(bands[0].shape[0], bands, groups),
            ],
            out_specs=image_specs + (pl.BlockSpec(sums, lambda g, _: (0, 0, 0, g)),),
            scratch_shapes=[
                pltpu.VMEM((positions, lanes), jnp.bfloat16),
                pltpu.VMEM((positions, lanes), jnp.float32),
                pltpu.VMEM((positions, lanes), jnp.bfloat16),
                pltpu.VMEM((positions, lanes), jnp.bfloat16),
                pltpu.VMEM((samples, size, lanes // 2), jnp.bfloat16),
            ],
        ),
        out_shape=images + (in_hbm(sums[:3] + (groups * sums[3],), jnp.float32),),
        compiler_params=params(32),
        cost_estimate=pl.CostEstimate(
            flops=8 * groups * positions * lanes * lanes,
            bytes_accessed=16 * groups * positions * lanes + 4 * groups * lanes * lanes,
            transcendentals=0,
        ),
        name="mix_backward",
    )(me, lat, unlat, *hbm(w1), b1, *hbm(w2), b2, *hbm(state, *bands))
    return results[: len(bands)], results[len(bands)]


def swap_with(values, axis, distance):
    pairs = [(i, i ^ distance) for i in range(lax.axis_size(axis))]
    return lax.ppermute(values, axis, pairs)


def waiting(values, arrived):
    return lax.optimization_barrier((values, tuple(arrived)))[0]


class Chain:
    def __init__(self):
        self.arrived = []

    def swap(self, values, axis, distance, depth):
        if len(self.arrived) >= depth:
            values = waiting(values, self.arrived[-depth:][:1])
        self.arrived.append(swap_with(values, axis, distance))
        return self.arrived[-1]


def mixed_order(size):
    far = list(range(size // 2, size))
    near = [offset for offset in (2, 3, 1) if offset < size // 2]
    near += list(range(4, size // 2))
    order = []
    while far or near:
        order += far[:1] + near[:1]
        far, near = far[1:], near[1:]
    return order


def pick(pair, side):
    return lax.dynamic_index_in_dim(pair, side, 0, keepdims=False)


class GroupSum:
    def __init__(self, chain, sums):
        self.chain = chain
        self.lanes = sums.shape[-1]
        self.side = lax.axis_index("dp")
        self.me = lax.axis_index("space")
        self.count = lax.axis_size("space") // 2
        self.held = sums.reshape(-1, self.lanes)

    def swap(self, values, axis, distance):
        return self.chain.swap(values, axis, distance, DEPTH_LATE)

    def halve(self, axis, distance, bit):
        pair = self.held.reshape(2, -1, self.lanes)
        given = pick(pair, 1 - bit)
        self.held = pick(pair, bit) + self.swap(given, axis, distance)

    def over_dp(self):
        self.halve("dp", 1, self.side)

    def over_next(self):
        self.halve("space", 1, self.me % 2)

    def scatter(self):
        shares = self.held.reshape(self.count, -1, self.lanes)
        place = self.me // 2
        total = pick(shares, place)
        for offset in range(1, self.count):
            given = pick(shares, place ^ offset).astype(jnp.bfloat16)
            total += self.swap(given, "space", 2 * offset).astype(jnp.float32)
        self.total = total.astype(jnp.bfloat16)

    def gather(self):
        taken = [self.total]
        for offset in range(1, self.count):
            taken.append(self.swap(self.total, "space", 2 * offset))
        self.quarter = jnp.stack(taken)

    def gather_next(self):
        self.half = jnp.stack([self.quarter, self.swap(self.quarter, "space", 1)])

    def gather_dp(self):
        self.other = self.swap(self.half, "dp", 1)


def finish_kernel(factor, me_ref, half_ref, other_ref, *out_refs):
    side, near, place = me_ref[0], me_ref[1], me_ref[2]
    run = half_ref.shape[2]
    for which in range(2):
        blocks_ref, bias_ref = out_refs[2 * which : 2 * which + 2]
        edge = blocks_ref.shape[-1]
        for part in range(2):
            for piece in range(half_ref.shape[1]):
                spot = (part ^ near, piece ^ place)
                own = half_ref[spot].astype(jnp.float32)
                value = jnp.where(side == which, own, other_ref[spot].astype(jnp.float32)) * factor
                first = piece * run
                count = max(0, min(edge - first, run))
                for block in range(blocks_ref.shape[1]):
                    lanes = slice(block * edge, (block + 1) * edge)
                    if count > 0:
                        blocks_ref[part, block, pl.ds(first, count)] = value[:count, lanes]
                    if first <= edge < first + run:
                        row = edge - first
                        bias_ref[part, pl.ds(block, 1)] = value[row : row + 1, lanes]


def finish_sums(here, half, other, factor, weight_shape, bias_shape):
    outs = [weight_shape, bias_shape] * 2
    return pl.pallas_call(
        functools.partial(finish_kernel, factor),
        out_shape=[jax.ShapeDtypeStruct(shape, jnp.float32) for shape in outs],
        in_specs=[pl.BlockSpec(memory_space=pltpu.SMEM)]
        + [pl.BlockSpec(memory_space=pltpu.VMEM)] * 2,
        out_specs=[pl.BlockSpec(memory_space=pltpu.VMEM)] * 4,
        compiler_params=pltpu.CompilerParams(vmem_limit_bytes=16 * MIB),
        cost_estimate=pl.CostEstimate(flops=0, bytes_accessed=4 * MIB, transcendentals=0),
        name="finish_sums",
    )(here, half, other)


def body(fields, cotangent, w_first, b_first, w_second, b_second):
    samples, rows, width, channels = fields.shape
    owners = lax.axis_size("space")
    lat_total = rows * owners
    modes = KW // owners
    count, edge = w_first.shape[1:3]
    groups = 2
    direct = 2 * modes % 16 == 0
    lead = owners if direct else 1

    order = mixed_order(owners)

    chain = Chain()

    def send(blocks, offsets, taken, depth):
        for offset in offsets:
            taken[offset] = chain.swap(blocks[offset], "space", offset, depth)

    def send_all(spectrum):
        spectrum = spectrum.reshape(samples, rows, owners, 2 * modes, channels)
        spectrum = jnp.transpose(spectrum, (2, 0, 1, 3, 4))
        arrived = lax.all_to_all(spectrum, "space", split_axis=0, concat_axis=0, tiled=True)
        return [jnp.transpose(arrived, (1, 0, 2, 3, 4)).reshape(-1, channels)]

    def send_all_back(bands):
        bands = bands.reshape(samples, owners, rows, 2 * modes, channels)
        bands = jnp.transpose(bands, (1, 0, 2, 3, 4))
        arrived = lax.all_to_all(bands, "space", split_axis=0, concat_axis=0, tiled=True)
        return [jnp.transpose(arrived, (1, 2, 0, 3, 4)).reshape(1, -1, channels)]

    me = lax.axis_index("space") if direct else 0
    me = jnp.full((1,), me, jnp.int32)
    plain, scaled = lon_tables(KW, width, owners)
    lat = lat_spread(lat_total, modes)

    spectrum = to_modes(me, plain, fields, lead)
    spectrum, cotangent, w_first, w_second = lax.optimization_barrier(
        (spectrum, cotangent, w_first, w_second)
    )
    cot_spec = to_modes(me, scaled, cotangent, lead)
    w1, w2 = spread_weights(groups, w_first, w_second)
    b1, b2 = block_bias(b_first, groups), block_bias(b_second, groups)
    positions = samples * lax.axis_size("dp") * lat_total * KW
    factor = 1.0 / math.sqrt(positions)

    if not direct:
        gathered = send_all(spectrum[0])
        image, state = forward_mid(me, lat, lat.T, gathered, w1, b1, w2, b2)
        image_band = send_all_back(image[0])
        gathered = send_all(cot_spec[0])
        grad_image, sums = backward_mid(me, lat, lat.T, gathered, w1, b1, w2, b2, state, count)
        grad_band = send_all_back(grad_image[0])
        output = to_cells(me, scaled.T, image_band, fields)
        grad_fields = to_cells(me, plain.T, grad_band, cotangent)
        sums = lax.psum(sums, ("space", "dp")) * factor
        grads = []
        for which in range(2):
            blocks = sums[which, :, :edge].reshape(2, edge, count, edge)
            grads.append(jnp.transpose(blocks, (0, 2, 1, 3)))
            grads.append(sums[which, :, edge].reshape(b_first.shape))
        return (output, grad_fields) + tuple(grads)

    gathered, cot_gathered = {0: spectrum[0]}, {0: cot_spec[0]}
    image_band, grad_band = {}, {}
    send(spectrum, order, gathered, DEPTH)
    send(cot_spec, order, cot_gathered, DEPTH)
    gathered = [gathered[offset] for offset in range(owners)]
    image, state = forward_mid(me, lat, lat.T, gathered, w1, b1, w2, b2)
    image, state = waiting((image, state), [cot_gathered[offset] for offset in order[:BESIDE[0]]])
    image_band[0] = image[0]
    send(image, order, image_band, DEPTH)
    cot_gathered = [cot_gathered[offset] for offset in range(owners)]
    grad_image, sums = backward_mid(
        me, lat, lat.T, cot_gathered, w1, b1, w2, b2, state, count
    )
    grad_image, sums = waiting(
        (grad_image, sums), [image_band[offset] for offset in order[:BESIDE[1]]]
    )
    grad_band[0] = grad_image[0]
    group_sum = GroupSum(chain, sums)
    steps = [
        group_sum.over_dp, group_sum.over_next, group_sum.scatter,
        group_sum.gather, group_sum.gather_next, group_sum.gather_dp,
    ]
    for place, offset in enumerate(order):
        for _ in range(STEPS_AHEAD.count(place)):
            steps.pop(0)()
        send(grad_image, [offset], grad_band, DEPTH_LATE)
    for step in steps:
        step()
    image_band = [image_band[offset] for offset in range(owners)]
    grad_band = [grad_band[offset] for offset in range(owners)]
    output = to_cells(me, scaled.T, image_band, fields)
    grad_fields = to_cells(me, plain.T, grad_band, cotangent)
    place = lax.axis_index("space")
    here = jnp.stack([lax.axis_index("dp"), place % 2, place // 2]).astype(jnp.int32)
    grads = finish_sums(
        here, group_sum.half, group_sum.other, factor, w_first.shape, b_first.shape
    )
    return (output, grad_fields) + tuple(grads)


def solution(mesh):
    split = P(("parts", "dp"), "space", None, None)
    in_specs = (split, split, P(), P(), P(), P())
    out_specs = (
        split,
        split,
        P("parts", None, None, None),
        P("parts", None, None),
        P("parts", None, None, None),
        P("parts", None, None),
    )
    return jax.shard_map(body, mesh=mesh, in_specs=in_specs, out_specs=out_specs, check_vma=False)
```

```python
import functools
import math

import jax
import jax.numpy as jnp
from jax import lax
from jax.experimental import pallas as pl
from jax.experimental.pallas import tpu as pltpu
from jax.sharding import PartitionSpec as P
import ml_dtypes
import numpy as np

KW = 64
shrink_level = 0.05
FIRST = 4
HELD = 5
MIB = 1024 * 1024


def product_of(former, latter):
    return jnp.dot(former, latter, preferred_element_type=jnp.float32)


def lon_tables(mode_count, cell_count, owners):
    wavenums = np.arange(mode_count, dtype=np.int32)
    columns = np.arange(cell_count, dtype=np.int32)
    phase_index = (wavenums[:, None] * columns[None, :] % cell_count).astype(np.float32)
    phases = phase_index * np.float32(2.0 * math.pi / cell_count)
    factor = np.float32(1.0 / math.sqrt(cell_count))
    forward = np.stack([np.cos(phases) * factor, -np.sin(phases) * factor])
    scaled = forward * np.where(wavenums == 0, 1.0, 2.0).astype(np.float32)[:, None]

    def ordered(table):
        split = table.reshape(2, owners, -1, cell_count).transpose(1, 0, 2, 3)
        return split.reshape(-1, cell_count).astype(ml_dtypes.bfloat16)

    return ordered(forward), ordered(scaled)


def lat_spread(row_count, modes):
    indices = np.arange(row_count, dtype=np.int32)
    phase_index = (indices[:, None] * indices[None, :] % row_count).astype(np.float32)
    phases = phase_index * np.float32(2.0 * math.pi / row_count)
    factor = np.float32(1.0 / math.sqrt(row_count))
    cosine = np.cos(phases) * factor
    sine_part = np.sin(phases) * factor
    table = np.stack([np.stack([cosine, sine_part], -1), np.stack([-sine_part, cosine], -1)])
    same = np.eye(modes, dtype=np.float32)
    spread = table[:, :, None, :, :, None] * same[None, None, :, None, None, :]
    size = 2 * row_count * modes
    return spread.reshape(size, size).astype(ml_dtypes.bfloat16)


def block_bias(bias, groups):
    return jnp.transpose(bias.reshape(2, groups, 1, -1), (1, 2, 0, 3)).reshape(groups, 1, -1)


def spread_kernel(*refs):
    half_way = len(refs) // 2
    for blocks_ref, joined_ref in zip(refs[:half_way], refs[half_way:]):
        _, per, size, _ = blocks_ref.shape
        width = per * size
        row = lax.broadcasted_iota(jnp.int32, (size, width), 0)
        lane = lax.broadcasted_iota(jnp.int32, (size, width), 1)
        for block in range(per):
            place = (row + block * size == lane).astype(jnp.bfloat16)
            real = product_of(blocks_ref[0, block], place).astype(jnp.bfloat16)
            imag = product_of(blocks_ref[1, block], place)
            upper = pl.ds(block * size, size)
            lower = pl.ds(width + block * size, size)
            joined_ref[0, upper, 0:width] = real
            joined_ref[0, upper, width : 2 * width] = imag.astype(jnp.bfloat16)
            joined_ref[0, lower, 0:width] = (-imag).astype(jnp.bfloat16)
            joined_ref[0, lower, width : 2 * width] = real


def spread_weights(groups, *weights):
    _, count, size, _ = weights[0].shape
    per = count // groups
    lanes = 2 * per * size
    shape = in_hbm((groups, lanes, lanes), jnp.bfloat16)
    return pl.pallas_call(
        spread_kernel,
        grid=(groups,),
        out_shape=(shape,) * len(weights),
        in_specs=[pl.BlockSpec((2, per, size, size), lambda g: (0, g, 0, 0))] * len(weights),
        out_specs=(group_spec(lanes, lanes),) * len(weights),
        compiler_params=params(12),
        cost_estimate=pl.CostEstimate(
            flops=len(weights) * 2 * count * size * size * lanes,
            bytes_accessed=len(weights) * 2 * groups * lanes * lanes,
            transcendentals=0,
        ),
        name="spread_weights",
    )(*weights)


def params(mebibytes):
    return pltpu.CompilerParams(
        vmem_limit_bytes=mebibytes * MIB, dimension_semantics=("arbitrary",)
    )


def place_of(me_ref, offset, rows):
    return pl.ds(pl.multiple_of((me_ref[0] ^ offset) * rows, rows), rows)


def in_hbm(shape, dtype):
    return pltpu.HBM(shape, dtype)


def hbm(*arrays):
    return [pltpu.with_memory_space_constraint(array, pltpu.HBM) for array in arrays]


def to_modes_kernel(me_ref, table_ref, cells_ref, *refs):
    modes_refs, held_ref = refs[:-1], refs[-1]
    rows = cells_ref.shape[1]
    share = modes_refs[0].shape[0] // rows
    for row in range(rows):
        spectrum = product_of(table_ref[...], cells_ref[0, row])
        held_ref[row] = spectrum.astype(jnp.bfloat16)
        for offset, modes_ref in enumerate(modes_refs):
            modes_ref[pl.ds(row * share, share)] = held_ref[row, place_of(me_ref, offset, share)]


def to_modes(me, table, cells, owners):
    samples, rows, width, channels = cells.shape
    size = table.shape[0]
    part = rows * size // owners
    return pl.pallas_call(
        to_modes_kernel,
        grid_spec=pltpu.PrefetchScalarGridSpec(
            num_scalar_prefetch=1,
            grid=(samples,),
            in_specs=[
                pl.BlockSpec((size, width), lambda b, _: (0, 0)),
                pl.BlockSpec((1, rows, width, channels), lambda b, _: (b, 0, 0, 0)),
            ],
            out_specs=(pl.BlockSpec((part, channels), lambda b, _: (b, 0)),) * owners,
            scratch_shapes=[pltpu.VMEM((rows, size, channels), jnp.bfloat16)],
        ),
        out_shape=(in_hbm((samples * part, channels), jnp.bfloat16),) * owners,
        compiler_params=params(12),
        cost_estimate=pl.CostEstimate(
            flops=2 * samples * rows * size * width * channels,
            bytes_accessed=2 * samples * rows * channels * (width + size),
            transcendentals=0,
        ),
        name="to_modes",
    )(me, table, cells)


def to_cells_kernel(me_ref, table_ref, base_ref, *refs):
    modes_refs, out_ref, held_ref = refs[:-2], refs[-2], refs[-1]
    rows = base_ref.shape[1]
    share = modes_refs[0].shape[-2] // rows
    for row in range(rows):
        run = pl.ds(row * share, share)
        if len(modes_refs) == 1:
            spectrum = modes_refs[0][:, run].reshape(held_ref.shape[1:])
        else:
            for offset, modes_ref in enumerate(modes_refs):
                held_ref[row, place_of(me_ref, offset, share)] = modes_ref[run]
            spectrum = held_ref[row]
        image = product_of(table_ref[...], spectrum)
        out_ref[0, row] = (base_ref[0, row].astype(jnp.float32) + image).astype(jnp.bfloat16)


def to_cells(me, table, modes, base):
    samples, rows, width, channels = base.shape
    size = table.shape[1]
    block = pl.BlockSpec((1, rows, width, channels), lambda b, _: (b, 0, 0, 0))
    if len(modes) == 1:
        lead = modes[0].shape[0]
        part = rows * size // lead
        specs = [pl.BlockSpec((lead, part, channels), lambda b, _: (0, b, 0))]
    else:
        part = rows * size // len(modes)
        specs = [pl.BlockSpec((part, channels), lambda b, _: (b, 0))] * len(modes)
    return pl.pallas_call(
        to_cells_kernel,
        grid_spec=pltpu.PrefetchScalarGridSpec(
            num_scalar_prefetch=1,
            grid=(samples,),
            in_specs=[pl.BlockSpec((width, size), lambda b, _: (0, 0)), block] + specs,
            out_specs=block,
            scratch_shapes=[pltpu.VMEM((rows, size, channels), jnp.bfloat16)],
        ),
        out_shape=jax.ShapeDtypeStruct(base.shape, jnp.bfloat16),
        compiler_params=params(12),
        cost_estimate=pl.CostEstimate(
            flops=2 * samples * rows * size * width * channels,
            bytes_accessed=2 * samples * rows * channels * (2 * width + size),
            transcendentals=0,
        ),
        name="to_cells",
    )(me, table, base, *hbm(*modes))


def sigmoid_of(values):
    return 0.5 + 0.5 * jnp.tanh(0.5 * values)


def mix_lat(me_ref, table_ref, bands_refs, band_ref, mixed_ref):
    samples, size, width = band_ref.shape
    part, half = size // len(bands_refs), size // 2
    for sample in range(samples):
        for offset, bands_ref in enumerate(bands_refs):
            place = place_of(me_ref, offset, part)
            band_ref[sample, place] = bands_ref[pl.ds(sample * part, part)]
        mixed = product_of(table_ref[...], band_ref[sample]).astype(jnp.bfloat16)
        spot = pl.ds(sample * half, half)
        mixed_ref[spot, 0:width] = mixed[:half]
        mixed_ref[spot, width : 2 * width] = mixed[half:]


def unmix_lat(me_ref, table_ref, mixed_ref, band_ref, bands_refs):
    samples, size, width = band_ref.shape
    part, half = size // len(bands_refs), size // 2
    for sample in range(samples):
        spot = pl.ds(sample * half, half)
        joined = jnp.concatenate(
            [mixed_ref[spot, 0:width], mixed_ref[spot, width : 2 * width]], axis=0
        )
        bands = product_of(table_ref[...], joined).astype(jnp.bfloat16)
        if len(bands_refs) == 1:
            lead = bands_refs[0].shape[0]
            run = pl.ds(sample * size // lead, size // lead)
            bands_refs[0][:, run] = bands.reshape(lead, size // lead, width)
        else:
            band_ref[sample] = bands
            for offset, bands_ref in enumerate(bands_refs):
                place = place_of(me_ref, offset, part)
                bands_ref[pl.ds(sample * part, part)] = band_ref[sample, place]


def activate(mixed_ref, w1_ref, b1_ref):
    pre = product_of(mixed_ref[0], w1_ref[0]) + b1_ref[0]
    logistic = sigmoid_of(pre)
    return logistic, pre * logistic


def bend(act_ref, w2_ref, b2_ref):
    out = product_of(act_ref[...], w2_ref[0]) + b2_ref[0]
    return out, jnp.tanh(out * (1.0 / shrink_level))


def forward_kernel(blocks, me_ref, lat_ref, unlat_ref, w1_ref, b1_ref, w2_ref, b2_ref, *refs):
    bands_refs, image_refs = refs[:blocks], refs[blocks : 2 * blocks]
    mixed_ref, act_ref, band_ref = refs[2 * blocks :]
    mix_lat(me_ref, lat_ref, bands_refs, band_ref, mixed_ref.at[0])
    act_ref[...] = activate(mixed_ref, w1_ref, b1_ref)[1].astype(jnp.bfloat16)
    out, bent = bend(act_ref, w2_ref, b2_ref)
    act_ref[...] = (out - shrink_level * bent).astype(jnp.bfloat16)
    unmix_lat(me_ref, unlat_ref, act_ref, band_ref, image_refs)


def backward_kernel(
    block_size, blocks, me_ref, lat_ref, unlat_ref, w1_ref, b1_ref, w2_ref, b2_ref, mixed_ref, *refs
):
    bands_refs, image_refs = refs[:blocks], refs[blocks : 2 * blocks]
    sums_ref, act_ref, gate_ref, cot_ref, kept_ref, band_ref = refs[2 * blocks :]
    transposed = (((1,), (1,)), ((), ()))
    summed = (((0,), (0,)), ((), ()))

    def times(former, latter, dims):
        return lax.dot_general(former, latter, dims, preferred_element_type=jnp.float32)

    def weight_sums(acts, grads, slot):
        width = acts.shape[1] // 2
        full = times(acts, grads, summed)
        real = full[:width, :width] + full[width:, width:]
        imag = full[:width, width:] - full[width:, :width]
        bias = jnp.sum(grads.astype(jnp.float32), axis=0, keepdims=True)
        size = block_size
        owner = lax.broadcasted_iota(jnp.int32, (size, width), 1) // size
        extra = sums_ref.shape[2] - size
        first = lax.broadcasted_iota(jnp.int32, (extra, width), 0) == 0
        for part, values in enumerate((real, imag)):
            joined = values[:size]
            for block in range(1, width // size):
                joined = jnp.where(owner == block, values[block * size : (block + 1) * size], joined)
            sums_ref[slot, part, 0:size] = joined.astype(sums_ref.dtype)
            row = bias[:, part * width : (part + 1) * width]
            sums_ref[slot, part, size:] = jnp.where(first, row, 0.0).astype(sums_ref.dtype)

    logistic, act = activate(mixed_ref, w1_ref, b1_ref)
    act_ref[...] = act.astype(jnp.bfloat16)
    gate_ref[...] = logistic + act * (1.0 - logistic)
    mix_lat(me_ref, lat_ref, bands_refs, band_ref, cot_ref)
    _, bent = bend(act_ref, w2_ref, b2_ref)
    kept_ref[...] = (cot_ref[...].astype(jnp.float32) * (bent * bent)).astype(jnp.bfloat16)
    back = times(kept_ref[...], w2_ref[0], transposed)
    cot_ref[...] = (back * gate_ref[...]).astype(jnp.bfloat16)
    weight_sums(act_ref[...], kept_ref[...], 1)
    kept_ref[...] = times(cot_ref[...], w1_ref[0], transposed).astype(jnp.bfloat16)
    weight_sums(mixed_ref[0], cot_ref[...], 0)
    unmix_lat(me_ref, unlat_ref, kept_ref, band_ref, image_refs)


def group_spec(*shape):
    return pl.BlockSpec((1,) + shape, lambda g, *_: (g,) + (0,) * len(shape))


def bands_specs(rows, bands, groups):
    block = (rows, bands[0].shape[1] // groups)
    return (pl.BlockSpec(block, lambda g, *_: (0, g)),) * len(bands)


def images_like(bands, samples, size, groups):
    if len(bands) > 1:
        shapes = tuple(in_hbm(band.shape, band.dtype) for band in bands)
        return shapes, bands_specs(bands[0].shape[0], bands, groups)
    channels = bands[0].shape[1]
    shape = (1, samples * size, channels)
    spec = pl.BlockSpec(shape[:2] + (channels // groups,), lambda g, *_: (0, 0, g))
    return (in_hbm(shape, jnp.bfloat16),), (spec,)


def forward_mid(me, lat, unlat, bands, w1, b1, w2, b2):
    groups, lanes, _ = w1.shape
    size = lat.shape[0]
    samples = bands[0].shape[0] * len(bands) // size
    positions = samples * size // 2
    table = pl.BlockSpec((size, size), lambda g, _: (0, 0))
    state = (groups, positions, lanes)
    specs = bands_specs(bands[0].shape[0], bands, groups)
    images, image_specs = images_like(bands, samples, size, groups)
    results = pl.pallas_call(
        functools.partial(forward_kernel, len(bands)),
        grid_spec=pltpu.PrefetchScalarGridSpec(
            num_scalar_prefetch=1,
            grid=(groups,),
            in_specs=[
                table, table,
                group_spec(lanes, lanes), group_spec(1, lanes),
                group_spec(lanes, lanes), group_spec(1, lanes),
                *specs,
            ],
            out_specs=image_specs + (group_spec(positions, lanes),),
            scratch_shapes=[
                pltpu.VMEM((positions, lanes), jnp.bfloat16),
                pltpu.VMEM((samples, size, lanes // 2), jnp.bfloat16),
            ],
        ),
        out_shape=images + (in_hbm(state, jnp.bfloat16),),
        compiler_params=params(28),
        cost_estimate=pl.CostEstimate(
            flops=4 * groups * positions * lanes * lanes,
            bytes_accessed=16 * groups * positions * lanes + 4 * groups * lanes * lanes,
            transcendentals=2 * groups * positions * lanes,
        ),
        name="mix_forward",
    )(me, lat, unlat, *hbm(w1), b1, *hbm(w2), b2, *hbm(*bands))
    return results[: len(bands)], results[len(bands)]


def backward_mid(me, lat, unlat, bands, w1, b1, w2, b2, state, count):
    groups, lanes, _ = w1.shape
    size = lat.shape[0]
    samples = bands[0].shape[0] * len(bands) // size
    positions = samples * size // 2
    table = pl.BlockSpec((size, size), lambda g, _: (0, 0))
    size_of_block = lanes // 2 // (count // groups)
    sums = (2, 2, size_of_block + 32, lanes // 2)
    images, image_specs = images_like(bands, samples, size, groups)
    results = pl.pallas_call(
        functools.partial(backward_kernel, size_of_block, len(bands)),
        grid_spec=pltpu.PrefetchScalarGridSpec(
            num_scalar_prefetch=1,
            grid=(groups,),
            in_specs=[
                table, table,
                group_spec(lanes, lanes), group_spec(1, lanes),
                group_spec(lanes, lanes), group_spec(1, lanes),
                group_spec(positions, lanes),
                *bands_specs(bands[0].shape[0], bands, groups),
            ],
            out_specs=image_specs + (pl.BlockSpec(sums, lambda g, _: (0, 0, 0, g)),),
            scratch_shapes=[
                pltpu.VMEM((positions, lanes), jnp.bfloat16),
                pltpu.VMEM((positions, lanes), jnp.float32),
                pltpu.VMEM((positions, lanes), jnp.bfloat16),
                pltpu.VMEM((positions, lanes), jnp.bfloat16),
                pltpu.VMEM((samples, size, lanes // 2), jnp.bfloat16),
            ],
        ),
        out_shape=images + (in_hbm(sums[:3] + (groups * sums[3],), jnp.float32),),
        compiler_params=params(32),
        cost_estimate=pl.CostEstimate(
            flops=8 * groups * positions * lanes * lanes,
            bytes_accessed=16 * groups * positions * lanes + 4 * groups * lanes * lanes,
            transcendentals=0,
        ),
        name="mix_backward",
    )(me, lat, unlat, *hbm(w1), b1, *hbm(w2), b2, *hbm(state, *bands))
    return results[: len(bands)], results[len(bands)]


def swap_with(values, axis, distance):
    pairs = [(i, i ^ distance) for i in range(lax.axis_size(axis))]
    return lax.ppermute(values, axis, pairs)


def waiting(values, arrived):
    return lax.optimization_barrier((values, tuple(arrived)))[0]


def mixed_order(size):
    far = list(range(size // 2, size))
    near = [offset for offset in (2, 3, 1) if offset < size // 2]
    near += list(range(4, size // 2))
    order = []
    while far or near:
        order += far[:1] + near[:1]
        far, near = far[1:], near[1:]
    return order


def pick(pair, side):
    return lax.dynamic_index_in_dim(pair, side, 0, keepdims=False)


class GroupSum:
    def __init__(self, sums):
        self.lanes = sums.shape[-1]
        self.side = lax.axis_index("dp")
        self.me = lax.axis_index("space")
        self.count = lax.axis_size("space") // 2
        self.held = sums.reshape(-1, self.lanes)

    def halve(self, axis, distance, bit):
        pair = self.held.reshape(2, -1, self.lanes)
        taken = swap_with(pick(pair, 1 - bit), axis, distance)
        self.held = pick(pair, bit) + taken
        return taken

    def over_dp(self):
        return self.halve("dp", 1, self.side)

    def over_next(self):
        return self.halve("space", 1, self.me % 2)

    def scatter(self, arrived):
        shares = waiting(self.held, arrived).reshape(self.count, -1, self.lanes)
        place = self.me // 2
        total = pick(shares, place)
        for offset in range(1, self.count):
            given = pick(shares, place ^ offset).astype(jnp.bfloat16)
            total += swap_with(given, "space", 2 * offset).astype(jnp.float32)
        self.total = total.astype(jnp.bfloat16)

    def gather(self, arrived):
        total = waiting(self.total, arrived)
        taken = [total]
        for offset in range(1, self.count):
            taken.append(swap_with(total, "space", 2 * offset))
        quarter = jnp.stack(taken)
        half = jnp.stack([quarter, swap_with(quarter, "space", 1)])
        return half, swap_with(half, "dp", 1)


def finish_kernel(factor, me_ref, half_ref, other_ref, *out_refs):
    side, near, place = me_ref[0], me_ref[1], me_ref[2]
    run = half_ref.shape[2]
    for which in range(2):
        blocks_ref, bias_ref = out_refs[2 * which : 2 * which + 2]
        edge = blocks_ref.shape[-1]
        for part in range(2):
            for piece in range(half_ref.shape[1]):
                spot = (part ^ near, piece ^ place)
                own = half_ref[spot].astype(jnp.float32)
                value = jnp.where(side == which, own, other_ref[spot].astype(jnp.float32)) * factor
                first = piece * run
                count = max(0, min(edge - first, run))
                for block in range(blocks_ref.shape[1]):
                    lanes = slice(block * edge, (block + 1) * edge)
                    if count > 0:
                        blocks_ref[part, block, pl.ds(first, count)] = value[:count, lanes]
                    if first <= edge < first + run:
                        row = edge - first
                        bias_ref[part, pl.ds(block, 1)] = value[row : row + 1, lanes]


def finish_sums(here, half, other, factor, weight_shape, bias_shape):
    outs = [weight_shape, bias_shape] * 2
    return pl.pallas_call(
        functools.partial(finish_kernel, factor),
        out_shape=[jax.ShapeDtypeStruct(shape, jnp.float32) for shape in outs],
        in_specs=[pl.BlockSpec(memory_space=pltpu.SMEM)]
        + [pl.BlockSpec(memory_space=pltpu.VMEM)] * 2,
        out_specs=[pl.BlockSpec(memory_space=pltpu.VMEM)] * 4,
        compiler_params=pltpu.CompilerParams(vmem_limit_bytes=16 * MIB),
        cost_estimate=pl.CostEstimate(flops=0, bytes_accessed=4 * MIB, transcendentals=0),
        name="finish_sums",
    )(here, half, other)


def body(fields, cotangent, w_first, b_first, w_second, b_second):
    samples, rows, width, channels = fields.shape
    owners = lax.axis_size("space")
    lat_total = rows * owners
    modes = KW // owners
    count, edge = w_first.shape[1:3]
    groups = 2
    direct = 2 * modes % 16 == 0
    lead = owners if direct else 1

    order = mixed_order(owners)

    def send(blocks, offsets, taken):
        for offset in offsets:
            taken[offset] = swap_with(blocks[offset], "space", offset)

    def send_all(spectrum):
        spectrum = spectrum.reshape(samples, rows, owners, 2 * modes, channels)
        spectrum = jnp.transpose(spectrum, (2, 0, 1, 3, 4))
        arrived = lax.all_to_all(spectrum, "space", split_axis=0, concat_axis=0, tiled=True)
        return [jnp.transpose(arrived, (1, 0, 2, 3, 4)).reshape(-1, channels)]

    def send_all_back(bands):
        bands = bands.reshape(samples, owners, rows, 2 * modes, channels)
        bands = jnp.transpose(bands, (1, 0, 2, 3, 4))
        arrived = lax.all_to_all(bands, "space", split_axis=0, concat_axis=0, tiled=True)
        return [jnp.transpose(arrived, (1, 2, 0, 3, 4)).reshape(1, -1, channels)]

    me = lax.axis_index("space") if direct else 0
    me = jnp.full((1,), me, jnp.int32)
    plain, scaled = lon_tables(KW, width, owners)
    lat = lat_spread(lat_total, modes)

    spectrum = to_modes(me, plain, fields, lead)
    spectrum, cotangent, w_first, w_second = lax.optimization_barrier(
        (spectrum, cotangent, w_first, w_second)
    )
    cot_spec = to_modes(me, scaled, cotangent, lead)
    w1, w2 = spread_weights(groups, w_first, w_second)
    b1, b2 = block_bias(b_first, groups), block_bias(b_second, groups)
    positions = samples * lax.axis_size("dp") * lat_total * KW
    factor = 1.0 / math.sqrt(positions)

    if not direct:
        gathered = send_all(spectrum[0])
        image, state = forward_mid(me, lat, lat.T, gathered, w1, b1, w2, b2)
        image_band = send_all_back(image[0])
        gathered = send_all(cot_spec[0])
        grad_image, sums = backward_mid(me, lat, lat.T, gathered, w1, b1, w2, b2, state, count)
        grad_band = send_all_back(grad_image[0])
        output = to_cells(me, scaled.T, image_band, fields)
        grad_fields = to_cells(me, plain.T, grad_band, cotangent)
        sums = lax.psum(sums, ("space", "dp")) * factor
        grads = []
        for which in range(2):
            blocks = sums[which, :, :edge].reshape(2, edge, count, edge)
            grads.append(jnp.transpose(blocks, (0, 2, 1, 3)))
            grads.append(sums[which, :, edge].reshape(b_first.shape))
        return (output, grad_fields) + tuple(grads)

    gathered, cot_gathered = {0: spectrum[0]}, {0: cot_spec[0]}
    send(spectrum, order, gathered)
    gathered = [gathered[offset] for offset in range(owners)]
    image, state = forward_mid(me, lat, lat.T, gathered, w1, b1, w2, b2)
    cot_spec, image = list(cot_spec), list(image)
    send(cot_spec, order[:FIRST], cot_gathered)
    cot_spec, image = waiting((cot_spec, image), [image[0]])
    send(cot_spec, order[FIRST:], cot_gathered)

    image_band = {0: image[0]}
    send(image, order, image_band)
    cot_gathered = [cot_gathered[offset] for offset in range(owners)]
    grad_image, sums = backward_mid(
        me, lat, lat.T, cot_gathered, w1, b1, w2, b2, state, count
    )
    early = [image_band[offset] for offset in order[:HELD]]
    late = [image_band[offset] for offset in order[HELD:]]
    grad_image, sums = waiting((list(grad_image), sums), early)
    group_sum = GroupSum(sums)
    over_dp = group_sum.over_dp()
    group_sum.held = waiting(group_sum.held, late[:1])
    over_next = group_sum.over_next()
    grad_band = {0: grad_image[0]}
    send(grad_image, order[:2], grad_band)
    grad_image = waiting(grad_image, late)
    send(grad_image, order[2:4], grad_band)
    grad_image = waiting(grad_image, [over_dp])
    send(grad_image, order[4:5], grad_band)
    grad_image = waiting(grad_image, [over_next])
    send(grad_image, order[5:], grad_band)
    arrived = [grad_band[offset] for offset in order]
    image_band = [image_band[offset] for offset in range(owners)]
    grad_band = [grad_band[offset] for offset in range(owners)]
    output = to_cells(me, scaled.T, image_band, fields)
    group_sum.scatter(arrived)
    half, other = group_sum.gather([output])
    grad_fields = to_cells(me, plain.T, grad_band, cotangent)
    place = lax.axis_index("space")
    here = jnp.stack([lax.axis_index("dp"), place % 2, place // 2]).astype(jnp.int32)
    grads = finish_sums(
        here, half, other, factor, w_first.shape, b_first.shape
    )
    return (output, grad_fields) + tuple(grads)


def solution(mesh):
    split = P(("parts", "dp"), "space", None, None)
    in_specs = (split, split, P(), P(), P(), P())
    out_specs = (
        split,
        split,
        P("parts", None, None, None),
        P("parts", None, None),
        P("parts", None, None, None),
        P("parts", None, None),
    )
    return jax.shard_map(body, mesh=mesh, in_specs=in_specs, out_specs=out_specs, check_vma=False)
```

```python
import functools
import math

import jax
import jax.numpy as jnp
from jax import lax
from jax.experimental import pallas as pl
from jax.experimental.pallas import tpu as pltpu
from jax.sharding import PartitionSpec as P
import ml_dtypes
import numpy as np

KW = 64
shrink_level = 0.05
FIRST = 4
HELD = 5
MIB = 1024 * 1024


def product_of(former, latter):
    return jnp.dot(former, latter, preferred_element_type=jnp.float32)


def lon_tables(mode_count, cell_count, owners):
    wavenums = np.arange(mode_count, dtype=np.int32)
    columns = np.arange(cell_count, dtype=np.int32)
    phase_index = (wavenums[:, None] * columns[None, :] % cell_count).astype(np.float32)
    phases = phase_index * np.float32(2.0 * math.pi / cell_count)
    factor = np.float32(1.0 / math.sqrt(cell_count))
    forward = np.stack([np.cos(phases) * factor, -np.sin(phases) * factor])
    scaled = forward * np.where(wavenums == 0, 1.0, 2.0).astype(np.float32)[:, None]

    def ordered(table):
        split = table.reshape(2, owners, -1, cell_count).transpose(1, 0, 2, 3)
        return split.reshape(-1, cell_count).astype(ml_dtypes.bfloat16)

    return ordered(forward), ordered(scaled)


def lat_spread(row_count, modes):
    indices = np.arange(row_count, dtype=np.int32)
    phase_index = (indices[:, None] * indices[None, :] % row_count).astype(np.float32)
    phases = phase_index * np.float32(2.0 * math.pi / row_count)
    factor = np.float32(1.0 / math.sqrt(row_count))
    cosine = np.cos(phases) * factor
    sine_part = np.sin(phases) * factor
    table = np.stack([np.stack([cosine, sine_part], -1), np.stack([-sine_part, cosine], -1)])
    same = np.eye(modes, dtype=np.float32)
    spread = table[:, :, None, :, :, None] * same[None, None, :, None, None, :]
    size = 2 * row_count * modes
    return spread.reshape(size, size).astype(ml_dtypes.bfloat16)


def block_bias(bias, groups):
    return jnp.transpose(bias.reshape(2, groups, 1, -1), (1, 2, 0, 3)).reshape(groups, 1, -1)


def spread_kernel(*refs):
    half_way = len(refs) // 2
    for blocks_ref, joined_ref in zip(refs[:half_way], refs[half_way:]):
        _, per, size, _ = blocks_ref.shape
        width = per * size
        row = lax.broadcasted_iota(jnp.int32, (size, width), 0)
        lane = lax.broadcasted_iota(jnp.int32, (size, width), 1)
        for block in range(per):
            place = (row + block * size == lane).astype(jnp.bfloat16)
            real = product_of(blocks_ref[0, block], place).astype(jnp.bfloat16)
            imag = product_of(blocks_ref[1, block], place)
            upper = pl.ds(block * size, size)
            lower = pl.ds(width + block * size, size)
            joined_ref[0, upper, 0:width] = real
            joined_ref[0, upper, width : 2 * width] = imag.astype(jnp.bfloat16)
            joined_ref[0, lower, 0:width] = (-imag).astype(jnp.bfloat16)
            joined_ref[0, lower, width : 2 * width] = real


def spread_weights(groups, *weights):
    _, count, size, _ = weights[0].shape
    per = count // groups
    lanes = 2 * per * size
    shape = in_hbm((groups, lanes, lanes), jnp.bfloat16)
    return pl.pallas_call(
        spread_kernel,
        grid=(groups,),
        out_shape=(shape,) * len(weights),
        in_specs=[pl.BlockSpec((2, per, size, size), lambda g: (0, g, 0, 0))] * len(weights),
        out_specs=(group_spec(lanes, lanes),) * len(weights),
        compiler_params=params(12),
        cost_estimate=pl.CostEstimate(
            flops=len(weights) * 2 * count * size * size * lanes,
            bytes_accessed=len(weights) * 2 * groups * lanes * lanes,
            transcendentals=0,
        ),
        name="spread_weights",
    )(*weights)


def params(mebibytes):
    return pltpu.CompilerParams(
        vmem_limit_bytes=mebibytes * MIB, dimension_semantics=("arbitrary",)
    )


def place_of(me_ref, offset, rows):
    return pl.ds(pl.multiple_of((me_ref[0] ^ offset) * rows, rows), rows)


def in_hbm(shape, dtype):
    return pltpu.HBM(shape, dtype)


def hbm(*arrays):
    return [pltpu.with_memory_space_constraint(array, pltpu.HBM) for array in arrays]


def to_modes_kernel(me_ref, table_ref, cells_ref, *refs):
    modes_refs, held_ref = refs[:-1], refs[-1]
    rows = cells_ref.shape[1]
    share = modes_refs[0].shape[0] // rows
    for row in range(rows):
        spectrum = product_of(table_ref[...], cells_ref[0, row])
        held_ref[row] = spectrum.astype(jnp.bfloat16)
        for offset, modes_ref in enumerate(modes_refs):
            modes_ref[pl.ds(row * share, share)] = held_ref[row, place_of(me_ref, offset, share)]


def to_modes(me, table, cells, owners):
    samples, rows, width, channels = cells.shape
    size = table.shape[0]
    part = rows * size // owners
    return pl.pallas_call(
        to_modes_kernel,
        grid_spec=pltpu.PrefetchScalarGridSpec(
            num_scalar_prefetch=1,
            grid=(samples,),
            in_specs=[
                pl.BlockSpec((size, width), lambda b, _: (0, 0)),
                pl.BlockSpec((1, rows, width, channels), lambda b, _: (b, 0, 0, 0)),
            ],
            out_specs=(pl.BlockSpec((part, channels), lambda b, _: (b, 0)),) * owners,
            scratch_shapes=[pltpu.VMEM((rows, size, channels), jnp.bfloat16)],
        ),
        out_shape=(in_hbm((samples * part, channels), jnp.bfloat16),) * owners,
        compiler_params=params(12),
        cost_estimate=pl.CostEstimate(
            flops=2 * samples * rows * size * width * channels,
            bytes_accessed=2 * samples * rows * channels * (width + size),
            transcendentals=0,
        ),
        name="to_modes",
    )(me, table, cells)


def to_cells_kernel(me_ref, table_ref, base_ref, *refs):
    modes_refs, out_ref, held_ref = refs[:-2], refs[-2], refs[-1]
    rows = base_ref.shape[1]
    share = modes_refs[0].shape[-2] // rows
    for row in range(rows):
        run = pl.ds(row * share, share)
        if len(modes_refs) == 1:
            spectrum = modes_refs[0][:, run].reshape(held_ref.shape[1:])
        else:
            for offset, modes_ref in enumerate(modes_refs):
                held_ref[row, place_of(me_ref, offset, share)] = modes_ref[run]
            spectrum = held_ref[row]
        image = product_of(table_ref[...], spectrum)
        out_ref[0, row] = (base_ref[0, row].astype(jnp.float32) + image).astype(jnp.bfloat16)


def to_cells(me, table, modes, base):
    samples, rows, width, channels = base.shape
    size = table.shape[1]
    block = pl.BlockSpec((1, rows, width, channels), lambda b, _: (b, 0, 0, 0))
    if len(modes) == 1:
        lead = modes[0].shape[0]
        part = rows * size // lead
        specs = [pl.BlockSpec((lead, part, channels), lambda b, _: (0, b, 0))]
    else:
        part = rows * size // len(modes)
        specs = [pl.BlockSpec((part, channels), lambda b, _: (b, 0))] * len(modes)
    return pl.pallas_call(
        to_cells_kernel,
        grid_spec=pltpu.PrefetchScalarGridSpec(
            num_scalar_prefetch=1,
            grid=(samples,),
            in_specs=[pl.BlockSpec((width, size), lambda b, _: (0, 0)), block] + specs,
            out_specs=block,
            scratch_shapes=[pltpu.VMEM((rows, size, channels), jnp.bfloat16)],
        ),
        out_shape=jax.ShapeDtypeStruct(base.shape, jnp.bfloat16),
        compiler_params=params(12),
        cost_estimate=pl.CostEstimate(
            flops=2 * samples * rows * size * width * channels,
            bytes_accessed=2 * samples * rows * channels * (2 * width + size),
            transcendentals=0,
        ),
        name="to_cells",
    )(me, table, base, *hbm(*modes))


def sigmoid_of(values):
    return 0.5 + 0.5 * jnp.tanh(0.5 * values)


def mix_lat(me_ref, table_ref, bands_refs, band_ref, mixed_ref):
    samples, size, width = band_ref.shape
    part, half = size // len(bands_refs), size // 2
    for sample in range(samples):
        for offset, bands_ref in enumerate(bands_refs):
            place = place_of(me_ref, offset, part)
            band_ref[sample, place] = bands_ref[pl.ds(sample * part, part)]
        mixed = product_of(table_ref[...], band_ref[sample]).astype(jnp.bfloat16)
        spot = pl.ds(sample * half, half)
        mixed_ref[spot, 0:width] = mixed[:half]
        mixed_ref[spot, width : 2 * width] = mixed[half:]


def unmix_lat(me_ref, table_ref, mixed_ref, band_ref, bands_refs):
    samples, size, width = band_ref.shape
    part, half = size // len(bands_refs), size // 2
    for sample in range(samples):
        spot = pl.ds(sample * half, half)
        joined = jnp.concatenate(
            [mixed_ref[spot, 0:width], mixed_ref[spot, width : 2 * width]], axis=0
        )
        bands = product_of(table_ref[...], joined).astype(jnp.bfloat16)
        if len(bands_refs) == 1:
            lead = bands_refs[0].shape[0]
            run = pl.ds(sample * size // lead, size // lead)
            bands_refs[0][:, run] = bands.reshape(lead, size // lead, width)
        else:
            band_ref[sample] = bands
            for offset, bands_ref in enumerate(bands_refs):
                place = place_of(me_ref, offset, part)
                bands_ref[pl.ds(sample * part, part)] = band_ref[sample, place]


def activate(mixed_ref, w1_ref, b1_ref):
    pre = product_of(mixed_ref[0], w1_ref[0]) + b1_ref[0]
    logistic = sigmoid_of(pre)
    return logistic, pre * logistic


def bend(act_ref, w2_ref, b2_ref):
    out = product_of(act_ref[...], w2_ref[0]) + b2_ref[0]
    return out, jnp.tanh(out * (1.0 / shrink_level))


def forward_kernel(blocks, me_ref, lat_ref, unlat_ref, w1_ref, b1_ref, w2_ref, b2_ref, *refs):
    bands_refs, image_refs = refs[:blocks], refs[blocks : 2 * blocks]
    mixed_ref, act_ref, band_ref = refs[2 * blocks :]
    mix_lat(me_ref, lat_ref, bands_refs, band_ref, mixed_ref.at[0])
    act_ref[...] = activate(mixed_ref, w1_ref, b1_ref)[1].astype(jnp.bfloat16)
    out, bent = bend(act_ref, w2_ref, b2_ref)
    act_ref[...] = (out - shrink_level * bent).astype(jnp.bfloat16)
    unmix_lat(me_ref, unlat_ref, act_ref, band_ref, image_refs)


def backward_kernel(
    block_size, blocks, me_ref, lat_ref, unlat_ref, w1_ref, b1_ref, w2_ref, b2_ref, mixed_ref, *refs
):
    bands_refs, image_refs = refs[:blocks], refs[blocks : 2 * blocks]
    sums_ref, act_ref, gate_ref, cot_ref, kept_ref, band_ref = refs[2 * blocks :]
    transposed = (((1,), (1,)), ((), ()))
    summed = (((0,), (0,)), ((), ()))

    def times(former, latter, dims):
        return lax.dot_general(former, latter, dims, preferred_element_type=jnp.float32)

    def weight_sums(acts, grads, slot):
        width = acts.shape[1] // 2
        full = times(acts, grads, summed)
        real = full[:width, :width] + full[width:, width:]
        imag = full[:width, width:] - full[width:, :width]
        bias = jnp.sum(grads.astype(jnp.float32), axis=0, keepdims=True)
        size = block_size
        owner = lax.broadcasted_iota(jnp.int32, (size, width), 1) // size
        extra = sums_ref.shape[2] - size
        first = lax.broadcasted_iota(jnp.int32, (extra, width), 0) == 0
        for part, values in enumerate((real, imag)):
            joined = values[:size]
            for block in range(1, width // size):
                joined = jnp.where(owner == block, values[block * size : (block + 1) * size], joined)
            sums_ref[slot, part, 0:size] = joined.astype(sums_ref.dtype)
            row = bias[:, part * width : (part + 1) * width]
            sums_ref[slot, part, size:] = jnp.where(first, row, 0.0).astype(sums_ref.dtype)

    logistic, act = activate(mixed_ref, w1_ref, b1_ref)
    act_ref[...] = act.astype(jnp.bfloat16)
    gate_ref[...] = logistic + act * (1.0 - logistic)
    mix_lat(me_ref, lat_ref, bands_refs, band_ref, cot_ref)
    _, bent = bend(act_ref, w2_ref, b2_ref)
    kept_ref[...] = (cot_ref[...].astype(jnp.float32) * (bent * bent)).astype(jnp.bfloat16)
    back = times(kept_ref[...], w2_ref[0], transposed)
    cot_ref[...] = (back * gate_ref[...]).astype(jnp.bfloat16)
    weight_sums(act_ref[...], kept_ref[...], 1)
    kept_ref[...] = times(cot_ref[...], w1_ref[0], transposed).astype(jnp.bfloat16)
    weight_sums(mixed_ref[0], cot_ref[...], 0)
    unmix_lat(me_ref, unlat_ref, kept_ref, band_ref, image_refs)


def group_spec(*shape):
    return pl.BlockSpec((1,) + shape, lambda g, *_: (g,) + (0,) * len(shape))


def bands_specs(rows, bands, groups):
    block = (rows, bands[0].shape[1] // groups)
    return (pl.BlockSpec(block, lambda g, *_: (0, g)),) * len(bands)


def images_like(bands, samples, size, groups):
    if len(bands) > 1:
        shapes = tuple(in_hbm(band.shape, band.dtype) for band in bands)
        return shapes, bands_specs(bands[0].shape[0], bands, groups)
    channels = bands[0].shape[1]
    shape = (1, samples * size, channels)
    spec = pl.BlockSpec(shape[:2] + (channels // groups,), lambda g, *_: (0, 0, g))
    return (in_hbm(shape, jnp.bfloat16),), (spec,)


def forward_mid(me, lat, unlat, bands, w1, b1, w2, b2):
    groups, lanes, _ = w1.shape
    size = lat.shape[0]
    samples = bands[0].shape[0] * len(bands) // size
    positions = samples * size // 2
    table = pl.BlockSpec((size, size), lambda g, _: (0, 0))
    state = (groups, positions, lanes)
    specs = bands_specs(bands[0].shape[0], bands, groups)
    images, image_specs = images_like(bands, samples, size, groups)
    results = pl.pallas_call(
        functools.partial(forward_kernel, len(bands)),
        grid_spec=pltpu.PrefetchScalarGridSpec(
            num_scalar_prefetch=1,
            grid=(groups,),
            in_specs=[
                table, table,
                group_spec(lanes, lanes), group_spec(1, lanes),
                group_spec(lanes, lanes), group_spec(1, lanes),
                *specs,
            ],
            out_specs=image_specs + (group_spec(positions, lanes),),
            scratch_shapes=[
                pltpu.VMEM((positions, lanes), jnp.bfloat16),
                pltpu.VMEM((samples, size, lanes // 2), jnp.bfloat16),
            ],
        ),
        out_shape=images + (in_hbm(state, jnp.bfloat16),),
        compiler_params=params(28),
        cost_estimate=pl.CostEstimate(
            flops=4 * groups * positions * lanes * lanes,
            bytes_accessed=16 * groups * positions * lanes + 4 * groups * lanes * lanes,
            transcendentals=2 * groups * positions * lanes,
        ),
        name="mix_forward",
    )(me, lat, unlat, *hbm(w1), b1, *hbm(w2), b2, *hbm(*bands))
    return results[: len(bands)], results[len(bands)]


def backward_mid(me, lat, unlat, bands, w1, b1, w2, b2, state, count):
    groups, lanes, _ = w1.shape
    size = lat.shape[0]
    samples = bands[0].shape[0] * len(bands) // size
    positions = samples * size // 2
    table = pl.BlockSpec((size, size), lambda g, _: (0, 0))
    size_of_block = lanes // 2 // (count // groups)
    sums = (2, 2, size_of_block + 32, lanes // 2)
    images, image_specs = images_like(bands, samples, size, groups)
    results = pl.pallas_call(
        functools.partial(backward_kernel, size_of_block, len(bands)),
        grid_spec=pltpu.PrefetchScalarGridSpec(
            num_scalar_prefetch=1,
            grid=(groups,),
            in_specs=[
                table, table,
                group_spec(lanes, lanes), group_spec(1, lanes),
                group_spec(lanes, lanes), group_spec(1, lanes),
                group_spec(positions, lanes),
                *bands_specs(bands[0].shape[0], bands, groups),
            ],
            out_specs=image_specs + (pl.BlockSpec(sums, lambda g, _: (0, 0, 0, g)),),
            scratch_shapes=[
                pltpu.VMEM((positions, lanes), jnp.bfloat16),
                pltpu.VMEM((positions, lanes), jnp.float32),
                pltpu.VMEM((positions, lanes), jnp.bfloat16),
                pltpu.VMEM((positions, lanes), jnp.bfloat16),
                pltpu.VMEM((samples, size, lanes // 2), jnp.bfloat16),
            ],
        ),
        out_shape=images + (in_hbm(sums[:3] + (groups * sums[3],), jnp.float32),),
        compiler_params=params(32),
        cost_estimate=pl.CostEstimate(
            flops=8 * groups * positions * lanes * lanes,
            bytes_accessed=16 * groups * positions * lanes + 4 * groups * lanes * lanes,
            transcendentals=0,
        ),
        name="mix_backward",
    )(me, lat, unlat, *hbm(w1), b1, *hbm(w2), b2, *hbm(state, *bands))
    return results[: len(bands)], results[len(bands)]


def swap_with(values, axis, distance):
    pairs = [(i, i ^ distance) for i in range(lax.axis_size(axis))]
    return lax.ppermute(values, axis, pairs)


def waiting(values, arrived):
    return lax.optimization_barrier((values, tuple(arrived)))[0]


def mixed_order(size):
    far = list(range(size // 2, size))
    near = [offset for offset in (2, 3, 1) if offset < size // 2]
    near += list(range(4, size // 2))
    order = []
    while far or near:
        order += far[:1] + near[:1]
        far, near = far[1:], near[1:]
    return order


def pick(pair, side):
    return lax.dynamic_index_in_dim(pair, side, 0, keepdims=False)


class GroupSum:
    def __init__(self, sums):
        self.lanes = sums.shape[-1]
        self.side = lax.axis_index("dp")
        self.me = lax.axis_index("space")
        self.count = lax.axis_size("space") // 2
        self.held = sums.reshape(-1, self.lanes)

    def halve(self, axis, distance, bit, arrived):
        pair = waiting(self.held, arrived).reshape(2, -1, self.lanes)
        self.held = pick(pair, bit) + swap_with(pick(pair, 1 - bit), axis, distance)

    def over_dp(self):
        self.halve("dp", 1, self.side, [])

    def over_next(self, arrived):
        self.halve("space", 1, self.me % 2, arrived)

    def scatter(self, arrived):
        shares = waiting(self.held, arrived).reshape(self.count, -1, self.lanes)
        place = self.me // 2
        total = pick(shares, place)
        for offset in range(1, self.count):
            given = pick(shares, place ^ offset).astype(jnp.bfloat16)
            total += swap_with(given, "space", 2 * offset).astype(jnp.float32)
        self.total = total.astype(jnp.bfloat16)

    def gather(self, arrived):
        total = waiting(self.total, arrived)
        taken = [total]
        for offset in range(1, self.count):
            taken.append(swap_with(total, "space", 2 * offset))
        self.quarter = jnp.stack(taken)

    def gather_next(self, arrived):
        quarter = waiting(self.quarter, arrived)
        self.half = jnp.stack([quarter, swap_with(quarter, "space", 1)])

    def gather_dp(self):
        return self.half, swap_with(self.half, "dp", 1)


def finish_kernel(factor, me_ref, half_ref, other_ref, *out_refs):
    side, near, place = me_ref[0], me_ref[1], me_ref[2]
    run = half_ref.shape[2]
    for which in range(2):
        blocks_ref, bias_ref = out_refs[2 * which : 2 * which + 2]
        edge = blocks_ref.shape[-1]
        for part in range(2):
            for piece in range(half_ref.shape[1]):
                spot = (part ^ near, piece ^ place)
                own = half_ref[spot].astype(jnp.float32)
                value = jnp.where(side == which, own, other_ref[spot].astype(jnp.float32)) * factor
                first = piece * run
                count = max(0, min(edge - first, run))
                for block in range(blocks_ref.shape[1]):
                    lanes = slice(block * edge, (block + 1) * edge)
                    if count > 0:
                        blocks_ref[part, block, pl.ds(first, count)] = value[:count, lanes]
                    if first <= edge < first + run:
                        row = edge - first
                        bias_ref[part, pl.ds(block, 1)] = value[row : row + 1, lanes]


def finish_sums(here, half, other, factor, weight_shape, bias_shape):
    outs = [weight_shape, bias_shape] * 2
    return pl.pallas_call(
        functools.partial(finish_kernel, factor),
        out_shape=[jax.ShapeDtypeStruct(shape, jnp.float32) for shape in outs],
        in_specs=[pl.BlockSpec(memory_space=pltpu.SMEM)]
        + [pl.BlockSpec(memory_space=pltpu.VMEM)] * 2,
        out_specs=[pl.BlockSpec(memory_space=pltpu.VMEM)] * 4,
        compiler_params=pltpu.CompilerParams(vmem_limit_bytes=16 * MIB),
        cost_estimate=pl.CostEstimate(flops=0, bytes_accessed=4 * MIB, transcendentals=0),
        name="finish_sums",
    )(here, half, other)


def body(fields, cotangent, w_first, b_first, w_second, b_second):
    samples, rows, width, channels = fields.shape
    owners = lax.axis_size("space")
    lat_total = rows * owners
    modes = KW // owners
    count, edge = w_first.shape[1:3]
    groups = 2
    direct = 2 * modes % 16 == 0
    lead = owners if direct else 1

    order = mixed_order(owners)

    def send(blocks, offsets, taken):
        for offset in offsets:
            taken[offset] = swap_with(blocks[offset], "space", offset)

    def send_all(spectrum):
        spectrum = spectrum.reshape(samples, rows, owners, 2 * modes, channels)
        spectrum = jnp.transpose(spectrum, (2, 0, 1, 3, 4))
        arrived = lax.all_to_all(spectrum, "space", split_axis=0, concat_axis=0, tiled=True)
        return [jnp.transpose(arrived, (1, 0, 2, 3, 4)).reshape(-1, channels)]

    def send_all_back(bands):
        bands = bands.reshape(samples, owners, rows, 2 * modes, channels)
        bands = jnp.transpose(bands, (1, 0, 2, 3, 4))
        arrived = lax.all_to_all(bands, "space", split_axis=0, concat_axis=0, tiled=True)
        return [jnp.transpose(arrived, (1, 2, 0, 3, 4)).reshape(1, -1, channels)]

    me = lax.axis_index("space") if direct else 0
    me = jnp.full((1,), me, jnp.int32)
    plain, scaled = lon_tables(KW, width, owners)
    lat = lat_spread(lat_total, modes)

    spectrum = to_modes(me, plain, fields, lead)
    spectrum, cotangent, w_first, w_second = lax.optimization_barrier(
        (spectrum, cotangent, w_first, w_second)
    )
    cot_spec = to_modes(me, scaled, cotangent, lead)
    w1, w2 = spread_weights(groups, w_first, w_second)
    b1, b2 = block_bias(b_first, groups), block_bias(b_second, groups)
    positions = samples * lax.axis_size("dp") * lat_total * KW
    factor = 1.0 / math.sqrt(positions)

    if not direct:
        gathered = send_all(spectrum[0])
        image, state = forward_mid(me, lat, lat.T, gathered, w1, b1, w2, b2)
        image_band = send_all_back(image[0])
        gathered = send_all(cot_spec[0])
        grad_image, sums = backward_mid(me, lat, lat.T, gathered, w1, b1, w2, b2, state, count)
        grad_band = send_all_back(grad_image[0])
        output = to_cells(me, scaled.T, image_band, fields)
        grad_fields = to_cells(me, plain.T, grad_band, cotangent)
        sums = lax.psum(sums, ("space", "dp")) * factor
        grads = []
        for which in range(2):
            blocks = sums[which, :, :edge].reshape(2, edge, count, edge)
            grads.append(jnp.transpose(blocks, (0, 2, 1, 3)))
            grads.append(sums[which, :, edge].reshape(b_first.shape))
        return (output, grad_fields) + tuple(grads)

    gathered, cot_gathered = {0: spectrum[0]}, {0: cot_spec[0]}
    send(spectrum, order, gathered)
    gathered = [gathered[offset] for offset in range(owners)]
    image, state = forward_mid(me, lat, lat.T, gathered, w1, b1, w2, b2)
    cot_spec, image = list(cot_spec), list(image)
    send(cot_spec, order[:FIRST], cot_gathered)
    cot_spec, image = waiting((cot_spec, image), [image[0]])
    send(cot_spec, order[FIRST:], cot_gathered)

    image_band = {0: image[0]}
    send(image, order, image_band)
    cot_gathered = [cot_gathered[offset] for offset in range(owners)]
    grad_image, sums = backward_mid(
        me, lat, lat.T, cot_gathered, w1, b1, w2, b2, state, count
    )
    early = [image_band[offset] for offset in order[:HELD]]
    late = [image_band[offset] for offset in order[HELD:]]
    grad_image, sums = waiting((list(grad_image), sums), early)
    group_sum = GroupSum(sums)
    group_sum.over_dp()
    group_sum.over_next(late)
    grad_band = {0: grad_image[0]}
    send(grad_image, order, grad_band)
    arrived = [grad_band[offset] for offset in order]
    image_band = [image_band[offset] for offset in range(owners)]
    grad_band = [grad_band[offset] for offset in range(owners)]
    output = to_cells(me, scaled.T, image_band, fields)
    group_sum.scatter(arrived[:2])
    group_sum.gather(arrived[2:4])
    group_sum.gather_next(arrived[4:] + [output])
    half, other = group_sum.gather_dp()
    grad_fields = to_cells(me, plain.T, grad_band, cotangent)
    place = lax.axis_index("space")
    here = jnp.stack([lax.axis_index("dp"), place % 2, place // 2]).astype(jnp.int32)
    grads = finish_sums(
        here, half, other, factor, w_first.shape, b_first.shape
    )
    return (output, grad_fields) + tuple(grads)


def solution(mesh):
    split = P(("parts", "dp"), "space", None, None)
    in_specs = (split, split, P(), P(), P(), P())
    out_specs = (
        split,
        split,
        P("parts", None, None, None),
        P("parts", None, None),
        P("parts", None, None, None),
        P("parts", None, None),
    )
    return jax.shard_map(body, mesh=mesh, in_specs=in_specs, out_specs=out_specs, check_vma=False)
```

```python
import functools
import math

import jax
import jax.numpy as jnp
from jax import lax
from jax.experimental import pallas as pl
from jax.experimental.layout import Layout, with_layout_constraint
from jax.experimental.pallas import tpu as pltpu
from jax.sharding import PartitionSpec as P
import ml_dtypes
import numpy as np

KW = 64
shrink_level = 0.05
FIRST = 4
HELD = 5
MIB = 1024 * 1024


def product_of(former, latter):
    return jnp.dot(former, latter, preferred_element_type=jnp.float32)


def lon_tables(mode_count, cell_count, owners):
    wavenums = np.arange(mode_count, dtype=np.int32)
    columns = np.arange(cell_count, dtype=np.int32)
    phase_index = (wavenums[:, None] * columns[None, :] % cell_count).astype(np.float32)
    phases = phase_index * np.float32(2.0 * math.pi / cell_count)
    factor = np.float32(1.0 / math.sqrt(cell_count))
    forward = np.stack([np.cos(phases) * factor, -np.sin(phases) * factor])
    scaled = forward * np.where(wavenums == 0, 1.0, 2.0).astype(np.float32)[:, None]

    def ordered(table):
        split = table.reshape(2, owners, -1, cell_count).transpose(1, 0, 2, 3)
        return split.reshape(-1, cell_count).astype(ml_dtypes.bfloat16)

    return ordered(forward), ordered(scaled)


def lat_spread(row_count, modes):
    indices = np.arange(row_count, dtype=np.int32)
    phase_index = (indices[:, None] * indices[None, :] % row_count).astype(np.float32)
    phases = phase_index * np.float32(2.0 * math.pi / row_count)
    factor = np.float32(1.0 / math.sqrt(row_count))
    cosine = np.cos(phases) * factor
    sine_part = np.sin(phases) * factor
    table = np.stack([np.stack([cosine, sine_part], -1), np.stack([-sine_part, cosine], -1)])
    same = np.eye(modes, dtype=np.float32)
    spread = table[:, :, None, :, :, None] * same[None, None, :, None, None, :]
    size = 2 * row_count * modes
    return spread.reshape(size, size).astype(ml_dtypes.bfloat16)


def block_bias(bias, groups):
    return jnp.transpose(bias.reshape(2, groups, 1, -1), (1, 2, 0, 3)).reshape(groups, 1, -1)


def spread_kernel(*refs):
    half_way = len(refs) // 2
    for blocks_ref, joined_ref in zip(refs[:half_way], refs[half_way:]):
        _, per, size, _ = blocks_ref.shape
        width = per * size
        row = lax.broadcasted_iota(jnp.int32, (size, width), 0)
        lane = lax.broadcasted_iota(jnp.int32, (size, width), 1)
        for block in range(per):
            place = (row + block * size == lane).astype(jnp.bfloat16)
            real = product_of(blocks_ref[0, block], place).astype(jnp.bfloat16)
            imag = product_of(blocks_ref[1, block], place)
            upper = pl.ds(block * size, size)
            lower = pl.ds(width + block * size, size)
            joined_ref[0, upper, 0:width] = real
            joined_ref[0, upper, width : 2 * width] = imag.astype(jnp.bfloat16)
            joined_ref[0, lower, 0:width] = (-imag).astype(jnp.bfloat16)
            joined_ref[0, lower, width : 2 * width] = real


def spread_weights(groups, *weights):
    _, count, size, _ = weights[0].shape
    per = count // groups
    lanes = 2 * per * size
    shape = in_hbm((groups, lanes, lanes), jnp.bfloat16)
    return pl.pallas_call(
        spread_kernel,
        grid=(groups,),
        out_shape=(shape,) * len(weights),
        in_specs=[pl.BlockSpec((2, per, size, size), lambda g: (0, g, 0, 0))] * len(weights),
        out_specs=(group_spec(lanes, lanes),) * len(weights),
        compiler_params=params(12),
        cost_estimate=pl.CostEstimate(
            flops=len(weights) * 2 * count * size * size * lanes,
            bytes_accessed=len(weights) * 2 * groups * lanes * lanes,
            transcendentals=0,
        ),
        name="spread_weights",
    )(*weights)


def params(mebibytes):
    return pltpu.CompilerParams(
        vmem_limit_bytes=mebibytes * MIB, dimension_semantics=("arbitrary",)
    )


def place_of(me_ref, offset, rows):
    return pl.ds(pl.multiple_of((me_ref[0] ^ offset) * rows, rows), rows)


def in_hbm(shape, dtype):
    return pltpu.HBM(shape, dtype)


def hbm(*arrays):
    return [pltpu.with_memory_space_constraint(array, pltpu.HBM) for array in arrays]


def to_modes_kernel(me_ref, table_ref, cells_ref, *refs):
    modes_refs, held_ref = refs[:-1], refs[-1]
    rows = cells_ref.shape[1]
    share = modes_refs[0].shape[0] // rows
    for row in range(rows):
        spectrum = product_of(table_ref[...], cells_ref[0, row])
        held_ref[row] = spectrum.astype(jnp.bfloat16)
        for offset, modes_ref in enumerate(modes_refs):
            modes_ref[pl.ds(row * share, share)] = held_ref[row, place_of(me_ref, offset, share)]


def to_modes(me, table, cells, owners):
    samples, rows, width, channels = cells.shape
    size = table.shape[0]
    part = rows * size // owners
    return pl.pallas_call(
        to_modes_kernel,
        grid_spec=pltpu.PrefetchScalarGridSpec(
            num_scalar_prefetch=1,
            grid=(samples,),
            in_specs=[
                pl.BlockSpec((size, width), lambda b, _: (0, 0)),
                pl.BlockSpec((1, rows, width, channels), lambda b, _: (b, 0, 0, 0)),
            ],
            out_specs=(pl.BlockSpec((part, channels), lambda b, _: (b, 0)),) * owners,
            scratch_shapes=[pltpu.VMEM((rows, size, channels), jnp.bfloat16)],
        ),
        out_shape=(in_hbm((samples * part, channels), jnp.bfloat16),) * owners,
        compiler_params=params(12),
        cost_estimate=pl.CostEstimate(
            flops=2 * samples * rows * size * width * channels,
            bytes_accessed=2 * samples * rows * channels * (width + size),
            transcendentals=0,
        ),
        name="to_modes",
    )(me, table, cells)


def to_cells_kernel(me_ref, table_ref, base_ref, *refs):
    modes_refs, out_ref, held_ref = refs[:-2], refs[-2], refs[-1]
    rows = base_ref.shape[1]
    share = modes_refs[0].shape[-2] // rows
    for row in range(rows):
        run = pl.ds(row * share, share)
        if len(modes_refs) == 1:
            spectrum = modes_refs[0][:, run].reshape(held_ref.shape[1:])
        else:
            for offset, modes_ref in enumerate(modes_refs):
                held_ref[row, place_of(me_ref, offset, share)] = modes_ref[run]
            spectrum = held_ref[row]
        image = product_of(table_ref[...], spectrum)
        out_ref[0, row] = (base_ref[0, row].astype(jnp.float32) + image).astype(jnp.bfloat16)


def to_cells(me, table, modes, base):
    samples, rows, width, channels = base.shape
    size = table.shape[1]
    block = pl.BlockSpec((1, rows, width, channels), lambda b, _: (b, 0, 0, 0))
    if len(modes) == 1:
        lead = modes[0].shape[0]
        part = rows * size // lead
        specs = [pl.BlockSpec((lead, part, channels), lambda b, _: (0, b, 0))]
    else:
        part = rows * size // len(modes)
        specs = [pl.BlockSpec((part, channels), lambda b, _: (b, 0))] * len(modes)
    return pl.pallas_call(
        to_cells_kernel,
        grid_spec=pltpu.PrefetchScalarGridSpec(
            num_scalar_prefetch=1,
            grid=(samples,),
            in_specs=[pl.BlockSpec((width, size), lambda b, _: (0, 0)), block] + specs,
            out_specs=block,
            scratch_shapes=[pltpu.VMEM((rows, size, channels), jnp.bfloat16)],
        ),
        out_shape=jax.ShapeDtypeStruct(base.shape, jnp.bfloat16),
        compiler_params=params(12),
        cost_estimate=pl.CostEstimate(
            flops=2 * samples * rows * size * width * channels,
            bytes_accessed=2 * samples * rows * channels * (2 * width + size),
            transcendentals=0,
        ),
        name="to_cells",
    )(me, table, base, *hbm(*modes))


def rows_inside(cells):
    inside = jnp.transpose(cells, (0, 2, 1, 3))
    return with_layout_constraint(inside, Layout(major_to_minor=(0, 1, 2, 3)))


def rows_outside(cells):
    return jnp.transpose(cells, (0, 2, 1, 3))


def sigmoid_of(values):
    return 0.5 + 0.5 * jnp.tanh(0.5 * values)


def mix_lat(me_ref, table_ref, bands_refs, band_ref, mixed_ref):
    samples, size, width = band_ref.shape
    part, half = size // len(bands_refs), size // 2
    for sample in range(samples):
        for offset, bands_ref in enumerate(bands_refs):
            place = place_of(me_ref, offset, part)
            band_ref[sample, place] = bands_ref[pl.ds(sample * part, part)]
        mixed = product_of(table_ref[...], band_ref[sample]).astype(jnp.bfloat16)
        spot = pl.ds(sample * half, half)
        mixed_ref[spot, 0:width] = mixed[:half]
        mixed_ref[spot, width : 2 * width] = mixed[half:]


def unmix_lat(me_ref, table_ref, mixed_ref, band_ref, bands_refs):
    samples, size, width = band_ref.shape
    part, half = size // len(bands_refs), size // 2
    for sample in range(samples):
        spot = pl.ds(sample * half, half)
        joined = jnp.concatenate(
            [mixed_ref[spot, 0:width], mixed_ref[spot, width : 2 * width]], axis=0
        )
        bands = product_of(table_ref[...], joined).astype(jnp.bfloat16)
        if len(bands_refs) == 1:
            lead = bands_refs[0].shape[0]
            run = pl.ds(sample * size // lead, size // lead)
            bands_refs[0][:, run] = bands.reshape(lead, size // lead, width)
        else:
            band_ref[sample] = bands
            for offset, bands_ref in enumerate(bands_refs):
                place = place_of(me_ref, offset, part)
                bands_ref[pl.ds(sample * part, part)] = band_ref[sample, place]


def activate(mixed_ref, w1_ref, b1_ref):
    pre = product_of(mixed_ref[0], w1_ref[0]) + b1_ref[0]
    logistic = sigmoid_of(pre)
    return logistic, pre * logistic


def bend(act_ref, w2_ref, b2_ref):
    out = product_of(act_ref[...], w2_ref[0]) + b2_ref[0]
    return out, jnp.tanh(out * (1.0 / shrink_level))


def forward_kernel(blocks, me_ref, lat_ref, unlat_ref, w1_ref, b1_ref, w2_ref, b2_ref, *refs):
    bands_refs, image_refs = refs[:blocks], refs[blocks : 2 * blocks]
    mixed_ref, act_ref, band_ref = refs[2 * blocks :]
    mix_lat(me_ref, lat_ref, bands_refs, band_ref, mixed_ref.at[0])
    act_ref[...] = activate(mixed_ref, w1_ref, b1_ref)[1].astype(jnp.bfloat16)
    out, bent = bend(act_ref, w2_ref, b2_ref)
    act_ref[...] = (out - shrink_level * bent).astype(jnp.bfloat16)
    unmix_lat(me_ref, unlat_ref, act_ref, band_ref, image_refs)


def backward_kernel(
    block_size, blocks, me_ref, lat_ref, unlat_ref, w1_ref, b1_ref, w2_ref, b2_ref, mixed_ref, *refs
):
    bands_refs, image_refs = refs[:blocks], refs[blocks : 2 * blocks]
    sums_ref, act_ref, gate_ref, cot_ref, kept_ref, band_ref = refs[2 * blocks :]
    transposed = (((1,), (1,)), ((), ()))
    summed = (((0,), (0,)), ((), ()))

    def times(former, latter, dims):
        return lax.dot_general(former, latter, dims, preferred_element_type=jnp.float32)

    def weight_sums(acts, grads, slot):
        width = acts.shape[1] // 2
        full = times(acts, grads, summed)
        real = full[:width, :width] + full[width:, width:]
        imag = full[:width, width:] - full[width:, :width]
        bias = jnp.sum(grads.astype(jnp.float32), axis=0, keepdims=True)
        size = block_size
        owner = lax.broadcasted_iota(jnp.int32, (size, width), 1) // size
        extra = sums_ref.shape[2] - size
        first = lax.broadcasted_iota(jnp.int32, (extra, width), 0) == 0
        for part, values in enumerate((real, imag)):
            joined = values[:size]
            for block in range(1, width // size):
                joined = jnp.where(owner == block, values[block * size : (block + 1) * size], joined)
            sums_ref[slot, part, 0:size] = joined.astype(sums_ref.dtype)
            row = bias[:, part * width : (part + 1) * width]
            sums_ref[slot, part, size:] = jnp.where(first, row, 0.0).astype(sums_ref.dtype)

    logistic, act = activate(mixed_ref, w1_ref, b1_ref)
    act_ref[...] = act.astype(jnp.bfloat16)
    gate_ref[...] = logistic + act * (1.0 - logistic)
    mix_lat(me_ref, lat_ref, bands_refs, band_ref, cot_ref)
    _, bent = bend(act_ref, w2_ref, b2_ref)
    kept_ref[...] = (cot_ref[...].astype(jnp.float32) * (bent * bent)).astype(jnp.bfloat16)
    back = times(kept_ref[...], w2_ref[0], transposed)
    cot_ref[...] = (back * gate_ref[...]).astype(jnp.bfloat16)
    weight_sums(act_ref[...], kept_ref[...], 1)
    kept_ref[...] = times(cot_ref[...], w1_ref[0], transposed).astype(jnp.bfloat16)
    weight_sums(mixed_ref[0], cot_ref[...], 0)
    unmix_lat(me_ref, unlat_ref, kept_ref, band_ref, image_refs)


def group_spec(*shape):
    return pl.BlockSpec((1,) + shape, lambda g, *_: (g,) + (0,) * len(shape))


def bands_specs(rows, bands, groups):
    block = (rows, bands[0].shape[1] // groups)
    return (pl.BlockSpec(block, lambda g, *_: (0, g)),) * len(bands)


def images_like(bands, samples, size, groups):
    if len(bands) > 1:
        shapes = tuple(in_hbm(band.shape, band.dtype) for band in bands)
        return shapes, bands_specs(bands[0].shape[0], bands, groups)
    channels = bands[0].shape[1]
    shape = (1, samples * size, channels)
    spec = pl.BlockSpec(shape[:2] + (channels // groups,), lambda g, *_: (0, 0, g))
    return (in_hbm(shape, jnp.bfloat16),), (spec,)


def forward_mid(me, lat, unlat, bands, w1, b1, w2, b2):
    groups, lanes, _ = w1.shape
    size = lat.shape[0]
    samples = bands[0].shape[0] * len(bands) // size
    positions = samples * size // 2
    table = pl.BlockSpec((size, size), lambda g, _: (0, 0))
    state = (groups, positions, lanes)
    specs = bands_specs(bands[0].shape[0], bands, groups)
    images, image_specs = images_like(bands, samples, size, groups)
    results = pl.pallas_call(
        functools.partial(forward_kernel, len(bands)),
        grid_spec=pltpu.PrefetchScalarGridSpec(
            num_scalar_prefetch=1,
            grid=(groups,),
            in_specs=[
                table, table,
                group_spec(lanes, lanes), group_spec(1, lanes),
                group_spec(lanes, lanes), group_spec(1, lanes),
                *specs,
            ],
            out_specs=image_specs + (group_spec(positions, lanes),),
            scratch_shapes=[
                pltpu.VMEM((positions, lanes), jnp.bfloat16),
                pltpu.VMEM((samples, size, lanes // 2), jnp.bfloat16),
            ],
        ),
        out_shape=images + (in_hbm(state, jnp.bfloat16),),
        compiler_params=params(28),
        cost_estimate=pl.CostEstimate(
            flops=4 * groups * positions * lanes * lanes,
            bytes_accessed=16 * groups * positions * lanes + 4 * groups * lanes * lanes,
            transcendentals=2 * groups * positions * lanes,
        ),
        name="mix_forward",
    )(me, lat, unlat, *hbm(w1), b1, *hbm(w2), b2, *hbm(*bands))
    return results[: len(bands)], results[len(bands)]


def backward_mid(me, lat, unlat, bands, w1, b1, w2, b2, state, count):
    groups, lanes, _ = w1.shape
    size = lat.shape[0]
    samples = bands[0].shape[0] * len(bands) // size
    positions = samples * size // 2
    table = pl.BlockSpec((size, size), lambda g, _: (0, 0))
    size_of_block = lanes // 2 // (count // groups)
    sums = (2, 2, size_of_block + 32, lanes // 2)
    images, image_specs = images_like(bands, samples, size, groups)
    results = pl.pallas_call(
        functools.partial(backward_kernel, size_of_block, len(bands)),
        grid_spec=pltpu.PrefetchScalarGridSpec(
            num_scalar_prefetch=1,
            grid=(groups,),
            in_specs=[
                table, table,
                group_spec(lanes, lanes), group_spec(1, lanes),
                group_spec(lanes, lanes), group_spec(1, lanes),
                group_spec(positions, lanes),
                *bands_specs(bands[0].shape[0], bands, groups),
            ],
            out_specs=image_specs + (pl.BlockSpec(sums, lambda g, _: (0, 0, 0, g)),),
            scratch_shapes=[
                pltpu.VMEM((positions, lanes), jnp.bfloat16),
                pltpu.VMEM((positions, lanes), jnp.float32),
                pltpu.VMEM((positions, lanes), jnp.bfloat16),
                pltpu.VMEM((positions, lanes), jnp.bfloat16),
                pltpu.VMEM((samples, size, lanes // 2), jnp.bfloat16),
            ],
        ),
        out_shape=images + (in_hbm(sums[:3] + (groups * sums[3],), jnp.float32),),
        compiler_params=params(32),
        cost_estimate=pl.CostEstimate(
            flops=8 * groups * positions * lanes * lanes,
            bytes_accessed=16 * groups * positions * lanes + 4 * groups * lanes * lanes,
            transcendentals=0,
        ),
        name="mix_backward",
    )(me, lat, unlat, *hbm(w1), b1, *hbm(w2), b2, *hbm(state, *bands))
    return results[: len(bands)], results[len(bands)]


def swap_with(values, axis, distance):
    pairs = [(i, i ^ distance) for i in range(lax.axis_size(axis))]
    return lax.ppermute(values, axis, pairs)


def waiting(values, arrived):
    return lax.optimization_barrier((values, tuple(arrived)))[0]


def mixed_order(size):
    far = list(range(size // 2, size))
    near = [offset for offset in (2, 3, 1) if offset < size // 2]
    near += list(range(4, size // 2))
    order = []
    while far or near:
        order += far[:1] + near[:1]
        far, near = far[1:], near[1:]
    return order


def pick(pair, side):
    return lax.dynamic_index_in_dim(pair, side, 0, keepdims=False)


class GroupSum:
    def __init__(self, sums):
        self.lanes = sums.shape[-1]
        self.side = lax.axis_index("dp")
        self.me = lax.axis_index("space")
        self.count = lax.axis_size("space") // 2
        self.held = sums.reshape(-1, self.lanes)

    def halve(self, axis, distance, bit, arrived):
        pair = waiting(self.held, arrived).reshape(2, -1, self.lanes)
        self.held = pick(pair, bit) + swap_with(pick(pair, 1 - bit), axis, distance)

    def over_dp(self):
        self.halve("dp", 1, self.side, [])

    def over_next(self, arrived):
        self.halve("space", 1, self.me % 2, arrived)

    def scatter(self, arrived):
        shares = waiting(self.held, arrived).reshape(self.count, -1, self.lanes)
        place = self.me // 2
        total = pick(shares, place)
        for offset in range(1, self.count):
            given = pick(shares, place ^ offset).astype(jnp.bfloat16)
            total += swap_with(given, "space", 2 * offset).astype(jnp.float32)
        self.total = total.astype(jnp.bfloat16)

    def gather(self, arrived):
        total = waiting(self.total, arrived)
        taken = [total]
        for offset in range(1, self.count):
            taken.append(swap_with(total, "space", 2 * offset))
        self.quarter = jnp.stack(taken)

    def gather_next(self, arrived):
        quarter = waiting(self.quarter, arrived)
        self.half = jnp.stack([quarter, swap_with(quarter, "space", 1)])

    def gather_dp(self, arrived):
        half = waiting(self.half, arrived)
        return half, swap_with(half, "dp", 1)


def finish_kernel(factor, me_ref, half_ref, other_ref, *out_refs):
    side, near, place = me_ref[0], me_ref[1], me_ref[2]
    run = half_ref.shape[2]
    for which in range(2):
        blocks_ref, bias_ref = out_refs[2 * which : 2 * which + 2]
        edge = blocks_ref.shape[-1]
        for part in range(2):
            for piece in range(half_ref.shape[1]):
                spot = (part ^ near, piece ^ place)
                own = half_ref[spot].astype(jnp.float32)
                value = jnp.where(side == which, own, other_ref[spot].astype(jnp.float32)) * factor
                first = piece * run
                count = max(0, min(edge - first, run))
                for block in range(blocks_ref.shape[1]):
                    lanes = slice(block * edge, (block + 1) * edge)
                    if count > 0:
                        blocks_ref[part, block, pl.ds(first, count)] = value[:count, lanes]
                    if first <= edge < first + run:
                        row = edge - first
                        bias_ref[part, pl.ds(block, 1)] = value[row : row + 1, lanes]


def finish_sums(here, half, other, factor, weight_shape, bias_shape):
    outs = [weight_shape, bias_shape] * 2
    return pl.pallas_call(
        functools.partial(finish_kernel, factor),
        out_shape=[jax.ShapeDtypeStruct(shape, jnp.float32) for shape in outs],
        in_specs=[pl.BlockSpec(memory_space=pltpu.SMEM)]
        + [pl.BlockSpec(memory_space=pltpu.VMEM)] * 2,
        out_specs=[pl.BlockSpec(memory_space=pltpu.VMEM)] * 4,
        compiler_params=pltpu.CompilerParams(vmem_limit_bytes=16 * MIB),
        cost_estimate=pl.CostEstimate(flops=0, bytes_accessed=4 * MIB, transcendentals=0),
        name="finish_sums",
    )(here, half, other)


def body(fields, cotangent, w_first, b_first, w_second, b_second):
    samples, rows, width, channels = fields.shape
    owners = lax.axis_size("space")
    lat_total = rows * owners
    modes = KW // owners
    count, edge = w_first.shape[1:3]
    groups = 2
    direct = 2 * modes % 16 == 0
    lead = owners if direct else 1

    order = mixed_order(owners)

    def send(blocks, offsets, taken):
        for offset in offsets:
            taken[offset] = swap_with(blocks[offset], "space", offset)

    def send_all(spectrum):
        spectrum = spectrum.reshape(samples, rows, owners, 2 * modes, channels)
        spectrum = jnp.transpose(spectrum, (2, 0, 1, 3, 4))
        arrived = lax.all_to_all(spectrum, "space", split_axis=0, concat_axis=0, tiled=True)
        return [jnp.transpose(arrived, (1, 0, 2, 3, 4)).reshape(-1, channels)]

    def send_all_back(bands):
        bands = bands.reshape(samples, owners, rows, 2 * modes, channels)
        bands = jnp.transpose(bands, (1, 0, 2, 3, 4))
        arrived = lax.all_to_all(bands, "space", split_axis=0, concat_axis=0, tiled=True)
        return [jnp.transpose(arrived, (1, 2, 0, 3, 4)).reshape(1, -1, channels)]

    me = lax.axis_index("space") if direct else 0
    me = jnp.full((1,), me, jnp.int32)
    plain, scaled = lon_tables(KW, width, owners)
    lat = lat_spread(lat_total, modes)

    spectrum = to_modes(me, plain, fields, lead)
    spectrum, cotangent, w_first, w_second = lax.optimization_barrier(
        (spectrum, cotangent, w_first, w_second)
    )
    cot_spec = to_modes(me, scaled, cotangent, lead)
    w1, w2 = spread_weights(groups, w_first, w_second)
    b1, b2 = block_bias(b_first, groups), block_bias(b_second, groups)
    positions = samples * lax.axis_size("dp") * lat_total * KW
    factor = 1.0 / math.sqrt(positions)

    if not direct:
        gathered = send_all(spectrum[0])
        image, state = forward_mid(me, lat, lat.T, gathered, w1, b1, w2, b2)
        image_band = send_all_back(image[0])
        gathered = send_all(cot_spec[0])
        grad_image, sums = backward_mid(me, lat, lat.T, gathered, w1, b1, w2, b2, state, count)
        grad_band = send_all_back(grad_image[0])
        output = to_cells(me, scaled.T, image_band, fields)
        grad_fields = to_cells(me, plain.T, grad_band, cotangent)
        sums = lax.psum(sums, ("space", "dp")) * factor
        grads = []
        for which in range(2):
            blocks = sums[which, :, :edge].reshape(2, edge, count, edge)
            grads.append(jnp.transpose(blocks, (0, 2, 1, 3)))
            grads.append(sums[which, :, edge].reshape(b_first.shape))
        return (output, grad_fields) + tuple(grads)

    gathered, cot_gathered = {0: spectrum[0]}, {0: cot_spec[0]}
    send(spectrum, order, gathered)
    gathered = [gathered[offset] for offset in range(owners)]
    image, state = forward_mid(me, lat, lat.T, gathered, w1, b1, w2, b2)
    cot_spec, image = list(cot_spec), list(image)
    send(cot_spec, order[:FIRST], cot_gathered)
    cot_spec, image = waiting((cot_spec, image), [image[0]])
    send(cot_spec, order[FIRST:], cot_gathered)

    image_band = {0: image[0]}
    send(image, order, image_band)
    cot_gathered = [cot_gathered[offset] for offset in range(owners)]
    grad_image, sums = backward_mid(
        me, lat, lat.T, cot_gathered, w1, b1, w2, b2, state, count
    )
    early = [image_band[offset] for offset in order[:HELD]]
    late = [image_band[offset] for offset in order[HELD:]]
    grad_image, sums = waiting((list(grad_image), sums), early)
    group_sum = GroupSum(sums)
    group_sum.over_dp()
    group_sum.over_next(late[:1])
    grad_band = {0: grad_image[0]}
    send(grad_image, order, grad_band)
    arrived = [grad_band[offset] for offset in order]
    image_band = [image_band[offset] for offset in range(owners)]
    grad_band = [grad_band[offset] for offset in range(owners)]
    again = waiting(fields, early[:1])
    output = rows_inside(to_cells(me, scaled.T, image_band, again))
    group_sum.scatter(late[1:] + arrived[:1])
    group_sum.gather(arrived[1:3])
    group_sum.quarter, output = lax.optimization_barrier((group_sum.quarter, output))
    group_sum.gather_next(arrived[3:6])
    half, other = group_sum.gather_dp(arrived[6:])
    grad_fields = rows_inside(to_cells(me, plain.T, grad_band, cotangent))
    place = lax.axis_index("space")
    here = jnp.stack([lax.axis_index("dp"), place % 2, place // 2]).astype(jnp.int32)
    grads = finish_sums(
        here, half, other, factor, w_first.shape, b_first.shape
    )
    return (rows_outside(output), rows_outside(grad_fields)) + tuple(grads)


def solution(mesh):
    split = P(("parts", "dp"), "space", None, None)
    in_specs = (split, split, P(), P(), P(), P())
    out_specs = (
        split,
        split,
        P("parts", None, None, None),
        P("parts", None, None),
        P("parts", None, None, None),
        P("parts", None, None),
    )
    return jax.shard_map(body, mesh=mesh, in_specs=in_specs, out_specs=out_specs, check_vma=False)
```

```python
import functools
import math

import jax
import jax.numpy as jnp
from jax import lax
from jax.experimental import pallas as pl
from jax.experimental.layout import Layout, with_layout_constraint
from jax.experimental.pallas import tpu as pltpu
from jax.sharding import PartitionSpec as P
import ml_dtypes
import numpy as np

KW = 64
shrink_level = 0.05
FIRST = 4
HELD = 3
MIB = 1024 * 1024


def product_of(former, latter):
    return jnp.dot(former, latter, preferred_element_type=jnp.float32)


def lon_tables(mode_count, cell_count, owners):
    wavenums = np.arange(mode_count, dtype=np.int32)
    columns = np.arange(cell_count, dtype=np.int32)
    phase_index = (wavenums[:, None] * columns[None, :] % cell_count).astype(np.float32)
    phases = phase_index * np.float32(2.0 * math.pi / cell_count)
    factor = np.float32(1.0 / math.sqrt(cell_count))
    forward = np.stack([np.cos(phases) * factor, -np.sin(phases) * factor])
    scaled = forward * np.where(wavenums == 0, 1.0, 2.0).astype(np.float32)[:, None]

    def ordered(table):
        split = table.reshape(2, owners, -1, cell_count).transpose(1, 0, 2, 3)
        return split.reshape(-1, cell_count).astype(ml_dtypes.bfloat16)

    return ordered(forward), ordered(scaled)


def lat_spread(row_count, modes):
    indices = np.arange(row_count, dtype=np.int32)
    phase_index = (indices[:, None] * indices[None, :] % row_count).astype(np.float32)
    phases = phase_index * np.float32(2.0 * math.pi / row_count)
    factor = np.float32(1.0 / math.sqrt(row_count))
    cosine = np.cos(phases) * factor
    sine_part = np.sin(phases) * factor
    table = np.stack([np.stack([cosine, sine_part], -1), np.stack([-sine_part, cosine], -1)])
    same = np.eye(modes, dtype=np.float32)
    spread = table[:, :, None, :, :, None] * same[None, None, :, None, None, :]
    size = 2 * row_count * modes
    return spread.reshape(size, size).astype(ml_dtypes.bfloat16)


def block_bias(bias, groups):
    return jnp.transpose(bias.reshape(2, groups, 1, -1), (1, 2, 0, 3)).reshape(groups, 1, -1)


def spread_kernel(*refs):
    half_way = len(refs) // 2
    for blocks_ref, joined_ref in zip(refs[:half_way], refs[half_way:]):
        _, per, size, _ = blocks_ref.shape
        width = per * size
        row = lax.broadcasted_iota(jnp.int32, (size, width), 0)
        lane = lax.broadcasted_iota(jnp.int32, (size, width), 1)
        for block in range(per):
            place = (row + block * size == lane).astype(jnp.bfloat16)
            real = product_of(blocks_ref[0, block], place).astype(jnp.bfloat16)
            imag = product_of(blocks_ref[1, block], place)
            upper = pl.ds(block * size, size)
            lower = pl.ds(width + block * size, size)
            joined_ref[0, upper, 0:width] = real
            joined_ref[0, upper, width : 2 * width] = imag.astype(jnp.bfloat16)
            joined_ref[0, lower, 0:width] = (-imag).astype(jnp.bfloat16)
            joined_ref[0, lower, width : 2 * width] = real


def spread_weights(groups, *weights):
    _, count, size, _ = weights[0].shape
    per = count // groups
    lanes = 2 * per * size
    shape = in_hbm((groups, lanes, lanes), jnp.bfloat16)
    return pl.pallas_call(
        spread_kernel,
        grid=(groups,),
        out_shape=(shape,) * len(weights),
        in_specs=[pl.BlockSpec((2, per, size, size), lambda g: (0, g, 0, 0))] * len(weights),
        out_specs=(group_spec(lanes, lanes),) * len(weights),
        compiler_params=params(12),
        cost_estimate=pl.CostEstimate(
            flops=len(weights) * 2 * count * size * size * lanes,
            bytes_accessed=len(weights) * 2 * groups * lanes * lanes,
            transcendentals=0,
        ),
        name="spread_weights",
    )(*weights)


def params(mebibytes):
    return pltpu.CompilerParams(
        vmem_limit_bytes=mebibytes * MIB, dimension_semantics=("arbitrary",)
    )


def place_of(me_ref, offset, rows):
    return pl.ds(pl.multiple_of((me_ref[0] ^ offset) * rows, rows), rows)


def in_hbm(shape, dtype):
    return pltpu.HBM(shape, dtype)


def hbm(*arrays):
    return [pltpu.with_memory_space_constraint(array, pltpu.HBM) for array in arrays]


def to_modes_kernel(me_ref, table_ref, cells_ref, *refs):
    modes_refs, held_ref = refs[:-1], refs[-1]
    rows = cells_ref.shape[1]
    share = modes_refs[0].shape[0] // rows
    for row in range(rows):
        spectrum = product_of(table_ref[...], cells_ref[0, row])
        held_ref[row] = spectrum.astype(jnp.bfloat16)
        for offset, modes_ref in enumerate(modes_refs):
            modes_ref[pl.ds(row * share, share)] = held_ref[row, place_of(me_ref, offset, share)]


def to_modes(me, table, cells, owners):
    samples, rows, width, channels = cells.shape
    size = table.shape[0]
    part = rows * size // owners
    return pl.pallas_call(
        to_modes_kernel,
        grid_spec=pltpu.PrefetchScalarGridSpec(
            num_scalar_prefetch=1,
            grid=(samples,),
            in_specs=[
                pl.BlockSpec((size, width), lambda b, _: (0, 0)),
                pl.BlockSpec((1, rows, width, channels), lambda b, _: (b, 0, 0, 0)),
            ],
            out_specs=(pl.BlockSpec((part, channels), lambda b, _: (b, 0)),) * owners,
            scratch_shapes=[pltpu.VMEM((rows, size, channels), jnp.bfloat16)],
        ),
        out_shape=(in_hbm((samples * part, channels), jnp.bfloat16),) * owners,
        compiler_params=params(12),
        cost_estimate=pl.CostEstimate(
            flops=2 * samples * rows * size * width * channels,
            bytes_accessed=2 * samples * rows * channels * (width + size),
            transcendentals=0,
        ),
        name="to_modes",
    )(me, table, cells)


def to_cells_kernel(me_ref, table_ref, base_ref, *refs):
    modes_refs, out_ref, held_ref = refs[:-2], refs[-2], refs[-1]
    rows = base_ref.shape[1]
    share = modes_refs[0].shape[-2] // rows
    for row in range(rows):
        run = pl.ds(row * share, share)
        if len(modes_refs) == 1:
            spectrum = modes_refs[0][:, run].reshape(held_ref.shape[1:])
        else:
            for offset, modes_ref in enumerate(modes_refs):
                held_ref[row, place_of(me_ref, offset, share)] = modes_ref[run]
            spectrum = held_ref[row]
        image = product_of(table_ref[...], spectrum)
        out_ref[0, row] = (base_ref[0, row].astype(jnp.float32) + image).astype(jnp.bfloat16)


def to_cells(me, table, modes, base):
    samples, rows, width, channels = base.shape
    size = table.shape[1]
    block = pl.BlockSpec((1, rows, width, channels), lambda b, _: (b, 0, 0, 0))
    if len(modes) == 1:
        lead = modes[0].shape[0]
        part = rows * size // lead
        specs = [pl.BlockSpec((lead, part, channels), lambda b, _: (0, b, 0))]
    else:
        part = rows * size // len(modes)
        specs = [pl.BlockSpec((part, channels), lambda b, _: (b, 0))] * len(modes)
    return pl.pallas_call(
        to_cells_kernel,
        grid_spec=pltpu.PrefetchScalarGridSpec(
            num_scalar_prefetch=1,
            grid=(samples,),
            in_specs=[pl.BlockSpec((width, size), lambda b, _: (0, 0)), block] + specs,
            out_specs=block,
            scratch_shapes=[pltpu.VMEM((rows, size, channels), jnp.bfloat16)],
        ),
        out_shape=jax.ShapeDtypeStruct(base.shape, jnp.bfloat16),
        compiler_params=params(12),
        cost_estimate=pl.CostEstimate(
            flops=2 * samples * rows * size * width * channels,
            bytes_accessed=2 * samples * rows * channels * (2 * width + size),
            transcendentals=0,
        ),
        name="to_cells",
    )(me, table, base, *hbm(*modes))


def rows_inside(cells):
    inside = jnp.transpose(cells, (0, 2, 1, 3))
    return with_layout_constraint(inside, Layout(major_to_minor=(0, 1, 2, 3)))


def rows_outside(cells):
    return jnp.transpose(cells, (0, 2, 1, 3))


def sigmoid_of(values):
    return 0.5 + 0.5 * jnp.tanh(0.5 * values)


def mix_lat(me_ref, table_ref, bands_refs, band_ref, mixed_ref):
    samples, size, width = band_ref.shape
    part, half = size // len(bands_refs), size // 2
    for sample in range(samples):
        for offset, bands_ref in enumerate(bands_refs):
            place = place_of(me_ref, offset, part)
            band_ref[sample, place] = bands_ref[pl.ds(sample * part, part)]
        mixed = product_of(table_ref[...], band_ref[sample]).astype(jnp.bfloat16)
        spot = pl.ds(sample * half, half)
        mixed_ref[spot, 0:width] = mixed[:half]
        mixed_ref[spot, width : 2 * width] = mixed[half:]


def unmix_lat(me_ref, table_ref, mixed_ref, band_ref, bands_refs):
    samples, size, width = band_ref.shape
    part, half = size // len(bands_refs), size // 2
    for sample in range(samples):
        spot = pl.ds(sample * half, half)
        joined = jnp.concatenate(
            [mixed_ref[spot, 0:width], mixed_ref[spot, width : 2 * width]], axis=0
        )
        bands = product_of(table_ref[...], joined).astype(jnp.bfloat16)
        if len(bands_refs) == 1:
            lead = bands_refs[0].shape[0]
            run = pl.ds(sample * size // lead, size // lead)
            bands_refs[0][:, run] = bands.reshape(lead, size // lead, width)
        else:
            band_ref[sample] = bands
            for offset, bands_ref in enumerate(bands_refs):
                place = place_of(me_ref, offset, part)
                bands_ref[pl.ds(sample * part, part)] = band_ref[sample, place]


def activate(mixed_ref, w1_ref, b1_ref):
    pre = product_of(mixed_ref[0], w1_ref[0]) + b1_ref[0]
    logistic = sigmoid_of(pre)
    return logistic, pre * logistic


def bend(act_ref, w2_ref, b2_ref):
    out = product_of(act_ref[...], w2_ref[0]) + b2_ref[0]
    return out, jnp.tanh(out * (1.0 / shrink_level))


def forward_kernel(blocks, me_ref, lat_ref, unlat_ref, w1_ref, b1_ref, w2_ref, b2_ref, *refs):
    bands_refs, image_refs = refs[:blocks], refs[blocks : 2 * blocks]
    mixed_ref, act_ref, band_ref = refs[2 * blocks :]
    mix_lat(me_ref, lat_ref, bands_refs, band_ref, mixed_ref.at[0])
    act_ref[...] = activate(mixed_ref, w1_ref, b1_ref)[1].astype(jnp.bfloat16)
    out, bent = bend(act_ref, w2_ref, b2_ref)
    act_ref[...] = (out - shrink_level * bent).astype(jnp.bfloat16)
    unmix_lat(me_ref, unlat_ref, act_ref, band_ref, image_refs)


def backward_kernel(
    block_size, blocks, me_ref, lat_ref, unlat_ref, w1_ref, b1_ref, w2_ref, b2_ref, mixed_ref, *refs
):
    bands_refs, image_refs = refs[:blocks], refs[blocks : 2 * blocks]
    sums_ref, act_ref, gate_ref, cot_ref, kept_ref, band_ref = refs[2 * blocks :]
    transposed = (((1,), (1,)), ((), ()))
    summed = (((0,), (0,)), ((), ()))

    def times(former, latter, dims):
        return lax.dot_general(former, latter, dims, preferred_element_type=jnp.float32)

    def weight_sums(acts, grads, slot):
        width = acts.shape[1] // 2
        full = times(acts, grads, summed)
        real = full[:width, :width] + full[width:, width:]
        imag = full[:width, width:] - full[width:, :width]
        bias = jnp.sum(grads.astype(jnp.float32), axis=0, keepdims=True)
        size = block_size
        owner = lax.broadcasted_iota(jnp.int32, (size, width), 1) // size
        extra = sums_ref.shape[2] - size
        first = lax.broadcasted_iota(jnp.int32, (extra, width), 0) == 0
        for part, values in enumerate((real, imag)):
            joined = values[:size]
            for block in range(1, width // size):
                joined = jnp.where(owner == block, values[block * size : (block + 1) * size], joined)
            sums_ref[slot, part, 0:size] = joined.astype(sums_ref.dtype)
            row = bias[:, part * width : (part + 1) * width]
            sums_ref[slot, part, size:] = jnp.where(first, row, 0.0).astype(sums_ref.dtype)

    logistic, act = activate(mixed_ref, w1_ref, b1_ref)
    act_ref[...] = act.astype(jnp.bfloat16)
    gate_ref[...] = logistic + act * (1.0 - logistic)
    mix_lat(me_ref, lat_ref, bands_refs, band_ref, cot_ref)
    _, bent = bend(act_ref, w2_ref, b2_ref)
    kept_ref[...] = (cot_ref[...].astype(jnp.float32) * (bent * bent)).astype(jnp.bfloat16)
    back = times(kept_ref[...], w2_ref[0], transposed)
    cot_ref[...] = (back * gate_ref[...]).astype(jnp.bfloat16)
    weight_sums(act_ref[...], kept_ref[...], 1)
    kept_ref[...] = times(cot_ref[...], w1_ref[0], transposed).astype(jnp.bfloat16)
    weight_sums(mixed_ref[0], cot_ref[...], 0)
    unmix_lat(me_ref, unlat_ref, kept_ref, band_ref, image_refs)


def group_spec(*shape):
    return pl.BlockSpec((1,) + shape, lambda g, *_: (g,) + (0,) * len(shape))


def bands_specs(rows, bands, groups):
    block = (rows, bands[0].shape[1] // groups)
    return (pl.BlockSpec(block, lambda g, *_: (0, g)),) * len(bands)


def images_like(bands, samples, size, groups):
    if len(bands) > 1:
        shapes = tuple(in_hbm(band.shape, band.dtype) for band in bands)
        return shapes, bands_specs(bands[0].shape[0], bands, groups)
    channels = bands[0].shape[1]
    shape = (1, samples * size, channels)
    spec = pl.BlockSpec(shape[:2] + (channels // groups,), lambda g, *_: (0, 0, g))
    return (in_hbm(shape, jnp.bfloat16),), (spec,)


def forward_mid(me, lat, unlat, bands, w1, b1, w2, b2):
    groups, lanes, _ = w1.shape
    size = lat.shape[0]
    samples = bands[0].shape[0] * len(bands) // size
    positions = samples * size // 2
    table = pl.BlockSpec((size, size), lambda g, _: (0, 0))
    state = (groups, positions, lanes)
    specs = bands_specs(bands[0].shape[0], bands, groups)
    images, image_specs = images_like(bands, samples, size, groups)
    results = pl.pallas_call(
        functools.partial(forward_kernel, len(bands)),
        grid_spec=pltpu.PrefetchScalarGridSpec(
            num_scalar_prefetch=1,
            grid=(groups,),
            in_specs=[
                table, table,
                group_spec(lanes, lanes), group_spec(1, lanes),
                group_spec(lanes, lanes), group_spec(1, lanes),
                *specs,
            ],
            out_specs=image_specs + (group_spec(positions, lanes),),
            scratch_shapes=[
                pltpu.VMEM((positions, lanes), jnp.bfloat16),
                pltpu.VMEM((samples, size, lanes // 2), jnp.bfloat16),
            ],
        ),
        out_shape=images + (in_hbm(state, jnp.bfloat16),),
        compiler_params=params(28),
        cost_estimate=pl.CostEstimate(
            flops=4 * groups * positions * lanes * lanes,
            bytes_accessed=16 * groups * positions * lanes + 4 * groups * lanes * lanes,
            transcendentals=2 * groups * positions * lanes,
        ),
        name="mix_forward",
    )(me, lat, unlat, *hbm(w1), b1, *hbm(w2), b2, *hbm(*bands))
    return results[: len(bands)], results[len(bands)]


def backward_mid(me, lat, unlat, bands, w1, b1, w2, b2, state, count):
    groups, lanes, _ = w1.shape
    size = lat.shape[0]
    samples = bands[0].shape[0] * len(bands) // size
    positions = samples * size // 2
    table = pl.BlockSpec((size, size), lambda g, _: (0, 0))
    size_of_block = lanes // 2 // (count // groups)
    sums = (2, 2, size_of_block + 32, lanes // 2)
    images, image_specs = images_like(bands, samples, size, groups)
    results = pl.pallas_call(
        functools.partial(backward_kernel, size_of_block, len(bands)),
        grid_spec=pltpu.PrefetchScalarGridSpec(
            num_scalar_prefetch=1,
            grid=(groups,),
            in_specs=[
                table, table,
                group_spec(lanes, lanes), group_spec(1, lanes),
                group_spec(lanes, lanes), group_spec(1, lanes),
                group_spec(positions, lanes),
                *bands_specs(bands[0].shape[0], bands, groups),
            ],
            out_specs=image_specs + (pl.BlockSpec(sums, lambda g, _: (0, 0, 0, g)),),
            scratch_shapes=[
                pltpu.VMEM((positions, lanes), jnp.bfloat16),
                pltpu.VMEM((positions, lanes), jnp.float32),
                pltpu.VMEM((positions, lanes), jnp.bfloat16),
                pltpu.VMEM((positions, lanes), jnp.bfloat16),
                pltpu.VMEM((samples, size, lanes // 2), jnp.bfloat16),
            ],
        ),
        out_shape=images + (in_hbm(sums[:3] + (groups * sums[3],), jnp.float32),),
        compiler_params=params(32),
        cost_estimate=pl.CostEstimate(
            flops=8 * groups * positions * lanes * lanes,
            bytes_accessed=16 * groups * positions * lanes + 4 * groups * lanes * lanes,
            transcendentals=0,
        ),
        name="mix_backward",
    )(me, lat, unlat, *hbm(w1), b1, *hbm(w2), b2, *hbm(state, *bands))
    return results[: len(bands)], results[len(bands)]


def swap_with(values, axis, distance):
    pairs = [(i, i ^ distance) for i in range(lax.axis_size(axis))]
    return lax.ppermute(values, axis, pairs)


def waiting(values, arrived):
    return lax.optimization_barrier((values, tuple(arrived)))[0]


def mixed_order(size):
    far = list(range(size // 2, size))
    near = [offset for offset in (2, 3, 1) if offset < size // 2]
    near += list(range(4, size // 2))
    order = []
    while far or near:
        order += far[:1] + near[:1]
        far, near = far[1:], near[1:]
    return order


def pick(pair, side):
    return lax.dynamic_index_in_dim(pair, side, 0, keepdims=False)


class GroupSum:
    def __init__(self, sums):
        self.lanes = sums.shape[-1]
        self.side = lax.axis_index("dp")
        self.me = lax.axis_index("space")
        self.count = lax.axis_size("space") // 2
        self.held = sums.reshape(-1, self.lanes)

    def halve(self, axis, distance, bit, kind, arrived):
        pair = waiting(self.held, arrived).reshape(2, -1, self.lanes)
        taken = swap_with(pick(pair, 1 - bit).astype(kind), axis, distance)
        self.held = pick(pair, bit) + taken.astype(jnp.float32)

    def over_dp(self):
        self.halve("dp", 1, self.side, jnp.float32, [])

    def over_next(self, arrived):
        self.halve("space", 1, self.me % 2, jnp.bfloat16, arrived)

    def scatter(self, arrived):
        shares = waiting(self.held, arrived).reshape(self.count, -1, self.lanes)
        place = self.me // 2
        total = pick(shares, place)
        for offset in range(1, self.count):
            given = pick(shares, place ^ offset).astype(jnp.bfloat16)
            total += swap_with(given, "space", 2 * offset).astype(jnp.float32)
        self.total = total.astype(jnp.bfloat16)

    def gather(self, arrived):
        total = waiting(self.total, arrived)
        taken = [total]
        for offset in range(1, self.count):
            taken.append(swap_with(total, "space", 2 * offset))
        self.quarter = jnp.stack(taken)

    def gather_next(self, arrived):
        quarter = waiting(self.quarter, arrived)
        self.half = jnp.stack([quarter, swap_with(quarter, "space", 1)])

    def gather_dp(self, arrived):
        half = waiting(self.half, arrived)
        return half, swap_with(half, "dp", 1)


def finish_kernel(factor, me_ref, half_ref, other_ref, *out_refs):
    side, near, place = me_ref[0], me_ref[1], me_ref[2]
    run = half_ref.shape[2]
    for which in range(2):
        blocks_ref, bias_ref = out_refs[2 * which : 2 * which + 2]
        edge = blocks_ref.shape[-1]
        for part in range(2):
            for piece in range(half_ref.shape[1]):
                spot = (part ^ near, piece ^ place)
                own = half_ref[spot].astype(jnp.float32)
                value = jnp.where(side == which, own, other_ref[spot].astype(jnp.float32)) * factor
                first = piece * run
                count = max(0, min(edge - first, run))
                for block in range(blocks_ref.shape[1]):
                    lanes = slice(block * edge, (block + 1) * edge)
                    if count > 0:
                        blocks_ref[part, block, pl.ds(first, count)] = value[:count, lanes]
                    if first <= edge < first + run:
                        row = edge - first
                        bias_ref[part, pl.ds(block, 1)] = value[row : row + 1, lanes]


def finish_sums(here, half, other, factor, weight_shape, bias_shape):
    outs = [weight_shape, bias_shape] * 2
    return pl.pallas_call(
        functools.partial(finish_kernel, factor),
        out_shape=[jax.ShapeDtypeStruct(shape, jnp.float32) for shape in outs],
        in_specs=[pl.BlockSpec(memory_space=pltpu.SMEM)]
        + [pl.BlockSpec(memory_space=pltpu.VMEM)] * 2,
        out_specs=[pl.BlockSpec(memory_space=pltpu.VMEM)] * 4,
        compiler_params=pltpu.CompilerParams(vmem_limit_bytes=16 * MIB),
        cost_estimate=pl.CostEstimate(flops=0, bytes_accessed=4 * MIB, transcendentals=0),
        name="finish_sums",
    )(here, half, other)


def body(fields, cotangent, w_first, b_first, w_second, b_second):
    samples, rows, width, channels = fields.shape
    owners = lax.axis_size("space")
    lat_total = rows * owners
    modes = KW // owners
    count, edge = w_first.shape[1:3]
    groups = 2
    direct = 2 * modes % 16 == 0
    lead = owners if direct else 1

    order = mixed_order(owners)

    def send(blocks, offsets, taken):
        for offset in offsets:
            taken[offset] = swap_with(blocks[offset], "space", offset)

    def send_all(spectrum):
        spectrum = spectrum.reshape(samples, rows, owners, 2 * modes, channels)
        spectrum = jnp.transpose(spectrum, (2, 0, 1, 3, 4))
        arrived = lax.all_to_all(spectrum, "space", split_axis=0, concat_axis=0, tiled=True)
        return [jnp.transpose(arrived, (1, 0, 2, 3, 4)).reshape(-1, channels)]

    def send_all_back(bands):
        bands = bands.reshape(samples, owners, rows, 2 * modes, channels)
        bands = jnp.transpose(bands, (1, 0, 2, 3, 4))
        arrived = lax.all_to_all(bands, "space", split_axis=0, concat_axis=0, tiled=True)
        return [jnp.transpose(arrived, (1, 2, 0, 3, 4)).reshape(1, -1, channels)]

    me = lax.axis_index("space") if direct else 0
    me = jnp.full((1,), me, jnp.int32)
    plain, scaled = lon_tables(KW, width, owners)
    lat = lat_spread(lat_total, modes)

    spectrum = to_modes(me, plain, fields, lead)
    spectrum, cotangent, w_first, w_second = lax.optimization_barrier(
        (spectrum, cotangent, w_first, w_second)
    )
    cot_spec = to_modes(me, scaled, cotangent, lead)
    w1, w2 = spread_weights(groups, w_first, w_second)
    b1, b2 = block_bias(b_first, groups), block_bias(b_second, groups)
    positions = samples * lax.axis_size("dp") * lat_total * KW
    factor = 1.0 / math.sqrt(positions)

    if not direct:
        gathered = send_all(spectrum[0])
        image, state = forward_mid(me, lat, lat.T, gathered, w1, b1, w2, b2)
        image_band = send_all_back(image[0])
        gathered = send_all(cot_spec[0])
        grad_image, sums = backward_mid(me, lat, lat.T, gathered, w1, b1, w2, b2, state, count)
        grad_band = send_all_back(grad_image[0])
        output = to_cells(me, scaled.T, image_band, fields)
        grad_fields = to_cells(me, plain.T, grad_band, cotangent)
        sums = lax.psum(sums, ("space", "dp")) * factor
        grads = []
        for which in range(2):
            blocks = sums[which, :, :edge].reshape(2, edge, count, edge)
            grads.append(jnp.transpose(blocks, (0, 2, 1, 3)))
            grads.append(sums[which, :, edge].reshape(b_first.shape))
        return (output, grad_fields) + tuple(grads)

    gathered, cot_gathered = {0: spectrum[0]}, {0: cot_spec[0]}
    send(spectrum, order, gathered)
    gathered = [gathered[offset] for offset in range(owners)]
    image, state = forward_mid(me, lat, lat.T, gathered, w1, b1, w2, b2)
    cot_spec, image = list(cot_spec), list(image)
    send(cot_spec, order[:FIRST], cot_gathered)
    cot_spec, image = waiting((cot_spec, image), [image[0]])
    send(cot_spec, order[FIRST:], cot_gathered)

    image_band = {0: image[0]}
    send(image, order, image_band)
    cot_gathered = [cot_gathered[offset] for offset in range(owners)]
    grad_image, sums = backward_mid(
        me, lat, lat.T, cot_gathered, w1, b1, w2, b2, state, count
    )
    early = [image_band[offset] for offset in order[:HELD]]
    late = [image_band[offset] for offset in order[HELD:]]
    grad_image, sums = waiting((list(grad_image), sums), early)
    group_sum = GroupSum(sums)
    group_sum.over_dp()
    group_sum.over_next(late[:2])
    grad_band = {0: grad_image[0]}
    send(grad_image, order, grad_band)
    arrived = [grad_band[offset] for offset in order]
    image_band = [image_band[offset] for offset in range(owners)]
    grad_band = [grad_band[offset] for offset in range(owners)]
    again = waiting(fields, early[:1])
    output = rows_inside(to_cells(me, scaled.T, image_band, again))
    group_sum.scatter(late[2:])
    group_sum.gather(arrived[:2])
    group_sum.quarter, output = lax.optimization_barrier((group_sum.quarter, output))
    group_sum.gather_next(arrived[2:4])
    half, other = group_sum.gather_dp(arrived[4:])
    grad_fields = rows_inside(to_cells(me, plain.T, grad_band, cotangent))
    place = lax.axis_index("space")
    here = jnp.stack([lax.axis_index("dp"), place % 2, place // 2]).astype(jnp.int32)
    grads = finish_sums(
        here, half, other, factor, w_first.shape, b_first.shape
    )
    return (rows_outside(output), rows_outside(grad_fields)) + tuple(grads)


def solution(mesh):
    split = P(("parts", "dp"), "space", None, None)
    in_specs = (split, split, P(), P(), P(), P())
    out_specs = (
        split,
        split,
        P("parts", None, None, None),
        P("parts", None, None),
        P("parts", None, None, None),
        P("parts", None, None),
    )
    return jax.shard_map(body, mesh=mesh, in_specs=in_specs, out_specs=out_specs, check_vma=False)
```

```python
import functools
import math

import jax
import jax.numpy as jnp
from jax import lax
from jax.experimental import pallas as pl
from jax.experimental.layout import Layout, with_layout_constraint
from jax.experimental.pallas import tpu as pltpu
from jax.sharding import PartitionSpec as P
import ml_dtypes
import numpy as np

KW = 64
shrink_level = 0.05
FIRST = 5
HELD = 3
MIB = 1024 * 1024


def product_of(former, latter):
    return jnp.dot(former, latter, preferred_element_type=jnp.float32)


def lon_tables(mode_count, cell_count, owners):
    wavenums = np.arange(mode_count, dtype=np.int32)
    columns = np.arange(cell_count, dtype=np.int32)
    phase_index = (wavenums[:, None] * columns[None, :] % cell_count).astype(np.float32)
    phases = phase_index * np.float32(2.0 * math.pi / cell_count)
    factor = np.float32(1.0 / math.sqrt(cell_count))
    forward = np.stack([np.cos(phases) * factor, -np.sin(phases) * factor])
    scaled = forward * np.where(wavenums == 0, 1.0, 2.0).astype(np.float32)[:, None]

    def ordered(table):
        split = table.reshape(2, owners, -1, cell_count).transpose(1, 0, 2, 3)
        return split.reshape(-1, cell_count).astype(ml_dtypes.bfloat16)

    return ordered(forward), ordered(scaled)


def lat_spread(row_count, modes):
    indices = np.arange(row_count, dtype=np.int32)
    phase_index = (indices[:, None] * indices[None, :] % row_count).astype(np.float32)
    phases = phase_index * np.float32(2.0 * math.pi / row_count)
    factor = np.float32(1.0 / math.sqrt(row_count))
    cosine = np.cos(phases) * factor
    sine_part = np.sin(phases) * factor
    table = np.stack([np.stack([cosine, sine_part], -1), np.stack([-sine_part, cosine], -1)])
    same = np.eye(modes, dtype=np.float32)
    spread = table[:, :, None, :, :, None] * same[None, None, :, None, None, :]
    size = 2 * row_count * modes
    return spread.reshape(size, size).astype(ml_dtypes.bfloat16)


def block_bias(bias, groups):
    return jnp.transpose(bias.reshape(2, groups, 1, -1), (1, 2, 0, 3)).reshape(groups, 1, -1)


def spread_kernel(*refs):
    half_way = len(refs) // 2
    for blocks_ref, joined_ref in zip(refs[:half_way], refs[half_way:]):
        _, per, size, _ = blocks_ref.shape
        width = per * size
        row = lax.broadcasted_iota(jnp.int32, (size, width), 0)
        lane = lax.broadcasted_iota(jnp.int32, (size, width), 1)
        for block in range(per):
            place = (row + block * size == lane).astype(jnp.bfloat16)
            real = product_of(blocks_ref[0, block], place).astype(jnp.bfloat16)
            imag = product_of(blocks_ref[1, block], place)
            upper = pl.ds(block * size, size)
            lower = pl.ds(width + block * size, size)
            joined_ref[0, upper, 0:width] = real
            joined_ref[0, upper, width : 2 * width] = imag.astype(jnp.bfloat16)
            joined_ref[0, lower, 0:width] = (-imag).astype(jnp.bfloat16)
            joined_ref[0, lower, width : 2 * width] = real


def spread_weights(groups, *weights):
    _, count, size, _ = weights[0].shape
    per = count // groups
    lanes = 2 * per * size
    shape = in_hbm((groups, lanes, lanes), jnp.bfloat16)
    return pl.pallas_call(
        spread_kernel,
        grid=(groups,),
        out_shape=(shape,) * len(weights),
        in_specs=[pl.BlockSpec((2, per, size, size), lambda g: (0, g, 0, 0))] * len(weights),
        out_specs=(group_spec(lanes, lanes),) * len(weights),
        compiler_params=params(12),
        cost_estimate=pl.CostEstimate(
            flops=len(weights) * 2 * count * size * size * lanes,
            bytes_accessed=len(weights) * 2 * groups * lanes * lanes,
            transcendentals=0,
        ),
        name="spread_weights",
    )(*weights)


def params(mebibytes):
    return pltpu.CompilerParams(
        vmem_limit_bytes=mebibytes * MIB, dimension_semantics=("arbitrary",)
    )


def place_of(me_ref, offset, rows):
    return pl.ds(pl.multiple_of((me_ref[0] ^ offset) * rows, rows), rows)


def in_hbm(shape, dtype):
    return pltpu.HBM(shape, dtype)


def hbm(*arrays):
    return [pltpu.with_memory_space_constraint(array, pltpu.HBM) for array in arrays]


def to_modes_kernel(me_ref, table_ref, cells_ref, *refs):
    modes_refs, held_ref = refs[:-1], refs[-1]
    rows = cells_ref.shape[1]
    share = modes_refs[0].shape[0] // rows
    for row in range(rows):
        spectrum = product_of(table_ref[...], cells_ref[0, row])
        held_ref[row] = spectrum.astype(jnp.bfloat16)
        for offset, modes_ref in enumerate(modes_refs):
            modes_ref[pl.ds(row * share, share)] = held_ref[row, place_of(me_ref, offset, share)]


def to_modes(me, table, cells, owners):
    samples, rows, width, channels = cells.shape
    size = table.shape[0]
    part = rows * size // owners
    return pl.pallas_call(
        to_modes_kernel,
        grid_spec=pltpu.PrefetchScalarGridSpec(
            num_scalar_prefetch=1,
            grid=(samples,),
            in_specs=[
                pl.BlockSpec((size, width), lambda b, _: (0, 0)),
                pl.BlockSpec((1, rows, width, channels), lambda b, _: (b, 0, 0, 0)),
            ],
            out_specs=(pl.BlockSpec((part, channels), lambda b, _: (b, 0)),) * owners,
            scratch_shapes=[pltpu.VMEM((rows, size, channels), jnp.bfloat16)],
        ),
        out_shape=(in_hbm((samples * part, channels), jnp.bfloat16),) * owners,
        compiler_params=params(12),
        cost_estimate=pl.CostEstimate(
            flops=2 * samples * rows * size * width * channels,
            bytes_accessed=2 * samples * rows * channels * (width + size),
            transcendentals=0,
        ),
        name="to_modes",
    )(me, table, cells)


def to_cells_kernel(me_ref, table_ref, base_ref, *refs):
    modes_refs, out_ref, held_ref = refs[:-2], refs[-2], refs[-1]
    rows = base_ref.shape[1]
    share = modes_refs[0].shape[-2] // rows
    for row in range(rows):
        run = pl.ds(row * share, share)
        if len(modes_refs) == 1:
            spectrum = modes_refs[0][:, run].reshape(held_ref.shape[1:])
        else:
            for offset, modes_ref in enumerate(modes_refs):
                held_ref[row, place_of(me_ref, offset, share)] = modes_ref[run]
            spectrum = held_ref[row]
        image = product_of(table_ref[...], spectrum)
        out_ref[0, row] = (base_ref[0, row].astype(jnp.float32) + image).astype(jnp.bfloat16)


def to_cells(me, table, modes, base):
    samples, rows, width, channels = base.shape
    size = table.shape[1]
    block = pl.BlockSpec((1, rows, width, channels), lambda b, _: (b, 0, 0, 0))
    if len(modes) == 1:
        lead = modes[0].shape[0]
        part = rows * size // lead
        specs = [pl.BlockSpec((lead, part, channels), lambda b, _: (0, b, 0))]
    else:
        part = rows * size // len(modes)
        specs = [pl.BlockSpec((part, channels), lambda b, _: (b, 0))] * len(modes)
    return pl.pallas_call(
        to_cells_kernel,
        grid_spec=pltpu.PrefetchScalarGridSpec(
            num_scalar_prefetch=1,
            grid=(samples,),
            in_specs=[pl.BlockSpec((width, size), lambda b, _: (0, 0)), block] + specs,
            out_specs=block,
            scratch_shapes=[pltpu.VMEM((rows, size, channels), jnp.bfloat16)],
        ),
        out_shape=jax.ShapeDtypeStruct(base.shape, jnp.bfloat16),
        compiler_params=params(12),
        cost_estimate=pl.CostEstimate(
            flops=2 * samples * rows * size * width * channels,
            bytes_accessed=2 * samples * rows * channels * (2 * width + size),
            transcendentals=0,
        ),
        name="to_cells",
    )(me, table, base, *hbm(*modes))


def rows_inside(cells):
    inside = jnp.transpose(cells, (0, 2, 1, 3))
    return with_layout_constraint(inside, Layout(major_to_minor=(0, 1, 2, 3)))


def rows_outside(cells):
    return jnp.transpose(cells, (0, 2, 1, 3))


def sigmoid_of(values):
    return 0.5 + 0.5 * jnp.tanh(0.5 * values)


def mix_lat(me_ref, table_ref, bands_refs, band_ref, mixed_ref):
    samples, size, width = band_ref.shape
    part, half = size // len(bands_refs), size // 2
    for sample in range(samples):
        for offset, bands_ref in enumerate(bands_refs):
            place = place_of(me_ref, offset, part)
            band_ref[sample, place] = bands_ref[pl.ds(sample * part, part)]
        mixed = product_of(table_ref[...], band_ref[sample]).astype(jnp.bfloat16)
        spot = pl.ds(sample * half, half)
        mixed_ref[spot, 0:width] = mixed[:half]
        mixed_ref[spot, width : 2 * width] = mixed[half:]


def unmix_lat(me_ref, table_ref, mixed_ref, band_ref, bands_refs):
    samples, size, width = band_ref.shape
    part, half = size // len(bands_refs), size // 2
    for sample in range(samples):
        spot = pl.ds(sample * half, half)
        joined = jnp.concatenate(
            [mixed_ref[spot, 0:width], mixed_ref[spot, width : 2 * width]], axis=0
        )
        bands = product_of(table_ref[...], joined).astype(jnp.bfloat16)
        if len(bands_refs) == 1:
            lead = bands_refs[0].shape[0]
            run = pl.ds(sample * size // lead, size // lead)
            bands_refs[0][:, run] = bands.reshape(lead, size // lead, width)
        else:
            band_ref[sample] = bands
            for offset, bands_ref in enumerate(bands_refs):
                place = place_of(me_ref, offset, part)
                bands_ref[pl.ds(sample * part, part)] = band_ref[sample, place]


def activate(mixed_ref, w1_ref, b1_ref):
    pre = product_of(mixed_ref[0], w1_ref[0]) + b1_ref[0]
    logistic = sigmoid_of(pre)
    return logistic, pre * logistic


def bend(act_ref, w2_ref, b2_ref):
    out = product_of(act_ref[...], w2_ref[0]) + b2_ref[0]
    return out, jnp.tanh(out * (1.0 / shrink_level))


def forward_kernel(blocks, me_ref, lat_ref, unlat_ref, w1_ref, b1_ref, w2_ref, b2_ref, *refs):
    bands_refs, image_refs = refs[:blocks], refs[blocks : 2 * blocks]
    mixed_ref, act_ref, band_ref = refs[2 * blocks :]
    mix_lat(me_ref, lat_ref, bands_refs, band_ref, mixed_ref.at[0])
    act_ref[...] = activate(mixed_ref, w1_ref, b1_ref)[1].astype(jnp.bfloat16)
    out, bent = bend(act_ref, w2_ref, b2_ref)
    act_ref[...] = (out - shrink_level * bent).astype(jnp.bfloat16)
    unmix_lat(me_ref, unlat_ref, act_ref, band_ref, image_refs)


def backward_kernel(
    block_size, blocks, me_ref, lat_ref, unlat_ref, w1_ref, b1_ref, w2_ref, b2_ref, mixed_ref, *refs
):
    bands_refs, image_refs = refs[:blocks], refs[blocks : 2 * blocks]
    sums_ref, act_ref, gate_ref, cot_ref, kept_ref, band_ref = refs[2 * blocks :]
    transposed = (((1,), (1,)), ((), ()))
    summed = (((0,), (0,)), ((), ()))

    def times(former, latter, dims):
        return lax.dot_general(former, latter, dims, preferred_element_type=jnp.float32)

    def weight_sums(acts, grads, slot):
        width = acts.shape[1] // 2
        full = times(acts, grads, summed)
        real = full[:width, :width] + full[width:, width:]
        imag = full[:width, width:] - full[width:, :width]
        bias = jnp.sum(grads.astype(jnp.float32), axis=0, keepdims=True)
        size = block_size
        owner = lax.broadcasted_iota(jnp.int32, (size, width), 1) // size
        extra = sums_ref.shape[2] - size
        first = lax.broadcasted_iota(jnp.int32, (extra, width), 0) == 0
        for part, values in enumerate((real, imag)):
            joined = values[:size]
            for block in range(1, width // size):
                joined = jnp.where(owner == block, values[block * size : (block + 1) * size], joined)
            sums_ref[slot, part, 0:size] = joined.astype(sums_ref.dtype)
            row = bias[:, part * width : (part + 1) * width]
            sums_ref[slot, part, size:] = jnp.where(first, row, 0.0).astype(sums_ref.dtype)

    logistic, act = activate(mixed_ref, w1_ref, b1_ref)
    act_ref[...] = act.astype(jnp.bfloat16)
    gate_ref[...] = logistic + act * (1.0 - logistic)
    mix_lat(me_ref, lat_ref, bands_refs, band_ref, cot_ref)
    _, bent = bend(act_ref, w2_ref, b2_ref)
    kept_ref[...] = (cot_ref[...].astype(jnp.float32) * (bent * bent)).astype(jnp.bfloat16)
    back = times(kept_ref[...], w2_ref[0], transposed)
    cot_ref[...] = (back * gate_ref[...]).astype(jnp.bfloat16)
    weight_sums(act_ref[...], kept_ref[...], 1)
    kept_ref[...] = times(cot_ref[...], w1_ref[0], transposed).astype(jnp.bfloat16)
    weight_sums(mixed_ref[0], cot_ref[...], 0)
    unmix_lat(me_ref, unlat_ref, kept_ref, band_ref, image_refs)


def group_spec(*shape):
    return pl.BlockSpec((1,) + shape, lambda g, *_: (g,) + (0,) * len(shape))


def bands_specs(rows, bands, groups):
    block = (rows, bands[0].shape[1] // groups)
    return (pl.BlockSpec(block, lambda g, *_: (0, g)),) * len(bands)


def images_like(bands, samples, size, groups):
    if len(bands) > 1:
        shapes = tuple(in_hbm(band.shape, band.dtype) for band in bands)
        return shapes, bands_specs(bands[0].shape[0], bands, groups)
    channels = bands[0].shape[1]
    shape = (1, samples * size, channels)
    spec = pl.BlockSpec(shape[:2] + (channels // groups,), lambda g, *_: (0, 0, g))
    return (in_hbm(shape, jnp.bfloat16),), (spec,)


def forward_mid(me, lat, unlat, bands, w1, b1, w2, b2):
    groups, lanes, _ = w1.shape
    size = lat.shape[0]
    samples = bands[0].shape[0] * len(bands) // size
    positions = samples * size // 2
    table = pl.BlockSpec((size, size), lambda g, _: (0, 0))
    state = (groups, positions, lanes)
    specs = bands_specs(bands[0].shape[0], bands, groups)
    images, image_specs = images_like(bands, samples, size, groups)
    results = pl.pallas_call(
        functools.partial(forward_kernel, len(bands)),
        grid_spec=pltpu.PrefetchScalarGridSpec(
            num_scalar_prefetch=1,
            grid=(groups,),
            in_specs=[
                table, table,
                group_spec(lanes, lanes), group_spec(1, lanes),
                group_spec(lanes, lanes), group_spec(1, lanes),
                *specs,
            ],
            out_specs=image_specs + (group_spec(positions, lanes),),
            scratch_shapes=[
                pltpu.VMEM((positions, lanes), jnp.bfloat16),
                pltpu.VMEM((samples, size, lanes // 2), jnp.bfloat16),
            ],
        ),
        out_shape=images + (in_hbm(state, jnp.bfloat16),),
        compiler_params=params(28),
        cost_estimate=pl.CostEstimate(
            flops=4 * groups * positions * lanes * lanes,
            bytes_accessed=16 * groups * positions * lanes + 4 * groups * lanes * lanes,
            transcendentals=2 * groups * positions * lanes,
        ),
        name="mix_forward",
    )(me, lat, unlat, *hbm(w1), b1, *hbm(w2), b2, *hbm(*bands))
    return results[: len(bands)], results[len(bands)]


def backward_mid(me, lat, unlat, bands, w1, b1, w2, b2, state, count):
    groups, lanes, _ = w1.shape
    size = lat.shape[0]
    samples = bands[0].shape[0] * len(bands) // size
    positions = samples * size // 2
    table = pl.BlockSpec((size, size), lambda g, _: (0, 0))
    size_of_block = lanes // 2 // (count // groups)
    sums = (2, 2, size_of_block + 32, lanes // 2)
    images, image_specs = images_like(bands, samples, size, groups)
    results = pl.pallas_call(
        functools.partial(backward_kernel, size_of_block, len(bands)),
        grid_spec=pltpu.PrefetchScalarGridSpec(
            num_scalar_prefetch=1,
            grid=(groups,),
            in_specs=[
                table, table,
                group_spec(lanes, lanes), group_spec(1, lanes),
                group_spec(lanes, lanes), group_spec(1, lanes),
                group_spec(positions, lanes),
                *bands_specs(bands[0].shape[0], bands, groups),
            ],
            out_specs=image_specs + (pl.BlockSpec(sums, lambda g, _: (0, 0, 0, g)),),
            scratch_shapes=[
                pltpu.VMEM((positions, lanes), jnp.bfloat16),
                pltpu.VMEM((positions, lanes), jnp.float32),
                pltpu.VMEM((positions, lanes), jnp.bfloat16),
                pltpu.VMEM((positions, lanes), jnp.bfloat16),
                pltpu.VMEM((samples, size, lanes // 2), jnp.bfloat16),
            ],
        ),
        out_shape=images + (in_hbm(sums[:3] + (groups * sums[3],), jnp.float32),),
        compiler_params=params(32),
        cost_estimate=pl.CostEstimate(
            flops=8 * groups * positions * lanes * lanes,
            bytes_accessed=16 * groups * positions * lanes + 4 * groups * lanes * lanes,
            transcendentals=0,
        ),
        name="mix_backward",
    )(me, lat, unlat, *hbm(w1), b1, *hbm(w2), b2, *hbm(state, *bands))
    return results[: len(bands)], results[len(bands)]


def swap_with(values, axis, distance):
    pairs = [(i, i ^ distance) for i in range(lax.axis_size(axis))]
    return lax.ppermute(values, axis, pairs)


def waiting(values, arrived):
    return lax.optimization_barrier((values, tuple(arrived)))[0]


def mixed_order(size):
    far = list(range(size // 2, size))
    near = [offset for offset in (2, 3, 1) if offset < size // 2]
    near += list(range(4, size // 2))
    order = []
    while far or near:
        order += far[:1] + near[:1]
        far, near = far[1:], near[1:]
    return order


def pick(pair, side):
    return lax.dynamic_index_in_dim(pair, side, 0, keepdims=False)


class GroupSum:
    def __init__(self, sums):
        self.lanes = sums.shape[-1]
        self.side = lax.axis_index("dp")
        self.me = lax.axis_index("space")
        self.count = lax.axis_size("space") // 2
        self.held = sums.reshape(-1, self.lanes)

    def halve(self, axis, distance, bit, kind, arrived):
        pair = waiting(self.held, arrived).reshape(2, -1, self.lanes)
        taken = swap_with(pick(pair, 1 - bit).astype(kind), axis, distance)
        self.held = pick(pair, bit) + taken.astype(jnp.float32)

    def over_dp(self):
        self.halve("dp", 1, self.side, jnp.float32, [])

    def over_next(self, arrived):
        self.halve("space", 1, self.me % 2, jnp.bfloat16, arrived)

    def scatter(self, arrived):
        shares = waiting(self.held, arrived).reshape(self.count, -1, self.lanes)
        place = self.me // 2
        total = pick(shares, place)
        for offset in range(1, self.count):
            given = pick(shares, place ^ offset).astype(jnp.bfloat16)
            total += swap_with(given, "space", 2 * offset).astype(jnp.float32)
        self.total = total.astype(jnp.bfloat16)

    def gather(self, arrived):
        total = waiting(self.total, arrived)
        taken = [total]
        for offset in range(1, self.count):
            taken.append(swap_with(total, "space", 2 * offset))
        self.quarter = jnp.stack(taken)

    def gather_next(self, arrived):
        quarter = waiting(self.quarter, arrived)
        self.half = jnp.stack([quarter, swap_with(quarter, "space", 1)])

    def gather_dp(self, arrived):
        half = waiting(self.half, arrived)
        return half, swap_with(half, "dp", 1)


def finish_kernel(factor, me_ref, half_ref, other_ref, *out_refs):
    side, near, place = me_ref[0], me_ref[1], me_ref[2]
    run = half_ref.shape[2]
    for which in range(2):
        blocks_ref, bias_ref = out_refs[2 * which : 2 * which + 2]
        edge = blocks_ref.shape[-1]
        for part in range(2):
            for piece in range(half_ref.shape[1]):
                spot = (part ^ near, piece ^ place)
                own = half_ref[spot].astype(jnp.float32)
                value = jnp.where(side == which, own, other_ref[spot].astype(jnp.float32)) * factor
                first = piece * run
                count = max(0, min(edge - first, run))
                for block in range(blocks_ref.shape[1]):
                    lanes = slice(block * edge, (block + 1) * edge)
                    if count > 0:
                        blocks_ref[part, block, pl.ds(first, count)] = value[:count, lanes]
                    if first <= edge < first + run:
                        row = edge - first
                        bias_ref[part, pl.ds(block, 1)] = value[row : row + 1, lanes]


def finish_sums(here, half, other, factor, weight_shape, bias_shape):
    outs = [weight_shape, bias_shape] * 2
    return pl.pallas_call(
        functools.partial(finish_kernel, factor),
        out_shape=[jax.ShapeDtypeStruct(shape, jnp.float32) for shape in outs],
        in_specs=[pl.BlockSpec(memory_space=pltpu.SMEM)]
        + [pl.BlockSpec(memory_space=pltpu.VMEM)] * 2,
        out_specs=[pl.BlockSpec(memory_space=pltpu.VMEM)] * 4,
        compiler_params=pltpu.CompilerParams(vmem_limit_bytes=16 * MIB),
        cost_estimate=pl.CostEstimate(flops=0, bytes_accessed=4 * MIB, transcendentals=0),
        name="finish_sums",
    )(here, half, other)


def body(fields, cotangent, w_first, b_first, w_second, b_second):
    samples, rows, width, channels = fields.shape
    owners = lax.axis_size("space")
    lat_total = rows * owners
    modes = KW // owners
    count, edge = w_first.shape[1:3]
    groups = 2
    direct = 2 * modes % 16 == 0
    lead = owners if direct else 1

    order = mixed_order(owners)

    def send(blocks, offsets, taken):
        for offset in offsets:
            taken[offset] = swap_with(blocks[offset], "space", offset)

    def send_all(spectrum):
        spectrum = spectrum.reshape(samples, rows, owners, 2 * modes, channels)
        spectrum = jnp.transpose(spectrum, (2, 0, 1, 3, 4))
        arrived = lax.all_to_all(spectrum, "space", split_axis=0, concat_axis=0, tiled=True)
        return [jnp.transpose(arrived, (1, 0, 2, 3, 4)).reshape(-1, channels)]

    def send_all_back(bands):
        bands = bands.reshape(samples, owners, rows, 2 * modes, channels)
        bands = jnp.transpose(bands, (1, 0, 2, 3, 4))
        arrived = lax.all_to_all(bands, "space", split_axis=0, concat_axis=0, tiled=True)
        return [jnp.transpose(arrived, (1, 2, 0, 3, 4)).reshape(1, -1, channels)]

    me = lax.axis_index("space") if direct else 0
    me = jnp.full((1,), me, jnp.int32)
    plain, scaled = lon_tables(KW, width, owners)
    lat = lat_spread(lat_total, modes)

    spectrum = to_modes(me, plain, fields, lead)
    spectrum, cotangent, w_first, w_second = lax.optimization_barrier(
        (spectrum, cotangent, w_first, w_second)
    )
    cot_spec = to_modes(me, scaled, cotangent, lead)
    w1, w2 = spread_weights(groups, w_first, w_second)
    b1, b2 = block_bias(b_first, groups), block_bias(b_second, groups)
    positions = samples * lax.axis_size("dp") * lat_total * KW
    factor = 1.0 / math.sqrt(positions)

    if not direct:
        gathered = send_all(spectrum[0])
        image, state = forward_mid(me, lat, lat.T, gathered, w1, b1, w2, b2)
        image_band = send_all_back(image[0])
        gathered = send_all(cot_spec[0])
        grad_image, sums = backward_mid(me, lat, lat.T, gathered, w1, b1, w2, b2, state, count)
        grad_band = send_all_back(grad_image[0])
        output = to_cells(me, scaled.T, image_band, fields)
        grad_fields = to_cells(me, plain.T, grad_band, cotangent)
        sums = lax.psum(sums, ("space", "dp")) * factor
        grads = []
        for which in range(2):
            blocks = sums[which, :, :edge].reshape(2, edge, count, edge)
            grads.append(jnp.transpose(blocks, (0, 2, 1, 3)))
            grads.append(sums[which, :, edge].reshape(b_first.shape))
        return (output, grad_fields) + tuple(grads)

    gathered, cot_gathered = {0: spectrum[0]}, {0: cot_spec[0]}
    send(spectrum, order, gathered)
    gathered = [gathered[offset] for offset in range(owners)]
    image, state = forward_mid(me, lat, lat.T, gathered, w1, b1, w2, b2)
    cot_spec, image = list(cot_spec), list(image)
    send(cot_spec, order[:FIRST], cot_gathered)
    cot_spec, image = waiting((cot_spec, image), [image[0]])
    send(cot_spec, order[FIRST:], cot_gathered)

    image_band = {0: image[0]}
    send(image, order, image_band)
    cot_gathered = [cot_gathered[offset] for offset in range(owners)]
    grad_image, sums = backward_mid(
        me, lat, lat.T, cot_gathered, w1, b1, w2, b2, state, count
    )
    early = [image_band[offset] for offset in order[:HELD]]
    late = [image_band[offset] for offset in order[HELD:]]
    grad_image, sums = waiting((list(grad_image), sums), early)
    group_sum = GroupSum(sums)
    group_sum.over_dp()
    group_sum.over_next(late[:2])
    grad_band = {0: grad_image[0]}
    send(grad_image, order, grad_band)
    arrived = [grad_band[offset] for offset in order]
    image_band = [image_band[offset] for offset in range(owners)]
    grad_band = [grad_band[offset] for offset in range(owners)]
    again = waiting(fields, early[:1])
    output = rows_inside(to_cells(me, scaled.T, image_band, again))
    group_sum.scatter(late[2:] + arrived[:1])
    group_sum.gather(arrived[1:3])
    group_sum.quarter, output = lax.optimization_barrier((group_sum.quarter, output))
    group_sum.gather_next(arrived[3:5])
    half, other = group_sum.gather_dp(arrived[5:])
    grad_fields = rows_inside(to_cells(me, plain.T, grad_band, cotangent))
    place = lax.axis_index("space")
    here = jnp.stack([lax.axis_index("dp"), place % 2, place // 2]).astype(jnp.int32)
    grads = finish_sums(
        here, half, other, factor, w_first.shape, b_first.shape
    )
    return (rows_outside(output), rows_outside(grad_fields)) + tuple(grads)


def solution(mesh):
    split = P(("parts", "dp"), "space", None, None)
    in_specs = (split, split, P(), P(), P(), P())
    out_specs = (
        split,
        split,
        P("parts", None, None, None),
        P("parts", None, None),
        P("parts", None, None, None),
        P("parts", None, None),
    )
    return jax.shard_map(body, mesh=mesh, in_specs=in_specs, out_specs=out_specs, check_vma=False)
```

```python
import functools
import math

import jax
import jax.numpy as jnp
from jax import lax
from jax.experimental import pallas as pl
from jax.experimental.layout import Layout, with_layout_constraint
from jax.experimental.pallas import tpu as pltpu
from jax.sharding import PartitionSpec as P
import ml_dtypes
import numpy as np

KW = 64
shrink_level = 0.05
FIRST = 5
HELD = 3
MIB = 1024 * 1024


def product_of(former, latter):
    return jnp.dot(former, latter, preferred_element_type=jnp.float32)


def lon_tables(mode_count, cell_count, owners):
    wavenums = np.arange(mode_count, dtype=np.int32)
    columns = np.arange(cell_count, dtype=np.int32)
    phase_index = (wavenums[:, None] * columns[None, :] % cell_count).astype(np.float32)
    phases = phase_index * np.float32(2.0 * math.pi / cell_count)
    factor = np.float32(1.0 / math.sqrt(cell_count))
    forward = np.stack([np.cos(phases) * factor, -np.sin(phases) * factor])
    scaled = forward * np.where(wavenums == 0, 1.0, 2.0).astype(np.float32)[:, None]

    def ordered(table):
        split = table.reshape(2, owners, -1, cell_count).transpose(1, 0, 2, 3)
        return split.reshape(-1, cell_count).astype(ml_dtypes.bfloat16)

    return ordered(forward), ordered(scaled)


def lat_spread(row_count, modes):
    indices = np.arange(row_count, dtype=np.int32)
    phase_index = (indices[:, None] * indices[None, :] % row_count).astype(np.float32)
    phases = phase_index * np.float32(2.0 * math.pi / row_count)
    factor = np.float32(1.0 / math.sqrt(row_count))
    cosine = np.cos(phases) * factor
    sine_part = np.sin(phases) * factor
    table = np.stack([np.stack([cosine, sine_part], -1), np.stack([-sine_part, cosine], -1)])
    same = np.eye(modes, dtype=np.float32)
    spread = table[:, :, None, :, :, None] * same[None, None, :, None, None, :]
    size = 2 * row_count * modes
    return spread.reshape(size, size).astype(ml_dtypes.bfloat16)


def block_bias(bias, groups):
    return jnp.transpose(bias.reshape(2, groups, 1, -1), (1, 2, 0, 3)).reshape(groups, 1, -1)


def spread_kernel(*refs):
    half_way = len(refs) // 2
    for blocks_ref, joined_ref in zip(refs[:half_way], refs[half_way:]):
        _, per, size, _ = blocks_ref.shape
        width = per * size
        row = lax.broadcasted_iota(jnp.int32, (size, width), 0)
        lane = lax.broadcasted_iota(jnp.int32, (size, width), 1)
        for block in range(per):
            place = (row + block * size == lane).astype(jnp.bfloat16)
            real = product_of(blocks_ref[0, block], place).astype(jnp.bfloat16)
            imag = product_of(blocks_ref[1, block], place)
            upper = pl.ds(block * size, size)
            lower = pl.ds(width + block * size, size)
            joined_ref[0, upper, 0:width] = real
            joined_ref[0, upper, width : 2 * width] = imag.astype(jnp.bfloat16)
            joined_ref[0, lower, 0:width] = (-imag).astype(jnp.bfloat16)
            joined_ref[0, lower, width : 2 * width] = real


def spread_weights(groups, *weights):
    _, count, size, _ = weights[0].shape
    per = count // groups
    lanes = 2 * per * size
    shape = in_hbm((groups, lanes, lanes), jnp.bfloat16)
    return pl.pallas_call(
        spread_kernel,
        grid=(groups,),
        out_shape=(shape,) * len(weights),
        in_specs=[pl.BlockSpec((2, per, size, size), lambda g: (0, g, 0, 0))] * len(weights),
        out_specs=(group_spec(lanes, lanes),) * len(weights),
        compiler_params=params(12),
        cost_estimate=pl.CostEstimate(
            flops=len(weights) * 2 * count * size * size * lanes,
            bytes_accessed=len(weights) * 2 * groups * lanes * lanes,
            transcendentals=0,
        ),
        name="spread_weights",
    )(*weights)


def params(mebibytes):
    return pltpu.CompilerParams(
        vmem_limit_bytes=mebibytes * MIB, dimension_semantics=("arbitrary",)
    )


def place_of(me_ref, offset, rows):
    return pl.ds(pl.multiple_of((me_ref[0] ^ offset) * rows, rows), rows)


def in_hbm(shape, dtype):
    return pltpu.HBM(shape, dtype)


def hbm(*arrays):
    return [pltpu.with_memory_space_constraint(array, pltpu.HBM) for array in arrays]


def with_offsets(refs):
    return [((len(refs) - place) % len(refs), ref) for place, ref in enumerate(refs)]


def to_modes_kernel(me_ref, table_ref, cells_ref, *refs):
    modes_refs, held_ref = refs[:-1], refs[-1]
    rows = cells_ref.shape[1]
    share = modes_refs[0].shape[0] // rows
    for row in range(rows):
        spectrum = product_of(table_ref[...], cells_ref[0, row])
        held_ref[row] = spectrum.astype(jnp.bfloat16)
        for offset, modes_ref in with_offsets(modes_refs):
            modes_ref[pl.ds(row * share, share)] = held_ref[row, place_of(me_ref, offset, share)]


def to_modes(me, table, cells, owners):
    samples, rows, width, channels = cells.shape
    size = table.shape[0]
    part = rows * size // owners
    return pl.pallas_call(
        to_modes_kernel,
        grid_spec=pltpu.PrefetchScalarGridSpec(
            num_scalar_prefetch=1,
            grid=(samples,),
            in_specs=[
                pl.BlockSpec((size, width), lambda b, _: (0, 0)),
                pl.BlockSpec((1, rows, width, channels), lambda b, _: (b, 0, 0, 0)),
            ],
            out_specs=(pl.BlockSpec((part, channels), lambda b, _: (b, 0)),) * owners,
            scratch_shapes=[pltpu.VMEM((rows, size, channels), jnp.bfloat16)],
        ),
        out_shape=(in_hbm((samples * part, channels), jnp.bfloat16),) * owners,
        compiler_params=params(12),
        cost_estimate=pl.CostEstimate(
            flops=2 * samples * rows * size * width * channels,
            bytes_accessed=2 * samples * rows * channels * (width + size),
            transcendentals=0,
        ),
        name="to_modes",
    )(me, table, cells)


def to_cells_kernel(me_ref, table_ref, base_ref, *refs):
    modes_refs, out_ref, held_ref = refs[:-2], refs[-2], refs[-1]
    rows = base_ref.shape[1]
    share = modes_refs[0].shape[-2] // rows
    for row in range(rows):
        run = pl.ds(row * share, share)
        if len(modes_refs) == 1:
            spectrum = modes_refs[0][:, run].reshape(held_ref.shape[1:])
        else:
            for offset, modes_ref in with_offsets(modes_refs):
                held_ref[row, place_of(me_ref, offset, share)] = modes_ref[run]
            spectrum = held_ref[row]
        image = product_of(table_ref[...], spectrum)
        out_ref[0, row] = (base_ref[0, row].astype(jnp.float32) + image).astype(jnp.bfloat16)


def to_cells(me, table, modes, base):
    samples, rows, width, channels = base.shape
    size = table.shape[1]
    block = pl.BlockSpec((1, rows, width, channels), lambda b, _: (b, 0, 0, 0))
    if len(modes) == 1:
        lead = modes[0].shape[0]
        part = rows * size // lead
        specs = [pl.BlockSpec((lead, part, channels), lambda b, _: (0, b, 0))]
    else:
        part = rows * size // len(modes)
        specs = [pl.BlockSpec((part, channels), lambda b, _: (b, 0))] * len(modes)
    return pl.pallas_call(
        to_cells_kernel,
        grid_spec=pltpu.PrefetchScalarGridSpec(
            num_scalar_prefetch=1,
            grid=(samples,),
            in_specs=[pl.BlockSpec((width, size), lambda b, _: (0, 0)), block] + specs,
            out_specs=block,
            scratch_shapes=[pltpu.VMEM((rows, size, channels), jnp.bfloat16)],
        ),
        out_shape=jax.ShapeDtypeStruct(base.shape, jnp.bfloat16),
        compiler_params=params(12),
        cost_estimate=pl.CostEstimate(
            flops=2 * samples * rows * size * width * channels,
            bytes_accessed=2 * samples * rows * channels * (2 * width + size),
            transcendentals=0,
        ),
        name="to_cells",
    )(me, table, base, *hbm(*modes))


def rows_inside(cells):
    inside = jnp.transpose(cells, (0, 2, 1, 3))
    return with_layout_constraint(inside, Layout(major_to_minor=(0, 1, 2, 3)))


def rows_outside(cells):
    return jnp.transpose(cells, (0, 2, 1, 3))


def sigmoid_of(values):
    return 0.5 + 0.5 * jnp.tanh(0.5 * values)


def mix_lat(me_ref, table_ref, bands_refs, band_ref, mixed_ref):
    samples, size, width = band_ref.shape
    part, half = size // len(bands_refs), size // 2
    for sample in range(samples):
        for offset, bands_ref in with_offsets(bands_refs):
            place = place_of(me_ref, offset, part)
            band_ref[sample, place] = bands_ref[pl.ds(sample * part, part)]
        mixed = product_of(table_ref[...], band_ref[sample]).astype(jnp.bfloat16)
        spot = pl.ds(sample * half, half)
        mixed_ref[spot, 0:width] = mixed[:half]
        mixed_ref[spot, width : 2 * width] = mixed[half:]


def unmix_lat(me_ref, table_ref, mixed_ref, band_ref, bands_refs):
    samples, size, width = band_ref.shape
    part, half = size // len(bands_refs), size // 2
    for sample in range(samples):
        spot = pl.ds(sample * half, half)
        joined = jnp.concatenate(
            [mixed_ref[spot, 0:width], mixed_ref[spot, width : 2 * width]], axis=0
        )
        bands = product_of(table_ref[...], joined).astype(jnp.bfloat16)
        if len(bands_refs) == 1:
            lead = bands_refs[0].shape[0]
            run = pl.ds(sample * size // lead, size // lead)
            bands_refs[0][:, run] = bands.reshape(lead, size // lead, width)
        else:
            band_ref[sample] = bands
            for offset, bands_ref in with_offsets(bands_refs):
                place = place_of(me_ref, offset, part)
                bands_ref[pl.ds(sample * part, part)] = band_ref[sample, place]


def activate(mixed_ref, w1_ref, b1_ref):
    pre = product_of(mixed_ref[0], w1_ref[0]) + b1_ref[0]
    logistic = sigmoid_of(pre)
    return logistic, pre * logistic


def bend(act_ref, w2_ref, b2_ref):
    out = product_of(act_ref[...], w2_ref[0]) + b2_ref[0]
    return out, jnp.tanh(out * (1.0 / shrink_level))


def forward_kernel(blocks, me_ref, lat_ref, unlat_ref, w1_ref, b1_ref, w2_ref, b2_ref, *refs):
    bands_refs, image_refs = refs[:blocks], refs[blocks : 2 * blocks]
    mixed_ref, act_ref, band_ref = refs[2 * blocks :]
    mix_lat(me_ref, lat_ref, bands_refs, band_ref, mixed_ref.at[0])
    act_ref[...] = activate(mixed_ref, w1_ref, b1_ref)[1].astype(jnp.bfloat16)
    out, bent = bend(act_ref, w2_ref, b2_ref)
    act_ref[...] = (out - shrink_level * bent).astype(jnp.bfloat16)
    unmix_lat(me_ref, unlat_ref, act_ref, band_ref, image_refs)


def backward_kernel(
    block_size, blocks, me_ref, lat_ref, unlat_ref, w1_ref, b1_ref, w2_ref, b2_ref, mixed_ref, *refs
):
    bands_refs, image_refs = refs[:blocks], refs[blocks : 2 * blocks]
    sums_ref, act_ref, gate_ref, cot_ref, kept_ref, band_ref = refs[2 * blocks :]
    transposed = (((1,), (1,)), ((), ()))
    summed = (((0,), (0,)), ((), ()))

    def times(former, latter, dims):
        return lax.dot_general(former, latter, dims, preferred_element_type=jnp.float32)

    def weight_sums(acts, grads, slot):
        width = acts.shape[1] // 2
        full = times(acts, grads, summed)
        real = full[:width, :width] + full[width:, width:]
        imag = full[:width, width:] - full[width:, :width]
        bias = jnp.sum(grads.astype(jnp.float32), axis=0, keepdims=True)
        size = block_size
        owner = lax.broadcasted_iota(jnp.int32, (size, width), 1) // size
        extra = sums_ref.shape[2] - size
        first = lax.broadcasted_iota(jnp.int32, (extra, width), 0) == 0
        for part, values in enumerate((real, imag)):
            joined = values[:size]
            for block in range(1, width // size):
                joined = jnp.where(owner == block, values[block * size : (block + 1) * size], joined)
            sums_ref[slot, part, 0:size] = joined.astype(sums_ref.dtype)
            row = bias[:, part * width : (part + 1) * width]
            sums_ref[slot, part, size:] = jnp.where(first, row, 0.0).astype(sums_ref.dtype)

    logistic, act = activate(mixed_ref, w1_ref, b1_ref)
    act_ref[...] = act.astype(jnp.bfloat16)
    gate_ref[...] = logistic + act * (1.0 - logistic)
    mix_lat(me_ref, lat_ref, bands_refs, band_ref, cot_ref)
    _, bent = bend(act_ref, w2_ref, b2_ref)
    kept_ref[...] = (cot_ref[...].astype(jnp.float32) * (bent * bent)).astype(jnp.bfloat16)
    back = times(kept_ref[...], w2_ref[0], transposed)
    cot_ref[...] = (back * gate_ref[...]).astype(jnp.bfloat16)
    weight_sums(act_ref[...], kept_ref[...], 1)
    kept_ref[...] = times(cot_ref[...], w1_ref[0], transposed).astype(jnp.bfloat16)
    weight_sums(mixed_ref[0], cot_ref[...], 0)
    unmix_lat(me_ref, unlat_ref, kept_ref, band_ref, image_refs)


def group_spec(*shape):
    return pl.BlockSpec((1,) + shape, lambda g, *_: (g,) + (0,) * len(shape))


def bands_specs(rows, bands, groups):
    block = (rows, bands[0].shape[1] // groups)
    return (pl.BlockSpec(block, lambda g, *_: (0, g)),) * len(bands)


def images_like(bands, samples, size, groups):
    if len(bands) > 1:
        shapes = tuple(in_hbm(band.shape, band.dtype) for band in bands)
        return shapes, bands_specs(bands[0].shape[0], bands, groups)
    channels = bands[0].shape[1]
    shape = (1, samples * size, channels)
    spec = pl.BlockSpec(shape[:2] + (channels // groups,), lambda g, *_: (0, 0, g))
    return (in_hbm(shape, jnp.bfloat16),), (spec,)


def forward_mid(me, lat, unlat, bands, w1, b1, w2, b2):
    groups, lanes, _ = w1.shape
    size = lat.shape[0]
    samples = bands[0].shape[0] * len(bands) // size
    positions = samples * size // 2
    table = pl.BlockSpec((size, size), lambda g, _: (0, 0))
    state = (groups, positions, lanes)
    specs = bands_specs(bands[0].shape[0], bands, groups)
    images, image_specs = images_like(bands, samples, size, groups)
    results = pl.pallas_call(
        functools.partial(forward_kernel, len(bands)),
        grid_spec=pltpu.PrefetchScalarGridSpec(
            num_scalar_prefetch=1,
            grid=(groups,),
            in_specs=[
                table, table,
                group_spec(lanes, lanes), group_spec(1, lanes),
                group_spec(lanes, lanes), group_spec(1, lanes),
                *specs,
            ],
            out_specs=image_specs + (group_spec(positions, lanes),),
            scratch_shapes=[
                pltpu.VMEM((positions, lanes), jnp.bfloat16),
                pltpu.VMEM((samples, size, lanes // 2), jnp.bfloat16),
            ],
        ),
        out_shape=images + (in_hbm(state, jnp.bfloat16),),
        compiler_params=params(28),
        cost_estimate=pl.CostEstimate(
            flops=4 * groups * positions * lanes * lanes,
            bytes_accessed=16 * groups * positions * lanes + 4 * groups * lanes * lanes,
            transcendentals=2 * groups * positions * lanes,
        ),
        name="mix_forward",
    )(me, lat, unlat, *hbm(w1), b1, *hbm(w2), b2, *hbm(*bands))
    return results[: len(bands)], results[len(bands)]


def backward_mid(me, lat, unlat, bands, w1, b1, w2, b2, state, count):
    groups, lanes, _ = w1.shape
    size = lat.shape[0]
    samples = bands[0].shape[0] * len(bands) // size
    positions = samples * size // 2
    table = pl.BlockSpec((size, size), lambda g, _: (0, 0))
    size_of_block = lanes // 2 // (count // groups)
    sums = (2, 2, size_of_block + 32, lanes // 2)
    images, image_specs = images_like(bands, samples, size, groups)
    results = pl.pallas_call(
        functools.partial(backward_kernel, size_of_block, len(bands)),
        grid_spec=pltpu.PrefetchScalarGridSpec(
            num_scalar_prefetch=1,
            grid=(groups,),
            in_specs=[
                table, table,
                group_spec(lanes, lanes), group_spec(1, lanes),
                group_spec(lanes, lanes), group_spec(1, lanes),
                group_spec(positions, lanes),
                *bands_specs(bands[0].shape[0], bands, groups),
            ],
            out_specs=image_specs + (pl.BlockSpec(sums, lambda g, _: (0, 0, 0, g)),),
            scratch_shapes=[
                pltpu.VMEM((positions, lanes), jnp.bfloat16),
                pltpu.VMEM((positions, lanes), jnp.float32),
                pltpu.VMEM((positions, lanes), jnp.bfloat16),
                pltpu.VMEM((positions, lanes), jnp.bfloat16),
                pltpu.VMEM((samples, size, lanes // 2), jnp.bfloat16),
            ],
        ),
        out_shape=images + (in_hbm(sums[:3] + (groups * sums[3],), jnp.float32),),
        compiler_params=params(32),
        cost_estimate=pl.CostEstimate(
            flops=8 * groups * positions * lanes * lanes,
            bytes_accessed=16 * groups * positions * lanes + 4 * groups * lanes * lanes,
            transcendentals=0,
        ),
        name="mix_backward",
    )(me, lat, unlat, *hbm(w1), b1, *hbm(w2), b2, *hbm(state, *bands))
    return results[: len(bands)], results[len(bands)]


def swap_with(values, axis, distance):
    pairs = [(i, i ^ distance) for i in range(lax.axis_size(axis))]
    return lax.ppermute(values, axis, pairs)


def waiting(values, arrived):
    return lax.optimization_barrier((values, tuple(arrived)))[0]


def mixed_order(size):
    far = list(range(size // 2, size))
    near = [offset for offset in (2, 3, 1) if offset < size // 2]
    near += list(range(4, size // 2))
    order = []
    while far or near:
        order += far[:1] + near[:1]
        far, near = far[1:], near[1:]
    return order


def pick(pair, side):
    return lax.dynamic_index_in_dim(pair, side, 0, keepdims=False)


class GroupSum:
    def __init__(self, sums):
        self.lanes = sums.shape[-1]
        self.side = lax.axis_index("dp")
        self.me = lax.axis_index("space")
        self.count = lax.axis_size("space") // 2
        self.held = sums.reshape(-1, self.lanes)

    def halve(self, axis, distance, bit, kind, arrived):
        pair = waiting(self.held, arrived).reshape(2, -1, self.lanes)
        taken = swap_with(pick(pair, 1 - bit).astype(kind), axis, distance)
        self.held = pick(pair, bit) + taken.astype(jnp.float32)

    def over_dp(self):
        self.halve("dp", 1, self.side, jnp.float32, [])

    def over_next(self, arrived):
        self.halve("space", 1, self.me % 2, jnp.bfloat16, arrived)

    def scatter(self, arrived):
        shares = waiting(self.held, arrived).reshape(self.count, -1, self.lanes)
        place = self.me // 2
        total = pick(shares, place)
        for offset in range(1, self.count):
            given = pick(shares, place ^ offset).astype(jnp.bfloat16)
            total += swap_with(given, "space", 2 * offset).astype(jnp.float32)
        self.total = total.astype(jnp.bfloat16)

    def gather(self, arrived):
        total = waiting(self.total, arrived)
        taken = [total]
        for offset in range(1, self.count):
            taken.append(swap_with(total, "space", 2 * offset))
        self.quarter = jnp.stack(taken)

    def gather_next(self, arrived):
        quarter = waiting(self.quarter, arrived)
        self.half = jnp.stack([quarter, swap_with(quarter, "space", 1)])

    def gather_dp(self, arrived):
        half = waiting(self.half, arrived)
        return half, swap_with(half, "dp", 1)


def finish_kernel(factor, me_ref, half_ref, other_ref, *out_refs):
    side, near, place = me_ref[0], me_ref[1], me_ref[2]
    run = half_ref.shape[2]
    for which in range(2):
        blocks_ref, bias_ref = out_refs[2 * which : 2 * which + 2]
        edge = blocks_ref.shape[-1]
        for part in range(2):
            for piece in range(half_ref.shape[1]):
                spot = (part ^ near, piece ^ place)
                own = half_ref[spot].astype(jnp.float32)
                value = jnp.where(side == which, own, other_ref[spot].astype(jnp.float32)) * factor
                first = piece * run
                count = max(0, min(edge - first, run))
                for block in range(blocks_ref.shape[1]):
                    lanes = slice(block * edge, (block + 1) * edge)
                    if count > 0:
                        blocks_ref[part, block, pl.ds(first, count)] = value[:count, lanes]
                    if first <= edge < first + run:
                        row = edge - first
                        bias_ref[part, pl.ds(block, 1)] = value[row : row + 1, lanes]


def finish_sums(here, half, other, factor, weight_shape, bias_shape):
    outs = [weight_shape, bias_shape] * 2
    return pl.pallas_call(
        functools.partial(finish_kernel, factor),
        out_shape=[jax.ShapeDtypeStruct(shape, jnp.float32) for shape in outs],
        in_specs=[pl.BlockSpec(memory_space=pltpu.SMEM)]
        + [pl.BlockSpec(memory_space=pltpu.VMEM)] * 2,
        out_specs=[pl.BlockSpec(memory_space=pltpu.VMEM)] * 4,
        compiler_params=pltpu.CompilerParams(vmem_limit_bytes=16 * MIB),
        cost_estimate=pl.CostEstimate(flops=0, bytes_accessed=4 * MIB, transcendentals=0),
        name="finish_sums",
    )(here, half, other)


def body(fields, cotangent, w_first, b_first, w_second, b_second):
    samples, rows, width, channels = fields.shape
    owners = lax.axis_size("space")
    lat_total = rows * owners
    modes = KW // owners
    count, edge = w_first.shape[1:3]
    groups = 2
    direct = 2 * modes % 16 == 0
    lead = owners if direct else 1

    order = mixed_order(owners)

    def place(offset):
        return (owners - offset) % owners

    def send(blocks, offsets, taken):
        for offset in offsets:
            taken[offset] = swap_with(blocks[place(offset)], "space", offset)

    def listed(taken):
        return [taken[place(at)] for at in range(owners)]

    def send_all(spectrum):
        spectrum = spectrum.reshape(samples, rows, owners, 2 * modes, channels)
        spectrum = jnp.transpose(spectrum, (2, 0, 1, 3, 4))
        arrived = lax.all_to_all(spectrum, "space", split_axis=0, concat_axis=0, tiled=True)
        return [jnp.transpose(arrived, (1, 0, 2, 3, 4)).reshape(-1, channels)]

    def send_all_back(bands):
        bands = bands.reshape(samples, owners, rows, 2 * modes, channels)
        bands = jnp.transpose(bands, (1, 0, 2, 3, 4))
        arrived = lax.all_to_all(bands, "space", split_axis=0, concat_axis=0, tiled=True)
        return [jnp.transpose(arrived, (1, 2, 0, 3, 4)).reshape(1, -1, channels)]

    me = lax.axis_index("space") if direct else 0
    me = jnp.full((1,), me, jnp.int32)
    plain, scaled = lon_tables(KW, width, owners)
    lat = lat_spread(lat_total, modes)

    spectrum = to_modes(me, plain, fields, lead)
    spectrum, cotangent, w_first, w_second = lax.optimization_barrier(
        (spectrum, cotangent, w_first, w_second)
    )
    cot_spec = to_modes(me, scaled, cotangent, lead)
    w1, w2 = spread_weights(groups, w_first, w_second)
    b1, b2 = block_bias(b_first, groups), block_bias(b_second, groups)
    positions = samples * lax.axis_size("dp") * lat_total * KW
    factor = 1.0 / math.sqrt(positions)

    if not direct:
        gathered = send_all(spectrum[0])
        image, state = forward_mid(me, lat, lat.T, gathered, w1, b1, w2, b2)
        image_band = send_all_back(image[0])
        gathered = send_all(cot_spec[0])
        grad_image, sums = backward_mid(me, lat, lat.T, gathered, w1, b1, w2, b2, state, count)
        grad_band = send_all_back(grad_image[0])
        output = to_cells(me, scaled.T, image_band, fields)
        grad_fields = to_cells(me, plain.T, grad_band, cotangent)
        sums = lax.psum(sums, ("space", "dp")) * factor
        grads = []
        for which in range(2):
            blocks = sums[which, :, :edge].reshape(2, edge, count, edge)
            grads.append(jnp.transpose(blocks, (0, 2, 1, 3)))
            grads.append(sums[which, :, edge].reshape(b_first.shape))
        return (output, grad_fields) + tuple(grads)

    gathered, cot_gathered = {0: spectrum[0]}, {0: cot_spec[0]}
    send(spectrum, order, gathered)
    gathered = listed(gathered)
    image, state = forward_mid(me, lat, lat.T, gathered, w1, b1, w2, b2)
    cot_spec, image = list(cot_spec), list(image)
    falling = range(owners - 1, 0, -1)
    send(cot_spec, falling[:FIRST], cot_gathered)
    cot_spec, image = waiting((cot_spec, image), [image[0]])
    send(cot_spec, falling[FIRST:], cot_gathered)

    image_band = {0: image[0]}
    send(image, order, image_band)
    cot_gathered = listed(cot_gathered)
    grad_image, sums = backward_mid(
        me, lat, lat.T, cot_gathered, w1, b1, w2, b2, state, count
    )
    early = [image_band[offset] for offset in order[:HELD]]
    late = [image_band[offset] for offset in order[HELD:]]
    grad_image, sums = waiting((list(grad_image), sums), early)
    group_sum = GroupSum(sums)
    group_sum.over_dp()
    group_sum.over_next(late[:2])
    grad_band = {0: grad_image[0]}
    send(grad_image, order, grad_band)
    arrived = [grad_band[offset] for offset in order]
    image_band = listed(image_band)
    grad_band = listed(grad_band)
    again = waiting(fields, early[:1])
    output = rows_inside(to_cells(me, scaled.T, image_band, again))
    group_sum.scatter(late[2:] + arrived[:1])
    group_sum.gather(arrived[1:3])
    group_sum.quarter, output = lax.optimization_barrier((group_sum.quarter, output))
    group_sum.gather_next(arrived[3:5])
    half, other = group_sum.gather_dp(arrived[5:])
    near = lax.axis_index("space")
    here = jnp.stack([lax.axis_index("dp"), near % 2, near // 2]).astype(jnp.int32)
    grads = finish_sums(here, half, other, factor, w_first.shape, b_first.shape)
    grad_fields = rows_inside(to_cells(me, plain.T, grad_band, cotangent))
    return (rows_outside(output), rows_outside(grad_fields)) + tuple(grads)


def solution(mesh):
    split = P(("parts", "dp"), "space", None, None)
    in_specs = (split, split, P(), P(), P(), P())
    out_specs = (
        split,
        split,
        P("parts", None, None, None),
        P("parts", None, None),
        P("parts", None, None, None),
        P("parts", None, None),
    )
    return jax.shard_map(body, mesh=mesh, in_specs=in_specs, out_specs=out_specs, check_vma=False)
```

```python
import functools
import math

import jax
import jax.numpy as jnp
from jax import lax
from jax.experimental import pallas as pl
from jax.experimental.layout import Layout, with_layout_constraint
from jax.experimental.pallas import tpu as pltpu
from jax.sharding import PartitionSpec as P
import ml_dtypes
import numpy as np

KW = 64
shrink_level = 0.05
FIRST = 5
HELD = 5
MIB = 1024 * 1024


def product_of(former, latter):
    return jnp.dot(former, latter, preferred_element_type=jnp.float32)


def lon_tables(mode_count, cell_count, owners):
    wavenums = np.arange(mode_count, dtype=np.int32)
    columns = np.arange(cell_count, dtype=np.int32)
    phase_index = (wavenums[:, None] * columns[None, :] % cell_count).astype(np.float32)
    phases = phase_index * np.float32(2.0 * math.pi / cell_count)
    factor = np.float32(1.0 / math.sqrt(cell_count))
    forward = np.stack([np.cos(phases) * factor, -np.sin(phases) * factor])
    scaled = forward * np.where(wavenums == 0, 1.0, 2.0).astype(np.float32)[:, None]

    def ordered(table):
        split = table.reshape(2, owners, -1, cell_count).transpose(1, 0, 2, 3)
        return split.reshape(-1, cell_count).astype(ml_dtypes.bfloat16)

    return ordered(forward), ordered(scaled)


def lat_spread(row_count, modes):
    indices = np.arange(row_count, dtype=np.int32)
    phase_index = (indices[:, None] * indices[None, :] % row_count).astype(np.float32)
    phases = phase_index * np.float32(2.0 * math.pi / row_count)
    factor = np.float32(1.0 / math.sqrt(row_count))
    cosine = np.cos(phases) * factor
    sine_part = np.sin(phases) * factor
    table = np.stack([np.stack([cosine, sine_part], -1), np.stack([-sine_part, cosine], -1)])
    same = np.eye(modes, dtype=np.float32)
    spread = table[:, :, None, :, :, None] * same[None, None, :, None, None, :]
    size = 2 * row_count * modes
    return spread.reshape(size, size).astype(ml_dtypes.bfloat16)


def block_bias(bias, groups):
    return jnp.transpose(bias.reshape(2, groups, 1, -1), (1, 2, 0, 3)).reshape(groups, 1, -1)


def spread_kernel(*refs):
    half_way = len(refs) // 2
    for blocks_ref, joined_ref in zip(refs[:half_way], refs[half_way:]):
        _, per, size, _ = blocks_ref.shape
        width = per * size
        row = lax.broadcasted_iota(jnp.int32, (size, width), 0)
        lane = lax.broadcasted_iota(jnp.int32, (size, width), 1)
        for block in range(per):
            place = (row + block * size == lane).astype(jnp.bfloat16)
            real = product_of(blocks_ref[0, block], place).astype(jnp.bfloat16)
            imag = product_of(blocks_ref[1, block], place)
            upper = pl.ds(block * size, size)
            lower = pl.ds(width + block * size, size)
            joined_ref[0, upper, 0:width] = real
            joined_ref[0, upper, width : 2 * width] = imag.astype(jnp.bfloat16)
            joined_ref[0, lower, 0:width] = (-imag).astype(jnp.bfloat16)
            joined_ref[0, lower, width : 2 * width] = real


def spread_weights(groups, *weights):
    _, count, size, _ = weights[0].shape
    per = count // groups
    lanes = 2 * per * size
    shape = in_hbm((groups, lanes, lanes), jnp.bfloat16)
    return pl.pallas_call(
        spread_kernel,
        grid=(groups,),
        out_shape=(shape,) * len(weights),
        in_specs=[pl.BlockSpec((2, per, size, size), lambda g: (0, g, 0, 0))] * len(weights),
        out_specs=(group_spec(lanes, lanes),) * len(weights),
        compiler_params=params(12),
        cost_estimate=pl.CostEstimate(
            flops=len(weights) * 2 * count * size * size * lanes,
            bytes_accessed=len(weights) * 2 * groups * lanes * lanes,
            transcendentals=0,
        ),
        name="spread_weights",
    )(*weights)


def params(mebibytes):
    return pltpu.CompilerParams(
        vmem_limit_bytes=mebibytes * MIB, dimension_semantics=("arbitrary",)
    )


def place_of(me_ref, offset, rows):
    return pl.ds(pl.multiple_of((me_ref[0] ^ offset) * rows, rows), rows)


def in_hbm(shape, dtype):
    return pltpu.HBM(shape, dtype)


def hbm(*arrays):
    return [pltpu.with_memory_space_constraint(array, pltpu.HBM) for array in arrays]


def with_offsets(refs):
    return [((len(refs) - place) % len(refs), ref) for place, ref in enumerate(refs)]


def to_modes_kernel(me_ref, table_ref, cells_ref, *refs):
    modes_refs, held_ref = refs[:-1], refs[-1]
    rows = cells_ref.shape[1]
    share = modes_refs[0].shape[0] // rows
    for row in range(rows):
        spectrum = product_of(table_ref[...], cells_ref[0, row])
        held_ref[row] = spectrum.astype(jnp.bfloat16)
        for offset, modes_ref in with_offsets(modes_refs):
            modes_ref[pl.ds(row * share, share)] = held_ref[row, place_of(me_ref, offset, share)]


def to_modes(me, table, cells, owners):
    samples, rows, width, channels = cells.shape
    size = table.shape[0]
    part = rows * size // owners
    return pl.pallas_call(
        to_modes_kernel,
        grid_spec=pltpu.PrefetchScalarGridSpec(
            num_scalar_prefetch=1,
            grid=(samples,),
            in_specs=[
                pl.BlockSpec((size, width), lambda b, _: (0, 0)),
                pl.BlockSpec((1, rows, width, channels), lambda b, _: (b, 0, 0, 0)),
            ],
            out_specs=(pl.BlockSpec((part, channels), lambda b, _: (b, 0)),) * owners,
            scratch_shapes=[pltpu.VMEM((rows, size, channels), jnp.bfloat16)],
        ),
        out_shape=(in_hbm((samples * part, channels), jnp.bfloat16),) * owners,
        compiler_params=params(12),
        cost_estimate=pl.CostEstimate(
            flops=2 * samples * rows * size * width * channels,
            bytes_accessed=2 * samples * rows * channels * (width + size),
            transcendentals=0,
        ),
        name="to_modes",
    )(me, table, cells)


def to_cells_kernel(me_ref, table_ref, base_ref, *refs):
    modes_refs, out_ref, held_ref = refs[:-2], refs[-2], refs[-1]
    rows = base_ref.shape[1]
    share = modes_refs[0].shape[-2] // rows
    for row in range(rows):
        run = pl.ds(row * share, share)
        if len(modes_refs) == 1:
            spectrum = modes_refs[0][:, run].reshape(held_ref.shape[1:])
        else:
            for offset, modes_ref in with_offsets(modes_refs):
                held_ref[row, place_of(me_ref, offset, share)] = modes_ref[run]
            spectrum = held_ref[row]
        image = product_of(table_ref[...], spectrum)
        out_ref[0, row] = (base_ref[0, row].astype(jnp.float32) + image).astype(jnp.bfloat16)


def to_cells(me, table, modes, base):
    samples, rows, width, channels = base.shape
    size = table.shape[1]
    block = pl.BlockSpec((1, rows, width, channels), lambda b, _: (b, 0, 0, 0))
    if len(modes) == 1:
        lead = modes[0].shape[0]
        part = rows * size // lead
        specs = [pl.BlockSpec((lead, part, channels), lambda b, _: (0, b, 0))]
    else:
        part = rows * size // len(modes)
        specs = [pl.BlockSpec((part, channels), lambda b, _: (b, 0))] * len(modes)
    return pl.pallas_call(
        to_cells_kernel,
        grid_spec=pltpu.PrefetchScalarGridSpec(
            num_scalar_prefetch=1,
            grid=(samples,),
            in_specs=[pl.BlockSpec((width, size), lambda b, _: (0, 0)), block] + specs,
            out_specs=block,
            scratch_shapes=[pltpu.VMEM((rows, size, channels), jnp.bfloat16)],
        ),
        out_shape=jax.ShapeDtypeStruct(base.shape, jnp.bfloat16),
        compiler_params=params(12),
        cost_estimate=pl.CostEstimate(
            flops=2 * samples * rows * size * width * channels,
            bytes_accessed=2 * samples * rows * channels * (2 * width + size),
            transcendentals=0,
        ),
        name="to_cells",
    )(me, table, base, *hbm(*modes))


def rows_inside(cells):
    inside = jnp.transpose(cells, (0, 2, 1, 3))
    return with_layout_constraint(inside, Layout(major_to_minor=(0, 1, 2, 3)))


def rows_outside(cells):
    return jnp.transpose(cells, (0, 2, 1, 3))


def sigmoid_of(values):
    return 0.5 + 0.5 * jnp.tanh(0.5 * values)


def mix_lat(me_ref, table_ref, bands_refs, band_ref, mixed_ref):
    samples, size, width = band_ref.shape
    part, half = size // len(bands_refs), size // 2
    for sample in range(samples):
        for offset, bands_ref in with_offsets(bands_refs):
            place = place_of(me_ref, offset, part)
            band_ref[sample, place] = bands_ref[pl.ds(sample * part, part)]
        mixed = product_of(table_ref[...], band_ref[sample]).astype(jnp.bfloat16)
        spot = pl.ds(sample * half, half)
        mixed_ref[spot, 0:width] = mixed[:half]
        mixed_ref[spot, width : 2 * width] = mixed[half:]


def unmix_lat(me_ref, table_ref, mixed_ref, band_ref, bands_refs):
    samples, size, width = band_ref.shape
    part, half = size // len(bands_refs), size // 2
    for sample in range(samples):
        spot = pl.ds(sample * half, half)
        joined = jnp.concatenate(
            [mixed_ref[spot, 0:width], mixed_ref[spot, width : 2 * width]], axis=0
        )
        bands = product_of(table_ref[...], joined).astype(jnp.bfloat16)
        if len(bands_refs) == 1:
            lead = bands_refs[0].shape[0]
            run = pl.ds(sample * size // lead, size // lead)
            bands_refs[0][:, run] = bands.reshape(lead, size // lead, width)
        else:
            band_ref[sample] = bands
            for offset, bands_ref in with_offsets(bands_refs):
                place = place_of(me_ref, offset, part)
                bands_ref[pl.ds(sample * part, part)] = band_ref[sample, place]


def activate(mixed_ref, w1_ref, b1_ref):
    pre = product_of(mixed_ref[0], w1_ref[0]) + b1_ref[0]
    logistic = sigmoid_of(pre)
    return logistic, pre * logistic


def bend(act_ref, w2_ref, b2_ref):
    out = product_of(act_ref[...], w2_ref[0]) + b2_ref[0]
    return out, jnp.tanh(out * (1.0 / shrink_level))


def forward_kernel(blocks, me_ref, lat_ref, unlat_ref, w1_ref, b1_ref, w2_ref, b2_ref, *refs):
    bands_refs, image_refs = refs[:blocks], refs[blocks : 2 * blocks]
    mixed_ref, act_ref, band_ref = refs[2 * blocks :]
    mix_lat(me_ref, lat_ref, bands_refs, band_ref, mixed_ref.at[0])
    act_ref[...] = activate(mixed_ref, w1_ref, b1_ref)[1].astype(jnp.bfloat16)
    out, bent = bend(act_ref, w2_ref, b2_ref)
    act_ref[...] = (out - shrink_level * bent).astype(jnp.bfloat16)
    unmix_lat(me_ref, unlat_ref, act_ref, band_ref, image_refs)


def backward_kernel(
    block_size, blocks, me_ref, lat_ref, unlat_ref, w1_ref, b1_ref, w2_ref, b2_ref, mixed_ref, *refs
):
    bands_refs, image_refs = refs[:blocks], refs[blocks : 2 * blocks]
    sums_ref, act_ref, gate_ref, cot_ref, kept_ref, band_ref = refs[2 * blocks :]
    transposed = (((1,), (1,)), ((), ()))
    summed = (((0,), (0,)), ((), ()))

    def times(former, latter, dims):
        return lax.dot_general(former, latter, dims, preferred_element_type=jnp.float32)

    def weight_sums(acts, grads, slot):
        width = acts.shape[1] // 2
        full = times(acts, grads, summed)
        real = full[:width, :width] + full[width:, width:]
        imag = full[:width, width:] - full[width:, :width]
        bias = jnp.sum(grads.astype(jnp.float32), axis=0, keepdims=True)
        size = block_size
        owner = lax.broadcasted_iota(jnp.int32, (size, width), 1) // size
        extra = sums_ref.shape[2] - size
        first = lax.broadcasted_iota(jnp.int32, (extra, width), 0) == 0
        for part, values in enumerate((real, imag)):
            joined = values[:size]
            for block in range(1, width // size):
                joined = jnp.where(owner == block, values[block * size : (block + 1) * size], joined)
            sums_ref[slot, part, 0:size] = joined.astype(sums_ref.dtype)
            row = bias[:, part * width : (part + 1) * width]
            sums_ref[slot, part, size:] = jnp.where(first, row, 0.0).astype(sums_ref.dtype)

    logistic, act = activate(mixed_ref, w1_ref, b1_ref)
    act_ref[...] = act.astype(jnp.bfloat16)
    gate_ref[...] = logistic + act * (1.0 - logistic)
    mix_lat(me_ref, lat_ref, bands_refs, band_ref, cot_ref)
    _, bent = bend(act_ref, w2_ref, b2_ref)
    kept_ref[...] = (cot_ref[...].astype(jnp.float32) * (bent * bent)).astype(jnp.bfloat16)
    back = times(kept_ref[...], w2_ref[0], transposed)
    cot_ref[...] = (back * gate_ref[...]).astype(jnp.bfloat16)
    weight_sums(act_ref[...], kept_ref[...], 1)
    kept_ref[...] = times(cot_ref[...], w1_ref[0], transposed).astype(jnp.bfloat16)
    weight_sums(mixed_ref[0], cot_ref[...], 0)
    unmix_lat(me_ref, unlat_ref, kept_ref, band_ref, image_refs)


def group_spec(*shape):
    return pl.BlockSpec((1,) + shape, lambda g, *_: (g,) + (0,) * len(shape))


def bands_specs(rows, bands, groups):
    block = (rows, bands[0].shape[1] // groups)
    return (pl.BlockSpec(block, lambda g, *_: (0, g)),) * len(bands)


def images_like(bands, samples, size, groups):
    if len(bands) > 1:
        shapes = tuple(in_hbm(band.shape, band.dtype) for band in bands)
        return shapes, bands_specs(bands[0].shape[0], bands, groups)
    channels = bands[0].shape[1]
    shape = (1, samples * size, channels)
    spec = pl.BlockSpec(shape[:2] + (channels // groups,), lambda g, *_: (0, 0, g))
    return (in_hbm(shape, jnp.bfloat16),), (spec,)


def forward_mid(me, lat, unlat, bands, w1, b1, w2, b2):
    groups, lanes, _ = w1.shape
    size = lat.shape[0]
    samples = bands[0].shape[0] * len(bands) // size
    positions = samples * size // 2
    table = pl.BlockSpec((size, size), lambda g, _: (0, 0))
    state = (groups, positions, lanes)
    specs = bands_specs(bands[0].shape[0], bands, groups)
    images, image_specs = images_like(bands, samples, size, groups)
    results = pl.pallas_call(
        functools.partial(forward_kernel, len(bands)),
        grid_spec=pltpu.PrefetchScalarGridSpec(
            num_scalar_prefetch=1,
            grid=(groups,),
            in_specs=[
                table, table,
                group_spec(lanes, lanes), group_spec(1, lanes),
                group_spec(lanes, lanes), group_spec(1, lanes),
                *specs,
            ],
            out_specs=image_specs + (group_spec(positions, lanes),),
            scratch_shapes=[
                pltpu.VMEM((positions, lanes), jnp.bfloat16),
                pltpu.VMEM((samples, size, lanes // 2), jnp.bfloat16),
            ],
        ),
        out_shape=images + (in_hbm(state, jnp.bfloat16),),
        compiler_params=params(28),
        cost_estimate=pl.CostEstimate(
            flops=4 * groups * positions * lanes * lanes,
            bytes_accessed=16 * groups * positions * lanes + 4 * groups * lanes * lanes,
            transcendentals=2 * groups * positions * lanes,
        ),
        name="mix_forward",
    )(me, lat, unlat, *hbm(w1), b1, *hbm(w2), b2, *hbm(*bands))
    return results[: len(bands)], results[len(bands)]


def backward_mid(me, lat, unlat, bands, w1, b1, w2, b2, state, count):
    groups, lanes, _ = w1.shape
    size = lat.shape[0]
    samples = bands[0].shape[0] * len(bands) // size
    positions = samples * size // 2
    table = pl.BlockSpec((size, size), lambda g, _: (0, 0))
    size_of_block = lanes // 2 // (count // groups)
    sums = (2, 2, size_of_block + 32, lanes // 2)
    images, image_specs = images_like(bands, samples, size, groups)
    results = pl.pallas_call(
        functools.partial(backward_kernel, size_of_block, len(bands)),
        grid_spec=pltpu.PrefetchScalarGridSpec(
            num_scalar_prefetch=1,
            grid=(groups,),
            in_specs=[
                table, table,
                group_spec(lanes, lanes), group_spec(1, lanes),
                group_spec(lanes, lanes), group_spec(1, lanes),
                group_spec(positions, lanes),
                *bands_specs(bands[0].shape[0], bands, groups),
            ],
            out_specs=image_specs + (pl.BlockSpec(sums, lambda g, _: (0, 0, 0, g)),),
            scratch_shapes=[
                pltpu.VMEM((positions, lanes), jnp.bfloat16),
                pltpu.VMEM((positions, lanes), jnp.float32),
                pltpu.VMEM((positions, lanes), jnp.bfloat16),
                pltpu.VMEM((positions, lanes), jnp.bfloat16),
                pltpu.VMEM((samples, size, lanes // 2), jnp.bfloat16),
            ],
        ),
        out_shape=images + (in_hbm(sums[:3] + (groups * sums[3],), jnp.float32),),
        compiler_params=params(32),
        cost_estimate=pl.CostEstimate(
            flops=8 * groups * positions * lanes * lanes,
            bytes_accessed=16 * groups * positions * lanes + 4 * groups * lanes * lanes,
            transcendentals=0,
        ),
        name="mix_backward",
    )(me, lat, unlat, *hbm(w1), b1, *hbm(w2), b2, *hbm(state, *bands))
    return results[: len(bands)], results[len(bands)]


def swap_with(values, axis, distance):
    pairs = [(i, i ^ distance) for i in range(lax.axis_size(axis))]
    return lax.ppermute(values, axis, pairs)


def waiting(values, arrived):
    return lax.optimization_barrier((values, tuple(arrived)))[0]


def mixed_order(size):
    far = list(range(size // 2, size))
    near = [offset for offset in (2, 3, 1) if offset < size // 2]
    near += list(range(4, size // 2))
    order = []
    while far or near:
        order += far[:1] + near[:1]
        far, near = far[1:], near[1:]
    return order


def pick(pair, side):
    return lax.dynamic_index_in_dim(pair, side, 0, keepdims=False)


class GroupSum:
    def __init__(self, sums):
        self.lanes = sums.shape[-1]
        self.side = lax.axis_index("dp")
        self.me = lax.axis_index("space")
        self.count = lax.axis_size("space") // 2
        self.held = sums.reshape(-1, self.lanes)

    def halve(self, axis, distance, bit, kind, arrived):
        pair = waiting(self.held, arrived).reshape(2, -1, self.lanes)
        taken = swap_with(pick(pair, 1 - bit).astype(kind), axis, distance)
        self.held = pick(pair, bit) + taken.astype(jnp.float32)

    def over_dp(self):
        self.halve("dp", 1, self.side, jnp.float32, [])

    def over_next(self, arrived):
        self.halve("space", 1, self.me % 2, jnp.bfloat16, arrived)

    def scatter(self, arrived):
        shares = waiting(self.held, arrived).reshape(self.count, -1, self.lanes)
        place = self.me // 2
        total = pick(shares, place)
        for offset in range(1, self.count):
            given = pick(shares, place ^ offset).astype(jnp.bfloat16)
            total += swap_with(given, "space", 2 * offset).astype(jnp.float32)
        self.total = total.astype(jnp.bfloat16)

    def gather(self, arrived):
        total = waiting(self.total, arrived)
        taken = [total]
        for offset in range(1, self.count):
            taken.append(swap_with(total, "space", 2 * offset))
        self.quarter = jnp.stack(taken)

    def gather_next(self, arrived):
        quarter = waiting(self.quarter, arrived)
        self.half = jnp.stack([quarter, swap_with(quarter, "space", 1)])

    def gather_dp(self, arrived):
        half = waiting(self.half, arrived)
        return half, swap_with(half, "dp", 1)


def finish_kernel(factor, me_ref, half_ref, other_ref, *out_refs):
    side, near, place = me_ref[0], me_ref[1], me_ref[2]
    run = half_ref.shape[2]
    for which in range(2):
        blocks_ref, bias_ref = out_refs[2 * which : 2 * which + 2]
        edge = blocks_ref.shape[-1]
        for part in range(2):
            for piece in range(half_ref.shape[1]):
                spot = (part ^ near, piece ^ place)
                own = half_ref[spot].astype(jnp.float32)
                value = jnp.where(side == which, own, other_ref[spot].astype(jnp.float32)) * factor
                first = piece * run
                count = max(0, min(edge - first, run))
                for block in range(blocks_ref.shape[1]):
                    lanes = slice(block * edge, (block + 1) * edge)
                    if count > 0:
                        blocks_ref[part, block, pl.ds(first, count)] = value[:count, lanes]
                    if first <= edge < first + run:
                        row = edge - first
                        bias_ref[part, pl.ds(block, 1)] = value[row : row + 1, lanes]


def finish_sums(here, half, other, factor, weight_shape, bias_shape):
    outs = [weight_shape, bias_shape] * 2
    return pl.pallas_call(
        functools.partial(finish_kernel, factor),
        out_shape=[jax.ShapeDtypeStruct(shape, jnp.float32) for shape in outs],
        in_specs=[pl.BlockSpec(memory_space=pltpu.SMEM)]
        + [pl.BlockSpec(memory_space=pltpu.VMEM)] * 2,
        out_specs=[pl.BlockSpec(memory_space=pltpu.VMEM)] * 4,
        compiler_params=pltpu.CompilerParams(vmem_limit_bytes=16 * MIB),
        cost_estimate=pl.CostEstimate(flops=0, bytes_accessed=4 * MIB, transcendentals=0),
        name="finish_sums",
    )(here, half, other)


def body(fields, cotangent, w_first, b_first, w_second, b_second):
    samples, rows, width, channels = fields.shape
    owners = lax.axis_size("space")
    lat_total = rows * owners
    modes = KW // owners
    count, edge = w_first.shape[1:3]
    groups = 2
    direct = 2 * modes % 16 == 0
    lead = owners if direct else 1

    order = mixed_order(owners)

    def place(offset):
        return (owners - offset) % owners

    def send(blocks, offsets, taken):
        for offset in offsets:
            taken[offset] = swap_with(blocks[place(offset)], "space", offset)

    def listed(taken):
        return [taken[place(at)] for at in range(owners)]

    def send_all(spectrum):
        spectrum = spectrum.reshape(samples, rows, owners, 2 * modes, channels)
        spectrum = jnp.transpose(spectrum, (2, 0, 1, 3, 4))
        arrived = lax.all_to_all(spectrum, "space", split_axis=0, concat_axis=0, tiled=True)
        return [jnp.transpose(arrived, (1, 0, 2, 3, 4)).reshape(-1, channels)]

    def send_all_back(bands):
        bands = bands.reshape(samples, owners, rows, 2 * modes, channels)
        bands = jnp.transpose(bands, (1, 0, 2, 3, 4))
        arrived = lax.all_to_all(bands, "space", split_axis=0, concat_axis=0, tiled=True)
        return [jnp.transpose(arrived, (1, 2, 0, 3, 4)).reshape(1, -1, channels)]

    me = lax.axis_index("space") if direct else 0
    me = jnp.full((1,), me, jnp.int32)
    plain, scaled = lon_tables(KW, width, owners)
    lat = lat_spread(lat_total, modes)

    spectrum = to_modes(me, plain, fields, lead)
    spectrum, cotangent, w_first, w_second = lax.optimization_barrier(
        (spectrum, cotangent, w_first, w_second)
    )
    cot_spec = to_modes(me, scaled, cotangent, lead)
    w1, w2 = spread_weights(groups, w_first, w_second)
    b1, b2 = block_bias(b_first, groups), block_bias(b_second, groups)
    positions = samples * lax.axis_size("dp") * lat_total * KW
    factor = 1.0 / math.sqrt(positions)

    if not direct:
        gathered = send_all(spectrum[0])
        image, state = forward_mid(me, lat, lat.T, gathered, w1, b1, w2, b2)
        image_band = send_all_back(image[0])
        gathered = send_all(cot_spec[0])
        grad_image, sums = backward_mid(me, lat, lat.T, gathered, w1, b1, w2, b2, state, count)
        grad_band = send_all_back(grad_image[0])
        output = to_cells(me, scaled.T, image_band, fields)
        grad_fields = to_cells(me, plain.T, grad_band, cotangent)
        sums = lax.psum(sums, ("space", "dp")) * factor
        grads = []
        for which in range(2):
            blocks = sums[which, :, :edge].reshape(2, edge, count, edge)
            grads.append(jnp.transpose(blocks, (0, 2, 1, 3)))
            grads.append(sums[which, :, edge].reshape(b_first.shape))
        return (output, grad_fields) + tuple(grads)

    gathered, cot_gathered = {0: spectrum[0]}, {0: cot_spec[0]}
    send(spectrum, order, gathered)
    gathered = listed(gathered)
    image, state = forward_mid(me, lat, lat.T, gathered, w1, b1, w2, b2)
    cot_spec, image = list(cot_spec), list(image)
    falling = range(owners - 1, 0, -1)
    send(cot_spec, falling[:FIRST], cot_gathered)
    cot_spec, image = waiting((cot_spec, image), [image[0]])
    send(cot_spec, falling[FIRST:], cot_gathered)

    image_band = {0: image[0]}
    send(image, order, image_band)
    cot_gathered = listed(cot_gathered)
    grad_image, sums = backward_mid(
        me, lat, lat.T, cot_gathered, w1, b1, w2, b2, state, count
    )
    early = [image_band[offset] for offset in order[:HELD]]
    late = [image_band[offset] for offset in order[HELD:]]
    grad_image, sums = waiting((list(grad_image), sums), early)
    group_sum = GroupSum(sums)
    group_sum.over_dp()
    group_sum.over_next(late[:1])
    grad_band = {0: grad_image[0]}
    send(grad_image, order, grad_band)
    arrived = [grad_band[offset] for offset in order]
    image_band = listed(image_band)
    grad_band = listed(grad_band)
    again = waiting(fields, early[:1])
    output = rows_inside(to_cells(me, scaled.T, image_band, again))
    group_sum.scatter(late[1:] + arrived[:1])
    group_sum.gather(arrived[1:3])
    group_sum.quarter, output = lax.optimization_barrier((group_sum.quarter, output))
    group_sum.gather_next(arrived[3:6])
    half, other = group_sum.gather_dp(arrived[6:])
    near = lax.axis_index("space")
    here = jnp.stack([lax.axis_index("dp"), near % 2, near // 2]).astype(jnp.int32)
    grads = finish_sums(here, half, other, factor, w_first.shape, b_first.shape)
    grad_fields = rows_inside(to_cells(me, plain.T, grad_band, cotangent))
    return (rows_outside(output), rows_outside(grad_fields)) + tuple(grads)


def solution(mesh):
    split = P(("parts", "dp"), "space", None, None)
    in_specs = (split, split, P(), P(), P(), P())
    out_specs = (
        split,
        split,
        P("parts", None, None, None),
        P("parts", None, None),
        P("parts", None, None, None),
        P("parts", None, None),
    )
    return jax.shard_map(body, mesh=mesh, in_specs=in_specs, out_specs=out_specs, check_vma=False)
```

```python
import functools
import math

import jax
import jax.numpy as jnp
from jax import lax
from jax.experimental import pallas as pl
from jax.experimental.layout import Layout, with_layout_constraint
from jax.experimental.pallas import tpu as pltpu
from jax.sharding import PartitionSpec as P
import ml_dtypes
import numpy as np

KW = 64
shrink_level = 0.05
FIRST = 5
HELD = 5
MIB = 1024 * 1024


def product_of(former, latter):
    return jnp.dot(former, latter, preferred_element_type=jnp.float32)


def lon_tables(mode_count, cell_count, owners):
    wavenums = np.arange(mode_count, dtype=np.int32)
    columns = np.arange(cell_count, dtype=np.int32)
    phase_index = (wavenums[:, None] * columns[None, :] % cell_count).astype(np.float32)
    phases = phase_index * np.float32(2.0 * math.pi / cell_count)
    factor = np.float32(1.0 / math.sqrt(cell_count))
    forward = np.stack([np.cos(phases) * factor, -np.sin(phases) * factor])
    scaled = forward * np.where(wavenums == 0, 1.0, 2.0).astype(np.float32)[:, None]

    def ordered(table):
        split = table.reshape(2, owners, -1, cell_count).transpose(1, 0, 2, 3)
        return split.reshape(-1, cell_count).astype(ml_dtypes.bfloat16)

    return ordered(forward), ordered(scaled)


def lat_spread(row_count, modes):
    indices = np.arange(row_count, dtype=np.int32)
    phase_index = (indices[:, None] * indices[None, :] % row_count).astype(np.float32)
    phases = phase_index * np.float32(2.0 * math.pi / row_count)
    factor = np.float32(1.0 / math.sqrt(row_count))
    cosine = np.cos(phases) * factor
    sine_part = np.sin(phases) * factor
    table = np.stack([np.stack([cosine, sine_part], -1), np.stack([-sine_part, cosine], -1)])
    same = np.eye(modes, dtype=np.float32)
    spread = table[:, :, None, :, :, None] * same[None, None, :, None, None, :]
    size = 2 * row_count * modes
    return spread.reshape(size, size).astype(ml_dtypes.bfloat16)


def block_bias(bias, groups):
    return jnp.transpose(bias.reshape(2, groups, 1, -1), (1, 2, 0, 3)).reshape(groups, 1, -1)


def spread_kernel(*refs):
    half_way = len(refs) // 2
    for blocks_ref, joined_ref in zip(refs[:half_way], refs[half_way:]):
        _, per, size, _ = blocks_ref.shape
        width = per * size
        row = lax.broadcasted_iota(jnp.int32, (size, width), 0)
        lane = lax.broadcasted_iota(jnp.int32, (size, width), 1)
        for block in range(per):
            place = (row + block * size == lane).astype(jnp.bfloat16)
            real = product_of(blocks_ref[0, block], place).astype(jnp.bfloat16)
            imag = product_of(blocks_ref[1, block], place)
            upper = pl.ds(block * size, size)
            lower = pl.ds(width + block * size, size)
            joined_ref[0, upper, 0:width] = real
            joined_ref[0, upper, width : 2 * width] = imag.astype(jnp.bfloat16)
            joined_ref[0, lower, 0:width] = (-imag).astype(jnp.bfloat16)
            joined_ref[0, lower, width : 2 * width] = real


def spread_weights(groups, *weights):
    _, count, size, _ = weights[0].shape
    per = count // groups
    lanes = 2 * per * size
    shape = in_hbm((groups, lanes, lanes), jnp.bfloat16)
    return pl.pallas_call(
        spread_kernel,
        grid=(groups,),
        out_shape=(shape,) * len(weights),
        in_specs=[pl.BlockSpec((2, per, size, size), lambda g: (0, g, 0, 0))] * len(weights),
        out_specs=(group_spec(lanes, lanes),) * len(weights),
        compiler_params=params(12),
        cost_estimate=pl.CostEstimate(
            flops=len(weights) * 2 * count * size * size * lanes,
            bytes_accessed=len(weights) * 2 * groups * lanes * lanes,
            transcendentals=0,
        ),
        name="spread_weights",
    )(*weights)


def params(mebibytes):
    return pltpu.CompilerParams(
        vmem_limit_bytes=mebibytes * MIB, dimension_semantics=("arbitrary",)
    )


def place_of(me_ref, offset, rows):
    return pl.ds(pl.multiple_of((me_ref[0] ^ offset) * rows, rows), rows)


def in_hbm(shape, dtype):
    return pltpu.HBM(shape, dtype)


def hbm(*arrays):
    return [pltpu.with_memory_space_constraint(array, pltpu.HBM) for array in arrays]


def with_offsets(refs):
    return [((len(refs) - place) % len(refs), ref) for place, ref in enumerate(refs)]


def to_modes_kernel(me_ref, table_ref, cells_ref, *refs):
    modes_refs, held_ref = refs[:-1], refs[-1]
    rows = cells_ref.shape[1]
    share = modes_refs[0].shape[0] // rows
    for row in range(rows):
        spectrum = product_of(table_ref[...], cells_ref[0, row])
        held_ref[row] = spectrum.astype(jnp.bfloat16)
        for offset, modes_ref in with_offsets(modes_refs):
            modes_ref[pl.ds(row * share, share)] = held_ref[row, place_of(me_ref, offset, share)]


def to_modes(me, table, cells, owners):
    samples, rows, width, channels = cells.shape
    size = table.shape[0]
    part = rows * size // owners
    return pl.pallas_call(
        to_modes_kernel,
        grid_spec=pltpu.PrefetchScalarGridSpec(
            num_scalar_prefetch=1,
            grid=(samples,),
            in_specs=[
                pl.BlockSpec((size, width), lambda b, _: (0, 0)),
                pl.BlockSpec((1, rows, width, channels), lambda b, _: (b, 0, 0, 0)),
            ],
            out_specs=(pl.BlockSpec((part, channels), lambda b, _: (b, 0)),) * owners,
            scratch_shapes=[pltpu.VMEM((rows, size, channels), jnp.bfloat16)],
        ),
        out_shape=(in_hbm((samples * part, channels), jnp.bfloat16),) * owners,
        compiler_params=params(12),
        cost_estimate=pl.CostEstimate(
            flops=2 * samples * rows * size * width * channels,
            bytes_accessed=2 * samples * rows * channels * (width + size),
            transcendentals=0,
        ),
        name="to_modes",
    )(me, table, cells)


def to_cells_kernel(me_ref, table_ref, base_ref, *refs):
    modes_refs, out_ref, held_ref = refs[:-2], refs[-2], refs[-1]
    rows = base_ref.shape[1]
    share = modes_refs[0].shape[-2] // rows
    for row in range(rows):
        run = pl.ds(row * share, share)
        if len(modes_refs) == 1:
            spectrum = modes_refs[0][:, run].reshape(held_ref.shape[1:])
        else:
            for offset, modes_ref in with_offsets(modes_refs):
                held_ref[row, place_of(me_ref, offset, share)] = modes_ref[run]
            spectrum = held_ref[row]
        image = product_of(table_ref[...], spectrum)
        out_ref[0, row] = (base_ref[0, row].astype(jnp.float32) + image).astype(jnp.bfloat16)


def to_cells(me, table, modes, base):
    samples, rows, width, channels = base.shape
    size = table.shape[1]
    block = pl.BlockSpec((1, rows, width, channels), lambda b, _: (b, 0, 0, 0))
    if len(modes) == 1:
        lead = modes[0].shape[0]
        part = rows * size // lead
        specs = [pl.BlockSpec((lead, part, channels), lambda b, _: (0, b, 0))]
    else:
        part = rows * size // len(modes)
        specs = [pl.BlockSpec((part, channels), lambda b, _: (b, 0))] * len(modes)
    return pl.pallas_call(
        to_cells_kernel,
        grid_spec=pltpu.PrefetchScalarGridSpec(
            num_scalar_prefetch=1,
            grid=(samples,),
            in_specs=[pl.BlockSpec((width, size), lambda b, _: (0, 0)), block] + specs,
            out_specs=block,
            scratch_shapes=[pltpu.VMEM((rows, size, channels), jnp.bfloat16)],
        ),
        out_shape=jax.ShapeDtypeStruct(base.shape, jnp.bfloat16),
        compiler_params=params(12),
        cost_estimate=pl.CostEstimate(
            flops=2 * samples * rows * size * width * channels,
            bytes_accessed=2 * samples * rows * channels * (2 * width + size),
            transcendentals=0,
        ),
        name="to_cells",
    )(me, table, base, *hbm(*modes))


def rows_inside(cells):
    inside = jnp.transpose(cells, (0, 2, 1, 3))
    return with_layout_constraint(inside, Layout(major_to_minor=(0, 1, 2, 3)))


def rows_outside(cells):
    return jnp.transpose(cells, (0, 2, 1, 3))


def sigmoid_of(values):
    return 0.5 + 0.5 * jnp.tanh(0.5 * values)


def mix_lat(me_ref, table_ref, bands_refs, band_ref, mixed_ref):
    samples, size, width = band_ref.shape
    part, half = size // len(bands_refs), size // 2
    for sample in range(samples):
        for offset, bands_ref in with_offsets(bands_refs):
            place = place_of(me_ref, offset, part)
            band_ref[sample, place] = bands_ref[pl.ds(sample * part, part)]
        mixed = product_of(table_ref[...], band_ref[sample]).astype(jnp.bfloat16)
        spot = pl.ds(sample * half, half)
        mixed_ref[spot, 0:width] = mixed[:half]
        mixed_ref[spot, width : 2 * width] = mixed[half:]


def unmix_lat(me_ref, table_ref, mixed_ref, band_ref, bands_refs):
    samples, size, width = band_ref.shape
    part, half = size // len(bands_refs), size // 2
    for sample in range(samples):
        spot = pl.ds(sample * half, half)
        joined = jnp.concatenate(
            [mixed_ref[spot, 0:width], mixed_ref[spot, width : 2 * width]], axis=0
        )
        bands = product_of(table_ref[...], joined).astype(jnp.bfloat16)
        if len(bands_refs) == 1:
            lead = bands_refs[0].shape[0]
            run = pl.ds(sample * size // lead, size // lead)
            bands_refs[0][:, run] = bands.reshape(lead, size // lead, width)
        else:
            band_ref[sample] = bands
            for offset, bands_ref in with_offsets(bands_refs):
                place = place_of(me_ref, offset, part)
                bands_ref[pl.ds(sample * part, part)] = band_ref[sample, place]


def activate(mixed_ref, w1_ref, b1_ref):
    pre = product_of(mixed_ref[0], w1_ref[0]) + b1_ref[0]
    logistic = sigmoid_of(pre)
    return logistic, pre * logistic


def bend(act_ref, w2_ref, b2_ref):
    out = product_of(act_ref[...], w2_ref[0]) + b2_ref[0]
    return out, jnp.tanh(out * (1.0 / shrink_level))


def forward_kernel(blocks, me_ref, lat_ref, unlat_ref, w1_ref, b1_ref, w2_ref, b2_ref, *refs):
    bands_refs, image_refs = refs[:blocks], refs[blocks : 2 * blocks]
    mixed_ref, act_ref, band_ref = refs[2 * blocks :]
    mix_lat(me_ref, lat_ref, bands_refs, band_ref, mixed_ref.at[0])
    act_ref[...] = activate(mixed_ref, w1_ref, b1_ref)[1].astype(jnp.bfloat16)
    out, bent = bend(act_ref, w2_ref, b2_ref)
    act_ref[...] = (out - shrink_level * bent).astype(jnp.bfloat16)
    unmix_lat(me_ref, unlat_ref, act_ref, band_ref, image_refs)


def backward_kernel(
    block_size, blocks, me_ref, lat_ref, unlat_ref, w1_ref, b1_ref, w2_ref, b2_ref, mixed_ref, *refs
):
    bands_refs, image_refs = refs[:blocks], refs[blocks : 2 * blocks]
    sums_ref, act_ref, gate_ref, cot_ref, kept_ref, band_ref = refs[2 * blocks :]
    transposed = (((1,), (1,)), ((), ()))
    summed = (((0,), (0,)), ((), ()))

    def times(former, latter, dims):
        return lax.dot_general(former, latter, dims, preferred_element_type=jnp.float32)

    def weight_sums(acts, grads, slot):
        width = acts.shape[1] // 2
        full = times(acts, grads, summed)
        real = full[:width, :width] + full[width:, width:]
        imag = full[:width, width:] - full[width:, :width]
        bias = jnp.sum(grads.astype(jnp.float32), axis=0, keepdims=True)
        size = block_size
        owner = lax.broadcasted_iota(jnp.int32, (size, width), 1) // size
        extra = sums_ref.shape[2] - size
        first = lax.broadcasted_iota(jnp.int32, (extra, width), 0) == 0
        for part, values in enumerate((real, imag)):
            joined = values[:size]
            for block in range(1, width // size):
                joined = jnp.where(owner == block, values[block * size : (block + 1) * size], joined)
            sums_ref[slot, part, 0:size] = joined.astype(sums_ref.dtype)
            row = bias[:, part * width : (part + 1) * width]
            sums_ref[slot, part, size:] = jnp.where(first, row, 0.0).astype(sums_ref.dtype)

    logistic, act = activate(mixed_ref, w1_ref, b1_ref)
    act_ref[...] = act.astype(jnp.bfloat16)
    gate_ref[...] = logistic + act * (1.0 - logistic)
    mix_lat(me_ref, lat_ref, bands_refs, band_ref, cot_ref)
    _, bent = bend(act_ref, w2_ref, b2_ref)
    kept_ref[...] = (cot_ref[...].astype(jnp.float32) * (bent * bent)).astype(jnp.bfloat16)
    back = times(kept_ref[...], w2_ref[0], transposed)
    cot_ref[...] = (back * gate_ref[...]).astype(jnp.bfloat16)
    weight_sums(act_ref[...], kept_ref[...], 1)
    kept_ref[...] = times(cot_ref[...], w1_ref[0], transposed).astype(jnp.bfloat16)
    weight_sums(mixed_ref[0], cot_ref[...], 0)
    unmix_lat(me_ref, unlat_ref, kept_ref, band_ref, image_refs)


def group_spec(*shape):
    return pl.BlockSpec((1,) + shape, lambda g, *_: (g,) + (0,) * len(shape))


def bands_specs(rows, bands, groups):
    block = (rows, bands[0].shape[1] // groups)
    return (pl.BlockSpec(block, lambda g, *_: (0, g)),) * len(bands)


def images_like(bands, samples, size, groups):
    if len(bands) > 1:
        shapes = tuple(in_hbm(band.shape, band.dtype) for band in bands)
        return shapes, bands_specs(bands[0].shape[0], bands, groups)
    channels = bands[0].shape[1]
    shape = (1, samples * size, channels)
    spec = pl.BlockSpec(shape[:2] + (channels // groups,), lambda g, *_: (0, 0, g))
    return (in_hbm(shape, jnp.bfloat16),), (spec,)


def forward_mid(me, lat, unlat, bands, w1, b1, w2, b2):
    groups, lanes, _ = w1.shape
    size = lat.shape[0]
    samples = bands[0].shape[0] * len(bands) // size
    positions = samples * size // 2
    table = pl.BlockSpec((size, size), lambda g, _: (0, 0))
    state = (groups, positions, lanes)
    specs = bands_specs(bands[0].shape[0], bands, groups)
    images, image_specs = images_like(bands, samples, size, groups)
    results = pl.pallas_call(
        functools.partial(forward_kernel, len(bands)),
        grid_spec=pltpu.PrefetchScalarGridSpec(
            num_scalar_prefetch=1,
            grid=(groups,),
            in_specs=[
                table, table,
                group_spec(lanes, lanes), group_spec(1, lanes),
                group_spec(lanes, lanes), group_spec(1, lanes),
                *specs,
            ],
            out_specs=image_specs + (group_spec(positions, lanes),),
            scratch_shapes=[
                pltpu.VMEM((positions, lanes), jnp.bfloat16),
                pltpu.VMEM((samples, size, lanes // 2), jnp.bfloat16),
            ],
        ),
        out_shape=images + (in_hbm(state, jnp.bfloat16),),
        compiler_params=params(28),
        cost_estimate=pl.CostEstimate(
            flops=4 * groups * positions * lanes * lanes,
            bytes_accessed=16 * groups * positions * lanes + 4 * groups * lanes * lanes,
            transcendentals=2 * groups * positions * lanes,
        ),
        name="mix_forward",
    )(me, lat, unlat, *hbm(w1), b1, *hbm(w2), b2, *hbm(*bands))
    return results[: len(bands)], results[len(bands)]


def backward_mid(me, lat, unlat, bands, w1, b1, w2, b2, state, count):
    groups, lanes, _ = w1.shape
    size = lat.shape[0]
    samples = bands[0].shape[0] * len(bands) // size
    positions = samples * size // 2
    table = pl.BlockSpec((size, size), lambda g, _: (0, 0))
    size_of_block = lanes // 2 // (count // groups)
    sums = (2, 2, size_of_block + 32, lanes // 2)
    images, image_specs = images_like(bands, samples, size, groups)
    results = pl.pallas_call(
        functools.partial(backward_kernel, size_of_block, len(bands)),
        grid_spec=pltpu.PrefetchScalarGridSpec(
            num_scalar_prefetch=1,
            grid=(groups,),
            in_specs=[
                table, table,
                group_spec(lanes, lanes), group_spec(1, lanes),
                group_spec(lanes, lanes), group_spec(1, lanes),
                group_spec(positions, lanes),
                *bands_specs(bands[0].shape[0], bands, groups),
            ],
            out_specs=image_specs + (pl.BlockSpec(sums, lambda g, _: (0, 0, 0, g)),),
            scratch_shapes=[
                pltpu.VMEM((positions, lanes), jnp.bfloat16),
                pltpu.VMEM((positions, lanes), jnp.float32),
                pltpu.VMEM((positions, lanes), jnp.bfloat16),
                pltpu.VMEM((positions, lanes), jnp.bfloat16),
                pltpu.VMEM((samples, size, lanes // 2), jnp.bfloat16),
            ],
        ),
        out_shape=images + (in_hbm(sums[:3] + (groups * sums[3],), jnp.float32),),
        compiler_params=params(32),
        cost_estimate=pl.CostEstimate(
            flops=8 * groups * positions * lanes * lanes,
            bytes_accessed=16 * groups * positions * lanes + 4 * groups * lanes * lanes,
            transcendentals=0,
        ),
        name="mix_backward",
    )(me, lat, unlat, *hbm(w1), b1, *hbm(w2), b2, *hbm(state, *bands))
    return results[: len(bands)], results[len(bands)]


def swap_with(values, axis, distance):
    pairs = [(i, i ^ distance) for i in range(lax.axis_size(axis))]
    return lax.ppermute(values, axis, pairs)


def waiting(values, arrived):
    return lax.optimization_barrier((values, tuple(arrived)))[0]


def mixed_order(size):
    far = list(range(size // 2, size))
    near = [offset for offset in (2, 3, 1) if offset < size // 2]
    near += list(range(4, size // 2))
    order = []
    for place, offset in enumerate(far):
        order += [offset] + near[place : place + 1] * (place < len(near) - 1)
    return order + near[-1:]


def pick(pair, side):
    return lax.dynamic_index_in_dim(pair, side, 0, keepdims=False)


class GroupSum:
    def __init__(self, sums):
        self.lanes = sums.shape[-1]
        self.side = lax.axis_index("dp")
        self.me = lax.axis_index("space")
        self.count = lax.axis_size("space") // 2
        self.held = sums.reshape(-1, self.lanes)

    def halve(self, axis, distance, bit, kind, arrived):
        pair = waiting(self.held, arrived).reshape(2, -1, self.lanes)
        taken = swap_with(pick(pair, 1 - bit).astype(kind), axis, distance)
        self.held = pick(pair, bit) + taken.astype(jnp.float32)

    def over_dp(self):
        self.halve("dp", 1, self.side, jnp.float32, [])

    def over_next(self, arrived):
        self.halve("space", 1, self.me % 2, jnp.bfloat16, arrived)

    def scatter(self, arrived):
        shares = waiting(self.held, arrived).reshape(self.count, -1, self.lanes)
        place = self.me // 2
        total = pick(shares, place)
        for offset in range(1, self.count):
            given = pick(shares, place ^ offset).astype(jnp.bfloat16)
            total += swap_with(given, "space", 2 * offset).astype(jnp.float32)
        self.total = total.astype(jnp.bfloat16)

    def gather(self, arrived):
        total = waiting(self.total, arrived)
        taken = [total]
        for offset in range(1, self.count):
            taken.append(swap_with(total, "space", 2 * offset))
        self.quarter = jnp.stack(taken)

    def gather_next(self, arrived):
        quarter = waiting(self.quarter, arrived)
        self.half = jnp.stack([quarter, swap_with(quarter, "space", 1)])

    def gather_dp(self, arrived):
        half = waiting(self.half, arrived)
        return half, swap_with(half, "dp", 1)


def finish_kernel(factor, me_ref, half_ref, other_ref, *out_refs):
    side, near, place = me_ref[0], me_ref[1], me_ref[2]
    run = half_ref.shape[2]
    for which in range(2):
        blocks_ref, bias_ref = out_refs[2 * which : 2 * which + 2]
        edge = blocks_ref.shape[-1]
        for part in range(2):
            for piece in range(half_ref.shape[1]):
                spot = (part ^ near, piece ^ place)
                own = half_ref[spot].astype(jnp.float32)
                value = jnp.where(side == which, own, other_ref[spot].astype(jnp.float32)) * factor
                first = piece * run
                count = max(0, min(edge - first, run))
                for block in range(blocks_ref.shape[1]):
                    lanes = slice(block * edge, (block + 1) * edge)
                    if count > 0:
                        blocks_ref[part, block, pl.ds(first, count)] = value[:count, lanes]
                    if first <= edge < first + run:
                        row = edge - first
                        bias_ref[part, pl.ds(block, 1)] = value[row : row + 1, lanes]


def finish_sums(here, half, other, factor, weight_shape, bias_shape):
    outs = [weight_shape, bias_shape] * 2
    return pl.pallas_call(
        functools.partial(finish_kernel, factor),
        out_shape=[jax.ShapeDtypeStruct(shape, jnp.float32) for shape in outs],
        in_specs=[pl.BlockSpec(memory_space=pltpu.SMEM)]
        + [pl.BlockSpec(memory_space=pltpu.VMEM)] * 2,
        out_specs=[pl.BlockSpec(memory_space=pltpu.VMEM)] * 4,
        compiler_params=pltpu.CompilerParams(vmem_limit_bytes=16 * MIB),
        cost_estimate=pl.CostEstimate(flops=0, bytes_accessed=4 * MIB, transcendentals=0),
        name="finish_sums",
    )(here, half, other)


def body(fields, cotangent, w_first, b_first, w_second, b_second):
    samples, rows, width, channels = fields.shape
    owners = lax.axis_size("space")
    lat_total = rows * owners
    modes = KW // owners
    count, edge = w_first.shape[1:3]
    groups = 2
    direct = 2 * modes % 16 == 0
    lead = owners if direct else 1

    order = mixed_order(owners)

    def place(offset):
        return (owners - offset) % owners

    def send(blocks, offsets, taken):
        for offset in offsets:
            taken[offset] = swap_with(blocks[place(offset)], "space", offset)

    def listed(taken):
        return [taken[place(at)] for at in range(owners)]

    def send_all(spectrum):
        spectrum = spectrum.reshape(samples, rows, owners, 2 * modes, channels)
        spectrum = jnp.transpose(spectrum, (2, 0, 1, 3, 4))
        arrived = lax.all_to_all(spectrum, "space", split_axis=0, concat_axis=0, tiled=True)
        return [jnp.transpose(arrived, (1, 0, 2, 3, 4)).reshape(-1, channels)]

    def send_all_back(bands):
        bands = bands.reshape(samples, owners, rows, 2 * modes, channels)
        bands = jnp.transpose(bands, (1, 0, 2, 3, 4))
        arrived = lax.all_to_all(bands, "space", split_axis=0, concat_axis=0, tiled=True)
        return [jnp.transpose(arrived, (1, 2, 0, 3, 4)).reshape(1, -1, channels)]

    me = lax.axis_index("space") if direct else 0
    me = jnp.full((1,), me, jnp.int32)
    plain, scaled = lon_tables(KW, width, owners)
    lat = lat_spread(lat_total, modes)

    spectrum = to_modes(me, plain, fields, lead)
    spectrum, cotangent, w_first, w_second = lax.optimization_barrier(
        (spectrum, cotangent, w_first, w_second)
    )
    cot_spec = to_modes(me, scaled, cotangent, lead)
    w1, w2 = spread_weights(groups, w_first, w_second)
    b1, b2 = block_bias(b_first, groups), block_bias(b_second, groups)
    positions = samples * lax.axis_size("dp") * lat_total * KW
    factor = 1.0 / math.sqrt(positions)

    if not direct:
        gathered = send_all(spectrum[0])
        image, state = forward_mid(me, lat, lat.T, gathered, w1, b1, w2, b2)
        image_band = send_all_back(image[0])
        gathered = send_all(cot_spec[0])
        grad_image, sums = backward_mid(me, lat, lat.T, gathered, w1, b1, w2, b2, state, count)
        grad_band = send_all_back(grad_image[0])
        output = to_cells(me, scaled.T, image_band, fields)
        grad_fields = to_cells(me, plain.T, grad_band, cotangent)
        sums = lax.psum(sums, ("space", "dp")) * factor
        grads = []
        for which in range(2):
            blocks = sums[which, :, :edge].reshape(2, edge, count, edge)
            grads.append(jnp.transpose(blocks, (0, 2, 1, 3)))
            grads.append(sums[which, :, edge].reshape(b_first.shape))
        return (output, grad_fields) + tuple(grads)

    gathered, cot_gathered = {0: spectrum[0]}, {0: cot_spec[0]}
    falling = range(owners - 1, 0, -1)
    send(spectrum, falling[:FIRST], gathered)
    spectrum = waiting(list(spectrum), [cot_spec[0], w1, w2])
    send(spectrum, falling[FIRST:], gathered)
    gathered = listed(gathered)
    image, state = forward_mid(me, lat, lat.T, gathered, w1, b1, w2, b2)
    cot_spec, image = list(cot_spec), list(image)
    send(cot_spec, falling[:FIRST], cot_gathered)
    cot_spec, image = waiting((cot_spec, image), [image[0]])
    send(cot_spec, falling[FIRST:], cot_gathered)

    image_band = {0: image[0]}
    send(image, order, image_band)
    cot_gathered = listed(cot_gathered)
    grad_image, sums = backward_mid(
        me, lat, lat.T, cot_gathered, w1, b1, w2, b2, state, count
    )
    early = [image_band[offset] for offset in order[:HELD]]
    late = [image_band[offset] for offset in order[HELD:]]
    grad_image, sums = waiting((list(grad_image), sums), early)
    group_sum = GroupSum(sums)
    group_sum.over_dp()
    group_sum.over_next(late[:1])
    grad_band = {0: grad_image[0]}
    send(grad_image, order, grad_band)
    arrived = [grad_band[offset] for offset in order]
    image_band = listed(image_band)
    grad_band = listed(grad_band)
    again = waiting(fields, early[:1])
    output = rows_inside(to_cells(me, scaled.T, image_band, again))
    group_sum.scatter(late[1:] + arrived[:1])
    group_sum.gather(arrived[1:3])
    group_sum.quarter, output = lax.optimization_barrier((group_sum.quarter, output))
    group_sum.gather_next(arrived[3:6])
    half, other = group_sum.gather_dp(arrived[6:])
    near = lax.axis_index("space")
    here = jnp.stack([lax.axis_index("dp"), near % 2, near // 2]).astype(jnp.int32)
    grads = finish_sums(here, half, other, factor, w_first.shape, b_first.shape)
    grad_fields = rows_inside(to_cells(me, plain.T, grad_band, cotangent))
    return (rows_outside(output), rows_outside(grad_fields)) + tuple(grads)


def solution(mesh):
    split = P(("parts", "dp"), "space", None, None)
    in_specs = (split, split, P(), P(), P(), P())
    out_specs = (
        split,
        split,
        P("parts", None, None, None),
        P("parts", None, None),
        P("parts", None, None, None),
        P("parts", None, None),
    )
    return jax.shard_map(body, mesh=mesh, in_specs=in_specs, out_specs=out_specs, check_vma=False)
```

```python
import functools
import math

import jax
import jax.numpy as jnp
from jax import lax
from jax.experimental import pallas as pl
from jax.experimental.layout import Layout, with_layout_constraint
from jax.experimental.pallas import tpu as pltpu
from jax.sharding import PartitionSpec as P
import ml_dtypes
import numpy as np

KW = 64
shrink_level = 0.05
FIRST = 5
HELD = 5
MIB = 1024 * 1024


def product_of(former, latter):
    return jnp.dot(former, latter, preferred_element_type=jnp.float32)


def lon_tables(mode_count, cell_count, owners):
    wavenums = np.arange(mode_count, dtype=np.int32)
    columns = np.arange(cell_count, dtype=np.int32)
    phase_index = (wavenums[:, None] * columns[None, :] % cell_count).astype(np.float32)
    phases = phase_index * np.float32(2.0 * math.pi / cell_count)
    factor = np.float32(1.0 / math.sqrt(cell_count))
    forward = np.stack([np.cos(phases) * factor, -np.sin(phases) * factor])
    scaled = forward * np.where(wavenums == 0, 1.0, 2.0).astype(np.float32)[:, None]

    def ordered(table):
        split = table.reshape(2, owners, -1, cell_count).transpose(1, 0, 2, 3)
        return split.reshape(-1, cell_count).astype(ml_dtypes.bfloat16)

    return ordered(forward), ordered(scaled)


def lat_spread(row_count, modes):
    indices = np.arange(row_count, dtype=np.int32)
    phase_index = (indices[:, None] * indices[None, :] % row_count).astype(np.float32)
    phases = phase_index * np.float32(2.0 * math.pi / row_count)
    factor = np.float32(1.0 / math.sqrt(row_count))
    cosine = np.cos(phases) * factor
    sine_part = np.sin(phases) * factor
    table = np.stack([np.stack([cosine, sine_part], -1), np.stack([-sine_part, cosine], -1)])
    same = np.eye(modes, dtype=np.float32)
    spread = table[:, :, None, :, :, None] * same[None, None, :, None, None, :]
    size = 2 * row_count * modes
    return spread.reshape(size, size).astype(ml_dtypes.bfloat16)


def block_bias(bias, groups):
    return jnp.transpose(bias.reshape(2, groups, 1, -1), (1, 2, 0, 3)).reshape(groups, 1, -1)


def spread_kernel(*refs):
    half_way = len(refs) // 2
    for blocks_ref, joined_ref in zip(refs[:half_way], refs[half_way:]):
        _, per, size, _ = blocks_ref.shape
        width = per * size
        row = lax.broadcasted_iota(jnp.int32, (size, width), 0)
        lane = lax.broadcasted_iota(jnp.int32, (size, width), 1)
        for block in range(per):
            place = (row + block * size == lane).astype(jnp.bfloat16)
            real = product_of(blocks_ref[0, block], place).astype(jnp.bfloat16)
            imag = product_of(blocks_ref[1, block], place)
            upper = pl.ds(block * size, size)
            lower = pl.ds(width + block * size, size)
            joined_ref[0, upper, 0:width] = real
            joined_ref[0, upper, width : 2 * width] = imag.astype(jnp.bfloat16)
            joined_ref[0, lower, 0:width] = (-imag).astype(jnp.bfloat16)
            joined_ref[0, lower, width : 2 * width] = real


def spread_weights(groups, *weights):
    _, count, size, _ = weights[0].shape
    per = count // groups
    lanes = 2 * per * size
    shape = in_hbm((groups, lanes, lanes), jnp.bfloat16)
    return pl.pallas_call(
        spread_kernel,
        grid=(groups,),
        out_shape=(shape,) * len(weights),
        in_specs=[pl.BlockSpec((2, per, size, size), lambda g: (0, g, 0, 0))] * len(weights),
        out_specs=(group_spec(lanes, lanes),) * len(weights),
        compiler_params=params(12),
        cost_estimate=pl.CostEstimate(
            flops=len(weights) * 2 * count * size * size * lanes,
            bytes_accessed=len(weights) * 2 * groups * lanes * lanes,
            transcendentals=0,
        ),
        name="spread_weights",
    )(*weights)


def params(mebibytes):
    return pltpu.CompilerParams(
        vmem_limit_bytes=mebibytes * MIB, dimension_semantics=("arbitrary",)
    )


def place_of(me_ref, offset, rows):
    return pl.ds(pl.multiple_of((me_ref[0] ^ offset) * rows, rows), rows)


def in_hbm(shape, dtype):
    return pltpu.HBM(shape, dtype)


def hbm(*arrays):
    return [pltpu.with_memory_space_constraint(array, pltpu.HBM) for array in arrays]


def with_offsets(refs):
    return [((len(refs) - place) % len(refs), ref) for place, ref in enumerate(refs)]


def to_modes_kernel(me_ref, table_ref, cells_ref, *refs):
    modes_refs, held_ref = refs[:-1], refs[-1]
    rows = cells_ref.shape[1]
    share = modes_refs[0].shape[0] // rows
    for row in range(rows):
        spectrum = product_of(table_ref[...], cells_ref[0, row])
        held_ref[row] = spectrum.astype(jnp.bfloat16)
        for offset, modes_ref in with_offsets(modes_refs):
            modes_ref[pl.ds(row * share, share)] = held_ref[row, place_of(me_ref, offset, share)]


def to_modes(me, table, cells, owners):
    samples, rows, width, channels = cells.shape
    size = table.shape[0]
    part = rows * size // owners
    return pl.pallas_call(
        to_modes_kernel,
        grid_spec=pltpu.PrefetchScalarGridSpec(
            num_scalar_prefetch=1,
            grid=(samples,),
            in_specs=[
                pl.BlockSpec((size, width), lambda b, _: (0, 0)),
                pl.BlockSpec((1, rows, width, channels), lambda b, _: (b, 0, 0, 0)),
            ],
            out_specs=(pl.BlockSpec((part, channels), lambda b, _: (b, 0)),) * owners,
            scratch_shapes=[pltpu.VMEM((rows, size, channels), jnp.bfloat16)],
        ),
        out_shape=(in_hbm((samples * part, channels), jnp.bfloat16),) * owners,
        compiler_params=params(12),
        cost_estimate=pl.CostEstimate(
            flops=2 * samples * rows * size * width * channels,
            bytes_accessed=2 * samples * rows * channels * (width + size),
            transcendentals=0,
        ),
        name="to_modes",
    )(me, table, cells)


def to_cells_kernel(me_ref, table_ref, base_ref, *refs):
    modes_refs, out_ref, held_ref = refs[:-2], refs[-2], refs[-1]
    rows = base_ref.shape[1]
    share = modes_refs[0].shape[-2] // rows
    for row in range(rows):
        run = pl.ds(row * share, share)
        if len(modes_refs) == 1:
            spectrum = modes_refs[0][:, run].reshape(held_ref.shape[1:])
        else:
            for offset, modes_ref in with_offsets(modes_refs):
                held_ref[row, place_of(me_ref, offset, share)] = modes_ref[run]
            spectrum = held_ref[row]
        image = product_of(table_ref[...], spectrum)
        out_ref[0, row] = (base_ref[0, row].astype(jnp.float32) + image).astype(jnp.bfloat16)


def to_cells(me, table, modes, base):
    samples, rows, width, channels = base.shape
    size = table.shape[1]
    block = pl.BlockSpec((1, rows, width, channels), lambda b, _: (b, 0, 0, 0))
    if len(modes) == 1:
        lead = modes[0].shape[0]
        part = rows * size // lead
        specs = [pl.BlockSpec((lead, part, channels), lambda b, _: (0, b, 0))]
    else:
        part = rows * size // len(modes)
        specs = [pl.BlockSpec((part, channels), lambda b, _: (b, 0))] * len(modes)
    return pl.pallas_call(
        to_cells_kernel,
        grid_spec=pltpu.PrefetchScalarGridSpec(
            num_scalar_prefetch=1,
            grid=(samples,),
            in_specs=[pl.BlockSpec((width, size), lambda b, _: (0, 0)), block] + specs,
            out_specs=block,
            scratch_shapes=[pltpu.VMEM((rows, size, channels), jnp.bfloat16)],
        ),
        out_shape=jax.ShapeDtypeStruct(base.shape, jnp.bfloat16),
        compiler_params=params(12),
        cost_estimate=pl.CostEstimate(
            flops=2 * samples * rows * size * width * channels,
            bytes_accessed=2 * samples * rows * channels * (2 * width + size),
            transcendentals=0,
        ),
        name="to_cells",
    )(me, table, base, *hbm(*modes))


def rows_inside(cells):
    inside = jnp.transpose(cells, (0, 2, 1, 3))
    return with_layout_constraint(inside, Layout(major_to_minor=(0, 1, 2, 3)))


def rows_outside(cells):
    return jnp.transpose(cells, (0, 2, 1, 3))


def sigmoid_of(values):
    return 0.5 + 0.5 * jnp.tanh(0.5 * values)


def mix_lat(me_ref, table_ref, bands_refs, band_ref, mixed_ref):
    samples, size, width = band_ref.shape
    part, half = size // len(bands_refs), size // 2
    for sample in range(samples):
        for offset, bands_ref in with_offsets(bands_refs):
            place = place_of(me_ref, offset, part)
            band_ref[sample, place] = bands_ref[pl.ds(sample * part, part)]
        mixed = product_of(table_ref[...], band_ref[sample]).astype(jnp.bfloat16)
        spot = pl.ds(sample * half, half)
        mixed_ref[spot, 0:width] = mixed[:half]
        mixed_ref[spot, width : 2 * width] = mixed[half:]


def unmix_lat(me_ref, table_ref, mixed_ref, band_ref, bands_refs):
    samples, size, width = band_ref.shape
    part, half = size // len(bands_refs), size // 2
    for sample in range(samples):
        spot = pl.ds(sample * half, half)
        joined = jnp.concatenate(
            [mixed_ref[spot, 0:width], mixed_ref[spot, width : 2 * width]], axis=0
        )
        bands = product_of(table_ref[...], joined).astype(jnp.bfloat16)
        if len(bands_refs) == 1:
            lead = bands_refs[0].shape[0]
            run = pl.ds(sample * size // lead, size // lead)
            bands_refs[0][:, run] = bands.reshape(lead, size // lead, width)
        else:
            band_ref[sample] = bands
            for offset, bands_ref in with_offsets(bands_refs):
                place = place_of(me_ref, offset, part)
                bands_ref[pl.ds(sample * part, part)] = band_ref[sample, place]


def activate(mixed_ref, w1_ref, b1_ref):
    pre = product_of(mixed_ref[0], w1_ref[0]) + b1_ref[0]
    logistic = sigmoid_of(pre)
    return logistic, pre * logistic


def bend(act_ref, w2_ref, b2_ref):
    out = product_of(act_ref[...], w2_ref[0]) + b2_ref[0]
    return out, jnp.tanh(out * (1.0 / shrink_level))


def forward_kernel(blocks, me_ref, lat_ref, unlat_ref, w1_ref, b1_ref, w2_ref, b2_ref, *refs):
    bands_refs, image_refs = refs[:blocks], refs[blocks : 2 * blocks]
    mixed_ref, act_ref, band_ref = refs[2 * blocks :]
    mix_lat(me_ref, lat_ref, bands_refs, band_ref, mixed_ref.at[0])
    act_ref[...] = activate(mixed_ref, w1_ref, b1_ref)[1].astype(jnp.bfloat16)
    out, bent = bend(act_ref, w2_ref, b2_ref)
    act_ref[...] = (out - shrink_level * bent).astype(jnp.bfloat16)
    unmix_lat(me_ref, unlat_ref, act_ref, band_ref, image_refs)


def backward_kernel(
    block_size, blocks, me_ref, lat_ref, unlat_ref, w1_ref, b1_ref, w2_ref, b2_ref, mixed_ref, *refs
):
    bands_refs, image_refs = refs[:blocks], refs[blocks : 2 * blocks]
    sums_ref, act_ref, gate_ref, cot_ref, kept_ref, band_ref = refs[2 * blocks :]
    transposed = (((1,), (1,)), ((), ()))
    summed = (((0,), (0,)), ((), ()))

    def times(former, latter, dims):
        return lax.dot_general(former, latter, dims, preferred_element_type=jnp.float32)

    def weight_sums(acts, grads, slot):
        width = acts.shape[1] // 2
        full = times(acts, grads, summed)
        real = full[:width, :width] + full[width:, width:]
        imag = full[:width, width:] - full[width:, :width]
        bias = jnp.sum(grads.astype(jnp.float32), axis=0, keepdims=True)
        size = block_size
        owner = lax.broadcasted_iota(jnp.int32, (size, width), 1) // size
        extra = sums_ref.shape[2] - size
        first = lax.broadcasted_iota(jnp.int32, (extra, width), 0) == 0
        for part, values in enumerate((real, imag)):
            joined = values[:size]
            for block in range(1, width // size):
                joined = jnp.where(owner == block, values[block * size : (block + 1) * size], joined)
            sums_ref[slot, part, 0:size] = joined.astype(sums_ref.dtype)
            row = bias[:, part * width : (part + 1) * width]
            sums_ref[slot, part, size:] = jnp.where(first, row, 0.0).astype(sums_ref.dtype)

    logistic, act = activate(mixed_ref, w1_ref, b1_ref)
    act_ref[...] = act.astype(jnp.bfloat16)
    gate_ref[...] = logistic + act * (1.0 - logistic)
    mix_lat(me_ref, lat_ref, bands_refs, band_ref, cot_ref)
    _, bent = bend(act_ref, w2_ref, b2_ref)
    kept_ref[...] = (cot_ref[...].astype(jnp.float32) * (bent * bent)).astype(jnp.bfloat16)
    back = times(kept_ref[...], w2_ref[0], transposed)
    cot_ref[...] = (back * gate_ref[...]).astype(jnp.bfloat16)
    weight_sums(act_ref[...], kept_ref[...], 1)
    kept_ref[...] = times(cot_ref[...], w1_ref[0], transposed).astype(jnp.bfloat16)
    weight_sums(mixed_ref[0], cot_ref[...], 0)
    unmix_lat(me_ref, unlat_ref, kept_ref, band_ref, image_refs)


def group_spec(*shape):
    return pl.BlockSpec((1,) + shape, lambda g, *_: (g,) + (0,) * len(shape))


def bands_specs(rows, bands, groups):
    block = (rows, bands[0].shape[1] // groups)
    return (pl.BlockSpec(block, lambda g, *_: (0, g)),) * len(bands)


def images_like(bands, samples, size, groups):
    if len(bands) > 1:
        shapes = tuple(in_hbm(band.shape, band.dtype) for band in bands)
        return shapes, bands_specs(bands[0].shape[0], bands, groups)
    channels = bands[0].shape[1]
    shape = (1, samples * size, channels)
    spec = pl.BlockSpec(shape[:2] + (channels // groups,), lambda g, *_: (0, 0, g))
    return (in_hbm(shape, jnp.bfloat16),), (spec,)


def forward_mid(me, lat, unlat, bands, w1, b1, w2, b2):
    groups, lanes, _ = w1.shape
    size = lat.shape[0]
    samples = bands[0].shape[0] * len(bands) // size
    positions = samples * size // 2
    table = pl.BlockSpec((size, size), lambda g, _: (0, 0))
    state = (groups, positions, lanes)
    specs = bands_specs(bands[0].shape[0], bands, groups)
    images, image_specs = images_like(bands, samples, size, groups)
    results = pl.pallas_call(
        functools.partial(forward_kernel, len(bands)),
        grid_spec=pltpu.PrefetchScalarGridSpec(
            num_scalar_prefetch=1,
            grid=(groups,),
            in_specs=[
                table, table,
                group_spec(lanes, lanes), group_spec(1, lanes),
                group_spec(lanes, lanes), group_spec(1, lanes),
                *specs,
            ],
            out_specs=image_specs + (group_spec(positions, lanes),),
            scratch_shapes=[
                pltpu.VMEM((positions, lanes), jnp.bfloat16),
                pltpu.VMEM((samples, size, lanes // 2), jnp.bfloat16),
            ],
        ),
        out_shape=images + (in_hbm(state, jnp.bfloat16),),
        compiler_params=params(28),
        cost_estimate=pl.CostEstimate(
            flops=4 * groups * positions * lanes * lanes,
            bytes_accessed=16 * groups * positions * lanes + 4 * groups * lanes * lanes,
            transcendentals=2 * groups * positions * lanes,
        ),
        name="mix_forward",
    )(me, lat, unlat, *hbm(w1), b1, *hbm(w2), b2, *hbm(*bands))
    return results[: len(bands)], results[len(bands)]


def backward_mid(me, lat, unlat, bands, w1, b1, w2, b2, state, count):
    groups, lanes, _ = w1.shape
    size = lat.shape[0]
    samples = bands[0].shape[0] * len(bands) // size
    positions = samples * size // 2
    table = pl.BlockSpec((size, size), lambda g, _: (0, 0))
    size_of_block = lanes // 2 // (count // groups)
    sums = (2, 2, size_of_block + 32, lanes // 2)
    images, image_specs = images_like(bands, samples, size, groups)
    results = pl.pallas_call(
        functools.partial(backward_kernel, size_of_block, len(bands)),
        grid_spec=pltpu.PrefetchScalarGridSpec(
            num_scalar_prefetch=1,
            grid=(groups,),
            in_specs=[
                table, table,
                group_spec(lanes, lanes), group_spec(1, lanes),
                group_spec(lanes, lanes), group_spec(1, lanes),
                group_spec(positions, lanes),
                *bands_specs(bands[0].shape[0], bands, groups),
            ],
            out_specs=image_specs + (pl.BlockSpec(sums, lambda g, _: (0, 0, 0, g)),),
            scratch_shapes=[
                pltpu.VMEM((positions, lanes), jnp.bfloat16),
                pltpu.VMEM((positions, lanes), jnp.float32),
                pltpu.VMEM((positions, lanes), jnp.bfloat16),
                pltpu.VMEM((positions, lanes), jnp.bfloat16),
                pltpu.VMEM((samples, size, lanes // 2), jnp.bfloat16),
            ],
        ),
        out_shape=images + (in_hbm(sums[:3] + (groups * sums[3],), jnp.float32),),
        compiler_params=params(32),
        cost_estimate=pl.CostEstimate(
            flops=8 * groups * positions * lanes * lanes,
            bytes_accessed=16 * groups * positions * lanes + 4 * groups * lanes * lanes,
            transcendentals=0,
        ),
        name="mix_backward",
    )(me, lat, unlat, *hbm(w1), b1, *hbm(w2), b2, *hbm(state, *bands))
    return results[: len(bands)], results[len(bands)]


def swap_with(values, axis, distance):
    pairs = [(i, i ^ distance) for i in range(lax.axis_size(axis))]
    return lax.ppermute(values, axis, pairs)


def waiting(values, arrived):
    return lax.optimization_barrier((values, tuple(arrived)))[0]


def mixed_order(size):
    far = list(range(size // 2, size))
    near = [offset for offset in (2, 3, 1) if offset < size // 2]
    near += list(range(4, size // 2))
    order = []
    for place, offset in enumerate(far):
        order += [offset] + near[place : place + 1] * (place < len(near) - 1)
    return order + near[-1:]


def pick(pair, side):
    return lax.dynamic_index_in_dim(pair, side, 0, keepdims=False)


class GroupSum:
    def __init__(self, sums):
        self.lanes = sums.shape[-1]
        self.side = lax.axis_index("dp")
        self.me = lax.axis_index("space")
        self.count = lax.axis_size("space") // 2
        self.held = sums.reshape(-1, self.lanes)

    def halve(self, axis, distance, bit, kind, arrived):
        pair = waiting(self.held, arrived).reshape(2, -1, self.lanes)
        taken = swap_with(pick(pair, 1 - bit).astype(kind), axis, distance)
        self.held = pick(pair, bit) + taken.astype(jnp.float32)

    def over_dp(self):
        self.halve("dp", 1, self.side, jnp.float32, [])

    def over_next(self, arrived):
        self.halve("space", 1, self.me % 2, jnp.bfloat16, arrived)

    def scatter(self, arrived):
        shares = waiting(self.held, arrived).reshape(self.count, -1, self.lanes)
        place = self.me // 2
        total = pick(shares, place)
        for offset in range(1, self.count):
            given = pick(shares, place ^ offset).astype(jnp.bfloat16)
            total += swap_with(given, "space", 2 * offset).astype(jnp.float32)
        self.total = total.astype(jnp.bfloat16)

    def gather(self, arrived):
        total = waiting(self.total, arrived)
        taken = [total]
        for offset in range(1, self.count):
            taken.append(swap_with(total, "space", 2 * offset))
        self.quarter = jnp.stack(taken)

    def gather_next(self, arrived):
        quarter = waiting(self.quarter, arrived)
        self.half = jnp.stack([quarter, swap_with(quarter, "space", 1)])

    def gather_dp(self, arrived):
        half = waiting(self.half, arrived)
        return half, swap_with(half, "dp", 1)


def finish_kernel(factor, me_ref, half_ref, other_ref, *out_refs):
    side, near, place = me_ref[0], me_ref[1], me_ref[2]
    run = half_ref.shape[2]
    for which in range(2):
        blocks_ref, bias_ref = out_refs[2 * which : 2 * which + 2]
        edge = blocks_ref.shape[-1]
        for part in range(2):
            for piece in range(half_ref.shape[1]):
                spot = (part ^ near, piece ^ place)
                own = half_ref[spot].astype(jnp.float32)
                value = jnp.where(side == which, own, other_ref[spot].astype(jnp.float32)) * factor
                first = piece * run
                count = max(0, min(edge - first, run))
                for block in range(blocks_ref.shape[1]):
                    lanes = slice(block * edge, (block + 1) * edge)
                    if count > 0:
                        blocks_ref[part, block, pl.ds(first, count)] = value[:count, lanes]
                    if first <= edge < first + run:
                        row = edge - first
                        bias_ref[part, pl.ds(block, 1)] = value[row : row + 1, lanes]


def finish_sums(here, half, other, factor, weight_shape, bias_shape):
    outs = [weight_shape, bias_shape] * 2
    return pl.pallas_call(
        functools.partial(finish_kernel, factor),
        out_shape=[jax.ShapeDtypeStruct(shape, jnp.float32) for shape in outs],
        in_specs=[pl.BlockSpec(memory_space=pltpu.SMEM)]
        + [pl.BlockSpec(memory_space=pltpu.VMEM)] * 2,
        out_specs=[pl.BlockSpec(memory_space=pltpu.VMEM)] * 4,
        compiler_params=pltpu.CompilerParams(vmem_limit_bytes=16 * MIB),
        cost_estimate=pl.CostEstimate(flops=0, bytes_accessed=4 * MIB, transcendentals=0),
        name="finish_sums",
    )(here, half, other)


def body(fields, cotangent, w_first, b_first, w_second, b_second):
    samples, rows, width, channels = fields.shape
    owners = lax.axis_size("space")
    lat_total = rows * owners
    modes = KW // owners
    count, edge = w_first.shape[1:3]
    groups = 2
    direct = 2 * modes % 16 == 0
    lead = owners if direct else 1

    order = mixed_order(owners)

    def place(offset):
        return (owners - offset) % owners

    def send(blocks, offsets, taken):
        for offset in offsets:
            taken[offset] = swap_with(blocks[place(offset)], "space", offset)

    def listed(taken):
        return [taken[place(at)] for at in range(owners)]

    def send_all(spectrum):
        spectrum = spectrum.reshape(samples, rows, owners, 2 * modes, channels)
        spectrum = jnp.transpose(spectrum, (2, 0, 1, 3, 4))
        arrived = lax.all_to_all(spectrum, "space", split_axis=0, concat_axis=0, tiled=True)
        return [jnp.transpose(arrived, (1, 0, 2, 3, 4)).reshape(-1, channels)]

    def send_all_back(bands):
        bands = bands.reshape(samples, owners, rows, 2 * modes, channels)
        bands = jnp.transpose(bands, (1, 0, 2, 3, 4))
        arrived = lax.all_to_all(bands, "space", split_axis=0, concat_axis=0, tiled=True)
        return [jnp.transpose(arrived, (1, 2, 0, 3, 4)).reshape(1, -1, channels)]

    me = lax.axis_index("space") if direct else 0
    me = jnp.full((1,), me, jnp.int32)
    plain, scaled = lon_tables(KW, width, owners)
    lat = lat_spread(lat_total, modes)

    spectrum = to_modes(me, plain, fields, lead)
    spectrum, cotangent, w_first, w_second = lax.optimization_barrier(
        (spectrum, cotangent, w_first, w_second)
    )
    cot_spec = to_modes(me, scaled, cotangent, lead)
    w1, w2 = spread_weights(groups, w_first, w_second)
    b1, b2 = block_bias(b_first, groups), block_bias(b_second, groups)
    positions = samples * lax.axis_size("dp") * lat_total * KW
    factor = 1.0 / math.sqrt(positions)

    if not direct:
        gathered = send_all(spectrum[0])
        image, state = forward_mid(me, lat, lat.T, gathered, w1, b1, w2, b2)
        image_band = send_all_back(image[0])
        gathered = send_all(cot_spec[0])
        grad_image, sums = backward_mid(me, lat, lat.T, gathered, w1, b1, w2, b2, state, count)
        grad_band = send_all_back(grad_image[0])
        output = to_cells(me, scaled.T, image_band, fields)
        grad_fields = to_cells(me, plain.T, grad_band, cotangent)
        sums = lax.psum(sums, ("space", "dp")) * factor
        grads = []
        for which in range(2):
            blocks = sums[which, :, :edge].reshape(2, edge, count, edge)
            grads.append(jnp.transpose(blocks, (0, 2, 1, 3)))
            grads.append(sums[which, :, edge].reshape(b_first.shape))
        return (output, grad_fields) + tuple(grads)

    gathered, cot_gathered = {0: spectrum[0]}, {0: cot_spec[0]}
    falling = range(owners - 1, 0, -1)
    send(spectrum, falling[:FIRST], gathered)
    spectrum = waiting(list(spectrum), [cot_spec[0], w1, w2])
    send(spectrum, falling[FIRST:], gathered)
    gathered = listed(gathered)
    image, state = forward_mid(me, lat, lat.T, gathered, w1, b1, w2, b2)
    cot_spec, image = list(cot_spec), list(image)
    send(cot_spec, falling[:FIRST], cot_gathered)
    cot_spec, image = waiting((cot_spec, image), [image[0]])
    send(cot_spec, falling[FIRST:], cot_gathered)

    image_band = {0: image[0]}
    send(image, order, image_band)
    cot_gathered = listed(cot_gathered)
    grad_image, sums = backward_mid(
        me, lat, lat.T, cot_gathered, w1, b1, w2, b2, state, count
    )
    early = [image_band[offset] for offset in order[:HELD]]
    late = [image_band[offset] for offset in order[HELD:]]
    grad_image, sums = waiting((list(grad_image), sums), early)
    group_sum = GroupSum(sums)
    group_sum.over_dp()
    group_sum.over_next(late[:1])
    grad_band = {0: grad_image[0]}
    send(grad_image, order, grad_band)
    arrived = [grad_band[offset] for offset in order]
    image_band = listed(image_band)
    grad_band = listed(grad_band)
    again = waiting(fields, early[:1])
    output = rows_inside(to_cells(me, scaled.T, image_band, again))
    group_sum.scatter(late[1:] + arrived[:1])
    group_sum.gather(arrived[1:3])
    group_sum.quarter, output = lax.optimization_barrier((group_sum.quarter, output))
    group_sum.gather_next(arrived[3:5])
    half, other = group_sum.gather_dp(arrived[5:])
    near = lax.axis_index("space")
    here = jnp.stack([lax.axis_index("dp"), near % 2, near // 2]).astype(jnp.int32)
    grads = finish_sums(here, half, other, factor, w_first.shape, b_first.shape)
    grad_fields = rows_inside(to_cells(me, plain.T, grad_band, cotangent))
    return (rows_outside(output), rows_outside(grad_fields)) + tuple(grads)


def solution(mesh):
    split = P(("parts", "dp"), "space", None, None)
    in_specs = (split, split, P(), P(), P(), P())
    out_specs = (
        split,
        split,
        P("parts", None, None, None),
        P("parts", None, None),
        P("parts", None, None, None),
        P("parts", None, None),
    )
    return jax.shard_map(body, mesh=mesh, in_specs=in_specs, out_specs=out_specs, check_vma=False)
```

```python
import functools
import math

import jax
import jax.numpy as jnp
from jax import lax
from jax.experimental import pallas as pl
from jax.experimental.layout import Layout, with_layout_constraint
from jax.experimental.pallas import tpu as pltpu
from jax.sharding import PartitionSpec as P
import ml_dtypes
import numpy as np

KW = 64
shrink_level = 0.05
FIRST = 5
HELD = 5
MIB = 1024 * 1024


def product_of(former, latter):
    return jnp.dot(former, latter, preferred_element_type=jnp.float32)


def lon_tables(mode_count, cell_count, owners):
    wavenums = np.arange(mode_count, dtype=np.int32)
    columns = np.arange(cell_count, dtype=np.int32)
    phase_index = (wavenums[:, None] * columns[None, :] % cell_count).astype(np.float32)
    phases = phase_index * np.float32(2.0 * math.pi / cell_count)
    factor = np.float32(1.0 / math.sqrt(cell_count))
    forward = np.stack([np.cos(phases) * factor, -np.sin(phases) * factor])
    scaled = forward * np.where(wavenums == 0, 1.0, 2.0).astype(np.float32)[:, None]

    def ordered(table):
        split = table.reshape(2, owners, -1, cell_count).transpose(1, 0, 2, 3)
        return split.reshape(-1, cell_count).astype(ml_dtypes.bfloat16)

    return ordered(forward), ordered(scaled)


def lat_spread(row_count, modes):
    indices = np.arange(row_count, dtype=np.int32)
    phase_index = (indices[:, None] * indices[None, :] % row_count).astype(np.float32)
    phases = phase_index * np.float32(2.0 * math.pi / row_count)
    factor = np.float32(1.0 / math.sqrt(row_count))
    cosine = np.cos(phases) * factor
    sine_part = np.sin(phases) * factor
    table = np.stack([np.stack([cosine, sine_part], -1), np.stack([-sine_part, cosine], -1)])
    same = np.eye(modes, dtype=np.float32)
    spread = table[:, :, None, :, :, None] * same[None, None, :, None, None, :]
    size = 2 * row_count * modes
    return spread.reshape(size, size).astype(ml_dtypes.bfloat16)


def block_bias(bias, groups):
    return jnp.transpose(bias.reshape(2, groups, 1, -1), (1, 2, 0, 3)).reshape(groups, 1, -1)


def spread_kernel(*refs):
    half_way = len(refs) // 2
    for blocks_ref, joined_ref in zip(refs[:half_way], refs[half_way:]):
        _, per, size, _ = blocks_ref.shape
        width = per * size
        row = lax.broadcasted_iota(jnp.int32, (size, width), 0)
        lane = lax.broadcasted_iota(jnp.int32, (size, width), 1)
        for block in range(per):
            place = (row + block * size == lane).astype(jnp.bfloat16)
            real = product_of(blocks_ref[0, block], place).astype(jnp.bfloat16)
            imag = product_of(blocks_ref[1, block], place)
            upper = pl.ds(block * size, size)
            lower = pl.ds(width + block * size, size)
            joined_ref[0, upper, 0:width] = real
            joined_ref[0, upper, width : 2 * width] = imag.astype(jnp.bfloat16)
            joined_ref[0, lower, 0:width] = (-imag).astype(jnp.bfloat16)
            joined_ref[0, lower, width : 2 * width] = real


def spread_weights(groups, *weights):
    _, count, size, _ = weights[0].shape
    per = count // groups
    lanes = 2 * per * size
    shape = in_hbm((groups, lanes, lanes), jnp.bfloat16)
    return pl.pallas_call(
        spread_kernel,
        grid=(groups,),
        out_shape=(shape,) * len(weights),
        in_specs=[pl.BlockSpec((2, per, size, size), lambda g: (0, g, 0, 0))] * len(weights),
        out_specs=(group_spec(lanes, lanes),) * len(weights),
        compiler_params=params(12),
        cost_estimate=pl.CostEstimate(
            flops=len(weights) * 2 * count * size * size * lanes,
            bytes_accessed=len(weights) * 2 * groups * lanes * lanes,
            transcendentals=0,
        ),
        name="spread_weights",
    )(*weights)


def params(mebibytes):
    return pltpu.CompilerParams(
        vmem_limit_bytes=mebibytes * MIB, dimension_semantics=("arbitrary",)
    )


def place_of(me_ref, offset, rows):
    return pl.ds(pl.multiple_of((me_ref[0] ^ offset) * rows, rows), rows)


def in_hbm(shape, dtype):
    return pltpu.HBM(shape, dtype)


def hbm(*arrays):
    return [pltpu.with_memory_space_constraint(array, pltpu.HBM) for array in arrays]


def with_offsets(refs):
    return [((len(refs) - place) % len(refs), ref) for place, ref in enumerate(refs)]


def to_modes_kernel(me_ref, table_ref, cells_ref, *refs):
    modes_refs, held_ref = refs[:-1], refs[-1]
    rows = cells_ref.shape[1]
    share = modes_refs[0].shape[0] // rows
    for row in range(rows):
        spectrum = product_of(table_ref[...], cells_ref[0, row])
        held_ref[row] = spectrum.astype(jnp.bfloat16)
        for offset, modes_ref in with_offsets(modes_refs):
            modes_ref[pl.ds(row * share, share)] = held_ref[row, place_of(me_ref, offset, share)]


def to_modes(me, table, cells, owners):
    samples, rows, width, channels = cells.shape
    size = table.shape[0]
    part = rows * size // owners
    return pl.pallas_call(
        to_modes_kernel,
        grid_spec=pltpu.PrefetchScalarGridSpec(
            num_scalar_prefetch=1,
            grid=(samples,),
            in_specs=[
                pl.BlockSpec((size, width), lambda b, _: (0, 0)),
                pl.BlockSpec((1, rows, width, channels), lambda b, _: (b, 0, 0, 0)),
            ],
            out_specs=(pl.BlockSpec((part, channels), lambda b, _: (b, 0)),) * owners,
            scratch_shapes=[pltpu.VMEM((rows, size, channels), jnp.bfloat16)],
        ),
        out_shape=(in_hbm((samples * part, channels), jnp.bfloat16),) * owners,
        compiler_params=params(12),
        cost_estimate=pl.CostEstimate(
            flops=2 * samples * rows * size * width * channels,
            bytes_accessed=2 * samples * rows * channels * (width + size),
            transcendentals=0,
        ),
        name="to_modes",
    )(me, table, cells)


def to_cells_kernel(me_ref, table_ref, base_ref, *refs):
    modes_refs, out_ref, held_ref = refs[:-2], refs[-2], refs[-1]
    rows = base_ref.shape[1]
    share = modes_refs[0].shape[-2] // rows
    for row in range(rows):
        run = pl.ds(row * share, share)
        if len(modes_refs) == 1:
            spectrum = modes_refs[0][:, run].reshape(held_ref.shape[1:])
        else:
            for offset, modes_ref in with_offsets(modes_refs):
                held_ref[row, place_of(me_ref, offset, share)] = modes_ref[run]
            spectrum = held_ref[row]
        image = product_of(table_ref[...], spectrum)
        out_ref[0, row] = (base_ref[0, row].astype(jnp.float32) + image).astype(jnp.bfloat16)


def to_cells(me, table, modes, base):
    samples, rows, width, channels = base.shape
    size = table.shape[1]
    block = pl.BlockSpec((1, rows, width, channels), lambda b, _: (b, 0, 0, 0))
    if len(modes) == 1:
        lead = modes[0].shape[0]
        part = rows * size // lead
        specs = [pl.BlockSpec((lead, part, channels), lambda b, _: (0, b, 0))]
    else:
        part = rows * size // len(modes)
        specs = [pl.BlockSpec((part, channels), lambda b, _: (b, 0))] * len(modes)
    return pl.pallas_call(
        to_cells_kernel,
        grid_spec=pltpu.PrefetchScalarGridSpec(
            num_scalar_prefetch=1,
            grid=(samples,),
            in_specs=[pl.BlockSpec((width, size), lambda b, _: (0, 0)), block] + specs,
            out_specs=block,
            scratch_shapes=[pltpu.VMEM((rows, size, channels), jnp.bfloat16)],
        ),
        out_shape=jax.ShapeDtypeStruct(base.shape, jnp.bfloat16),
        compiler_params=params(12),
        cost_estimate=pl.CostEstimate(
            flops=2 * samples * rows * size * width * channels,
            bytes_accessed=2 * samples * rows * channels * (2 * width + size),
            transcendentals=0,
        ),
        name="to_cells",
    )(me, table, base, *hbm(*modes))


def rows_inside(cells):
    inside = jnp.transpose(cells, (0, 2, 1, 3))
    return with_layout_constraint(inside, Layout(major_to_minor=(0, 1, 2, 3)))


def rows_outside(cells):
    return jnp.transpose(cells, (0, 2, 1, 3))


def sigmoid_of(values):
    return 0.5 + 0.5 * jnp.tanh(0.5 * values)


def mix_lat(me_ref, table_ref, bands_refs, band_ref, mixed_ref):
    samples, size, width = band_ref.shape
    part, half = size // len(bands_refs), size // 2
    for sample in range(samples):
        for offset, bands_ref in with_offsets(bands_refs):
            place = place_of(me_ref, offset, part)
            band_ref[sample, place] = bands_ref[pl.ds(sample * part, part)]
        mixed = product_of(table_ref[...], band_ref[sample]).astype(jnp.bfloat16)
        spot = pl.ds(sample * half, half)
        mixed_ref[spot, 0:width] = mixed[:half]
        mixed_ref[spot, width : 2 * width] = mixed[half:]


def unmix_lat(me_ref, table_ref, mixed_ref, band_ref, bands_refs):
    samples, size, width = band_ref.shape
    part, half = size // len(bands_refs), size // 2
    for sample in range(samples):
        spot = pl.ds(sample * half, half)
        joined = jnp.concatenate(
            [mixed_ref[spot, 0:width], mixed_ref[spot, width : 2 * width]], axis=0
        )
        bands = product_of(table_ref[...], joined).astype(jnp.bfloat16)
        if len(bands_refs) == 1:
            lead = bands_refs[0].shape[0]
            run = pl.ds(sample * size // lead, size // lead)
            bands_refs[0][:, run] = bands.reshape(lead, size // lead, width)
        else:
            band_ref[sample] = bands
            for offset, bands_ref in with_offsets(bands_refs):
                place = place_of(me_ref, offset, part)
                bands_ref[pl.ds(sample * part, part)] = band_ref[sample, place]


def activate(mixed_ref, w1_ref, b1_ref):
    pre = product_of(mixed_ref[0], w1_ref[0]) + b1_ref[0]
    logistic = sigmoid_of(pre)
    return logistic, pre * logistic


def bend(act_ref, w2_ref, b2_ref):
    out = product_of(act_ref[...], w2_ref[0]) + b2_ref[0]
    return out, jnp.tanh(out * (1.0 / shrink_level))


def forward_kernel(blocks, me_ref, lat_ref, unlat_ref, w1_ref, b1_ref, w2_ref, b2_ref, *refs):
    bands_refs, image_refs = refs[:blocks], refs[blocks : 2 * blocks]
    mixed_ref, act_ref, band_ref = refs[2 * blocks :]
    mix_lat(me_ref, lat_ref, bands_refs, band_ref, mixed_ref.at[0])
    act_ref[...] = activate(mixed_ref, w1_ref, b1_ref)[1].astype(jnp.bfloat16)
    out, bent = bend(act_ref, w2_ref, b2_ref)
    act_ref[...] = (out - shrink_level * bent).astype(jnp.bfloat16)
    unmix_lat(me_ref, unlat_ref, act_ref, band_ref, image_refs)


def backward_kernel(
    block_size, blocks, me_ref, lat_ref, unlat_ref, w1_ref, b1_ref, w2_ref, b2_ref, mixed_ref, *refs
):
    bands_refs, image_refs = refs[:blocks], refs[blocks : 2 * blocks]
    sums_ref, act_ref, gate_ref, cot_ref, kept_ref, band_ref = refs[2 * blocks :]
    transposed = (((1,), (1,)), ((), ()))
    summed = (((0,), (0,)), ((), ()))

    def times(former, latter, dims):
        return lax.dot_general(former, latter, dims, preferred_element_type=jnp.float32)

    def weight_sums(acts, grads, slot):
        width = acts.shape[1] // 2
        full = times(acts, grads, summed)
        real = full[:width, :width] + full[width:, width:]
        imag = full[:width, width:] - full[width:, :width]
        bias = jnp.sum(grads.astype(jnp.float32), axis=0, keepdims=True)
        size = block_size
        owner = lax.broadcasted_iota(jnp.int32, (size, width), 1) // size
        extra = sums_ref.shape[2] - size
        first = lax.broadcasted_iota(jnp.int32, (extra, width), 0) == 0
        for part, values in enumerate((real, imag)):
            joined = values[:size]
            for block in range(1, width // size):
                joined = jnp.where(owner == block, values[block * size : (block + 1) * size], joined)
            sums_ref[slot, part, 0:size] = joined.astype(sums_ref.dtype)
            row = bias[:, part * width : (part + 1) * width]
            sums_ref[slot, part, size:] = jnp.where(first, row, 0.0).astype(sums_ref.dtype)

    logistic, act = activate(mixed_ref, w1_ref, b1_ref)
    act_ref[...] = act.astype(jnp.bfloat16)
    gate_ref[...] = logistic + act * (1.0 - logistic)
    mix_lat(me_ref, lat_ref, bands_refs, band_ref, cot_ref)
    _, bent = bend(act_ref, w2_ref, b2_ref)
    kept_ref[...] = (cot_ref[...].astype(jnp.float32) * (bent * bent)).astype(jnp.bfloat16)
    back = times(kept_ref[...], w2_ref[0], transposed)
    cot_ref[...] = (back * gate_ref[...]).astype(jnp.bfloat16)
    weight_sums(act_ref[...], kept_ref[...], 1)
    kept_ref[...] = times(cot_ref[...], w1_ref[0], transposed).astype(jnp.bfloat16)
    weight_sums(mixed_ref[0], cot_ref[...], 0)
    unmix_lat(me_ref, unlat_ref, kept_ref, band_ref, image_refs)


def group_spec(*shape):
    return pl.BlockSpec((1,) + shape, lambda g, *_: (g,) + (0,) * len(shape))


def bands_specs(rows, bands, groups):
    block = (rows, bands[0].shape[1] // groups)
    return (pl.BlockSpec(block, lambda g, *_: (0, g)),) * len(bands)


def images_like(bands, samples, size, groups):
    if len(bands) > 1:
        shapes = tuple(in_hbm(band.shape, band.dtype) for band in bands)
        return shapes, bands_specs(bands[0].shape[0], bands, groups)
    channels = bands[0].shape[1]
    shape = (1, samples * size, channels)
    spec = pl.BlockSpec(shape[:2] + (channels // groups,), lambda g, *_: (0, 0, g))
    return (in_hbm(shape, jnp.bfloat16),), (spec,)


def forward_mid(me, lat, unlat, bands, w1, b1, w2, b2):
    groups, lanes, _ = w1.shape
    size = lat.shape[0]
    samples = bands[0].shape[0] * len(bands) // size
    positions = samples * size // 2
    table = pl.BlockSpec((size, size), lambda g, _: (0, 0))
    state = (groups, positions, lanes)
    specs = bands_specs(bands[0].shape[0], bands, groups)
    images, image_specs = images_like(bands, samples, size, groups)
    results = pl.pallas_call(
        functools.partial(forward_kernel, len(bands)),
        grid_spec=pltpu.PrefetchScalarGridSpec(
            num_scalar_prefetch=1,
            grid=(groups,),
            in_specs=[
                table, table,
                group_spec(lanes, lanes), group_spec(1, lanes),
                group_spec(lanes, lanes), group_spec(1, lanes),
                *specs,
            ],
            out_specs=image_specs + (group_spec(positions, lanes),),
            scratch_shapes=[
                pltpu.VMEM((positions, lanes), jnp.bfloat16),
                pltpu.VMEM((samples, size, lanes // 2), jnp.bfloat16),
            ],
        ),
        out_shape=images + (in_hbm(state, jnp.bfloat16),),
        compiler_params=params(28),
        cost_estimate=pl.CostEstimate(
            flops=4 * groups * positions * lanes * lanes,
            bytes_accessed=16 * groups * positions * lanes + 4 * groups * lanes * lanes,
            transcendentals=2 * groups * positions * lanes,
        ),
        name="mix_forward",
    )(me, lat, unlat, *hbm(w1), b1, *hbm(w2), b2, *hbm(*bands))
    return results[: len(bands)], results[len(bands)]


def backward_mid(me, lat, unlat, bands, w1, b1, w2, b2, state, count):
    groups, lanes, _ = w1.shape
    size = lat.shape[0]
    samples = bands[0].shape[0] * len(bands) // size
    positions = samples * size // 2
    table = pl.BlockSpec((size, size), lambda g, _: (0, 0))
    size_of_block = lanes // 2 // (count // groups)
    sums = (2, 2, size_of_block + 32, lanes // 2)
    images, image_specs = images_like(bands, samples, size, groups)
    results = pl.pallas_call(
        functools.partial(backward_kernel, size_of_block, len(bands)),
        grid_spec=pltpu.PrefetchScalarGridSpec(
            num_scalar_prefetch=1,
            grid=(groups,),
            in_specs=[
                table, table,
                group_spec(lanes, lanes), group_spec(1, lanes),
                group_spec(lanes, lanes), group_spec(1, lanes),
                group_spec(positions, lanes),
                *bands_specs(bands[0].shape[0], bands, groups),
            ],
            out_specs=image_specs + (pl.BlockSpec(sums, lambda g, _: (0, 0, 0, g)),),
            scratch_shapes=[
                pltpu.VMEM((positions, lanes), jnp.bfloat16),
                pltpu.VMEM((positions, lanes), jnp.float32),
                pltpu.VMEM((positions, lanes), jnp.bfloat16),
                pltpu.VMEM((positions, lanes), jnp.bfloat16),
                pltpu.VMEM((samples, size, lanes // 2), jnp.bfloat16),
            ],
        ),
        out_shape=images + (in_hbm(sums[:3] + (groups * sums[3],), jnp.float32),),
        compiler_params=params(32),
        cost_estimate=pl.CostEstimate(
            flops=8 * groups * positions * lanes * lanes,
            bytes_accessed=16 * groups * positions * lanes + 4 * groups * lanes * lanes,
            transcendentals=0,
        ),
        name="mix_backward",
    )(me, lat, unlat, *hbm(w1), b1, *hbm(w2), b2, *hbm(state, *bands))
    return results[: len(bands)], results[len(bands)]


def swap_with(values, axis, distance):
    pairs = [(i, i ^ distance) for i in range(lax.axis_size(axis))]
    return lax.ppermute(values, axis, pairs)


def waiting(values, arrived):
    return lax.optimization_barrier((values, tuple(arrived)))[0]


def mixed_order(size):
    far = list(range(size // 2, size))
    near = [offset for offset in (2, 3, 1) if offset < size // 2]
    near += list(range(4, size // 2))
    order = []
    for place, offset in enumerate(far):
        order += [offset] + near[place : place + 1] * (place < len(near) - 1)
    return order + near[-1:]


def pick(pair, side):
    return lax.dynamic_index_in_dim(pair, side, 0, keepdims=False)


class GroupSum:
    def __init__(self, sums):
        self.lanes = sums.shape[-1]
        self.side = lax.axis_index("dp")
        self.me = lax.axis_index("space")
        self.count = lax.axis_size("space") // 2
        self.held = sums.reshape(-1, self.lanes)

    def halve(self, axis, distance, bit, kind, arrived):
        pair = waiting(self.held, arrived).reshape(2, -1, self.lanes)
        taken = swap_with(pick(pair, 1 - bit).astype(kind), axis, distance)
        self.held = pick(pair, bit) + taken.astype(jnp.float32)

    def over_dp(self):
        self.halve("dp", 1, self.side, jnp.float32, [])

    def over_next(self, arrived):
        self.halve("space", 1, self.me % 2, jnp.bfloat16, arrived)

    def scatter(self, arrived):
        shares = waiting(self.held, arrived).reshape(self.count, -1, self.lanes)
        place = self.me // 2
        total = pick(shares, place)
        for offset in range(1, self.count):
            given = pick(shares, place ^ offset).astype(jnp.bfloat16)
            total += swap_with(given, "space", 2 * offset).astype(jnp.float32)
        self.total = total.astype(jnp.bfloat16)

    def gather(self, arrived):
        total = waiting(self.total, arrived)
        taken = [total]
        for offset in range(1, self.count):
            taken.append(swap_with(total, "space", 2 * offset))
        self.quarter = jnp.stack(taken)

    def gather_next(self, arrived):
        quarter = waiting(self.quarter, arrived)
        self.half = jnp.stack([quarter, swap_with(quarter, "space", 1)])

    def gather_dp(self, arrived):
        half = waiting(self.half, arrived)
        return half, swap_with(half, "dp", 1)


def finish_kernel(factor, me_ref, half_ref, other_ref, *out_refs):
    side, near, place = me_ref[0], me_ref[1], me_ref[2]
    run = half_ref.shape[2]
    for which in range(2):
        blocks_ref, bias_ref = out_refs[2 * which : 2 * which + 2]
        edge = blocks_ref.shape[-1]
        for part in range(2):
            for piece in range(half_ref.shape[1]):
                spot = (part ^ near, piece ^ place)
                own = half_ref[spot].astype(jnp.float32)
                value = jnp.where(side == which, own, other_ref[spot].astype(jnp.float32)) * factor
                first = piece * run
                count = max(0, min(edge - first, run))
                for block in range(blocks_ref.shape[1]):
                    lanes = slice(block * edge, (block + 1) * edge)
                    if count > 0:
                        blocks_ref[part, block, pl.ds(first, count)] = value[:count, lanes]
                    if first <= edge < first + run:
                        row = edge - first
                        bias_ref[part, pl.ds(block, 1)] = value[row : row + 1, lanes]


def finish_sums(here, half, other, factor, weight_shape, bias_shape):
    outs = [weight_shape, bias_shape] * 2
    return pl.pallas_call(
        functools.partial(finish_kernel, factor),
        out_shape=[jax.ShapeDtypeStruct(shape, jnp.float32) for shape in outs],
        in_specs=[pl.BlockSpec(memory_space=pltpu.SMEM)]
        + [pl.BlockSpec(memory_space=pltpu.VMEM)] * 2,
        out_specs=[pl.BlockSpec(memory_space=pltpu.VMEM)] * 4,
        compiler_params=pltpu.CompilerParams(vmem_limit_bytes=16 * MIB),
        cost_estimate=pl.CostEstimate(flops=0, bytes_accessed=4 * MIB, transcendentals=0),
        name="finish_sums",
    )(here, half, other)


def body(fields, cotangent, w_first, b_first, w_second, b_second):
    samples, rows, width, channels = fields.shape
    owners = lax.axis_size("space")
    lat_total = rows * owners
    modes = KW // owners
    count, edge = w_first.shape[1:3]
    groups = 2
    direct = 2 * modes % 16 == 0
    lead = owners if direct else 1

    order = mixed_order(owners)

    def place(offset):
        return (owners - offset) % owners

    def send(blocks, offsets, taken):
        for offset in offsets:
            taken[offset] = swap_with(blocks[place(offset)], "space", offset)

    def listed(taken):
        return [taken[place(at)] for at in range(owners)]

    def send_all(spectrum):
        spectrum = spectrum.reshape(samples, rows, owners, 2 * modes, channels)
        spectrum = jnp.transpose(spectrum, (2, 0, 1, 3, 4))
        arrived = lax.all_to_all(spectrum, "space", split_axis=0, concat_axis=0, tiled=True)
        return [jnp.transpose(arrived, (1, 0, 2, 3, 4)).reshape(-1, channels)]

    def send_all_back(bands):
        bands = bands.reshape(samples, owners, rows, 2 * modes, channels)
        bands = jnp.transpose(bands, (1, 0, 2, 3, 4))
        arrived = lax.all_to_all(bands, "space", split_axis=0, concat_axis=0, tiled=True)
        return [jnp.transpose(arrived, (1, 2, 0, 3, 4)).reshape(1, -1, channels)]

    me = lax.axis_index("space") if direct else 0
    me = jnp.full((1,), me, jnp.int32)
    plain, scaled = lon_tables(KW, width, owners)
    lat = lat_spread(lat_total, modes)

    spectrum = to_modes(me, plain, fields, lead)
    spectrum, cotangent, w_first, w_second = lax.optimization_barrier(
        (spectrum, cotangent, w_first, w_second)
    )
    cot_spec = to_modes(me, scaled, cotangent, lead)
    w1, w2 = spread_weights(groups, w_first, w_second)
    b1, b2 = block_bias(b_first, groups), block_bias(b_second, groups)
    positions = samples * lax.axis_size("dp") * lat_total * KW
    factor = 1.0 / math.sqrt(positions)

    if not direct:
        gathered = send_all(spectrum[0])
        image, state = forward_mid(me, lat, lat.T, gathered, w1, b1, w2, b2)
        image_band = send_all_back(image[0])
        gathered = send_all(cot_spec[0])
        grad_image, sums = backward_mid(me, lat, lat.T, gathered, w1, b1, w2, b2, state, count)
        grad_band = send_all_back(grad_image[0])
        output = to_cells(me, scaled.T, image_band, fields)
        grad_fields = to_cells(me, plain.T, grad_band, cotangent)
        sums = lax.psum(sums, ("space", "dp")) * factor
        grads = []
        for which in range(2):
            blocks = sums[which, :, :edge].reshape(2, edge, count, edge)
            grads.append(jnp.transpose(blocks, (0, 2, 1, 3)))
            grads.append(sums[which, :, edge].reshape(b_first.shape))
        return (output, grad_fields) + tuple(grads)

    gathered, cot_gathered = {0: spectrum[0]}, {0: cot_spec[0]}
    falling = range(owners - 1, 0, -1)
    send(spectrum, falling[:FIRST], gathered)
    spectrum = waiting(list(spectrum), [cot_spec[0], w1, w2])
    send(spectrum, falling[FIRST:], gathered)
    gathered = listed(gathered)
    image, state = forward_mid(me, lat, lat.T, gathered, w1, b1, w2, b2)
    cot_spec, image = list(cot_spec), list(image)
    send(cot_spec, falling[:FIRST], cot_gathered)
    cot_spec, image = waiting((cot_spec, image), [image[0]])
    send(cot_spec, falling[FIRST:], cot_gathered)

    image_band = {0: image[0]}
    send(image, order, image_band)
    cot_gathered = listed(cot_gathered)
    grad_image, sums = backward_mid(
        me, lat, lat.T, cot_gathered, w1, b1, w2, b2, state, count
    )
    early = [image_band[offset] for offset in order[:HELD]]
    late = [image_band[offset] for offset in order[HELD:]]
    grad_image, sums = waiting((list(grad_image), sums), early)
    group_sum = GroupSum(sums)
    group_sum.over_dp()
    group_sum.over_next(late[:1])
    grad_band = {0: grad_image[0]}
    send(grad_image, order, grad_band)
    arrived = [grad_band[offset] for offset in order]
    image_band = listed(image_band)
    grad_band = listed(grad_band)
    again = waiting(fields, early[:1])
    output = rows_inside(to_cells(me, scaled.T, image_band, again))
    group_sum.scatter(late[1:] + arrived[:1])
    group_sum.gather(arrived[1:3])
    group_sum.gather_next(arrived[3:5])
    group_sum.half, output = lax.optimization_barrier((group_sum.half, output))
    half, other = group_sum.gather_dp(arrived[5:])
    near = lax.axis_index("space")
    here = jnp.stack([lax.axis_index("dp"), near % 2, near // 2]).astype(jnp.int32)
    grads = finish_sums(here, half, other, factor, w_first.shape, b_first.shape)
    grad_fields = rows_inside(to_cells(me, plain.T, grad_band, cotangent))
    return (rows_outside(output), rows_outside(grad_fields)) + tuple(grads)


def solution(mesh):
    split = P(("parts", "dp"), "space", None, None)
    in_specs = (split, split, P(), P(), P(), P())
    out_specs = (
        split,
        split,
        P("parts", None, None, None),
        P("parts", None, None),
        P("parts", None, None, None),
        P("parts", None, None),
    )
    return jax.shard_map(body, mesh=mesh, in_specs=in_specs, out_specs=out_specs, check_vma=False)
```

```python
import functools
import math

import jax
import jax.numpy as jnp
from jax import lax
from jax.experimental import pallas as pl
from jax.experimental.layout import Layout, with_layout_constraint
from jax.experimental.pallas import tpu as pltpu
from jax.sharding import PartitionSpec as P
import ml_dtypes
import numpy as np

KW = 64
shrink_level = 0.05
FIRST = 5
HELD = 5
MIB = 1024 * 1024


def product_of(former, latter):
    return jnp.dot(former, latter, preferred_element_type=jnp.float32)


def lon_tables(mode_count, cell_count, owners):
    wavenums = np.arange(mode_count, dtype=np.int32)
    columns = np.arange(cell_count, dtype=np.int32)
    phase_index = (wavenums[:, None] * columns[None, :] % cell_count).astype(np.float32)
    phases = phase_index * np.float32(2.0 * math.pi / cell_count)
    factor = np.float32(1.0 / math.sqrt(cell_count))
    forward = np.stack([np.cos(phases) * factor, -np.sin(phases) * factor])
    scaled = forward * np.where(wavenums == 0, 1.0, 2.0).astype(np.float32)[:, None]

    def ordered(table):
        split = table.reshape(2, owners, -1, cell_count).transpose(1, 0, 2, 3)
        return split.reshape(-1, cell_count).astype(ml_dtypes.bfloat16)

    return ordered(forward), ordered(scaled)


def lat_spread(row_count, modes):
    indices = np.arange(row_count, dtype=np.int32)
    phase_index = (indices[:, None] * indices[None, :] % row_count).astype(np.float32)
    phases = phase_index * np.float32(2.0 * math.pi / row_count)
    factor = np.float32(1.0 / math.sqrt(row_count))
    cosine = np.cos(phases) * factor
    sine_part = np.sin(phases) * factor
    table = np.stack([np.stack([cosine, sine_part], -1), np.stack([-sine_part, cosine], -1)])
    same = np.eye(modes, dtype=np.float32)
    spread = table[:, :, None, :, :, None] * same[None, None, :, None, None, :]
    size = 2 * row_count * modes
    return spread.reshape(size, size).astype(ml_dtypes.bfloat16)


def block_bias(bias, groups):
    return jnp.transpose(bias.reshape(2, groups, 1, -1), (1, 2, 0, 3)).reshape(groups, 1, -1)


def spread_kernel(*refs):
    half_way = len(refs) // 2
    for blocks_ref, joined_ref in zip(refs[:half_way], refs[half_way:]):
        _, per, size, _ = blocks_ref.shape
        width = per * size
        row = lax.broadcasted_iota(jnp.int32, (size, width), 0)
        lane = lax.broadcasted_iota(jnp.int32, (size, width), 1)
        for block in range(per):
            place = (row + block * size == lane).astype(jnp.bfloat16)
            real = product_of(blocks_ref[0, block], place).astype(jnp.bfloat16)
            imag = product_of(blocks_ref[1, block], place)
            upper = pl.ds(block * size, size)
            lower = pl.ds(width + block * size, size)
            joined_ref[0, upper, 0:width] = real
            joined_ref[0, upper, width : 2 * width] = imag.astype(jnp.bfloat16)
            joined_ref[0, lower, 0:width] = (-imag).astype(jnp.bfloat16)
            joined_ref[0, lower, width : 2 * width] = real


def spread_weights(groups, *weights):
    _, count, size, _ = weights[0].shape
    per = count // groups
    lanes = 2 * per * size
    shape = in_hbm((groups, lanes, lanes), jnp.bfloat16)
    return pl.pallas_call(
        spread_kernel,
        grid=(groups,),
        out_shape=(shape,) * len(weights),
        in_specs=[pl.BlockSpec((2, per, size, size), lambda g: (0, g, 0, 0))] * len(weights),
        out_specs=(group_spec(lanes, lanes),) * len(weights),
        compiler_params=params(12),
        cost_estimate=pl.CostEstimate(
            flops=len(weights) * 2 * count * size * size * lanes,
            bytes_accessed=len(weights) * 2 * groups * lanes * lanes,
            transcendentals=0,
        ),
        name="spread_weights",
    )(*weights)


def params(mebibytes):
    return pltpu.CompilerParams(
        vmem_limit_bytes=mebibytes * MIB, dimension_semantics=("arbitrary",)
    )


def place_of(me_ref, offset, rows):
    return pl.ds(pl.multiple_of((me_ref[0] ^ offset) * rows, rows), rows)


def in_hbm(shape, dtype):
    return pltpu.HBM(shape, dtype)


def hbm(*arrays):
    return [pltpu.with_memory_space_constraint(array, pltpu.HBM) for array in arrays]


def with_offsets(refs):
    return [((len(refs) - place) % len(refs), ref) for place, ref in enumerate(refs)]


def to_modes_kernel(me_ref, table_ref, cells_ref, *refs):
    modes_refs, held_ref = refs[:-1], refs[-1]
    rows = cells_ref.shape[1]
    share = modes_refs[0].shape[0] // rows
    for row in range(rows):
        spectrum = product_of(table_ref[...], cells_ref[0, row])
        held_ref[row] = spectrum.astype(jnp.bfloat16)
        for offset, modes_ref in with_offsets(modes_refs):
            modes_ref[pl.ds(row * share, share)] = held_ref[row, place_of(me_ref, offset, share)]


def to_modes(me, table, cells, owners):
    samples, rows, width, channels = cells.shape
    size = table.shape[0]
    part = rows * size // owners
    return pl.pallas_call(
        to_modes_kernel,
        grid_spec=pltpu.PrefetchScalarGridSpec(
            num_scalar_prefetch=1,
            grid=(samples,),
            in_specs=[
                pl.BlockSpec((size, width), lambda b, _: (0, 0)),
                pl.BlockSpec((1, rows, width, channels), lambda b, _: (b, 0, 0, 0)),
            ],
            out_specs=(pl.BlockSpec((part, channels), lambda b, _: (b, 0)),) * owners,
            scratch_shapes=[pltpu.VMEM((rows, size, channels), jnp.bfloat16)],
        ),
        out_shape=(in_hbm((samples * part, channels), jnp.bfloat16),) * owners,
        compiler_params=params(12),
        cost_estimate=pl.CostEstimate(
            flops=2 * samples * rows * size * width * channels,
            bytes_accessed=2 * samples * rows * channels * (width + size),
            transcendentals=0,
        ),
        name="to_modes",
    )(me, table, cells)


def to_cells_kernel(me_ref, table_ref, base_ref, *refs):
    modes_refs, out_ref, held_ref = refs[:-2], refs[-2], refs[-1]
    rows = base_ref.shape[1]
    share = modes_refs[0].shape[-2] // rows
    for row in range(rows):
        run = pl.ds(row * share, share)
        if len(modes_refs) == 1:
            spectrum = modes_refs[0][:, run].reshape(held_ref.shape[1:])
        else:
            for offset, modes_ref in with_offsets(modes_refs):
                held_ref[row, place_of(me_ref, offset, share)] = modes_ref[run]
            spectrum = held_ref[row]
        image = product_of(table_ref[...], spectrum)
        out_ref[0, row] = (base_ref[0, row].astype(jnp.float32) + image).astype(jnp.bfloat16)


def to_cells(me, table, modes, base):
    samples, rows, width, channels = base.shape
    size = table.shape[1]
    block = pl.BlockSpec((1, rows, width, channels), lambda b, _: (b, 0, 0, 0))
    if len(modes) == 1:
        lead = modes[0].shape[0]
        part = rows * size // lead
        specs = [pl.BlockSpec((lead, part, channels), lambda b, _: (0, b, 0))]
    else:
        part = rows * size // len(modes)
        specs = [pl.BlockSpec((part, channels), lambda b, _: (b, 0))] * len(modes)
    return pl.pallas_call(
        to_cells_kernel,
        grid_spec=pltpu.PrefetchScalarGridSpec(
            num_scalar_prefetch=1,
            grid=(samples,),
            in_specs=[pl.BlockSpec((width, size), lambda b, _: (0, 0)), block] + specs,
            out_specs=block,
            scratch_shapes=[pltpu.VMEM((rows, size, channels), jnp.bfloat16)],
        ),
        out_shape=jax.ShapeDtypeStruct(base.shape, jnp.bfloat16),
        compiler_params=params(12),
        cost_estimate=pl.CostEstimate(
            flops=2 * samples * rows * size * width * channels,
            bytes_accessed=2 * samples * rows * channels * (2 * width + size),
            transcendentals=0,
        ),
        name="to_cells",
    )(me, table, base, *hbm(*modes))


def rows_inside(cells):
    inside = jnp.transpose(cells, (0, 2, 1, 3))
    return with_layout_constraint(inside, Layout(major_to_minor=(0, 1, 2, 3)))


def rows_outside(cells):
    return jnp.transpose(cells, (0, 2, 1, 3))


def sigmoid_of(values):
    return 0.5 + 0.5 * jnp.tanh(0.5 * values)


def mix_lat(me_ref, table_ref, bands_refs, band_ref, mixed_ref):
    samples, size, width = band_ref.shape
    part, half = size // len(bands_refs), size // 2
    for sample in range(samples):
        for offset, bands_ref in with_offsets(bands_refs):
            place = place_of(me_ref, offset, part)
            band_ref[sample, place] = bands_ref[pl.ds(sample * part, part)]
        mixed = product_of(table_ref[...], band_ref[sample]).astype(jnp.bfloat16)
        spot = pl.ds(sample * half, half)
        mixed_ref[spot, 0:width] = mixed[:half]
        mixed_ref[spot, width : 2 * width] = mixed[half:]


def unmix_lat(me_ref, table_ref, mixed_ref, band_ref, bands_refs):
    samples, size, width = band_ref.shape
    part, half = size // len(bands_refs), size // 2
    for sample in range(samples):
        spot = pl.ds(sample * half, half)
        joined = jnp.concatenate(
            [mixed_ref[spot, 0:width], mixed_ref[spot, width : 2 * width]], axis=0
        )
        bands = product_of(table_ref[...], joined).astype(jnp.bfloat16)
        if len(bands_refs) == 1:
            lead = bands_refs[0].shape[0]
            run = pl.ds(sample * size // lead, size // lead)
            bands_refs[0][:, run] = bands.reshape(lead, size // lead, width)
        else:
            band_ref[sample] = bands
            for offset, bands_ref in with_offsets(bands_refs):
                place = place_of(me_ref, offset, part)
                bands_ref[pl.ds(sample * part, part)] = band_ref[sample, place]


def activate(mixed_ref, w1_ref, b1_ref):
    pre = product_of(mixed_ref[0], w1_ref[0]) + b1_ref[0]
    logistic = sigmoid_of(pre)
    return logistic, pre * logistic


def bend(act_ref, w2_ref, b2_ref):
    out = product_of(act_ref[...], w2_ref[0]) + b2_ref[0]
    return out, jnp.tanh(out * (1.0 / shrink_level))


def forward_kernel(blocks, me_ref, lat_ref, unlat_ref, w1_ref, b1_ref, w2_ref, b2_ref, *refs):
    bands_refs, image_refs = refs[:blocks], refs[blocks : 2 * blocks]
    mixed_ref, act_ref, band_ref = refs[2 * blocks :]
    mix_lat(me_ref, lat_ref, bands_refs, band_ref, mixed_ref.at[0])
    act_ref[...] = activate(mixed_ref, w1_ref, b1_ref)[1].astype(jnp.bfloat16)
    out, bent = bend(act_ref, w2_ref, b2_ref)
    act_ref[...] = (out - shrink_level * bent).astype(jnp.bfloat16)
    unmix_lat(me_ref, unlat_ref, act_ref, band_ref, image_refs)


def backward_kernel(
    block_size, blocks, me_ref, lat_ref, unlat_ref, w1_ref, b1_ref, w2_ref, b2_ref, mixed_ref, *refs
):
    bands_refs, image_refs = refs[:blocks], refs[blocks : 2 * blocks]
    sums_ref, act_ref, gate_ref, cot_ref, kept_ref, band_ref = refs[2 * blocks :]
    transposed = (((1,), (1,)), ((), ()))
    summed = (((0,), (0,)), ((), ()))

    def times(former, latter, dims):
        return lax.dot_general(former, latter, dims, preferred_element_type=jnp.float32)

    def weight_sums(acts, grads, slot):
        width = acts.shape[1] // 2
        full = times(acts, grads, summed)
        real = full[:width, :width] + full[width:, width:]
        imag = full[:width, width:] - full[width:, :width]
        bias = jnp.sum(grads.astype(jnp.float32), axis=0, keepdims=True)
        size = block_size
        owner = lax.broadcasted_iota(jnp.int32, (size, width), 1) // size
        extra = sums_ref.shape[2] - size
        first = lax.broadcasted_iota(jnp.int32, (extra, width), 0) == 0
        for part, values in enumerate((real, imag)):
            joined = values[:size]
            for block in range(1, width // size):
                joined = jnp.where(owner == block, values[block * size : (block + 1) * size], joined)
            sums_ref[slot, part, 0:size] = joined.astype(sums_ref.dtype)
            row = bias[:, part * width : (part + 1) * width]
            sums_ref[slot, part, size:] = jnp.where(first, row, 0.0).astype(sums_ref.dtype)

    logistic, act = activate(mixed_ref, w1_ref, b1_ref)
    act_ref[...] = act.astype(jnp.bfloat16)
    gate_ref[...] = logistic + act * (1.0 - logistic)
    mix_lat(me_ref, lat_ref, bands_refs, band_ref, cot_ref)
    _, bent = bend(act_ref, w2_ref, b2_ref)
    kept_ref[...] = (cot_ref[...].astype(jnp.float32) * (bent * bent)).astype(jnp.bfloat16)
    back = times(kept_ref[...], w2_ref[0], transposed)
    cot_ref[...] = (back * gate_ref[...]).astype(jnp.bfloat16)
    weight_sums(act_ref[...], kept_ref[...], 1)
    kept_ref[...] = times(cot_ref[...], w1_ref[0], transposed).astype(jnp.bfloat16)
    weight_sums(mixed_ref[0], cot_ref[...], 0)
    unmix_lat(me_ref, unlat_ref, kept_ref, band_ref, image_refs)


def group_spec(*shape):
    return pl.BlockSpec((1,) + shape, lambda g, *_: (g,) + (0,) * len(shape))


def bands_specs(rows, bands, groups):
    block = (rows, bands[0].shape[1] // groups)
    return (pl.BlockSpec(block, lambda g, *_: (0, g)),) * len(bands)


def images_like(bands, samples, size, groups):
    if len(bands) > 1:
        shapes = tuple(in_hbm(band.shape, band.dtype) for band in bands)
        return shapes, bands_specs(bands[0].shape[0], bands, groups)
    channels = bands[0].shape[1]
    shape = (1, samples * size, channels)
    spec = pl.BlockSpec(shape[:2] + (channels // groups,), lambda g, *_: (0, 0, g))
    return (in_hbm(shape, jnp.bfloat16),), (spec,)


def forward_mid(me, lat, unlat, bands, w1, b1, w2, b2):
    groups, lanes, _ = w1.shape
    size = lat.shape[0]
    samples = bands[0].shape[0] * len(bands) // size
    positions = samples * size // 2
    table = pl.BlockSpec((size, size), lambda g, _: (0, 0))
    state = (groups, positions, lanes)
    specs = bands_specs(bands[0].shape[0], bands, groups)
    images, image_specs = images_like(bands, samples, size, groups)
    results = pl.pallas_call(
        functools.partial(forward_kernel, len(bands)),
        grid_spec=pltpu.PrefetchScalarGridSpec(
            num_scalar_prefetch=1,
            grid=(groups,),
            in_specs=[
                table, table,
                group_spec(lanes, lanes), group_spec(1, lanes),
                group_spec(lanes, lanes), group_spec(1, lanes),
                *specs,
            ],
            out_specs=image_specs + (group_spec(positions, lanes),),
            scratch_shapes=[
                pltpu.VMEM((positions, lanes), jnp.bfloat16),
                pltpu.VMEM((samples, size, lanes // 2), jnp.bfloat16),
            ],
        ),
        out_shape=images + (in_hbm(state, jnp.bfloat16),),
        compiler_params=params(28),
        cost_estimate=pl.CostEstimate(
            flops=4 * groups * positions * lanes * lanes,
            bytes_accessed=16 * groups * positions * lanes + 4 * groups * lanes * lanes,
            transcendentals=2 * groups * positions * lanes,
        ),
        name="mix_forward",
    )(me, lat, unlat, *hbm(w1), b1, *hbm(w2), b2, *hbm(*bands))
    return results[: len(bands)], results[len(bands)]


def backward_mid(me, lat, unlat, bands, w1, b1, w2, b2, state, count):
    groups, lanes, _ = w1.shape
    size = lat.shape[0]
    samples = bands[0].shape[0] * len(bands) // size
    positions = samples * size // 2
    table = pl.BlockSpec((size, size), lambda g, _: (0, 0))
    size_of_block = lanes // 2 // (count // groups)
    sums = (2, 2, size_of_block + 32, lanes // 2)
    images, image_specs = images_like(bands, samples, size, groups)
    results = pl.pallas_call(
        functools.partial(backward_kernel, size_of_block, len(bands)),
        grid_spec=pltpu.PrefetchScalarGridSpec(
            num_scalar_prefetch=1,
            grid=(groups,),
            in_specs=[
                table, table,
                group_spec(lanes, lanes), group_spec(1, lanes),
                group_spec(lanes, lanes), group_spec(1, lanes),
                group_spec(positions, lanes),
                *bands_specs(bands[0].shape[0], bands, groups),
            ],
            out_specs=image_specs + (pl.BlockSpec(sums, lambda g, _: (0, 0, 0, g)),),
            scratch_shapes=[
                pltpu.VMEM((positions, lanes), jnp.bfloat16),
                pltpu.VMEM((positions, lanes), jnp.float32),
                pltpu.VMEM((positions, lanes), jnp.bfloat16),
                pltpu.VMEM((positions, lanes), jnp.bfloat16),
                pltpu.VMEM((samples, size, lanes // 2), jnp.bfloat16),
            ],
        ),
        out_shape=images + (in_hbm(sums[:3] + (groups * sums[3],), jnp.float32),),
        compiler_params=params(32),
        cost_estimate=pl.CostEstimate(
            flops=8 * groups * positions * lanes * lanes,
            bytes_accessed=16 * groups * positions * lanes + 4 * groups * lanes * lanes,
            transcendentals=0,
        ),
        name="mix_backward",
    )(me, lat, unlat, *hbm(w1), b1, *hbm(w2), b2, *hbm(state, *bands))
    return results[: len(bands)], results[len(bands)]


def swap_with(values, axis, distance):
    pairs = [(i, i ^ distance) for i in range(lax.axis_size(axis))]
    return lax.ppermute(values, axis, pairs)


def waiting(values, arrived):
    return lax.optimization_barrier((values, tuple(arrived)))[0]


def mixed_order(size):
    far = list(range(size // 2, size))
    near = [offset for offset in (2, 3, 1) if offset < size // 2]
    near += list(range(4, size // 2))
    order = []
    for place, offset in enumerate(far):
        order += [offset] + near[place : place + 1] * (place < len(near) - 1)
    return order + near[-1:]


def pick(pair, side):
    return lax.dynamic_index_in_dim(pair, side, 0, keepdims=False)


class GroupSum:
    def __init__(self, sums):
        self.lanes = sums.shape[-1]
        self.side = lax.axis_index("dp")
        self.me = lax.axis_index("space")
        self.count = lax.axis_size("space") // 2
        self.held = sums.reshape(-1, self.lanes)

    def halve(self, axis, distance, bit, kind, arrived):
        pair = waiting(self.held, arrived).reshape(2, -1, self.lanes)
        taken = swap_with(pick(pair, 1 - bit).astype(kind), axis, distance)
        self.held = pick(pair, bit) + taken.astype(jnp.float32)

    def over_dp(self):
        self.halve("dp", 1, self.side, jnp.float32, [])

    def over_next(self, arrived):
        self.halve("space", 1, self.me % 2, jnp.bfloat16, arrived)

    def scatter(self, arrived):
        shares = waiting(self.held, arrived).reshape(self.count, -1, self.lanes)
        place = self.me // 2
        total = pick(shares, place)
        for offset in range(1, self.count):
            given = pick(shares, place ^ offset).astype(jnp.bfloat16)
            total += swap_with(given, "space", 2 * offset).astype(jnp.float32)
        self.total = total.astype(jnp.bfloat16)

    def gather(self, arrived):
        total = waiting(self.total, arrived)
        taken = [total]
        for offset in range(1, self.count):
            taken.append(swap_with(total, "space", 2 * offset))
        self.quarter = jnp.stack(taken)

    def gather_next(self, arrived):
        quarter = waiting(self.quarter, arrived)
        self.half = jnp.stack([quarter, swap_with(quarter, "space", 1)])

    def gather_dp(self, arrived):
        half = waiting(self.half, arrived)
        return half, swap_with(half, "dp", 1)


def finish_kernel(factor, me_ref, half_ref, other_ref, *out_refs):
    side, near, place = me_ref[0], me_ref[1], me_ref[2]
    run = half_ref.shape[2]
    for which in range(2):
        blocks_ref, bias_ref = out_refs[2 * which : 2 * which + 2]
        edge = blocks_ref.shape[-1]
        for part in range(2):
            for piece in range(half_ref.shape[1]):
                spot = (part ^ near, piece ^ place)
                own = half_ref[spot].astype(jnp.float32)
                value = jnp.where(side == which, own, other_ref[spot].astype(jnp.float32)) * factor
                first = piece * run
                count = max(0, min(edge - first, run))
                for block in range(blocks_ref.shape[1]):
                    lanes = slice(block * edge, (block + 1) * edge)
                    if count > 0:
                        blocks_ref[part, block, pl.ds(first, count)] = value[:count, lanes]
                    if first <= edge < first + run:
                        row = edge - first
                        bias_ref[part, pl.ds(block, 1)] = value[row : row + 1, lanes]


def finish_sums(here, half, other, factor, weight_shape, bias_shape):
    outs = [weight_shape, bias_shape] * 2
    return pl.pallas_call(
        functools.partial(finish_kernel, factor),
        out_shape=[jax.ShapeDtypeStruct(shape, jnp.float32) for shape in outs],
        in_specs=[pl.BlockSpec(memory_space=pltpu.SMEM)]
        + [pl.BlockSpec(memory_space=pltpu.VMEM)] * 2,
        out_specs=[pl.BlockSpec(memory_space=pltpu.VMEM)] * 4,
        compiler_params=pltpu.CompilerParams(vmem_limit_bytes=16 * MIB),
        cost_estimate=pl.CostEstimate(flops=0, bytes_accessed=4 * MIB, transcendentals=0),
        name="finish_sums",
    )(here, half, other)


def body(fields, cotangent, w_first, b_first, w_second, b_second):
    samples, rows, width, channels = fields.shape
    owners = lax.axis_size("space")
    lat_total = rows * owners
    modes = KW // owners
    count, edge = w_first.shape[1:3]
    groups = 2
    direct = 2 * modes % 16 == 0
    lead = owners if direct else 1

    order = mixed_order(owners)

    def place(offset):
        return (owners - offset) % owners

    def send(blocks, offsets, taken):
        for offset in offsets:
            taken[offset] = swap_with(blocks[place(offset)], "space", offset)

    def listed(taken):
        return [taken[place(at)] for at in range(owners)]

    def send_all(spectrum):
        spectrum = spectrum.reshape(samples, rows, owners, 2 * modes, channels)
        spectrum = jnp.transpose(spectrum, (2, 0, 1, 3, 4))
        arrived = lax.all_to_all(spectrum, "space", split_axis=0, concat_axis=0, tiled=True)
        return [jnp.transpose(arrived, (1, 0, 2, 3, 4)).reshape(-1, channels)]

    def send_all_back(bands):
        bands = bands.reshape(samples, owners, rows, 2 * modes, channels)
        bands = jnp.transpose(bands, (1, 0, 2, 3, 4))
        arrived = lax.all_to_all(bands, "space", split_axis=0, concat_axis=0, tiled=True)
        return [jnp.transpose(arrived, (1, 2, 0, 3, 4)).reshape(1, -1, channels)]

    me = lax.axis_index("space") if direct else 0
    me = jnp.full((1,), me, jnp.int32)
    plain, scaled = lon_tables(KW, width, owners)
    lat = lat_spread(lat_total, modes)

    spectrum = to_modes(me, plain, fields, lead)
    spectrum, cotangent, w_first, w_second = lax.optimization_barrier(
        (spectrum, cotangent, w_first, w_second)
    )
    cot_spec = to_modes(me, scaled, cotangent, lead)
    w1, w2 = spread_weights(groups, w_first, w_second)
    b1, b2 = block_bias(b_first, groups), block_bias(b_second, groups)
    positions = samples * lax.axis_size("dp") * lat_total * KW
    factor = 1.0 / math.sqrt(positions)

    if not direct:
        gathered = send_all(spectrum[0])
        image, state = forward_mid(me, lat, lat.T, gathered, w1, b1, w2, b2)
        image_band = send_all_back(image[0])
        gathered = send_all(cot_spec[0])
        grad_image, sums = backward_mid(me, lat, lat.T, gathered, w1, b1, w2, b2, state, count)
        grad_band = send_all_back(grad_image[0])
        output = to_cells(me, scaled.T, image_band, fields)
        grad_fields = to_cells(me, plain.T, grad_band, cotangent)
        sums = lax.psum(sums, ("space", "dp")) * factor
        grads = []
        for which in range(2):
            blocks = sums[which, :, :edge].reshape(2, edge, count, edge)
            grads.append(jnp.transpose(blocks, (0, 2, 1, 3)))
            grads.append(sums[which, :, edge].reshape(b_first.shape))
        return (output, grad_fields) + tuple(grads)

    gathered, cot_gathered = {0: spectrum[0]}, {0: cot_spec[0]}
    falling = range(owners - 1, 0, -1)
    send(spectrum, falling[:FIRST], gathered)
    spectrum = waiting(list(spectrum), [cot_spec[0], w1, w2])
    send(spectrum, falling[FIRST:], gathered)
    gathered = listed(gathered)
    image, state = forward_mid(me, lat, lat.T, gathered, w1, b1, w2, b2)
    cot_spec, image = list(cot_spec), list(image)
    send(cot_spec, falling[:FIRST], cot_gathered)
    cot_spec, image = waiting((cot_spec, image), [image[0]])
    send(cot_spec, falling[FIRST:], cot_gathered)

    image_band = {0: image[0]}
    send(image, order, image_band)
    cot_gathered = listed(cot_gathered)
    grad_image, sums = backward_mid(
        me, lat, lat.T, cot_gathered, w1, b1, w2, b2, state, count
    )
    early = [image_band[offset] for offset in order[:HELD]]
    late = [image_band[offset] for offset in order[HELD:]]
    grad_image, sums = waiting((list(grad_image), sums), early)
    group_sum = GroupSum(sums)
    group_sum.over_dp()
    again = with_layout_constraint(waiting(fields, early[:1]), Layout(major_to_minor=(0, 1, 2, 3)))
    group_sum.held, again = lax.optimization_barrier((group_sum.held, again))
    group_sum.over_next(late[:1])
    grad_band = {0: grad_image[0]}
    send(grad_image, order, grad_band)
    arrived = [grad_band[offset] for offset in order]
    image_band = listed(image_band)
    grad_band = listed(grad_band)
    output = rows_inside(to_cells(me, scaled.T, image_band, again))
    group_sum.scatter(late[1:] + arrived[:1])
    group_sum.gather(arrived[1:3])
    group_sum.gather_next(arrived[3:5])
    group_sum.half, output = lax.optimization_barrier((group_sum.half, output))
    half, other = group_sum.gather_dp(arrived[5:])
    near = lax.axis_index("space")
    here = jnp.stack([lax.axis_index("dp"), near % 2, near // 2]).astype(jnp.int32)
    grads = finish_sums(here, half, other, factor, w_first.shape, b_first.shape)
    grad_fields = rows_inside(to_cells(me, plain.T, grad_band, cotangent))
    return (rows_outside(output), rows_outside(grad_fields)) + tuple(grads)


def solution(mesh):
    split = P(("parts", "dp"), "space", None, None)
    in_specs = (split, split, P(), P(), P(), P())
    out_specs = (
        split,
        split,
        P("parts", None, None, None),
        P("parts", None, None),
        P("parts", None, None, None),
        P("parts", None, None),
    )
    return jax.shard_map(body, mesh=mesh, in_specs=in_specs, out_specs=out_specs, check_vma=False)
```

```python
import functools
import math

import jax
import jax.numpy as jnp
from jax import lax
from jax.experimental import pallas as pl
from jax.experimental.layout import Layout, with_layout_constraint
from jax.experimental.pallas import tpu as pltpu
from jax.sharding import PartitionSpec as P
import ml_dtypes
import numpy as np

KW = 64
shrink_level = 0.05
FIRST = 5
HELD = 5
MIB = 1024 * 1024


def product_of(former, latter):
    return jnp.dot(former, latter, preferred_element_type=jnp.float32)


def lon_tables(mode_count, cell_count, owners):
    wavenums = np.arange(mode_count, dtype=np.int32)
    columns = np.arange(cell_count, dtype=np.int32)
    phase_index = (wavenums[:, None] * columns[None, :] % cell_count).astype(np.float32)
    phases = phase_index * np.float32(2.0 * math.pi / cell_count)
    factor = np.float32(1.0 / math.sqrt(cell_count))
    forward = np.stack([np.cos(phases) * factor, -np.sin(phases) * factor])
    scaled = forward * np.where(wavenums == 0, 1.0, 2.0).astype(np.float32)[:, None]

    def ordered(table):
        split = table.reshape(2, owners, -1, cell_count).transpose(1, 0, 2, 3)
        return split.reshape(-1, cell_count).astype(ml_dtypes.bfloat16)

    return ordered(forward), ordered(scaled)


def lat_spread(row_count, modes):
    indices = np.arange(row_count, dtype=np.int32)
    phase_index = (indices[:, None] * indices[None, :] % row_count).astype(np.float32)
    phases = phase_index * np.float32(2.0 * math.pi / row_count)
    factor = np.float32(1.0 / math.sqrt(row_count))
    cosine = np.cos(phases) * factor
    sine_part = np.sin(phases) * factor
    table = np.stack([np.stack([cosine, sine_part], -1), np.stack([-sine_part, cosine], -1)])
    same = np.eye(modes, dtype=np.float32)
    spread = table[:, :, None, :, :, None] * same[None, None, :, None, None, :]
    size = 2 * row_count * modes
    return spread.reshape(size, size).astype(ml_dtypes.bfloat16)


def block_bias(bias, groups):
    return jnp.transpose(bias.reshape(2, groups, 1, -1), (1, 2, 0, 3)).reshape(groups, 1, -1)


def spread_kernel(*refs):
    half_way = len(refs) // 2
    for blocks_ref, joined_ref in zip(refs[:half_way], refs[half_way:]):
        _, per, size, _ = blocks_ref.shape
        width = per * size
        row = lax.broadcasted_iota(jnp.int32, (size, width), 0)
        lane = lax.broadcasted_iota(jnp.int32, (size, width), 1)
        for block in range(per):
            place = (row + block * size == lane).astype(jnp.bfloat16)
            real = product_of(blocks_ref[0, block], place).astype(jnp.bfloat16)
            imag = product_of(blocks_ref[1, block], place)
            upper = pl.ds(block * size, size)
            lower = pl.ds(width + block * size, size)
            joined_ref[0, upper, 0:width] = real
            joined_ref[0, upper, width : 2 * width] = imag.astype(jnp.bfloat16)
            joined_ref[0, lower, 0:width] = (-imag).astype(jnp.bfloat16)
            joined_ref[0, lower, width : 2 * width] = real


def spread_weights(groups, *weights):
    _, count, size, _ = weights[0].shape
    per = count // groups
    lanes = 2 * per * size
    shape = in_hbm((groups, lanes, lanes), jnp.bfloat16)
    return pl.pallas_call(
        spread_kernel,
        grid=(groups,),
        out_shape=(shape,) * len(weights),
        in_specs=[pl.BlockSpec((2, per, size, size), lambda g: (0, g, 0, 0))] * len(weights),
        out_specs=(group_spec(lanes, lanes),) * len(weights),
        compiler_params=params(12),
        cost_estimate=pl.CostEstimate(
            flops=len(weights) * 2 * count * size * size * lanes,
            bytes_accessed=len(weights) * 2 * groups * lanes * lanes,
            transcendentals=0,
        ),
        name="spread_weights",
    )(*weights)


def params(mebibytes):
    return pltpu.CompilerParams(
        vmem_limit_bytes=mebibytes * MIB, dimension_semantics=("arbitrary",)
    )


def place_of(me_ref, offset, rows):
    return pl.ds(pl.multiple_of((me_ref[0] ^ offset) * rows, rows), rows)


def in_hbm(shape, dtype):
    return pltpu.HBM(shape, dtype)


def hbm(*arrays):
    return [pltpu.with_memory_space_constraint(array, pltpu.HBM) for array in arrays]


def with_offsets(refs):
    return [((len(refs) - place) % len(refs), ref) for place, ref in enumerate(refs)]


def to_modes_kernel(me_ref, table_ref, cells_ref, *refs):
    modes_refs, held_ref = refs[:-1], refs[-1]
    rows = cells_ref.shape[1]
    share = modes_refs[0].shape[0] // rows
    for row in range(rows):
        spectrum = product_of(table_ref[...], cells_ref[0, row])
        held_ref[row] = spectrum.astype(jnp.bfloat16)
        for offset, modes_ref in with_offsets(modes_refs):
            modes_ref[pl.ds(row * share, share)] = held_ref[row, place_of(me_ref, offset, share)]


def to_modes(me, table, cells, owners):
    samples, rows, width, channels = cells.shape
    size = table.shape[0]
    part = rows * size // owners
    return pl.pallas_call(
        to_modes_kernel,
        grid_spec=pltpu.PrefetchScalarGridSpec(
            num_scalar_prefetch=1,
            grid=(samples,),
            in_specs=[
                pl.BlockSpec((size, width), lambda b, _: (0, 0)),
                pl.BlockSpec((1, rows, width, channels), lambda b, _: (b, 0, 0, 0)),
            ],
            out_specs=(pl.BlockSpec((part, channels), lambda b, _: (b, 0)),) * owners,
            scratch_shapes=[pltpu.VMEM((rows, size, channels), jnp.bfloat16)],
        ),
        out_shape=(in_hbm((samples * part, channels), jnp.bfloat16),) * owners,
        compiler_params=params(12),
        cost_estimate=pl.CostEstimate(
            flops=2 * samples * rows * size * width * channels,
            bytes_accessed=2 * samples * rows * channels * (width + size),
            transcendentals=0,
        ),
        name="to_modes",
    )(me, table, cells)


def to_cells_kernel(me_ref, table_ref, base_ref, *refs):
    modes_refs, out_ref, held_ref = refs[:-2], refs[-2], refs[-1]
    rows = base_ref.shape[1]
    share = modes_refs[0].shape[-2] // rows
    for row in range(rows):
        run = pl.ds(row * share, share)
        if len(modes_refs) == 1:
            spectrum = modes_refs[0][:, run].reshape(held_ref.shape[1:])
        else:
            for offset, modes_ref in with_offsets(modes_refs):
                held_ref[row, place_of(me_ref, offset, share)] = modes_ref[run]
            spectrum = held_ref[row]
        image = product_of(table_ref[...], spectrum)
        out_ref[0, row] = (base_ref[0, row].astype(jnp.float32) + image).astype(jnp.bfloat16)


def to_cells(me, table, modes, base):
    samples, rows, width, channels = base.shape
    size = table.shape[1]
    block = pl.BlockSpec((1, rows, width, channels), lambda b, _: (b, 0, 0, 0))
    if len(modes) == 1:
        lead = modes[0].shape[0]
        part = rows * size // lead
        specs = [pl.BlockSpec((lead, part, channels), lambda b, _: (0, b, 0))]
    else:
        part = rows * size // len(modes)
        specs = [pl.BlockSpec((part, channels), lambda b, _: (b, 0))] * len(modes)
    return pl.pallas_call(
        to_cells_kernel,
        grid_spec=pltpu.PrefetchScalarGridSpec(
            num_scalar_prefetch=1,
            grid=(samples,),
            in_specs=[pl.BlockSpec((width, size), lambda b, _: (0, 0)), block] + specs,
            out_specs=block,
            scratch_shapes=[pltpu.VMEM((rows, size, channels), jnp.bfloat16)],
        ),
        out_shape=jax.ShapeDtypeStruct(base.shape, jnp.bfloat16),
        compiler_params=params(12),
        cost_estimate=pl.CostEstimate(
            flops=2 * samples * rows * size * width * channels,
            bytes_accessed=2 * samples * rows * channels * (2 * width + size),
            transcendentals=0,
        ),
        name="to_cells",
    )(me, table, base, *hbm(*modes))


def rows_inside(cells):
    inside = jnp.transpose(cells, (0, 2, 1, 3))
    return with_layout_constraint(inside, Layout(major_to_minor=(0, 1, 2, 3)))


def rows_outside(cells):
    return jnp.transpose(cells, (0, 2, 1, 3))


def sigmoid_of(values):
    return 0.5 + 0.5 * jnp.tanh(0.5 * values)


def mix_lat(me_ref, table_ref, bands_refs, band_ref, mixed_ref):
    samples, size, width = band_ref.shape
    part, half = size // len(bands_refs), size // 2
    for sample in range(samples):
        for offset, bands_ref in with_offsets(bands_refs):
            place = place_of(me_ref, offset, part)
            band_ref[sample, place] = bands_ref[pl.ds(sample * part, part)]
        mixed = product_of(table_ref[...], band_ref[sample]).astype(jnp.bfloat16)
        spot = pl.ds(sample * half, half)
        mixed_ref[spot, 0:width] = mixed[:half]
        mixed_ref[spot, width : 2 * width] = mixed[half:]


def unmix_lat(me_ref, table_ref, mixed_ref, band_ref, bands_refs):
    samples, size, width = band_ref.shape
    part, half = size // len(bands_refs), size // 2
    for sample in range(samples):
        spot = pl.ds(sample * half, half)
        joined = jnp.concatenate(
            [mixed_ref[spot, 0:width], mixed_ref[spot, width : 2 * width]], axis=0
        )
        bands = product_of(table_ref[...], joined).astype(jnp.bfloat16)
        if len(bands_refs) == 1:
            lead = bands_refs[0].shape[0]
            run = pl.ds(sample * size // lead, size // lead)
            bands_refs[0][:, run] = bands.reshape(lead, size // lead, width)
        else:
            band_ref[sample] = bands
            for offset, bands_ref in with_offsets(bands_refs):
                place = place_of(me_ref, offset, part)
                bands_ref[pl.ds(sample * part, part)] = band_ref[sample, place]


def activate(mixed_ref, w1_ref, b1_ref):
    pre = product_of(mixed_ref[0], w1_ref[0]) + b1_ref[0]
    logistic = sigmoid_of(pre)
    return logistic, pre * logistic


def bend(act_ref, w2_ref, b2_ref):
    out = product_of(act_ref[...], w2_ref[0]) + b2_ref[0]
    return out, jnp.tanh(out * (1.0 / shrink_level))


def forward_kernel(blocks, me_ref, lat_ref, unlat_ref, w1_ref, b1_ref, w2_ref, b2_ref, *refs):
    bands_refs, image_refs = refs[:blocks], refs[blocks : 2 * blocks]
    mixed_ref, act_ref, band_ref = refs[2 * blocks :]
    mix_lat(me_ref, lat_ref, bands_refs, band_ref, mixed_ref.at[0])
    act_ref[...] = activate(mixed_ref, w1_ref, b1_ref)[1].astype(jnp.bfloat16)
    out, bent = bend(act_ref, w2_ref, b2_ref)
    act_ref[...] = (out - shrink_level * bent).astype(jnp.bfloat16)
    unmix_lat(me_ref, unlat_ref, act_ref, band_ref, image_refs)


def backward_kernel(
    block_size, blocks, me_ref, lat_ref, unlat_ref, w1_ref, b1_ref, w2_ref, b2_ref, mixed_ref, *refs
):
    bands_refs, image_refs = refs[:blocks], refs[blocks : 2 * blocks]
    sums_ref, act_ref, gate_ref, cot_ref, kept_ref, band_ref = refs[2 * blocks :]
    transposed = (((1,), (1,)), ((), ()))
    summed = (((0,), (0,)), ((), ()))

    def times(former, latter, dims):
        return lax.dot_general(former, latter, dims, preferred_element_type=jnp.float32)

    def weight_sums(acts, grads, slot):
        width = acts.shape[1] // 2
        full = times(acts, grads, summed)
        real = full[:width, :width] + full[width:, width:]
        imag = full[:width, width:] - full[width:, :width]
        bias = jnp.sum(grads.astype(jnp.float32), axis=0, keepdims=True)
        size = block_size
        owner = lax.broadcasted_iota(jnp.int32, (size, width), 1) // size
        extra = sums_ref.shape[2] - size
        first = lax.broadcasted_iota(jnp.int32, (extra, width), 0) == 0
        for part, values in enumerate((real, imag)):
            joined = values[:size]
            for block in range(1, width // size):
                joined = jnp.where(owner == block, values[block * size : (block + 1) * size], joined)
            sums_ref[slot, part, 0:size] = joined.astype(sums_ref.dtype)
            row = bias[:, part * width : (part + 1) * width]
            sums_ref[slot, part, size:] = jnp.where(first, row, 0.0).astype(sums_ref.dtype)

    logistic, act = activate(mixed_ref, w1_ref, b1_ref)
    act_ref[...] = act.astype(jnp.bfloat16)
    gate_ref[...] = logistic + act * (1.0 - logistic)
    mix_lat(me_ref, lat_ref, bands_refs, band_ref, cot_ref)
    _, bent = bend(act_ref, w2_ref, b2_ref)
    kept_ref[...] = (cot_ref[...].astype(jnp.float32) * (bent * bent)).astype(jnp.bfloat16)
    back = times(kept_ref[...], w2_ref[0], transposed)
    cot_ref[...] = (back * gate_ref[...]).astype(jnp.bfloat16)
    weight_sums(act_ref[...], kept_ref[...], 1)
    kept_ref[...] = times(cot_ref[...], w1_ref[0], transposed).astype(jnp.bfloat16)
    weight_sums(mixed_ref[0], cot_ref[...], 0)
    unmix_lat(me_ref, unlat_ref, kept_ref, band_ref, image_refs)


def group_spec(*shape):
    return pl.BlockSpec((1,) + shape, lambda g, *_: (g,) + (0,) * len(shape))


def bands_specs(rows, bands, groups):
    block = (rows, bands[0].shape[1] // groups)
    return (pl.BlockSpec(block, lambda g, *_: (0, g)),) * len(bands)


def images_like(bands, samples, size, groups):
    if len(bands) > 1:
        shapes = tuple(in_hbm(band.shape, band.dtype) for band in bands)
        return shapes, bands_specs(bands[0].shape[0], bands, groups)
    channels = bands[0].shape[1]
    shape = (1, samples * size, channels)
    spec = pl.BlockSpec(shape[:2] + (channels // groups,), lambda g, *_: (0, 0, g))
    return (in_hbm(shape, jnp.bfloat16),), (spec,)


def forward_mid(me, lat, unlat, bands, w1, b1, w2, b2):
    groups, lanes, _ = w1.shape
    size = lat.shape[0]
    samples = bands[0].shape[0] * len(bands) // size
    positions = samples * size // 2
    table = pl.BlockSpec((size, size), lambda g, _: (0, 0))
    state = (groups, positions, lanes)
    specs = bands_specs(bands[0].shape[0], bands, groups)
    images, image_specs = images_like(bands, samples, size, groups)
    results = pl.pallas_call(
        functools.partial(forward_kernel, len(bands)),
        grid_spec=pltpu.PrefetchScalarGridSpec(
            num_scalar_prefetch=1,
            grid=(groups,),
            in_specs=[
                table, table,
                group_spec(lanes, lanes), group_spec(1, lanes),
                group_spec(lanes, lanes), group_spec(1, lanes),
                *specs,
            ],
            out_specs=image_specs + (group_spec(positions, lanes),),
            scratch_shapes=[
                pltpu.VMEM((positions, lanes), jnp.bfloat16),
                pltpu.VMEM((samples, size, lanes // 2), jnp.bfloat16),
            ],
        ),
        out_shape=images + (in_hbm(state, jnp.bfloat16),),
        compiler_params=params(28),
        cost_estimate=pl.CostEstimate(
            flops=4 * groups * positions * lanes * lanes,
            bytes_accessed=16 * groups * positions * lanes + 4 * groups * lanes * lanes,
            transcendentals=2 * groups * positions * lanes,
        ),
        name="mix_forward",
    )(me, lat, unlat, *hbm(w1), b1, *hbm(w2), b2, *hbm(*bands))
    return results[: len(bands)], results[len(bands)]


def backward_mid(me, lat, unlat, bands, w1, b1, w2, b2, state, count):
    groups, lanes, _ = w1.shape
    size = lat.shape[0]
    samples = bands[0].shape[0] * len(bands) // size
    positions = samples * size // 2
    table = pl.BlockSpec((size, size), lambda g, _: (0, 0))
    size_of_block = lanes // 2 // (count // groups)
    sums = (2, 2, size_of_block + 32, lanes // 2)
    images, image_specs = images_like(bands, samples, size, groups)
    results = pl.pallas_call(
        functools.partial(backward_kernel, size_of_block, len(bands)),
        grid_spec=pltpu.PrefetchScalarGridSpec(
            num_scalar_prefetch=1,
            grid=(groups,),
            in_specs=[
                table, table,
                group_spec(lanes, lanes), group_spec(1, lanes),
                group_spec(lanes, lanes), group_spec(1, lanes),
                group_spec(positions, lanes),
                *bands_specs(bands[0].shape[0], bands, groups),
            ],
            out_specs=image_specs + (pl.BlockSpec(sums, lambda g, _: (0, 0, 0, g)),),
            scratch_shapes=[
                pltpu.VMEM((positions, lanes), jnp.bfloat16),
                pltpu.VMEM((positions, lanes), jnp.float32),
                pltpu.VMEM((positions, lanes), jnp.bfloat16),
                pltpu.VMEM((positions, lanes), jnp.bfloat16),
                pltpu.VMEM((samples, size, lanes // 2), jnp.bfloat16),
            ],
        ),
        out_shape=images + (in_hbm(sums[:3] + (groups * sums[3],), jnp.float32),),
        compiler_params=params(32),
        cost_estimate=pl.CostEstimate(
            flops=8 * groups * positions * lanes * lanes,
            bytes_accessed=16 * groups * positions * lanes + 4 * groups * lanes * lanes,
            transcendentals=0,
        ),
        name="mix_backward",
    )(me, lat, unlat, *hbm(w1), b1, *hbm(w2), b2, *hbm(state, *bands))
    return results[: len(bands)], results[len(bands)]


def swap_with(values, axis, distance):
    pairs = [(i, i ^ distance) for i in range(lax.axis_size(axis))]
    return lax.ppermute(values, axis, pairs)


def waiting(values, arrived):
    return lax.optimization_barrier((values, tuple(arrived)))[0]


def mixed_order(size):
    far = list(range(size // 2, size))
    near = [offset for offset in (2, 3, 1) if offset < size // 2]
    near += list(range(4, size // 2))
    order = []
    for place, offset in enumerate(far):
        order += [offset] + near[place : place + 1] * (place < len(near) - 1)
    return order + near[-1:]


def pick(pair, side):
    return lax.dynamic_index_in_dim(pair, side, 0, keepdims=False)


class GroupSum:
    def __init__(self, sums):
        self.lanes = sums.shape[-1]
        self.side = lax.axis_index("dp")
        self.me = lax.axis_index("space")
        self.count = lax.axis_size("space") // 2
        self.held = sums.reshape(-1, self.lanes)

    def halve(self, axis, distance, bit, kind, arrived):
        pair = waiting(self.held, arrived).reshape(2, -1, self.lanes)
        taken = swap_with(pick(pair, 1 - bit).astype(kind), axis, distance)
        self.held = pick(pair, bit) + taken.astype(jnp.float32)

    def over_dp(self):
        self.halve("dp", 1, self.side, jnp.float32, [])

    def over_next(self, arrived):
        self.halve("space", 1, self.me % 2, jnp.bfloat16, arrived)

    def scatter(self, arrived):
        shares = waiting(self.held, arrived).reshape(self.count, -1, self.lanes)
        place = self.me // 2
        total = pick(shares, place)
        for offset in range(1, self.count):
            given = pick(shares, place ^ offset).astype(jnp.bfloat16)
            total += swap_with(given, "space", 2 * offset).astype(jnp.float32)
        self.total = total.astype(jnp.bfloat16)

    def gather(self, arrived):
        total = waiting(self.total, arrived)
        taken = [total]
        for offset in range(1, self.count):
            taken.append(swap_with(total, "space", 2 * offset))
        self.quarter = jnp.stack(taken)

    def gather_next(self, arrived):
        quarter = waiting(self.quarter, arrived)
        self.half = jnp.stack([quarter, swap_with(quarter, "space", 1)])

    def gather_dp(self, arrived):
        half = waiting(self.half, arrived)
        return half, swap_with(half, "dp", 1)


def finish_kernel(factor, me_ref, half_ref, other_ref, *out_refs):
    side, near, place = me_ref[0], me_ref[1], me_ref[2]
    run = half_ref.shape[2]
    for which in range(2):
        blocks_ref, bias_ref = out_refs[2 * which : 2 * which + 2]
        edge = blocks_ref.shape[-1]
        for part in range(2):
            for piece in range(half_ref.shape[1]):
                spot = (part ^ near, piece ^ place)
                own = half_ref[spot].astype(jnp.float32)
                value = jnp.where(side == which, own, other_ref[spot].astype(jnp.float32)) * factor
                first = piece * run
                count = max(0, min(edge - first, run))
                for block in range(blocks_ref.shape[1]):
                    lanes = slice(block * edge, (block + 1) * edge)
                    if count > 0:
                        blocks_ref[part, block, pl.ds(first, count)] = value[:count, lanes]
                    if first <= edge < first + run:
                        row = edge - first
                        bias_ref[part, pl.ds(block, 1)] = value[row : row + 1, lanes]


def finish_sums(here, half, other, factor, weight_shape, bias_shape):
    outs = [weight_shape, bias_shape] * 2
    return pl.pallas_call(
        functools.partial(finish_kernel, factor),
        out_shape=[jax.ShapeDtypeStruct(shape, jnp.float32) for shape in outs],
        in_specs=[pl.BlockSpec(memory_space=pltpu.SMEM)]
        + [pl.BlockSpec(memory_space=pltpu.VMEM)] * 2,
        out_specs=[pl.BlockSpec(memory_space=pltpu.VMEM)] * 4,
        compiler_params=pltpu.CompilerParams(vmem_limit_bytes=16 * MIB),
        cost_estimate=pl.CostEstimate(flops=0, bytes_accessed=4 * MIB, transcendentals=0),
        name="finish_sums",
    )(here, half, other)


def body(fields, cotangent, w_first, b_first, w_second, b_second):
    samples, rows, width, channels = fields.shape
    owners = lax.axis_size("space")
    lat_total = rows * owners
    modes = KW // owners
    count, edge = w_first.shape[1:3]
    groups = 2
    direct = 2 * modes % 16 == 0
    lead = owners if direct else 1

    order = mixed_order(owners)

    def place(offset):
        return (owners - offset) % owners

    def send(blocks, offsets, taken):
        for offset in offsets:
            taken[offset] = swap_with(blocks[place(offset)], "space", offset)

    def listed(taken):
        return [taken[place(at)] for at in range(owners)]

    def send_all(spectrum):
        spectrum = spectrum.reshape(samples, rows, owners, 2 * modes, channels)
        spectrum = jnp.transpose(spectrum, (2, 0, 1, 3, 4))
        arrived = lax.all_to_all(spectrum, "space", split_axis=0, concat_axis=0, tiled=True)
        return [jnp.transpose(arrived, (1, 0, 2, 3, 4)).reshape(-1, channels)]

    def send_all_back(bands):
        bands = bands.reshape(samples, owners, rows, 2 * modes, channels)
        bands = jnp.transpose(bands, (1, 0, 2, 3, 4))
        arrived = lax.all_to_all(bands, "space", split_axis=0, concat_axis=0, tiled=True)
        return [jnp.transpose(arrived, (1, 2, 0, 3, 4)).reshape(1, -1, channels)]

    me = lax.axis_index("space") if direct else 0
    me = jnp.full((1,), me, jnp.int32)
    plain, scaled = lon_tables(KW, width, owners)
    lat = lat_spread(lat_total, modes)

    spectrum = to_modes(me, plain, fields, lead)
    spectrum, cotangent, w_first, w_second = lax.optimization_barrier(
        (spectrum, cotangent, w_first, w_second)
    )
    cot_spec = to_modes(me, scaled, cotangent, lead)
    w1, w2 = spread_weights(groups, w_first, w_second)
    b1, b2 = block_bias(b_first, groups), block_bias(b_second, groups)
    positions = samples * lax.axis_size("dp") * lat_total * KW
    factor = 1.0 / math.sqrt(positions)

    if not direct:
        gathered = send_all(spectrum[0])
        image, state = forward_mid(me, lat, lat.T, gathered, w1, b1, w2, b2)
        image_band = send_all_back(image[0])
        gathered = send_all(cot_spec[0])
        grad_image, sums = backward_mid(me, lat, lat.T, gathered, w1, b1, w2, b2, state, count)
        grad_band = send_all_back(grad_image[0])
        output = to_cells(me, scaled.T, image_band, fields)
        grad_fields = to_cells(me, plain.T, grad_band, cotangent)
        sums = lax.psum(sums, ("space", "dp")) * factor
        grads = []
        for which in range(2):
            blocks = sums[which, :, :edge].reshape(2, edge, count, edge)
            grads.append(jnp.transpose(blocks, (0, 2, 1, 3)))
            grads.append(sums[which, :, edge].reshape(b_first.shape))
        return (output, grad_fields) + tuple(grads)

    gathered, cot_gathered = {0: spectrum[0]}, {0: cot_spec[0]}
    falling = range(owners - 1, 0, -1)
    send(spectrum, falling[:FIRST], gathered)
    spectrum = waiting(list(spectrum), [cot_spec[0], w1, w2])
    send(spectrum, falling[FIRST:], gathered)
    gathered = listed(gathered)
    image, state = forward_mid(me, lat, lat.T, gathered, w1, b1, w2, b2)
    cot_spec, image = list(cot_spec), list(image)
    send(cot_spec, falling[:FIRST], cot_gathered)
    cot_spec, image = waiting((cot_spec, image), [image[0]])
    send(cot_spec, falling[FIRST:], cot_gathered)

    image_band = {0: image[0]}
    send(image, order, image_band)
    cot_gathered = listed(cot_gathered)
    grad_image, sums = backward_mid(
        me, lat, lat.T, cot_gathered, w1, b1, w2, b2, state, count
    )
    early = [image_band[offset] for offset in order[:HELD]]
    late = [image_band[offset] for offset in order[HELD:]]
    grad_image, sums = waiting((list(grad_image), sums), early)
    group_sum = GroupSum(sums)
    group_sum.over_dp()
    group_sum.over_next(early)
    grad_band = {0: grad_image[0]}
    send(grad_image, order, grad_band)
    arrived = [grad_band[offset] for offset in order]
    image_band = listed(image_band)
    grad_band = listed(grad_band)
    again = waiting(fields, early[:1])
    output = rows_inside(to_cells(me, scaled.T, image_band, again))
    group_sum.scatter(late + arrived[:1])
    group_sum.gather(arrived[1:3])
    group_sum.gather_next(arrived[3:5])
    group_sum.half, output = lax.optimization_barrier((group_sum.half, output))
    half, other = group_sum.gather_dp(arrived[5:])
    near = lax.axis_index("space")
    here = jnp.stack([lax.axis_index("dp"), near % 2, near // 2]).astype(jnp.int32)
    grads = finish_sums(here, half, other, factor, w_first.shape, b_first.shape)
    grad_fields = rows_inside(to_cells(me, plain.T, grad_band, cotangent))
    return (rows_outside(output), rows_outside(grad_fields)) + tuple(grads)


def solution(mesh):
    split = P(("parts", "dp"), "space", None, None)
    in_specs = (split, split, P(), P(), P(), P())
    out_specs = (
        split,
        split,
        P("parts", None, None, None),
        P("parts", None, None),
        P("parts", None, None, None),
        P("parts", None, None),
    )
    return jax.shard_map(body, mesh=mesh, in_specs=in_specs, out_specs=out_specs, check_vma=False)
```
